32 devices in a mesh: grp: 2 (over y), chan: 2 (over x), tm: 4 (over z), pol: 2 (over core).
Axes of the slice: x: 2, y: 2, z: 4, core: 2. Of those that a mesh axis runs over, the one named last changes fastest.
Arguments:
- voltages: bfloat16 [4, 2, 256, 32768], P('grp', 'pol', 'chan', 'tm'), parts along dimension 0, may hold values from -6 to 6
- taps_filter: float32 [16, 2048], replicated, may hold values from -1.5 to 1.5
- tile_a: int32 [14, 64], replicated, may hold values from 0 to 255
- tile_b: int32 [14, 64], replicated, may hold values from 0 to 255
- tile_owner: int32 [14], replicated, may hold values from 0 to 1, as said below
- tile_flags: int32 [14, 16], replicated, may hold values 0 or 1
Outputs:
- visibility: float32 [16, 256, 4, 2, 64, 128], P('pol', ('chan', 'tm'), 'grp'), parts along dimension 2
The draws below stay inside these ranges and needn't reach their ends.
There are 2 independent parts, one for each index of `grp`. The reference program is written for one: setup_inputs(seed, part) draws one part's arguments, and reference() takes and returns one part's arrays. A program takes and returns all parts, laid end to end along the dimension named above; an argument that names none is the same for every part. Nothing has to cross between parts.
Inputs may be any that keep to these rules, and one draw needn't show every extreme that they name: `tile_owner`: one owner holds exactly 8 tiles and the other owner holds all the rest.
All inputs are finite; a program needn't handle non-finite values.
Results may differ from the reference program's by a relative error of at most 0.0035.
Values may be sent and summed in bfloat16 or wider, within the bound.
No kernel may reach another device: no remote copies, remote signals or barrier semaphores. Data moves between devices by JAX's collectives and lax.ppermute only.
A program may use at most 128 MiB of HBM per device.

```python
import math
import jax
import jax.numpy as jnp
from jax import lax

S = 256
C = 2048
TAPS = 16
AVG = 8
TS = 64
NTILE = 14
CAP = 8
T_SIZE = 16
GROUPS = 256
N_POL = 2


def draw_tile_owner(key, part):
    heavier = jax.random.randint(jax.random.fold_in(key, 11), (), 0, 2)
    order = jax.random.permutation(jax.random.fold_in(key, 12), NTILE)
    ranked = jnp.where(jnp.arange(NTILE) < CAP, heavier, 1 - heavier)
    return jnp.take(ranked, order).astype(jnp.int32)


def set_ends(drawn, key, least, largest):
    spot = [jax.random.randint(jax.random.fold_in(key, axis), (), 0, length) for axis, length in enumerate(drawn.shape)]
    longest = drawn.shape.index(max(drawn.shape))
    neighbour = spot[:longest] + [(spot[longest] + 1) % drawn.shape[longest]] + spot[longest + 1:]
    return drawn.at[tuple(spot)].set(least).at[tuple(neighbour)].set(largest)


def block_scale(key, extent, shards, smallest, high):
    gain, own = 1.0, jax.random.fold_in(key, 6)
    for axis_at, blocks in shards:
        steps = jnp.exp(jax.random.uniform(jax.random.fold_in(own, axis_at), (blocks,), jnp.float32, smallest / len(shards), high / len(shards)))
        gain = gain * jnp.repeat(steps, extent[axis_at] // blocks).reshape([-1 if axis == axis_at else 1 for axis in range(len(extent))])
    return gain


def noise(own_key, dims, deviation, limit, split=(), held_as=jnp.bfloat16):
    values = deviation * jax.random.normal(own_key, dims, jnp.float32)
    if split:
        values = values * block_scale(own_key, dims, split, -0.22, 0.18)
    return jnp.clip(values, -limit, limit).astype(held_as)


def setup_inputs(seed: int = 0, part: int = 0) -> dict:
    key_of = jax.random.split(jax.random.key(seed), 7)
    part_keys = jax.random.split(jax.random.fold_in(key_of[6], part), 7)
    return {
        "voltages": noise(part_keys[0], (2, 2, S, T_SIZE * C), 1.0, 6.0, ((1, 2), (2, 2), (3, 4))),
        "taps_filter": noise(key_of[1], (TAPS, C), TAPS ** -0.5, 1.5, (), jnp.float32),
        "tile_a": set_ends(jax.random.randint(key_of[2], (NTILE, TS), 0, S), jax.random.fold_in(key_of[2], 1), 0, S - 1).astype(jnp.int32),
        "tile_b": set_ends(jax.random.randint(key_of[3], (NTILE, TS), 0, S), jax.random.fold_in(key_of[3], 1), 0, S - 1).astype(jnp.int32),
        "tile_owner": draw_tile_owner(jax.random.fold_in(key_of[6], 71), part),
        "tile_flags": set_ends((jax.random.randint(key_of[5], (NTILE, T_SIZE), 0, 4) < 3).astype(jnp.int32), jax.random.fold_in(key_of[5], 1), 0, 1),
    }


def station_spectra(samples, taps_filter):
    blocks = samples.astype(jnp.float32).reshape(2, 2, T_SIZE, C)
    padded = jnp.pad(blocks, ((0, 0), (0, 0), (TAPS - 1, 0), (0, 0)))
    filtered = jnp.zeros((2, 2, T_SIZE, C), jnp.float32)
    for tap_index in range(TAPS):
        start = TAPS - 1 - tap_index
        filtered = filtered + taps_filter[tap_index] * padded[:, :, start:start + T_SIZE]
    transformed = jnp.fft.fft(filtered[0] + 1j * filtered[1], axis=-1) / math.sqrt(C)
    return jnp.stack([jnp.real(transformed), jnp.imag(transformed)]).astype(jnp.bfloat16)

def tile_result(arranged, rows_a, rows_b, flags):
    weight = jnp.tile(flags.astype(jnp.bfloat16), AVG)
    left_rows = (jnp.take(arranged, rows_a, axis=2) * weight).astype(jnp.float32)
    right_rows = jnp.take(arranged, rows_b, axis=2).astype(jnp.float32)
    exact_mode = lax.Precision.HIGHEST
    form = 'pank,qbnk->npaqb'
    real_part = jnp.einsum(form, left_rows[0], right_rows[0], precision=exact_mode) + jnp.einsum(form, left_rows[1], right_rows[1], precision=exact_mode)
    imag_part = jnp.einsum(form, left_rows[1], right_rows[0], precision=exact_mode) - jnp.einsum(form, left_rows[0], right_rows[1], precision=exact_mode)
    result = jnp.stack([real_part, imag_part], axis=1) * (1.0 / (AVG * T_SIZE))
    return result.reshape(GROUPS, 2, 2, TS, 2 * TS)

def reference(voltages, taps_filter, tile_a, tile_b, tile_owner, tile_flags):
    by_station = jnp.moveaxis(voltages, 2, 0)
    spectra = lax.map(lambda samples: station_spectra(samples, taps_filter), by_station)
    arranged = spectra.reshape(S, 2, 2, T_SIZE, GROUPS, AVG)
    arranged = arranged.transpose(1, 2, 0, 4, 5, 3).reshape(2, 2, S, GROUPS, AVG * T_SIZE)
    tile_results = lax.map(lambda items: tile_result(arranged, items[0], items[1], items[2]), (tile_a, tile_b, tile_flags))
    slots = []
    for holder in range(N_POL):
        chosen = tile_owner == holder
        listed = jnp.nonzero(chosen, size=CAP, fill_value=0)[0].astype(jnp.int32)
        tally = jnp.sum(chosen.astype(jnp.int32))
        active = jnp.arange(CAP, dtype=jnp.int32) < tally
        picked = jnp.take(tile_results, listed, axis=0)
        slots.append(jnp.where(active[:, None, None, None, None, None], picked, jnp.zeros_like(picked)))
    return jnp.concatenate(slots, axis=0)
```

```python
import math

import jax
import jax.numpy as jnp
import numpy as np
from jax import lax
from jax.experimental import pallas as pl
from jax.experimental.pallas import tpu as pltpu
from jax.sharding import PartitionSpec as P

AVG = 8
CAP = 8
RADIX = 16
LANES = 128
ROWS = 16


radix_first = 32


def from_behind(value, axis, steps):
    count = lax.axis_size(axis)
    first, last = (max(0, -steps), min(count, count - steps))
    return lax.ppermute(value, axis, [(source, source + steps) for source in range(first, last)])


def fourier(filtered):
    length = filtered.shape[-1]
    second = length // radix_first
    exact_mode = lax.Precision.HIGHEST
    grid = filtered.reshape(filtered.shape[:-1] + (radix_first, second))
    outer = jnp.arange(radix_first, dtype=jnp.int32)
    inner = jnp.arange(second, dtype=jnp.int32)
    phase_one = (
        2.0
        * math.pi
        / radix_first
        * (outer[:, None] * outer[None, :] % radix_first).astype(jnp.float32)
    )
    phase_twist = 2.0 * math.pi / length * (outer[:, None] * inner[None, :]).astype(jnp.float32)
    phase_two = (
        2.0 * math.pi / second * (inner[:, None] * inner[None, :] % second).astype(jnp.float32)
    )
    cos_one, sin_one = (jnp.cos(phase_one), jnp.sin(phase_one))
    cos_twist, sin_twist = (jnp.cos(phase_twist), jnp.sin(phase_twist))
    cos_two, sin_two = (jnp.cos(phase_two), jnp.sin(phase_two))
    first_form = "fk,stkj->stfj"
    section_re = jnp.einsum(first_form, cos_one, grid[0], precision=exact_mode) + jnp.einsum(
        first_form, sin_one, grid[1], precision=exact_mode
    )
    section_im = jnp.einsum(first_form, cos_one, grid[1], precision=exact_mode) - jnp.einsum(
        first_form, sin_one, grid[0], precision=exact_mode
    )
    turned_re = section_re * cos_twist + section_im * sin_twist
    turned_im = section_im * cos_twist - section_re * sin_twist
    second_form = "gj,stfj->stgf"
    final_re = jnp.einsum(second_form, cos_two, turned_re, precision=exact_mode) + jnp.einsum(
        second_form, sin_two, turned_im, precision=exact_mode
    )
    final_im = jnp.einsum(second_form, cos_two, turned_im, precision=exact_mode) - jnp.einsum(
        second_form, sin_two, turned_re, precision=exact_mode
    )
    joined = jnp.stack([final_re, final_im]).reshape(filtered.shape)
    return joined * (1.0 / math.sqrt(length))


def correlate(full, rows_a, rows_b, flags, group_count):
    depth = full.shape[4]
    weight = jnp.tile(flags.astype(jnp.bfloat16), depth // flags.shape[0])
    left_rows = jnp.take(full, rows_a, axis=2) * weight
    right_rows = jnp.take(full, rows_b, axis=2)
    stacked_left = jnp.stack(
        [
            jnp.concatenate([left_rows[0], left_rows[1]], axis=-1),
            jnp.concatenate([left_rows[1], -left_rows[0]], axis=-1),
        ]
    )
    joined_right = jnp.concatenate([right_rows[0], right_rows[1]], axis=-1)
    result = jnp.einsum(
        "rpank,qbnk->nrpaqb", stacked_left, joined_right, preferred_element_type=jnp.float32
    )
    width = rows_a.shape[0]
    return result.reshape(group_count, 2, 2, width, 2 * width) * (1.0 / depth)


def on_device_any(voltages, taps_filter, tile_a, tile_b, tile_owner, tile_flags):
    history = taps_filter.shape[0] - 1
    length = taps_filter.shape[1]
    stations = voltages.shape[2]
    frames = voltages.shape[3] // length
    local_blocks = voltages.reshape(2, stations, frames, length)
    hop_count = -(-history // frames)
    sending = local_blocks
    extended = local_blocks
    for hop_index in range(hop_count):
        sending = from_behind(sending, "tm", 1)
        extended = jnp.concatenate([sending, extended], axis=2)
    extended = extended[:, :, extended.shape[2] - history - frames :]
    filtered = jnp.zeros((2, stations, frames, length), jnp.float32)
    for tap_index in range(history + 1):
        start = history - tap_index
        filtered = filtered + taps_filter[tap_index] * extended[
            :, :, start : start + frames
        ].astype(jnp.float32)
    spectra = fourier(filtered).astype(jnp.bfloat16)
    chan_count = lax.axis_size("chan")
    time_count = lax.axis_size("tm")
    narrow = length // (chan_count * time_count)
    outgoing = spectra.reshape(2, stations, frames, chan_count, time_count, narrow)
    outgoing = outgoing.transpose(0, 3, 4, 5, 1, 2)
    flat = outgoing.reshape(2, chan_count * time_count, narrow, stations * frames)
    moved = lax.all_to_all(flat, ("chan", "tm"), split_axis=1, concat_axis=1, tiled=True)
    moved = moved.reshape(2, chan_count, time_count, narrow, stations, frames)
    bands = narrow // AVG
    every_station = chan_count * stations
    spectra_count = time_count * frames
    arranged = moved.transpose(0, 1, 4, 3, 2, 5).reshape(
        2, 1, every_station, bands, AVG * spectra_count
    )
    full = lax.all_gather(arranged, "pol", axis=1, tiled=True)
    position = lax.axis_index("pol")
    width = tile_a.shape[1]
    capacity = CAP
    held = tile_owner == position
    listed = jnp.nonzero(held, size=capacity, fill_value=0)[0].astype(jnp.int32)
    tally = jnp.sum(held.astype(jnp.int32))
    initial = jnp.zeros((capacity, bands, 2, 2, width, 2 * width), jnp.float32)

    def fill_slot(slot, results):
        chosen_tile = listed[slot]
        return results.at[slot].set(
            correlate(
                full, tile_a[chosen_tile], tile_b[chosen_tile], tile_flags[chosen_tile], bands
            )
        )

    visibility = lax.fori_loop(0, tally, fill_slot, initial)
    return visibility


def fourier_tables(length):
    low = np.arange(RADIX)
    lane = np.arange(LANES)
    turn = 2.0 * np.pi / length * np.outer(low, lane)
    twiddle = np.stack([np.cos(turn), np.sin(turn)]).astype(np.float32)
    angle = 2.0 * np.pi / LANES * (np.outer(lane, lane) % LANES)
    cos, sin = np.cos(angle) / math.sqrt(length), np.sin(angle) / math.sqrt(length)
    matrix = np.block([[cos, sin], [-sin, cos]]).astype(np.float32)
    high = matrix.astype(jnp.bfloat16)
    rest = (matrix - high.astype(np.float32)).astype(jnp.bfloat16)
    return twiddle, np.stack([high, rest])


def butterflies(values):
    count = len(values)
    if count == 1:
        return values
    even, odd = butterflies(values[0::2]), butterflies(values[1::2])
    first, second = [], []
    for index in range(count // 2):
        (a, b), (c, d) = even[index], odd[index]
        if index == 0:
            e, f = c, d
        elif 4 * index == count:
            e, f = d, -c
        elif 8 * index == count:
            root = math.sqrt(0.5)
            e, f = (c + d) * root, (d - c) * root
        elif 8 * index == 3 * count:
            root = math.sqrt(0.5)
            e, f = (d - c) * root, -(c + d) * root
        else:
            turn = 2.0 * math.pi * index / count
            cos, sin = math.cos(turn), math.sin(turn)
            e, f = c * cos + d * sin, d * cos - c * sin
        first.append((a + e, b + f))
        second.append((a - e, b - f))
    return first + second


def channelise_kernel(
    frames, x_ref, taps_ref, twiddle_ref, matrix_ref, out_ref, fil_ref, zr_ref, zi_ref, w_ref
):
    sources = x_ref.shape[0]
    spectra = sources * frames
    length = taps_ref.shape[1]
    taps = taps_ref.shape[0]
    depth = RADIX * spectra
    z_refs = (zr_ref, zi_ref)

    @pl.loop(0, RADIX)
    def _(section):
        at = pl.multiple_of(section * LANES, LANES)
        weights = [taps_ref[pl.ds(m, 1), pl.ds(at, LANES)] for m in range(taps)]
        for part in range(2):
            blocks = []
            for t in range(spectra):
                lane = pl.multiple_of((t % frames) * length + section * LANES, LANES)
                blocks.append(x_ref[t // frames, part, :, pl.ds(lane, LANES)].astype(jnp.float32))
            for t in range(spectra):
                total = weights[0] * blocks[t]
                for m in range(1, min(t + 1, taps)):
                    total = total + weights[m] * blocks[t - m]
                fil_ref[section, t, part] = total

    @pl.loop(0, spectra)
    def _(t):
        for half in range(ROWS // 8):
            values = [
                tuple(fil_ref[section, t, part, pl.ds(half * 8, 8), :] for part in range(2))
                for section in range(RADIX)
            ]
            for low, (re, im) in enumerate(butterflies(values)):
                if low:
                    cos = twiddle_ref[0, pl.ds(low, 1), :]
                    sin = twiddle_ref[1, pl.ds(low, 1), :]
                    re, im = re * cos + im * sin, im * cos - re * sin
                rows = pl.ds(half * 8 * depth + low * spectra + t, 8, stride=depth)
                zr_ref[rows, :] = re
                zi_ref[rows, :] = im

    form = (((1,), (1,)), ((), ()))
    high_matrix, low_matrix = matrix_ref[0], matrix_ref[1]
    halves = depth // LANES

    @pl.loop(0, ROWS)
    def _(station):
        rows = pl.ds(pl.multiple_of(station * depth, depth), depth)
        value = jnp.concatenate([ref[rows, :] for ref in z_refs], axis=1)
        high = value.astype(jnp.bfloat16)
        rest = (value - high.astype(jnp.float32)).astype(jnp.bfloat16)
        total = lax.dot_general(high_matrix, high, form, preferred_element_type=jnp.float32)
        total += lax.dot_general(high_matrix, rest, form, preferred_element_type=jnp.float32)
        total += lax.dot_general(low_matrix, high, form, preferred_element_type=jnp.float32)
        for half in range(halves):
            for part in range(2):
                rows = pl.ds((half * 2 + part) * ROWS + station, LANES, stride=halves * 2 * ROWS)
                w_ref[rows, :] = total[
                    part * LANES : (part + 1) * LANES, half * LANES : (half + 1) * LANES
                ]

    piece = 256

    @pl.loop(0, out_ref.shape[0] // piece)
    def _(index):
        rows = pl.ds(pl.multiple_of(index * piece, piece), piece)
        out_ref[rows, :] = w_ref[rows, :].astype(jnp.bfloat16)


def channelise(blocks, taps_filter, tables, frames):
    sources = blocks.shape[0]
    length = taps_filter.shape[1]
    spectra = sources * frames
    twiddle, matrix = tables
    out_rows = length // AVG * 2 * ROWS
    whole = pl.BlockSpec(memory_space=pltpu.VMEM)
    flat = pl.pallas_call(
        lambda *refs: channelise_kernel(frames, *refs),
        out_shape=jax.ShapeDtypeStruct((out_rows, LANES), jnp.bfloat16),
        in_specs=[whole] * 4,
        out_specs=whole,
        scratch_shapes=[
            pltpu.VMEM((RADIX, spectra, 2, ROWS, LANES), jnp.float32),
            pltpu.VMEM((ROWS * RADIX * spectra, LANES), jnp.float32),
            pltpu.VMEM((ROWS * RADIX * spectra, LANES), jnp.float32),
            pltpu.VMEM((out_rows, LANES), jnp.float32),
        ],
        compiler_params=pltpu.CompilerParams(vmem_limit_bytes=40 * 2**20),
        cost_estimate=pl.CostEstimate(
            flops=9 * 10**9, bytes_accessed=4 * 2**20, transcendentals=0
        ),
        name="channelise",
    )(blocks, taps_filter, jnp.asarray(twiddle), jnp.asarray(matrix))
    return flat.reshape(length // AVG, 2, ROWS, LANES)


def correlate_kernel(chunks, width, *refs):
    sel_ref, weight_ref = refs[:2]
    x_refs = refs[2 : 2 + chunks]
    out_ref, x_all, rows_all = refs[2 + chunks :]
    tiles = out_ref.shape[0]
    chunk_rows = x_all.shape[0] // chunks
    for chunk, x_ref in enumerate(x_refs):
        for pol in range(2):
            for part in range(2):
                x_all[
                    chunk * chunk_rows : (chunk + 1) * chunk_rows,
                    (pol * 2 + part) * LANES : (pol * 2 + part + 1) * LANES,
                ] = x_ref[pol, :, 0, part].reshape(chunk_rows, LANES)
    step = 2
    for first in range(0, tiles, step):
        rows = slice(first * 2 * width, (first + step) * 2 * width)
        picked = jnp.dot(sel_ref[rows, :], x_all[...], preferred_element_type=jnp.float32)
        for tile in range(first, first + step):
            base = (tile - first) * 2 * width
            left = picked[base : base + width] * weight_ref[pl.ds(tile, 1), :]
            right = picked[base + width : base + 2 * width]
            rows_all[tile * 2 * width : tile * 2 * width + width, :] = left.astype(jnp.bfloat16)
            rows_all[tile * 2 * width + width : (tile + 1) * 2 * width, :] = right.astype(
                jnp.bfloat16
            )
    form = (((1,), (1,)), ((), ()))
    for tile in range(tiles):
        at = tile * 2 * width
        left = jnp.concatenate(
            [rows_all[at : at + width, pol * 2 * LANES : (pol + 1) * 2 * LANES] for pol in range(2)]
        )
        at += width
        right = jnp.concatenate(
            [rows_all[at : at + width, pol * 2 * LANES : (pol + 1) * 2 * LANES] for pol in range(2)]
        )
        turned = jnp.concatenate([-right[:, LANES:], right[:, :LANES]], axis=1)
        both = jnp.concatenate([right, turned])
        result = lax.dot_general(left, both, form, preferred_element_type=jnp.float32)
        for part in range(2):
            out_ref[tile, 0, part] = result[:, part * 2 * width : (part + 1) * 2 * width].reshape(
                2, width, 2 * width
            )


def correlate_tiles(chunks, select, weight, width):
    sources, bands = chunks[0].shape[1:3]
    tiles = weight.shape[0]
    block = (2, sources, 1, 2, ROWS, LANES)
    station_rows = len(chunks) * sources * ROWS
    return pl.pallas_call(
        lambda *refs: correlate_kernel(len(chunks), width, *refs),
        grid=(bands,),
        out_shape=jax.ShapeDtypeStruct((tiles, bands, 2, 2, width, 2 * width), jnp.float32),
        in_specs=[
            pl.BlockSpec(select.shape, lambda g: (0, 0)),
            pl.BlockSpec(weight.shape, lambda g: (0, 0)),
        ]
        + [pl.BlockSpec(block, lambda g: (0, 0, g, 0, 0, 0))] * len(chunks),
        out_specs=pl.BlockSpec(
            (tiles, 1, 2, 2, width, 2 * width), lambda g: (0, g, 0, 0, 0, 0)
        ),
        scratch_shapes=[
            pltpu.VMEM((station_rows, 4 * LANES), jnp.bfloat16),
            pltpu.VMEM((tiles * 2 * width, 4 * LANES), jnp.bfloat16),
        ],
        compiler_params=pltpu.CompilerParams(vmem_limit_bytes=32 * 2**20),
        cost_estimate=pl.CostEstimate(
            flops=13 * 10**9, bytes_accessed=42 * 2**20, transcendentals=0
        ),
        name="correlate",
    )(select, weight, *chunks)


def tile_tables(tile_a, tile_b, tile_owner, tile_flags, row_of):
    tiles = tile_owner.shape[0]
    held = tile_owner == lax.axis_index("pol")
    order = jnp.arange(tiles, dtype=jnp.int32)
    rank = jnp.sum((held[None, :] & (order[None, :] < order[:, None])).astype(jnp.int32), axis=1)
    slots = jnp.arange(CAP, dtype=jnp.int32)
    pick = (held[None, :] & (rank[None, :] == slots[:, None])).astype(jnp.int32)
    sides = jnp.stack([row_of(tile_a), row_of(tile_b)], axis=1) + 1
    rows = jnp.sum(pick[:, :, None, None] * sides[None], axis=1) - 1
    flags = jnp.sum(pick[:, :, None] * tile_flags[None], axis=1).astype(jnp.float32)
    return rows, flags


def on_device_chunks(voltages, taps_filter, tile_a, tile_b, tile_owner, tile_flags):
    length = taps_filter.shape[1]
    stations = voltages.shape[2]
    frames = voltages.shape[3] // length
    chan_count, time_count = lax.axis_size("chan"), lax.axis_size("tm")
    owners = chan_count * time_count
    chunk_count = stations // (time_count * ROWS)
    width = tile_a.shape[1]
    bands = length // AVG // owners
    tables = fourier_tables(length)

    def row_of(station):
        column = station // stations
        rest = station % stations
        block, inside = rest // (chunk_count * ROWS), rest % (chunk_count * ROWS)
        source = column * time_count + block
        return (inside // ROWS) * (owners * ROWS) + source * ROWS + inside % ROWS

    rows, flags = tile_tables(tile_a, tile_b, tile_owner, tile_flags, row_of)
    total_rows = chunk_count * owners * ROWS
    select = (rows[..., None] == jnp.arange(total_rows, dtype=jnp.int32)).astype(jnp.bfloat16)
    select = select.reshape(CAP * 2 * width, total_rows)
    depth = AVG * time_count * frames
    weight = jnp.tile(flags * (1.0 / depth), (1, 4 * AVG))

    pieces = voltages.reshape(2, time_count, chunk_count, ROWS, frames * length)
    received = []
    for chunk in range(chunk_count):
        sending = pieces[:, :, chunk].transpose(1, 0, 2, 3)
        blocks = lax.all_to_all(sending, "tm", split_axis=0, concat_axis=0, tiled=True)
        spectra = channelise(blocks, taps_filter, tables, frames)
        spectra = spectra.reshape(owners, bands, 2, ROWS, LANES)
        moved = lax.all_to_all(spectra, ("chan", "tm"), split_axis=0, concat_axis=0, tiled=True)
        received.append(lax.all_gather(moved, "pol", axis=0, tiled=False))
    return correlate_tiles(received, select, weight, width)


def on_device(voltages, taps_filter, tile_a, tile_b, tile_owner, tile_flags):
    taps, length = taps_filter.shape
    frames = voltages.shape[3] // length
    time_count = lax.axis_size("tm")
    fits = (
        length == RADIX * LANES
        and AVG * time_count * frames == LANES
        and voltages.shape[2] % (time_count * ROWS) == 0
        and 2 * tile_a.shape[1] == LANES
    )
    form = on_device_chunks if fits else on_device_any
    return form(voltages, taps_filter, tile_a, tile_b, tile_owner, tile_flags)


def solution(mesh):
    return jax.shard_map(
        on_device,
        mesh=mesh,
        in_specs=(P("grp", "pol", "chan", "tm"), P(), P(), P(), P(), P()),
        out_specs=P("pol", ("chan", "tm"), "grp", None, None, None),
        check_vma=False,
    )
```

```python
import math

import jax
import jax.numpy as jnp
import numpy as np
from jax import lax
from jax.experimental import pallas as pl
from jax.experimental.pallas import tpu as pltpu
from jax.sharding import PartitionSpec as P

AVG = 8
CAP = 8
RADIX = 16
LANES = 128
ROWS = 16


radix_first = 32


def from_behind(value, axis, steps):
    count = lax.axis_size(axis)
    first, last = (max(0, -steps), min(count, count - steps))
    return lax.ppermute(value, axis, [(source, source + steps) for source in range(first, last)])


def fourier(filtered):
    length = filtered.shape[-1]
    second = length // radix_first
    exact_mode = lax.Precision.HIGHEST
    grid = filtered.reshape(filtered.shape[:-1] + (radix_first, second))
    outer = jnp.arange(radix_first, dtype=jnp.int32)
    inner = jnp.arange(second, dtype=jnp.int32)
    phase_one = (
        2.0
        * math.pi
        / radix_first
        * (outer[:, None] * outer[None, :] % radix_first).astype(jnp.float32)
    )
    phase_twist = 2.0 * math.pi / length * (outer[:, None] * inner[None, :]).astype(jnp.float32)
    phase_two = (
        2.0 * math.pi / second * (inner[:, None] * inner[None, :] % second).astype(jnp.float32)
    )
    cos_one, sin_one = (jnp.cos(phase_one), jnp.sin(phase_one))
    cos_twist, sin_twist = (jnp.cos(phase_twist), jnp.sin(phase_twist))
    cos_two, sin_two = (jnp.cos(phase_two), jnp.sin(phase_two))
    first_form = "fk,stkj->stfj"
    section_re = jnp.einsum(first_form, cos_one, grid[0], precision=exact_mode) + jnp.einsum(
        first_form, sin_one, grid[1], precision=exact_mode
    )
    section_im = jnp.einsum(first_form, cos_one, grid[1], precision=exact_mode) - jnp.einsum(
        first_form, sin_one, grid[0], precision=exact_mode
    )
    turned_re = section_re * cos_twist + section_im * sin_twist
    turned_im = section_im * cos_twist - section_re * sin_twist
    second_form = "gj,stfj->stgf"
    final_re = jnp.einsum(second_form, cos_two, turned_re, precision=exact_mode) + jnp.einsum(
        second_form, sin_two, turned_im, precision=exact_mode
    )
    final_im = jnp.einsum(second_form, cos_two, turned_im, precision=exact_mode) - jnp.einsum(
        second_form, sin_two, turned_re, precision=exact_mode
    )
    joined = jnp.stack([final_re, final_im]).reshape(filtered.shape)
    return joined * (1.0 / math.sqrt(length))


def correlate(full, rows_a, rows_b, flags, group_count):
    depth = full.shape[4]
    weight = jnp.tile(flags.astype(jnp.bfloat16), depth // flags.shape[0])
    left_rows = jnp.take(full, rows_a, axis=2) * weight
    right_rows = jnp.take(full, rows_b, axis=2)
    stacked_left = jnp.stack(
        [
            jnp.concatenate([left_rows[0], left_rows[1]], axis=-1),
            jnp.concatenate([left_rows[1], -left_rows[0]], axis=-1),
        ]
    )
    joined_right = jnp.concatenate([right_rows[0], right_rows[1]], axis=-1)
    result = jnp.einsum(
        "rpank,qbnk->nrpaqb", stacked_left, joined_right, preferred_element_type=jnp.float32
    )
    width = rows_a.shape[0]
    return result.reshape(group_count, 2, 2, width, 2 * width) * (1.0 / depth)


def on_device_any(voltages, taps_filter, tile_a, tile_b, tile_owner, tile_flags):
    history = taps_filter.shape[0] - 1
    length = taps_filter.shape[1]
    stations = voltages.shape[2]
    frames = voltages.shape[3] // length
    local_blocks = voltages.reshape(2, stations, frames, length)
    hop_count = -(-history // frames)
    sending = local_blocks
    extended = local_blocks
    for hop_index in range(hop_count):
        sending = from_behind(sending, "tm", 1)
        extended = jnp.concatenate([sending, extended], axis=2)
    extended = extended[:, :, extended.shape[2] - history - frames :]
    filtered = jnp.zeros((2, stations, frames, length), jnp.float32)
    for tap_index in range(history + 1):
        start = history - tap_index
        filtered = filtered + taps_filter[tap_index] * extended[
            :, :, start : start + frames
        ].astype(jnp.float32)
    spectra = fourier(filtered).astype(jnp.bfloat16)
    chan_count = lax.axis_size("chan")
    time_count = lax.axis_size("tm")
    narrow = length // (chan_count * time_count)
    outgoing = spectra.reshape(2, stations, frames, chan_count, time_count, narrow)
    outgoing = outgoing.transpose(0, 3, 4, 5, 1, 2)
    flat = outgoing.reshape(2, chan_count * time_count, narrow, stations * frames)
    moved = lax.all_to_all(flat, ("chan", "tm"), split_axis=1, concat_axis=1, tiled=True)
    moved = moved.reshape(2, chan_count, time_count, narrow, stations, frames)
    bands = narrow // AVG
    every_station = chan_count * stations
    spectra_count = time_count * frames
    arranged = moved.transpose(0, 1, 4, 3, 2, 5).reshape(
        2, 1, every_station, bands, AVG * spectra_count
    )
    full = lax.all_gather(arranged, "pol", axis=1, tiled=True)
    position = lax.axis_index("pol")
    width = tile_a.shape[1]
    capacity = CAP
    held = tile_owner == position
    listed = jnp.nonzero(held, size=capacity, fill_value=0)[0].astype(jnp.int32)
    tally = jnp.sum(held.astype(jnp.int32))
    initial = jnp.zeros((capacity, bands, 2, 2, width, 2 * width), jnp.float32)

    def fill_slot(slot, results):
        chosen_tile = listed[slot]
        return results.at[slot].set(
            correlate(
                full, tile_a[chosen_tile], tile_b[chosen_tile], tile_flags[chosen_tile], bands
            )
        )

    visibility = lax.fori_loop(0, tally, fill_slot, initial)
    return visibility


def fourier_tables(length):
    low = np.arange(RADIX)
    lane = np.arange(LANES)
    turn = 2.0 * np.pi / length * np.outer(low, lane)
    twiddle = np.stack([np.cos(turn), np.sin(turn)]).astype(np.float32)
    angle = 2.0 * np.pi / LANES * (np.outer(lane, lane) % LANES)
    cos, sin = np.cos(angle) / math.sqrt(length), np.sin(angle) / math.sqrt(length)
    matrix = np.block([[cos, sin], [-sin, cos]]).astype(np.float32)
    high = matrix.astype(jnp.bfloat16)
    rest = (matrix - high.astype(np.float32)).astype(jnp.bfloat16)
    return twiddle, np.stack([high, rest])


def butterflies(values):
    count = len(values)
    if count == 1:
        return values
    even, odd = butterflies(values[0::2]), butterflies(values[1::2])
    first, second = [], []
    for index in range(count // 2):
        (a, b), (c, d) = even[index], odd[index]
        if index == 0:
            e, f = c, d
        elif 4 * index == count:
            e, f = d, -c
        elif 8 * index == count:
            root = math.sqrt(0.5)
            e, f = (c + d) * root, (d - c) * root
        elif 8 * index == 3 * count:
            root = math.sqrt(0.5)
            e, f = (d - c) * root, -(c + d) * root
        else:
            turn = 2.0 * math.pi * index / count
            cos, sin = math.cos(turn), math.sin(turn)
            e, f = c * cos + d * sin, d * cos - c * sin
        first.append((a + e, b + f))
        second.append((a - e, b - f))
    return first + second


def channelise_kernel(frames, chunk, place_ref, own_ref, *refs):
    sources = refs[-6].shape[0]
    come_refs = refs[: sources - 1]
    taps_ref, twiddle_ref, matrix_ref = refs[sources - 1 : sources + 2]
    out_refs = refs[sources + 2 : -6]
    x_ref, fil_ref, zr_ref, zi_ref, w_ref, sems = refs[-6:]
    chan, tm = place_ref[0], place_ref[1]
    columns = len(out_refs) // sources
    own_rows = pl.multiple_of((tm * (own_ref.shape[1] // (sources * ROWS)) + chunk) * ROWS, ROWS)
    copies = []
    for behind in range(sources):
        block = come_refs[behind - 1] if behind else own_ref.at[:, pl.ds(own_rows, ROWS), :]
        slot = lax.rem(tm - behind + sources, sources)
        copies.append(pltpu.make_async_copy(block, x_ref.at[slot], sems.at[behind]))
    for copy in copies:
        copy.start()
    for copy in copies:
        copy.wait()
    spectra = sources * frames
    length = taps_ref.shape[1]
    taps = taps_ref.shape[0]
    depth = RADIX * spectra
    z_refs = (zr_ref, zi_ref)

    @pl.loop(0, RADIX)
    def _(section):
        at = pl.multiple_of(section * LANES, LANES)
        weights = [taps_ref[pl.ds(m, 1), pl.ds(at, LANES)] for m in range(taps)]
        for part in range(2):
            blocks = []
            for t in range(spectra):
                lane = pl.multiple_of((t % frames) * length + section * LANES, LANES)
                blocks.append(x_ref[t // frames, part, :, pl.ds(lane, LANES)].astype(jnp.float32))
            for t in range(spectra):
                total = weights[0] * blocks[t]
                for m in range(1, min(t + 1, taps)):
                    total = total + weights[m] * blocks[t - m]
                fil_ref[section, t, part] = total

    @pl.loop(0, spectra)
    def _(t):
        for half in range(ROWS // 8):
            values = [
                tuple(fil_ref[section, t, part, pl.ds(half * 8, 8), :] for part in range(2))
                for section in range(RADIX)
            ]
            for low, (re, im) in enumerate(butterflies(values)):
                if low:
                    cos = twiddle_ref[0, pl.ds(low, 1), :]
                    sin = twiddle_ref[1, pl.ds(low, 1), :]
                    re, im = re * cos + im * sin, im * cos - re * sin
                rows = pl.ds(half * 8 * depth + low * spectra + t, 8, stride=depth)
                zr_ref[rows, :] = re
                zi_ref[rows, :] = im

    form = (((1,), (1,)), ((), ()))
    high_matrix, low_matrix = matrix_ref[0], matrix_ref[1]
    halves = depth // LANES

    @pl.loop(0, ROWS)
    def _(station):
        rows = pl.ds(pl.multiple_of(station * depth, depth), depth)
        value = jnp.concatenate([ref[rows, :] for ref in z_refs], axis=1)
        high = value.astype(jnp.bfloat16)
        rest = (value - high.astype(jnp.float32)).astype(jnp.bfloat16)
        total = lax.dot_general(high_matrix, high, form, preferred_element_type=jnp.float32)
        total += lax.dot_general(high_matrix, rest, form, preferred_element_type=jnp.float32)
        total += lax.dot_general(low_matrix, high, form, preferred_element_type=jnp.float32)
        for half in range(halves):
            for part in range(2):
                rows = pl.ds((half * 2 + part) * ROWS + station, LANES, stride=halves * 2 * ROWS)
                w_ref[rows, :] = total[
                    part * LANES : (part + 1) * LANES, half * LANES : (half + 1) * LANES
                ]

    piece = 256
    share = out_refs[0].shape[0]
    for number, out_ref in enumerate(out_refs):
        column = lax.rem(chan + number // sources, columns)
        owner = column * sources + lax.rem(tm + number % sources, sources)
        for step in range(share // piece):
            rows = pl.ds(pl.multiple_of(owner * share + step * piece, piece), piece)
            out_ref[step * piece : (step + 1) * piece, :] = w_ref[rows, :].astype(jnp.bfloat16)


def channelise(place, chunk, voltages, come, taps_filter, tables, frames, owners):
    sources = 1 + len(come)
    length = taps_filter.shape[1]
    spectra = sources * frames
    twiddle, matrix = tables
    out_rows = length // AVG * 2 * ROWS
    whole = pl.BlockSpec(memory_space=pltpu.VMEM)
    share = out_rows // owners
    flat = pl.pallas_call(
        lambda *refs: channelise_kernel(frames, chunk, *refs),
        out_shape=[jax.ShapeDtypeStruct((share, LANES), jnp.bfloat16)] * owners,
        in_specs=[pl.BlockSpec(memory_space=pltpu.SMEM)]
        + [pl.BlockSpec(memory_space=pl.ANY)] * sources
        + [whole] * 3,
        out_specs=[whole] * owners,
        scratch_shapes=[
            pltpu.VMEM((sources, 2, ROWS, frames * length), jnp.bfloat16),
            pltpu.VMEM((RADIX, spectra, 2, ROWS, LANES), jnp.float32),
            pltpu.VMEM((ROWS * RADIX * spectra, LANES), jnp.float32),
            pltpu.VMEM((ROWS * RADIX * spectra, LANES), jnp.float32),
            pltpu.VMEM((out_rows, LANES), jnp.float32),
            pltpu.SemaphoreType.DMA((sources,)),
        ],
        compiler_params=pltpu.CompilerParams(vmem_limit_bytes=40 * 2**20),
        cost_estimate=pl.CostEstimate(
            flops=9 * 10**9, bytes_accessed=4 * 2**20, transcendentals=0
        ),
        name="channelise",
    )(place, voltages, *come, taps_filter, jnp.asarray(twiddle), jnp.asarray(matrix))
    return [piece.reshape(length // AVG // owners, 2, ROWS, LANES) for piece in flat]


def correlate_kernel(chunks, width, *refs):
    sel_ref, weight_ref = refs[:2]
    x_refs = refs[2 : 2 + chunks]
    out_ref, x_all, rows_all = refs[2 + chunks :]
    tiles = out_ref.shape[0]
    chunk_rows = x_all.shape[0] // chunks
    for chunk, x_ref in enumerate(x_refs):
        for pol in range(2):
            for part in range(2):
                x_all[
                    chunk * chunk_rows : (chunk + 1) * chunk_rows,
                    (pol * 2 + part) * LANES : (pol * 2 + part + 1) * LANES,
                ] = x_ref[pol, :, 0, part].reshape(chunk_rows, LANES)
    step = 2
    for first in range(0, tiles, step):
        rows = slice(first * 2 * width, (first + step) * 2 * width)
        picked = jnp.dot(sel_ref[rows, :], x_all[...], preferred_element_type=jnp.float32)
        for tile in range(first, first + step):
            base = (tile - first) * 2 * width
            left = picked[base : base + width] * weight_ref[pl.ds(tile, 1), :]
            right = picked[base + width : base + 2 * width]
            rows_all[tile * 2 * width : tile * 2 * width + width, :] = left.astype(jnp.bfloat16)
            rows_all[tile * 2 * width + width : (tile + 1) * 2 * width, :] = right.astype(
                jnp.bfloat16
            )
    form = (((1,), (1,)), ((), ()))
    for tile in range(tiles):
        at = tile * 2 * width
        left = jnp.concatenate(
            [rows_all[at : at + width, pol * 2 * LANES : (pol + 1) * 2 * LANES] for pol in range(2)]
        )
        at += width
        right = jnp.concatenate(
            [rows_all[at : at + width, pol * 2 * LANES : (pol + 1) * 2 * LANES] for pol in range(2)]
        )
        turned = jnp.concatenate([-right[:, LANES:], right[:, :LANES]], axis=1)
        both = jnp.concatenate([right, turned])
        result = lax.dot_general(left, both, form, preferred_element_type=jnp.float32)
        for part in range(2):
            out_ref[tile, 0, part] = result[:, part * 2 * width : (part + 1) * 2 * width].reshape(
                2, width, 2 * width
            )


def correlate_tiles(chunks, select, weight, width):
    sources, bands = chunks[0].shape[1:3]
    tiles = weight.shape[0]
    block = (2, sources, 1, 2, ROWS, LANES)
    station_rows = len(chunks) * sources * ROWS
    return pl.pallas_call(
        lambda *refs: correlate_kernel(len(chunks), width, *refs),
        grid=(bands,),
        out_shape=jax.ShapeDtypeStruct((tiles, bands, 2, 2, width, 2 * width), jnp.float32),
        in_specs=[
            pl.BlockSpec(select.shape, lambda g: (0, 0)),
            pl.BlockSpec(weight.shape, lambda g: (0, 0)),
        ]
        + [pl.BlockSpec(block, lambda g: (0, 0, g, 0, 0, 0))] * len(chunks),
        out_specs=pl.BlockSpec(
            (tiles, 1, 2, 2, width, 2 * width), lambda g: (0, g, 0, 0, 0, 0)
        ),
        scratch_shapes=[
            pltpu.VMEM((station_rows, 4 * LANES), jnp.bfloat16),
            pltpu.VMEM((tiles * 2 * width, 4 * LANES), jnp.bfloat16),
        ],
        compiler_params=pltpu.CompilerParams(vmem_limit_bytes=32 * 2**20),
        cost_estimate=pl.CostEstimate(
            flops=13 * 10**9, bytes_accessed=42 * 2**20, transcendentals=0
        ),
        name="correlate",
    )(select, weight, *chunks)


def tile_tables(tile_a, tile_b, tile_owner, tile_flags, row_of):
    tiles = tile_owner.shape[0]
    held = tile_owner == lax.axis_index("pol")
    order = jnp.arange(tiles, dtype=jnp.int32)
    rank = jnp.sum((held[None, :] & (order[None, :] < order[:, None])).astype(jnp.int32), axis=1)
    slots = jnp.arange(CAP, dtype=jnp.int32)
    pick = (held[None, :] & (rank[None, :] == slots[:, None])).astype(jnp.int32)
    sides = jnp.stack([row_of(tile_a), row_of(tile_b)], axis=1) + 1
    rows = jnp.sum(pick[:, :, None, None] * sides[None], axis=1) - 1
    flags = jnp.sum(pick[:, :, None] * tile_flags[None], axis=1).astype(jnp.float32)
    return rows, flags


def on_device_chunks(voltages, taps_filter, tile_a, tile_b, tile_owner, tile_flags):
    length = taps_filter.shape[1]
    stations = voltages.shape[2]
    frames = voltages.shape[3] // length
    chan_count, time_count = lax.axis_size("chan"), lax.axis_size("tm")
    owners = chan_count * time_count
    chunk_count = stations // (time_count * ROWS)
    width = tile_a.shape[1]
    bands = length // AVG // owners
    tables = fourier_tables(length)

    chan, tm = lax.axis_index("chan"), lax.axis_index("tm")
    place = jnp.stack([chan, tm]).astype(jnp.int32)

    def row_of(station):
        column, rest = station // stations, station % stations
        block, inside = rest // (chunk_count * ROWS), rest % (chunk_count * ROWS)
        across = (chan - column) % chan_count
        behind = (tm - block) % time_count
        piece = across * time_count + behind
        return ((inside // ROWS) * owners + piece) * ROWS + inside % ROWS

    rows, flags = tile_tables(tile_a, tile_b, tile_owner, tile_flags, row_of)
    total_rows = chunk_count * owners * ROWS
    select = (rows[..., None] == jnp.arange(total_rows, dtype=jnp.int32)).astype(jnp.bfloat16)
    select = select.reshape(CAP * 2 * width, total_rows)
    depth = AVG * time_count * frames
    weight = jnp.tile(flags * (1.0 / depth), (1, 4 * AVG))

    samples = voltages.reshape(2, stations, frames * length)

    def ahead(value, across, along):
        pairs = [
            (x * time_count + z, (x + across) % chan_count * time_count + (z + along) % time_count)
            for x in range(chan_count)
            for z in range(time_count)
        ]
        return lax.ppermute(value, ("chan", "tm"), pairs)

    def block_for(chunk, along):
        first = ((tm + along) % time_count * chunk_count + chunk) * ROWS
        return lax.dynamic_slice(samples, (0, first, 0), (2, ROWS, frames * length))

    come = [
        [ahead(block_for(chunk, along), 0, along) for along in range(1, time_count)]
        for chunk in range(chunk_count)
    ]
    received = []
    for chunk in range(chunk_count):
        spectra = channelise(
            place, chunk, samples, come[chunk], taps_filter, tables, frames, owners
        )
        moved = jnp.stack(
            spectra[:1]
            + [
                ahead(spectra[owner], owner // time_count, owner % time_count)
                for owner in range(1, owners)
            ]
        )
        received.append(lax.all_gather(moved, "pol", axis=0, tiled=False))
    return correlate_tiles(received, select, weight, width)


def on_device(voltages, taps_filter, tile_a, tile_b, tile_owner, tile_flags):
    taps, length = taps_filter.shape
    frames = voltages.shape[3] // length
    time_count = lax.axis_size("tm")
    fits = (
        length == RADIX * LANES
        and AVG * time_count * frames == LANES
        and voltages.shape[2] % (time_count * ROWS) == 0
        and 2 * tile_a.shape[1] == LANES
    )
    form = on_device_chunks if fits else on_device_any
    return form(voltages, taps_filter, tile_a, tile_b, tile_owner, tile_flags)


def solution(mesh):
    return jax.shard_map(
        on_device,
        mesh=mesh,
        in_specs=(P("grp", "pol", "chan", "tm"), P(), P(), P(), P(), P()),
        out_specs=P("pol", ("chan", "tm"), "grp", None, None, None),
        check_vma=False,
    )
```

```python
import math

import jax
import jax.numpy as jnp
import numpy as np
from jax import lax
from jax.experimental import pallas as pl
from jax.experimental.pallas import tpu as pltpu
from jax.sharding import PartitionSpec as P

AVG = 8
CAP = 8
RADIX = 16
LANES = 128
ROWS = 16


radix_first = 32


def from_behind(value, axis, steps):
    count = lax.axis_size(axis)
    first, last = (max(0, -steps), min(count, count - steps))
    return lax.ppermute(value, axis, [(source, source + steps) for source in range(first, last)])


def fourier(filtered):
    length = filtered.shape[-1]
    second = length // radix_first
    exact_mode = lax.Precision.HIGHEST
    grid = filtered.reshape(filtered.shape[:-1] + (radix_first, second))
    outer = jnp.arange(radix_first, dtype=jnp.int32)
    inner = jnp.arange(second, dtype=jnp.int32)
    phase_one = (
        2.0
        * math.pi
        / radix_first
        * (outer[:, None] * outer[None, :] % radix_first).astype(jnp.float32)
    )
    phase_twist = 2.0 * math.pi / length * (outer[:, None] * inner[None, :]).astype(jnp.float32)
    phase_two = (
        2.0 * math.pi / second * (inner[:, None] * inner[None, :] % second).astype(jnp.float32)
    )
    cos_one, sin_one = (jnp.cos(phase_one), jnp.sin(phase_one))
    cos_twist, sin_twist = (jnp.cos(phase_twist), jnp.sin(phase_twist))
    cos_two, sin_two = (jnp.cos(phase_two), jnp.sin(phase_two))
    first_form = "fk,stkj->stfj"
    section_re = jnp.einsum(first_form, cos_one, grid[0], precision=exact_mode) + jnp.einsum(
        first_form, sin_one, grid[1], precision=exact_mode
    )
    section_im = jnp.einsum(first_form, cos_one, grid[1], precision=exact_mode) - jnp.einsum(
        first_form, sin_one, grid[0], precision=exact_mode
    )
    turned_re = section_re * cos_twist + section_im * sin_twist
    turned_im = section_im * cos_twist - section_re * sin_twist
    second_form = "gj,stfj->stgf"
    final_re = jnp.einsum(second_form, cos_two, turned_re, precision=exact_mode) + jnp.einsum(
        second_form, sin_two, turned_im, precision=exact_mode
    )
    final_im = jnp.einsum(second_form, cos_two, turned_im, precision=exact_mode) - jnp.einsum(
        second_form, sin_two, turned_re, precision=exact_mode
    )
    joined = jnp.stack([final_re, final_im]).reshape(filtered.shape)
    return joined * (1.0 / math.sqrt(length))


def correlate(full, rows_a, rows_b, flags, group_count):
    depth = full.shape[4]
    weight = jnp.tile(flags.astype(jnp.bfloat16), depth // flags.shape[0])
    left_rows = jnp.take(full, rows_a, axis=2) * weight
    right_rows = jnp.take(full, rows_b, axis=2)
    stacked_left = jnp.stack(
        [
            jnp.concatenate([left_rows[0], left_rows[1]], axis=-1),
            jnp.concatenate([left_rows[1], -left_rows[0]], axis=-1),
        ]
    )
    joined_right = jnp.concatenate([right_rows[0], right_rows[1]], axis=-1)
    result = jnp.einsum(
        "rpank,qbnk->nrpaqb", stacked_left, joined_right, preferred_element_type=jnp.float32
    )
    width = rows_a.shape[0]
    return result.reshape(group_count, 2, 2, width, 2 * width) * (1.0 / depth)


def on_device_any(voltages, taps_filter, tile_a, tile_b, tile_owner, tile_flags):
    history = taps_filter.shape[0] - 1
    length = taps_filter.shape[1]
    stations = voltages.shape[2]
    frames = voltages.shape[3] // length
    local_blocks = voltages.reshape(2, stations, frames, length)
    hop_count = -(-history // frames)
    sending = local_blocks
    extended = local_blocks
    for hop_index in range(hop_count):
        sending = from_behind(sending, "tm", 1)
        extended = jnp.concatenate([sending, extended], axis=2)
    extended = extended[:, :, extended.shape[2] - history - frames :]
    filtered = jnp.zeros((2, stations, frames, length), jnp.float32)
    for tap_index in range(history + 1):
        start = history - tap_index
        filtered = filtered + taps_filter[tap_index] * extended[
            :, :, start : start + frames
        ].astype(jnp.float32)
    spectra = fourier(filtered).astype(jnp.bfloat16)
    chan_count = lax.axis_size("chan")
    time_count = lax.axis_size("tm")
    narrow = length // (chan_count * time_count)
    outgoing = spectra.reshape(2, stations, frames, chan_count, time_count, narrow)
    outgoing = outgoing.transpose(0, 3, 4, 5, 1, 2)
    flat = outgoing.reshape(2, chan_count * time_count, narrow, stations * frames)
    moved = lax.all_to_all(flat, ("chan", "tm"), split_axis=1, concat_axis=1, tiled=True)
    moved = moved.reshape(2, chan_count, time_count, narrow, stations, frames)
    bands = narrow // AVG
    every_station = chan_count * stations
    spectra_count = time_count * frames
    arranged = moved.transpose(0, 1, 4, 3, 2, 5).reshape(
        2, 1, every_station, bands, AVG * spectra_count
    )
    full = lax.all_gather(arranged, "pol", axis=1, tiled=True)
    position = lax.axis_index("pol")
    width = tile_a.shape[1]
    capacity = CAP
    held = tile_owner == position
    listed = jnp.nonzero(held, size=capacity, fill_value=0)[0].astype(jnp.int32)
    tally = jnp.sum(held.astype(jnp.int32))
    initial = jnp.zeros((capacity, bands, 2, 2, width, 2 * width), jnp.float32)

    def fill_slot(slot, results):
        chosen_tile = listed[slot]
        return results.at[slot].set(
            correlate(
                full, tile_a[chosen_tile], tile_b[chosen_tile], tile_flags[chosen_tile], bands
            )
        )

    visibility = lax.fori_loop(0, tally, fill_slot, initial)
    return visibility


def fourier_tables(length):
    low = np.arange(RADIX)
    lane = np.arange(LANES)
    turn = 2.0 * np.pi / length * np.outer(low, lane)
    twiddle = np.stack([np.cos(turn), np.sin(turn)]).astype(np.float32)
    angle = 2.0 * np.pi / LANES * (np.outer(lane, lane) % LANES)
    cos, sin = np.cos(angle) / math.sqrt(length), np.sin(angle) / math.sqrt(length)
    matrix = np.block([[cos, sin], [-sin, cos]]).astype(np.float32)
    high = matrix.astype(jnp.bfloat16)
    rest = (matrix - high.astype(np.float32)).astype(jnp.bfloat16)
    return twiddle, np.stack([high, rest])


def butterflies(values):
    count = len(values)
    if count == 1:
        return values
    even, odd = butterflies(values[0::2]), butterflies(values[1::2])
    first, second = [], []
    for index in range(count // 2):
        (a, b), (c, d) = even[index], odd[index]
        if index == 0:
            e, f = c, d
        elif 4 * index == count:
            e, f = d, -c
        elif 8 * index == count:
            root = math.sqrt(0.5)
            e, f = (c + d) * root, (d - c) * root
        elif 8 * index == 3 * count:
            root = math.sqrt(0.5)
            e, f = (d - c) * root, -(c + d) * root
        else:
            turn = 2.0 * math.pi * index / count
            cos, sin = math.cos(turn), math.sin(turn)
            e, f = c * cos + d * sin, d * cos - c * sin
        first.append((a + e, b + f))
        second.append((a - e, b - f))
    return first + second


def channelise_kernel(frames, chunk, columns, plan, place_ref, own_ref, *refs):
    sources = refs[-6].shape[0]
    come_refs = refs[: sources - 1]
    taps_ref, twiddle_ref, matrix_ref = refs[sources - 1 : sources + 2]
    out_refs = refs[sources + 2 : -6]
    x_ref, fil_ref, zr_ref, zi_ref, w_ref, sems = refs[-6:]
    chan, tm = place_ref[0], place_ref[1]
    own_rows = pl.multiple_of((tm * (own_ref.shape[1] // (sources * ROWS)) + chunk) * ROWS, ROWS)
    copies = []
    for behind in range(sources):
        block = come_refs[behind - 1] if behind else own_ref.at[:, pl.ds(own_rows, ROWS), :]
        slot = lax.rem(tm - behind + sources, sources)
        copies.append(pltpu.make_async_copy(block, x_ref.at[slot], sems.at[behind]))
    for copy in copies:
        copy.start()
    for copy in copies:
        copy.wait()
    spectra = sources * frames
    length = taps_ref.shape[1]
    taps = taps_ref.shape[0]
    depth = RADIX * spectra
    z_refs = (zr_ref, zi_ref)

    @pl.loop(0, RADIX)
    def _(section):
        at = pl.multiple_of(section * LANES, LANES)
        weights = [taps_ref[pl.ds(m, 1), pl.ds(at, LANES)] for m in range(taps)]
        for part in range(2):
            blocks = []
            for t in range(spectra):
                lane = pl.multiple_of((t % frames) * length + section * LANES, LANES)
                blocks.append(x_ref[t // frames, part, :, pl.ds(lane, LANES)].astype(jnp.float32))
            for t in range(spectra):
                total = weights[0] * blocks[t]
                for m in range(1, min(t + 1, taps)):
                    total = total + weights[m] * blocks[t - m]
                fil_ref[section, t, part] = total

    @pl.loop(0, spectra)
    def _(t):
        for half in range(ROWS // 8):
            values = [
                tuple(fil_ref[section, t, part, pl.ds(half * 8, 8), :] for part in range(2))
                for section in range(RADIX)
            ]
            for low, (re, im) in enumerate(butterflies(values)):
                if low:
                    cos = twiddle_ref[0, pl.ds(low, 1), :]
                    sin = twiddle_ref[1, pl.ds(low, 1), :]
                    re, im = re * cos + im * sin, im * cos - re * sin
                rows = pl.ds(half * 8 * depth + low * spectra + t, 8, stride=depth)
                zr_ref[rows, :] = re
                zi_ref[rows, :] = im

    form = (((1,), (1,)), ((), ()))
    high_matrix, low_matrix = matrix_ref[0], matrix_ref[1]
    halves = depth // LANES

    @pl.loop(0, ROWS)
    def _(station):
        rows = pl.ds(pl.multiple_of(station * depth, depth), depth)
        value = jnp.concatenate([ref[rows, :] for ref in z_refs], axis=1)
        high = value.astype(jnp.bfloat16)
        rest = (value - high.astype(jnp.float32)).astype(jnp.bfloat16)
        total = lax.dot_general(high_matrix, high, form, preferred_element_type=jnp.float32)
        total += lax.dot_general(high_matrix, rest, form, preferred_element_type=jnp.float32)
        total += lax.dot_general(low_matrix, high, form, preferred_element_type=jnp.float32)
        for half in range(halves):
            for part in range(2):
                rows = pl.ds((half * 2 + part) * ROWS + station, LANES, stride=halves * 2 * ROWS)
                w_ref[rows, :] = total[
                    part * LANES : (part + 1) * LANES, half * LANES : (half + 1) * LANES
                ]

    share = w_ref.shape[0] // (columns * sources)
    band_rows = 2 * ROWS
    piece = 8 * band_rows
    for blocks, out_ref in zip(plan, out_refs):
        at = 0
        for across, along, start, stop in blocks:
            owner = lax.rem(chan + across, columns) * sources + lax.rem(tm + along, sources)
            for row in range(start * band_rows, stop * band_rows, piece):
                rows = pl.ds(pl.multiple_of(owner * share + row, piece), piece)
                out_ref[at : at + piece, :] = w_ref[rows, :].astype(jnp.bfloat16)
                at += piece


def channelise(place, chunk, voltages, come, taps_filter, tables, frames, columns, plan):
    sources = 1 + len(come)
    length = taps_filter.shape[1]
    spectra = sources * frames
    twiddle, matrix = tables
    out_rows = length // AVG * 2 * ROWS
    whole = pl.BlockSpec(memory_space=pltpu.VMEM)
    counts = [sum(stop - start for _, _, start, stop in blocks) for blocks in plan]
    flat = pl.pallas_call(
        lambda *refs: channelise_kernel(frames, chunk, columns, plan, *refs),
        out_shape=[
            jax.ShapeDtypeStruct((count * 2 * ROWS, LANES), jnp.bfloat16) for count in counts
        ],
        in_specs=[pl.BlockSpec(memory_space=pltpu.SMEM)]
        + [pl.BlockSpec(memory_space=pl.ANY)] * sources
        + [whole] * 3,
        out_specs=[whole] * len(plan),
        scratch_shapes=[
            pltpu.VMEM((sources, 2, ROWS, frames * length), jnp.bfloat16),
            pltpu.VMEM((RADIX, spectra, 2, ROWS, LANES), jnp.float32),
            pltpu.VMEM((ROWS * RADIX * spectra, LANES), jnp.float32),
            pltpu.VMEM((ROWS * RADIX * spectra, LANES), jnp.float32),
            pltpu.VMEM((out_rows, LANES), jnp.float32),
            pltpu.SemaphoreType.DMA((sources,)),
        ],
        compiler_params=pltpu.CompilerParams(vmem_limit_bytes=40 * 2**20),
        cost_estimate=pl.CostEstimate(
            flops=9 * 10**9, bytes_accessed=4 * 2**20, transcendentals=0
        ),
        name="channelise",
    )(place, voltages, *come, taps_filter, jnp.asarray(twiddle), jnp.asarray(matrix))
    return [piece.reshape(count, 2, ROWS, LANES) for piece, count in zip(flat, counts)]


def correlate_kernel(places, starts, width, place_ref, sel_ref, weight_ref, *refs):
    x_refs, (out_ref, x_all, rows_all) = refs[: 2 * len(starts)], refs[-3:]
    tiles = out_ref.shape[0]
    band = pl.program_id(0)
    own = pl.multiple_of(place_ref[2] * 2 * LANES, 2 * LANES)
    other = pl.multiple_of((1 - place_ref[2]) * 2 * LANES, 2 * LANES)
    for number, (start, rows) in enumerate(zip(starts, places)):
        for side, lanes in enumerate((own, other)):
            x_ref = x_refs[2 * number + side]
            share = x_ref.shape[0] // len(rows)
            for block, at in enumerate(rows):
                for part in range(2):
                    x_all[at : at + ROWS, pl.ds(lanes + part * LANES, LANES)] = x_ref[
                        block * share + start + band, part
                    ]
    step = 2
    for first in range(0, tiles, step):
        rows = slice(first * 2 * width, (first + step) * 2 * width)
        picked = jnp.dot(sel_ref[rows, :], x_all[...], preferred_element_type=jnp.float32)
        for tile in range(first, first + step):
            base = (tile - first) * 2 * width
            left = picked[base : base + width] * weight_ref[pl.ds(tile, 1), :]
            right = picked[base + width : base + 2 * width]
            rows_all[tile * 2 * width : tile * 2 * width + width, :] = left.astype(jnp.bfloat16)
            rows_all[tile * 2 * width + width : (tile + 1) * 2 * width, :] = right.astype(
                jnp.bfloat16
            )
    form = (((1,), (1,)), ((), ()))
    for tile in range(tiles):
        at = tile * 2 * width
        left = jnp.concatenate(
            [rows_all[at : at + width, pol * 2 * LANES : (pol + 1) * 2 * LANES] for pol in range(2)]
        )
        at += width
        right = jnp.concatenate(
            [rows_all[at : at + width, pol * 2 * LANES : (pol + 1) * 2 * LANES] for pol in range(2)]
        )
        turned = jnp.concatenate([-right[:, LANES:], right[:, :LANES]], axis=1)
        both = jnp.concatenate([right, turned])
        result = lax.dot_general(left, both, form, preferred_element_type=jnp.float32)
        for part in range(2):
            out_ref[tile, 0, part] = result[:, part * 2 * width : (part + 1) * 2 * width].reshape(
                2, width, 2 * width
            )


def correlate_tiles(
    place, select, weight, pieces, places, starts, width, first, count, bands, earlier
):
    tiles = weight.shape[0]
    whole = pl.BlockSpec(memory_space=pltpu.VMEM)
    more = [] if earlier is None else [earlier]
    return pl.pallas_call(
        lambda *refs: correlate_kernel(places, starts, width, *refs),
        grid=(count,),
        out_shape=jax.ShapeDtypeStruct((tiles, bands, 2, 2, width, 2 * width), jnp.float32),
        in_specs=[pl.BlockSpec(memory_space=pltpu.SMEM)]
        + [whole] * (2 + len(pieces))
        + [pl.BlockSpec(memory_space=pl.ANY)] * len(more),
        out_specs=pl.BlockSpec(
            (tiles, 1, 2, 2, width, 2 * width), lambda g: (0, g + first, 0, 0, 0, 0)
        ),
        scratch_shapes=[
            pltpu.VMEM((select.shape[1], 4 * LANES), jnp.bfloat16),
            pltpu.VMEM((tiles * 2 * width, 4 * LANES), jnp.bfloat16),
        ],
        input_output_aliases={3 + len(pieces): 0} if more else {},
        compiler_params=pltpu.CompilerParams(vmem_limit_bytes=32 * 2**20),
        cost_estimate=pl.CostEstimate(
            flops=13 * 10**9 * count // bands,
            bytes_accessed=42 * 2**20 * count // bands,
            transcendentals=0,
        ),
        name="correlate",
    )(place, select, weight, *pieces, *more)


def tile_tables(tile_a, tile_b, tile_owner, tile_flags, row_of):
    tiles = tile_owner.shape[0]
    held = tile_owner == lax.axis_index("pol")
    order = jnp.arange(tiles, dtype=jnp.int32)
    rank = jnp.sum((held[None, :] & (order[None, :] < order[:, None])).astype(jnp.int32), axis=1)
    slots = jnp.arange(CAP, dtype=jnp.int32)
    pick = (held[None, :] & (rank[None, :] == slots[:, None])).astype(jnp.int32)
    sides = jnp.stack([row_of(tile_a), row_of(tile_b)], axis=1) + 1
    rows = jnp.sum(pick[:, :, None, None] * sides[None], axis=1) - 1
    flags = jnp.sum(pick[:, :, None] * tile_flags[None], axis=1).astype(jnp.float32)
    return rows, flags


def on_device_chunks(voltages, taps_filter, tile_a, tile_b, tile_owner, tile_flags):
    length = taps_filter.shape[1]
    stations = voltages.shape[2]
    frames = voltages.shape[3] // length
    chan_count, time_count = lax.axis_size("chan"), lax.axis_size("tm")
    owners = chan_count * time_count
    chunk_count = stations // (time_count * ROWS)
    width = tile_a.shape[1]
    bands = length // AVG // owners
    tables = fourier_tables(length)

    chan, tm = lax.axis_index("chan"), lax.axis_index("tm")
    place = jnp.stack([chan, tm, lax.axis_index("pol")]).astype(jnp.int32)

    def row_of(station):
        column, rest = station // stations, station % stations
        block, inside = rest // (chunk_count * ROWS), rest % (chunk_count * ROWS)
        across = (chan - column) % chan_count
        behind = (tm - block) % time_count
        piece = across * time_count + behind
        return ((inside // ROWS) * owners + piece) * ROWS + inside % ROWS

    rows, flags = tile_tables(tile_a, tile_b, tile_owner, tile_flags, row_of)
    total_rows = chunk_count * owners * ROWS
    select = (rows[..., None] == jnp.arange(total_rows, dtype=jnp.int32)).astype(jnp.bfloat16)
    select = select.reshape(CAP * 2 * width, total_rows)
    depth = AVG * time_count * frames
    weight = jnp.tile(flags * (1.0 / depth), (1, 4 * AVG))

    samples = voltages.reshape(2, stations, frames * length)

    def travel(value, axes, distances):
        sizes = [lax.axis_size(axis) for axis in axes]
        pairs = []
        for index in np.ndindex(*sizes):
            target = [(i + d) % n for i, d, n in zip(index, distances, sizes)]
            pairs.append(tuple(int(np.ravel_multi_index(x, sizes)) for x in (index, target)))
        return lax.ppermute(value, axes, pairs)

    def after(values, earlier):
        return lax.optimization_barrier((list(values), list(earlier)))

    def block_for(chunk, distance):
        first = ((tm + distance) % time_count * chunk_count + chunk) * ROWS
        return lax.dynamic_slice(samples, (0, first, 0), (2, ROWS, frames * length))

    def turn_time(blocks):
        return [travel(block, ("tm",), (d,)) for d, block in zip(distances, blocks)]

    def filtered(chunk, arrived, plan):
        arrived = [arrived[distances.index(d)] for d in range(1, time_count)]
        return channelise(
            place, chunk, samples, arrived, taps_filter, tables, frames, chan_count, plan
        )

    distances = [2, 1, 3]
    half = bands // 2
    every = [(x, z) for z in distances + [0] for x in range(2)]
    away = [pair for pair in every if any(pair)]
    spare = 1

    first = turn_time([block_for(0, d) for d in distances])
    blocks, held = after([block_for(1, d) for d in distances], first[:-spare])
    first[:-spare] = held
    second = turn_time(blocks)

    plan = [[(x, z, 0, bands)] for x, z in every]
    spectra = dict(zip(every, filtered(0, first, plan)))
    blocks, held = after([spectra[pair] for pair in away], second[:-spare])
    second[:-spare] = held
    moved_first = [travel(v, ("chan", "tm"), pair) for pair, v in zip(away, blocks)]

    plan = [[(x, z, 0, half)] for x, z in every]
    plan += [[(x, z, half, bands) for z in range(time_count)] for x in range(2)]
    *low, near, far = filtered(1, second, plan)
    low = dict(zip(every, low))
    (*blocks, far), held = after([low[pair] for pair in away] + [far], moved_first[:-spare])
    moved_first[:-spare] = held
    moved_low = [travel(v, ("chan", "tm"), pair) for pair, v in zip(away, blocks)]
    far = travel(far, ("chan",), (1,))
    near, far = (v.reshape(time_count, half, 2, ROWS, LANES) for v in (near, far))
    high = [jnp.stack([near[z], far[z]]) for z in range(time_count)]
    blocks, held = after([high[d] for d in distances], moved_low[:-spare])
    moved_low[:-spare] = held
    moved_high = [travel(v, ("tm",), (d,)) for d, v in zip(distances, blocks)]

    def rows_for(chunk, x, z):
        return ((chunk * chan_count + x) * time_count + z) * ROWS

    def with_other(values):
        return [side for v in values for side in (v, travel(v, ("pol",), (1,)))]

    own_first = [spectra[0, 0]] + moved_first
    own_low = [low[0, 0]] + moved_low
    order = [(0, 0)] + away
    both_first = with_other(own_first)
    both_low = with_other(own_low)
    places = [[rows_for(0, x, z)] for x, z in order] + [[rows_for(1, x, z)] for x, z in order]
    visibility = correlate_tiles(
        place, select, weight, both_first + both_low, places, [0] * 16, width,
        0, half, bands, None,
    )
    own_high = [high[0]] + moved_high
    own_high, (visibility,) = after(own_high, [visibility])
    both_high = [v.reshape(2 * half, 2, ROWS, LANES) for v in with_other(own_high)]
    places = places[:8] + [[rows_for(1, x, z) for x in range(2)] for z in [0] + distances]
    return correlate_tiles(
        place, select, weight, both_first + both_high, places, [half] * 8 + [0] * 4, width,
        half, half, bands, visibility,
    )


def on_device(voltages, taps_filter, tile_a, tile_b, tile_owner, tile_flags):
    taps, length = taps_filter.shape
    frames = voltages.shape[3] // length
    time_count = lax.axis_size("tm")
    fits = (
        length == RADIX * LANES
        and AVG * time_count * frames == LANES
        and 2 * tile_a.shape[1] == LANES
        and voltages.shape[2] == 2 * time_count * ROWS
        and (lax.axis_size("chan"), time_count) == (2, 4)
    )
    form = on_device_chunks if fits else on_device_any
    return form(voltages, taps_filter, tile_a, tile_b, tile_owner, tile_flags)


def solution(mesh):
    return jax.shard_map(
        on_device,
        mesh=mesh,
        in_specs=(P("grp", "pol", "chan", "tm"), P(), P(), P(), P(), P()),
        out_specs=P("pol", ("chan", "tm"), "grp", None, None, None),
        check_vma=False,
    )
```

```python
import math

import jax
import jax.numpy as jnp
import numpy as np
from jax import lax
from jax.experimental import pallas as pl
from jax.experimental.pallas import tpu as pltpu
from jax.sharding import PartitionSpec as P

AVG = 8
CAP = 8
RADIX = 16
LANES = 128
ROWS = 16


radix_first = 32


def from_behind(value, axis, steps):
    count = lax.axis_size(axis)
    first, last = (max(0, -steps), min(count, count - steps))
    return lax.ppermute(value, axis, [(source, source + steps) for source in range(first, last)])


def fourier(filtered):
    length = filtered.shape[-1]
    second = length // radix_first
    exact_mode = lax.Precision.HIGHEST
    grid = filtered.reshape(filtered.shape[:-1] + (radix_first, second))
    outer = jnp.arange(radix_first, dtype=jnp.int32)
    inner = jnp.arange(second, dtype=jnp.int32)
    phase_one = (
        2.0
        * math.pi
        / radix_first
        * (outer[:, None] * outer[None, :] % radix_first).astype(jnp.float32)
    )
    phase_twist = 2.0 * math.pi / length * (outer[:, None] * inner[None, :]).astype(jnp.float32)
    phase_two = (
        2.0 * math.pi / second * (inner[:, None] * inner[None, :] % second).astype(jnp.float32)
    )
    cos_one, sin_one = (jnp.cos(phase_one), jnp.sin(phase_one))
    cos_twist, sin_twist = (jnp.cos(phase_twist), jnp.sin(phase_twist))
    cos_two, sin_two = (jnp.cos(phase_two), jnp.sin(phase_two))
    first_form = "fk,stkj->stfj"
    section_re = jnp.einsum(first_form, cos_one, grid[0], precision=exact_mode) + jnp.einsum(
        first_form, sin_one, grid[1], precision=exact_mode
    )
    section_im = jnp.einsum(first_form, cos_one, grid[1], precision=exact_mode) - jnp.einsum(
        first_form, sin_one, grid[0], precision=exact_mode
    )
    turned_re = section_re * cos_twist + section_im * sin_twist
    turned_im = section_im * cos_twist - section_re * sin_twist
    second_form = "gj,stfj->stgf"
    final_re = jnp.einsum(second_form, cos_two, turned_re, precision=exact_mode) + jnp.einsum(
        second_form, sin_two, turned_im, precision=exact_mode
    )
    final_im = jnp.einsum(second_form, cos_two, turned_im, precision=exact_mode) - jnp.einsum(
        second_form, sin_two, turned_re, precision=exact_mode
    )
    joined = jnp.stack([final_re, final_im]).reshape(filtered.shape)
    return joined * (1.0 / math.sqrt(length))


def correlate(full, rows_a, rows_b, flags, group_count):
    depth = full.shape[4]
    weight = jnp.tile(flags.astype(jnp.bfloat16), depth // flags.shape[0])
    left_rows = jnp.take(full, rows_a, axis=2) * weight
    right_rows = jnp.take(full, rows_b, axis=2)
    stacked_left = jnp.stack(
        [
            jnp.concatenate([left_rows[0], left_rows[1]], axis=-1),
            jnp.concatenate([left_rows[1], -left_rows[0]], axis=-1),
        ]
    )
    joined_right = jnp.concatenate([right_rows[0], right_rows[1]], axis=-1)
    result = jnp.einsum(
        "rpank,qbnk->nrpaqb", stacked_left, joined_right, preferred_element_type=jnp.float32
    )
    width = rows_a.shape[0]
    return result.reshape(group_count, 2, 2, width, 2 * width) * (1.0 / depth)


def on_device_any(voltages, taps_filter, tile_a, tile_b, tile_owner, tile_flags):
    history = taps_filter.shape[0] - 1
    length = taps_filter.shape[1]
    stations = voltages.shape[2]
    frames = voltages.shape[3] // length
    local_blocks = voltages.reshape(2, stations, frames, length)
    hop_count = -(-history // frames)
    sending = local_blocks
    extended = local_blocks
    for hop_index in range(hop_count):
        sending = from_behind(sending, "tm", 1)
        extended = jnp.concatenate([sending, extended], axis=2)
    extended = extended[:, :, extended.shape[2] - history - frames :]
    filtered = jnp.zeros((2, stations, frames, length), jnp.float32)
    for tap_index in range(history + 1):
        start = history - tap_index
        filtered = filtered + taps_filter[tap_index] * extended[
            :, :, start : start + frames
        ].astype(jnp.float32)
    spectra = fourier(filtered).astype(jnp.bfloat16)
    chan_count = lax.axis_size("chan")
    time_count = lax.axis_size("tm")
    narrow = length // (chan_count * time_count)
    outgoing = spectra.reshape(2, stations, frames, chan_count, time_count, narrow)
    outgoing = outgoing.transpose(0, 3, 4, 5, 1, 2)
    flat = outgoing.reshape(2, chan_count * time_count, narrow, stations * frames)
    moved = lax.all_to_all(flat, ("chan", "tm"), split_axis=1, concat_axis=1, tiled=True)
    moved = moved.reshape(2, chan_count, time_count, narrow, stations, frames)
    bands = narrow // AVG
    every_station = chan_count * stations
    spectra_count = time_count * frames
    arranged = moved.transpose(0, 1, 4, 3, 2, 5).reshape(
        2, 1, every_station, bands, AVG * spectra_count
    )
    full = lax.all_gather(arranged, "pol", axis=1, tiled=True)
    position = lax.axis_index("pol")
    width = tile_a.shape[1]
    capacity = CAP
    held = tile_owner == position
    listed = jnp.nonzero(held, size=capacity, fill_value=0)[0].astype(jnp.int32)
    tally = jnp.sum(held.astype(jnp.int32))
    initial = jnp.zeros((capacity, bands, 2, 2, width, 2 * width), jnp.float32)

    def fill_slot(slot, results):
        chosen_tile = listed[slot]
        return results.at[slot].set(
            correlate(
                full, tile_a[chosen_tile], tile_b[chosen_tile], tile_flags[chosen_tile], bands
            )
        )

    visibility = lax.fori_loop(0, tally, fill_slot, initial)
    return visibility


def fourier_tables(length):
    low = np.arange(RADIX)
    lane = np.arange(LANES)
    turn = 2.0 * np.pi / length * np.outer(low, lane)
    twiddle = np.stack([np.cos(turn), np.sin(turn)]).astype(np.float32)
    angle = 2.0 * np.pi / LANES * (np.outer(lane, lane) % LANES)
    cos, sin = np.cos(angle) / math.sqrt(length), np.sin(angle) / math.sqrt(length)
    matrix = np.block([[cos, sin], [-sin, cos]]).astype(np.float32)
    high = matrix.astype(jnp.bfloat16)
    rest = (matrix - high.astype(np.float32)).astype(jnp.bfloat16)
    return twiddle, np.stack([high, rest])


def butterflies(values):
    count = len(values)
    if count == 1:
        return values
    even, odd = butterflies(values[0::2]), butterflies(values[1::2])
    first, second = [], []
    for index in range(count // 2):
        (a, b), (c, d) = even[index], odd[index]
        if index == 0:
            e, f = c, d
        elif 4 * index == count:
            e, f = d, -c
        elif 8 * index == count:
            root = math.sqrt(0.5)
            e, f = (c + d) * root, (d - c) * root
        elif 8 * index == 3 * count:
            root = math.sqrt(0.5)
            e, f = (d - c) * root, -(c + d) * root
        else:
            turn = 2.0 * math.pi * index / count
            cos, sin = math.cos(turn), math.sin(turn)
            e, f = c * cos + d * sin, d * cos - c * sin
        first.append((a + e, b + f))
        second.append((a - e, b - f))
    return first + second


def channelise_kernel(frames, chunk, columns, plan, place_ref, own_ref, *refs):
    sources = refs[-6].shape[0]
    come_refs = refs[: sources - 1]
    taps_ref, twiddle_ref, matrix_ref = refs[sources - 1 : sources + 2]
    out_refs = refs[sources + 2 : -6]
    x_ref, fil_ref, zr_ref, zi_ref, w_ref, sems = refs[-6:]
    chan, tm = place_ref[0], place_ref[1]
    own_rows = pl.multiple_of((tm * (own_ref.shape[1] // (sources * ROWS)) + chunk) * ROWS, ROWS)
    copies = []
    for behind in range(sources):
        block = come_refs[behind - 1] if behind else own_ref.at[:, pl.ds(own_rows, ROWS), :]
        slot = lax.rem(tm - behind + sources, sources)
        copies.append(pltpu.make_async_copy(block, x_ref.at[slot], sems.at[behind]))
    for copy in copies:
        copy.start()
    for copy in copies:
        copy.wait()
    spectra = sources * frames
    length = taps_ref.shape[1]
    taps = taps_ref.shape[0]
    depth = RADIX * spectra
    z_refs = (zr_ref, zi_ref)

    @pl.loop(0, RADIX)
    def _(section):
        at = pl.multiple_of(section * LANES, LANES)
        weights = [taps_ref[pl.ds(m, 1), pl.ds(at, LANES)] for m in range(taps)]
        for part in range(2):
            blocks = []
            for t in range(spectra):
                lane = pl.multiple_of((t % frames) * length + section * LANES, LANES)
                blocks.append(x_ref[t // frames, part, :, pl.ds(lane, LANES)].astype(jnp.float32))
            for t in range(spectra):
                total = weights[0] * blocks[t]
                for m in range(1, min(t + 1, taps)):
                    total = total + weights[m] * blocks[t - m]
                fil_ref[section, t, part] = total

    @pl.loop(0, spectra)
    def _(t):
        for half in range(ROWS // 8):
            values = [
                tuple(fil_ref[section, t, part, pl.ds(half * 8, 8), :] for part in range(2))
                for section in range(RADIX)
            ]
            for low, (re, im) in enumerate(butterflies(values)):
                if low:
                    cos = twiddle_ref[0, pl.ds(low, 1), :]
                    sin = twiddle_ref[1, pl.ds(low, 1), :]
                    re, im = re * cos + im * sin, im * cos - re * sin
                rows = pl.ds(half * 8 * depth + low * spectra + t, 8, stride=depth)
                zr_ref[rows, :] = re
                zi_ref[rows, :] = im

    form = (((1,), (1,)), ((), ()))
    high_matrix, low_matrix = matrix_ref[0], matrix_ref[1]
    halves = depth // LANES

    @pl.loop(0, ROWS)
    def _(station):
        rows = pl.ds(pl.multiple_of(station * depth, depth), depth)
        value = jnp.concatenate([ref[rows, :] for ref in z_refs], axis=1)
        high = value.astype(jnp.bfloat16)
        rest = (value - high.astype(jnp.float32)).astype(jnp.bfloat16)
        total = lax.dot_general(high_matrix, high, form, preferred_element_type=jnp.float32)
        total += lax.dot_general(high_matrix, rest, form, preferred_element_type=jnp.float32)
        total += lax.dot_general(low_matrix, high, form, preferred_element_type=jnp.float32)
        for half in range(halves):
            for part in range(2):
                rows = pl.ds((half * 2 + part) * ROWS + station, LANES, stride=halves * 2 * ROWS)
                w_ref[rows, :] = total[
                    part * LANES : (part + 1) * LANES, half * LANES : (half + 1) * LANES
                ]

    share = w_ref.shape[0] // (columns * sources)
    band_rows = 2 * ROWS
    piece = 8 * band_rows
    for blocks, out_ref in zip(plan, out_refs):
        at = 0
        for across, along, start, stop in blocks:
            owner = lax.rem(chan + across, columns) * sources + lax.rem(tm + along, sources)
            for row in range(start * band_rows, stop * band_rows, piece):
                rows = pl.ds(pl.multiple_of(owner * share + row, piece), piece)
                out_ref[at : at + piece, :] = w_ref[rows, :].astype(jnp.bfloat16)
                at += piece


def channelise(place, chunk, voltages, come, taps_filter, tables, frames, columns, plan):
    sources = 1 + len(come)
    length = taps_filter.shape[1]
    spectra = sources * frames
    twiddle, matrix = tables
    out_rows = length // AVG * 2 * ROWS
    whole = pl.BlockSpec(memory_space=pltpu.VMEM)
    counts = [sum(stop - start for _, _, start, stop in blocks) for blocks in plan]
    flat = pl.pallas_call(
        lambda *refs: channelise_kernel(frames, chunk, columns, plan, *refs),
        out_shape=[
            jax.ShapeDtypeStruct((count * 2 * ROWS, LANES), jnp.bfloat16) for count in counts
        ],
        in_specs=[pl.BlockSpec(memory_space=pltpu.SMEM)]
        + [pl.BlockSpec(memory_space=pl.ANY)] * sources
        + [whole] * 3,
        out_specs=[whole] * len(plan),
        scratch_shapes=[
            pltpu.VMEM((sources, 2, ROWS, frames * length), jnp.bfloat16),
            pltpu.VMEM((RADIX, spectra, 2, ROWS, LANES), jnp.float32),
            pltpu.VMEM((ROWS * RADIX * spectra, LANES), jnp.float32),
            pltpu.VMEM((ROWS * RADIX * spectra, LANES), jnp.float32),
            pltpu.VMEM((out_rows, LANES), jnp.float32),
            pltpu.SemaphoreType.DMA((sources,)),
        ],
        compiler_params=pltpu.CompilerParams(vmem_limit_bytes=40 * 2**20),
        cost_estimate=pl.CostEstimate(
            flops=9 * 10**9, bytes_accessed=4 * 2**20, transcendentals=0
        ),
        name="channelise",
    )(place, voltages, *come, taps_filter, jnp.asarray(twiddle), jnp.asarray(matrix))
    return [piece.reshape(count, 2, ROWS, LANES) for piece, count in zip(flat, counts)]


def correlate_kernel(places, starts, width, place_ref, sel_ref, weight_ref, *refs):
    x_refs, (out_ref, x_all, rows_all, sems) = refs[: 2 * len(starts)], refs[-4:]
    tiles = out_ref.shape[0]
    band = pl.program_id(0)
    bands = x_all.shape[1]
    spans = [(0, 1), (1, bands)]

    def copies(span):
        first, last = spans[span]
        number = 0
        for index, (start, rows) in enumerate(zip(starts, places)):
            for side in range(2):
                x_ref = x_refs[2 * index + side]
                pol = lax.rem(place_ref[2] + side, 2)
                share = x_ref.shape[0] // len(rows)
                for block, at in enumerate(rows):
                    yield pltpu.make_async_copy(
                        x_ref.at[pl.ds(block * share + start + first, last - first)],
                        x_all.at[pol, pl.ds(first, last - first), :, pl.ds(at, ROWS), :],
                        sems.at[span, number],
                    )
                    number += 1

    @pl.when(band == 0)
    def _():
        for span in range(2):
            for copy in copies(span):
                copy.start()
        for copy in copies(0):
            copy.wait()

    @pl.when(band == 1)
    def _():
        for copy in copies(1):
            copy.wait()

    for pol in range(2):
        lanes = slice(pol * 2 * LANES, (pol + 1) * 2 * LANES)
        value = jnp.concatenate([x_all[pol, band, part] for part in range(2)], axis=1)
        picked = jnp.dot(sel_ref[...], value, preferred_element_type=jnp.float32)
        for tile in range(tiles):
            at = tile * 2 * width
            left = picked[at : at + width] * weight_ref[pl.ds(tile, 1), :]
            right = picked[at + width : at + 2 * width]
            rows_all[at : at + width, lanes] = left.astype(jnp.bfloat16)
            rows_all[at + width : at + 2 * width, lanes] = right.astype(jnp.bfloat16)
    form = (((1,), (1,)), ((), ()))
    for tile in range(tiles):
        at = tile * 2 * width
        left = jnp.concatenate(
            [rows_all[at : at + width, pol * 2 * LANES : (pol + 1) * 2 * LANES] for pol in range(2)]
        )
        at += width
        right = jnp.concatenate(
            [rows_all[at : at + width, pol * 2 * LANES : (pol + 1) * 2 * LANES] for pol in range(2)]
        )
        turned = jnp.concatenate([left[:, LANES:], -left[:, :LANES]], axis=1)
        both = jnp.concatenate([left, turned])
        result = lax.dot_general(both, right, form, preferred_element_type=jnp.float32)
        out_ref[tile, 0] = result.reshape(2, 2, width, 2 * width)


def correlate_tiles(
    place, select, weight, pieces, places, starts, width, first, count, bands, earlier
):
    tiles = weight.shape[0]
    whole = pl.BlockSpec(memory_space=pltpu.VMEM)
    more = [] if earlier is None else [earlier]
    blocks = 2 * sum(len(rows) for rows in places)
    return pl.pallas_call(
        lambda *refs: correlate_kernel(places, starts, width, *refs),
        grid=(count,),
        out_shape=jax.ShapeDtypeStruct((tiles, bands, 2, 2, width, 2 * width), jnp.float32),
        in_specs=[pl.BlockSpec(memory_space=pltpu.SMEM)]
        + [whole] * 2
        + [pl.BlockSpec(memory_space=pl.ANY)] * (len(pieces) + len(more)),
        out_specs=pl.BlockSpec(
            (tiles, 1, 2, 2, width, 2 * width), lambda g: (0, g + first, 0, 0, 0, 0)
        ),
        scratch_shapes=[
            pltpu.VMEM((2, count, 2, select.shape[1], LANES), jnp.bfloat16),
            pltpu.VMEM((tiles * 2 * width, 4 * LANES), jnp.bfloat16),
            pltpu.SemaphoreType.DMA((2, blocks)),
        ],
        input_output_aliases={3 + len(pieces): 0} if more else {},
        compiler_params=pltpu.CompilerParams(vmem_limit_bytes=32 * 2**20),
        cost_estimate=pl.CostEstimate(
            flops=13 * 10**9 * count // bands,
            bytes_accessed=42 * 2**20 * count // bands,
            transcendentals=0,
        ),
        name="correlate",
    )(place, select, weight, *pieces, *more)


def tile_tables(tile_a, tile_b, tile_owner, tile_flags, row_of):
    tiles = tile_owner.shape[0]
    held = tile_owner == lax.axis_index("pol")
    order = jnp.arange(tiles, dtype=jnp.int32)
    rank = jnp.sum((held[None, :] & (order[None, :] < order[:, None])).astype(jnp.int32), axis=1)
    slots = jnp.arange(CAP, dtype=jnp.int32)
    pick = (held[None, :] & (rank[None, :] == slots[:, None])).astype(jnp.int32)
    sides = jnp.stack([row_of(tile_a), row_of(tile_b)], axis=1) + 1
    rows = jnp.sum(pick[:, :, None, None] * sides[None], axis=1) - 1
    flags = jnp.sum(pick[:, :, None] * tile_flags[None], axis=1).astype(jnp.float32)
    return rows, flags


def on_device_chunks(voltages, taps_filter, tile_a, tile_b, tile_owner, tile_flags):
    length = taps_filter.shape[1]
    stations = voltages.shape[2]
    frames = voltages.shape[3] // length
    chan_count, time_count = lax.axis_size("chan"), lax.axis_size("tm")
    owners = chan_count * time_count
    chunk_count = stations // (time_count * ROWS)
    width = tile_a.shape[1]
    bands = length // AVG // owners
    tables = fourier_tables(length)

    chan, tm = lax.axis_index("chan"), lax.axis_index("tm")
    place = jnp.stack([chan, tm, lax.axis_index("pol")]).astype(jnp.int32)

    def row_of(station):
        column, rest = station // stations, station % stations
        block, inside = rest // (chunk_count * ROWS), rest % (chunk_count * ROWS)
        across = (chan - column) % chan_count
        behind = (tm - block) % time_count
        piece = across * time_count + behind
        return ((inside // ROWS) * owners + piece) * ROWS + inside % ROWS

    rows, flags = tile_tables(tile_a, tile_b, tile_owner, tile_flags, row_of)
    total_rows = chunk_count * owners * ROWS
    select = (rows[..., None] == jnp.arange(total_rows, dtype=jnp.int32)).astype(jnp.bfloat16)
    select = select.reshape(CAP * 2 * width, total_rows)
    depth = AVG * time_count * frames
    weight = jnp.tile(flags * (1.0 / depth), (1, 2 * AVG))

    samples = voltages.reshape(2, stations, frames * length)

    def travel(value, axes, distances):
        sizes = [lax.axis_size(axis) for axis in axes]
        pairs = []
        for index in np.ndindex(*sizes):
            target = [(i + d) % n for i, d, n in zip(index, distances, sizes)]
            pairs.append(tuple(int(np.ravel_multi_index(x, sizes)) for x in (index, target)))
        return lax.ppermute(value, axes, pairs)

    def after(values, earlier):
        return lax.optimization_barrier((list(values), list(earlier)))

    def block_for(values, chunk, distance):
        first = ((tm + distance) % time_count * chunk_count + chunk) * ROWS
        return lax.dynamic_slice(values, (0, first, 0), (2, ROWS, frames * length))

    def turn_time(blocks):
        return [travel(block, ("tm",), (d,)) for d, block in zip(distances, blocks)]

    def filtered(chunk, arrived, plan):
        arrived = [arrived[distances.index(d)] for d in range(1, time_count)]
        return channelise(
            place, chunk, samples, arrived, taps_filter, tables, frames, chan_count, plan
        )

    def across(values):
        return [travel(v, ("chan",), (1,)) for v in values]

    def columns(near, far):
        return jnp.stack([near, far])

    distances = [2, 1, 3]
    half = bands // 2
    spare = 1

    blocks = [block_for(samples, 0, d) for d in distances]
    blocks, (again,) = after(blocks, [samples])
    first = turn_time(blocks)
    blocks, held = after([block_for(again, 1, d) for d in distances], first[:-spare])
    first[:-spare] = held
    second = turn_time(blocks)

    plan = [[(x, z, 0, bands)] for x in range(2) for z in range(time_count)]
    spectra = filtered(0, first, plan)
    far, second[:1] = after(spectra[time_count:], second[:1])
    near, far = spectra[:time_count], across(far)
    mixed = [columns(near[z], far[z]) for z in range(time_count)]
    blocks, held = after([mixed[d] for d in distances], second[:-spare] + [select, weight])
    second[:-spare], (select, weight) = held[:-2], held[-2:]
    own_first = [mixed[0]] + turn_time(blocks)

    plan = [
        [(x, z, start, start + half) for z in range(time_count)]
        for start in (0, half)
        for x in range(2)
    ]
    spectra = filtered(1, second, plan)
    spectra = [v.reshape(time_count, half, 2, ROWS, LANES) for v in spectra]
    far, own_first[1:2] = after([spectra[1], spectra[3]], own_first[1:2])
    far_low, far_high = across(far)
    mixed = [columns(spectra[0][z], far_low[z]) for z in range(time_count)]
    blocks, held = after([mixed[d] for d in distances], own_first[1:-spare])
    own_first[1:-spare] = held
    own_low = [mixed[0]] + turn_time(blocks)
    mixed = [columns(spectra[2][z], far_high[z]) for z in range(time_count)]

    def with_other(values):
        values = [v.reshape((-1,) + v.shape[2:]) for v in values]
        return [side for v in values for side in (v, travel(v, ("pol",), (1,)))]

    both_first = with_other(own_first)
    blocks, held = after([mixed[d] for d in distances], own_low[1:-spare] + both_first[1::2])
    own_low[1:-spare], both_first[1::2] = held[: -time_count], held[-time_count:]
    own_high = [mixed[0]] + turn_time(blocks)

    both_low = with_other(own_low)
    places = [
        [((chunk * chan_count + x) * time_count + z) * ROWS for x in range(chan_count)]
        for chunk in range(chunk_count)
        for z in [0] + distances
    ]
    visibility = correlate_tiles(
        place, select, weight, both_first + both_low, places, [0] * 8, width,
        0, half, bands, None,
    )
    own_high, (visibility,) = after(own_high, [visibility])
    both_high = with_other(own_high)
    return correlate_tiles(
        place, select, weight, both_first + both_high, places, [half] * 4 + [0] * 4, width,
        half, half, bands, visibility,
    )


def on_device(voltages, taps_filter, tile_a, tile_b, tile_owner, tile_flags):
    taps, length = taps_filter.shape
    frames = voltages.shape[3] // length
    time_count = lax.axis_size("tm")
    fits = (
        length == RADIX * LANES
        and AVG * time_count * frames == LANES
        and 2 * tile_a.shape[1] == LANES
        and voltages.shape[2] == 2 * time_count * ROWS
        and (lax.axis_size("chan"), time_count) == (2, 4)
    )
    form = on_device_chunks if fits else on_device_any
    return form(voltages, taps_filter, tile_a, tile_b, tile_owner, tile_flags)


def solution(mesh):
    return jax.shard_map(
        on_device,
        mesh=mesh,
        in_specs=(P("grp", "pol", "chan", "tm"), P(), P(), P(), P(), P()),
        out_specs=P("pol", ("chan", "tm"), "grp", None, None, None),
        check_vma=False,
    )
```

```python
import math

import jax
import jax.numpy as jnp
import numpy as np
from jax import lax
from jax.experimental import pallas as pl
from jax.experimental.pallas import tpu as pltpu
from jax.sharding import PartitionSpec as P

AVG = 8
CAP = 8
RADIX = 16
LANES = 128
ROWS = 16


radix_first = 32


def from_behind(value, axis, steps):
    count = lax.axis_size(axis)
    first, last = (max(0, -steps), min(count, count - steps))
    return lax.ppermute(value, axis, [(source, source + steps) for source in range(first, last)])


def fourier(filtered):
    length = filtered.shape[-1]
    second = length // radix_first
    exact_mode = lax.Precision.HIGHEST
    grid = filtered.reshape(filtered.shape[:-1] + (radix_first, second))
    outer = jnp.arange(radix_first, dtype=jnp.int32)
    inner = jnp.arange(second, dtype=jnp.int32)
    phase_one = (
        2.0
        * math.pi
        / radix_first
        * (outer[:, None] * outer[None, :] % radix_first).astype(jnp.float32)
    )
    phase_twist = 2.0 * math.pi / length * (outer[:, None] * inner[None, :]).astype(jnp.float32)
    phase_two = (
        2.0 * math.pi / second * (inner[:, None] * inner[None, :] % second).astype(jnp.float32)
    )
    cos_one, sin_one = (jnp.cos(phase_one), jnp.sin(phase_one))
    cos_twist, sin_twist = (jnp.cos(phase_twist), jnp.sin(phase_twist))
    cos_two, sin_two = (jnp.cos(phase_two), jnp.sin(phase_two))
    first_form = "fk,stkj->stfj"
    section_re = jnp.einsum(first_form, cos_one, grid[0], precision=exact_mode) + jnp.einsum(
        first_form, sin_one, grid[1], precision=exact_mode
    )
    section_im = jnp.einsum(first_form, cos_one, grid[1], precision=exact_mode) - jnp.einsum(
        first_form, sin_one, grid[0], precision=exact_mode
    )
    turned_re = section_re * cos_twist + section_im * sin_twist
    turned_im = section_im * cos_twist - section_re * sin_twist
    second_form = "gj,stfj->stgf"
    final_re = jnp.einsum(second_form, cos_two, turned_re, precision=exact_mode) + jnp.einsum(
        second_form, sin_two, turned_im, precision=exact_mode
    )
    final_im = jnp.einsum(second_form, cos_two, turned_im, precision=exact_mode) - jnp.einsum(
        second_form, sin_two, turned_re, precision=exact_mode
    )
    joined = jnp.stack([final_re, final_im]).reshape(filtered.shape)
    return joined * (1.0 / math.sqrt(length))


def correlate(full, rows_a, rows_b, flags, group_count):
    depth = full.shape[4]
    weight = jnp.tile(flags.astype(jnp.bfloat16), depth // flags.shape[0])
    left_rows = jnp.take(full, rows_a, axis=2) * weight
    right_rows = jnp.take(full, rows_b, axis=2)
    stacked_left = jnp.stack(
        [
            jnp.concatenate([left_rows[0], left_rows[1]], axis=-1),
            jnp.concatenate([left_rows[1], -left_rows[0]], axis=-1),
        ]
    )
    joined_right = jnp.concatenate([right_rows[0], right_rows[1]], axis=-1)
    result = jnp.einsum(
        "rpank,qbnk->nrpaqb", stacked_left, joined_right, preferred_element_type=jnp.float32
    )
    width = rows_a.shape[0]
    return result.reshape(group_count, 2, 2, width, 2 * width) * (1.0 / depth)


def on_device_any(voltages, taps_filter, tile_a, tile_b, tile_owner, tile_flags):
    history = taps_filter.shape[0] - 1
    length = taps_filter.shape[1]
    stations = voltages.shape[2]
    frames = voltages.shape[3] // length
    local_blocks = voltages.reshape(2, stations, frames, length)
    hop_count = -(-history // frames)
    sending = local_blocks
    extended = local_blocks
    for hop_index in range(hop_count):
        sending = from_behind(sending, "tm", 1)
        extended = jnp.concatenate([sending, extended], axis=2)
    extended = extended[:, :, extended.shape[2] - history - frames :]
    filtered = jnp.zeros((2, stations, frames, length), jnp.float32)
    for tap_index in range(history + 1):
        start = history - tap_index
        filtered = filtered + taps_filter[tap_index] * extended[
            :, :, start : start + frames
        ].astype(jnp.float32)
    spectra = fourier(filtered).astype(jnp.bfloat16)
    chan_count = lax.axis_size("chan")
    time_count = lax.axis_size("tm")
    narrow = length // (chan_count * time_count)
    outgoing = spectra.reshape(2, stations, frames, chan_count, time_count, narrow)
    outgoing = outgoing.transpose(0, 3, 4, 5, 1, 2)
    flat = outgoing.reshape(2, chan_count * time_count, narrow, stations * frames)
    moved = lax.all_to_all(flat, ("chan", "tm"), split_axis=1, concat_axis=1, tiled=True)
    moved = moved.reshape(2, chan_count, time_count, narrow, stations, frames)
    bands = narrow // AVG
    every_station = chan_count * stations
    spectra_count = time_count * frames
    arranged = moved.transpose(0, 1, 4, 3, 2, 5).reshape(
        2, 1, every_station, bands, AVG * spectra_count
    )
    full = lax.all_gather(arranged, "pol", axis=1, tiled=True)
    position = lax.axis_index("pol")
    width = tile_a.shape[1]
    capacity = CAP
    held = tile_owner == position
    listed = jnp.nonzero(held, size=capacity, fill_value=0)[0].astype(jnp.int32)
    tally = jnp.sum(held.astype(jnp.int32))
    initial = jnp.zeros((capacity, bands, 2, 2, width, 2 * width), jnp.float32)

    def fill_slot(slot, results):
        chosen_tile = listed[slot]
        return results.at[slot].set(
            correlate(
                full, tile_a[chosen_tile], tile_b[chosen_tile], tile_flags[chosen_tile], bands
            )
        )

    visibility = lax.fori_loop(0, tally, fill_slot, initial)
    return visibility


def fourier_tables(length):
    low = np.arange(RADIX)
    lane = np.arange(LANES)
    turn = 2.0 * np.pi / length * np.outer(low, lane)
    twiddle = np.stack([np.cos(turn), np.sin(turn)]).astype(np.float32)
    angle = 2.0 * np.pi / LANES * (np.outer(lane, lane) % LANES)
    cos, sin = np.cos(angle) / math.sqrt(length), np.sin(angle) / math.sqrt(length)
    matrix = np.block([[cos, sin], [-sin, cos]]).astype(np.float32)
    high = matrix.astype(jnp.bfloat16)
    rest = (matrix - high.astype(np.float32)).astype(jnp.bfloat16)
    return twiddle, np.stack([high, rest])


def butterflies(values):
    count = len(values)
    if count == 1:
        return values
    even, odd = butterflies(values[0::2]), butterflies(values[1::2])
    first, second = [], []
    for index in range(count // 2):
        (a, b), (c, d) = even[index], odd[index]
        if index == 0:
            e, f = c, d
        elif 4 * index == count:
            e, f = d, -c
        elif 8 * index == count:
            root = math.sqrt(0.5)
            e, f = (c + d) * root, (d - c) * root
        elif 8 * index == 3 * count:
            root = math.sqrt(0.5)
            e, f = (d - c) * root, -(c + d) * root
        else:
            turn = 2.0 * math.pi * index / count
            cos, sin = math.cos(turn), math.sin(turn)
            e, f = c * cos + d * sin, d * cos - c * sin
        first.append((a + e, b + f))
        second.append((a - e, b - f))
    return first + second


def channelise_kernel(frames, chunk, columns, plan, place_ref, own_ref, *refs):
    sources = refs[-6].shape[0]
    come_refs = refs[: sources - 1]
    taps_ref, twiddle_ref, matrix_ref = refs[sources - 1 : sources + 2]
    out_refs = refs[sources + 2 : -6]
    x_ref, fil_ref, zr_ref, zi_ref, w_ref, sems = refs[-6:]
    chan, tm = place_ref[0], place_ref[1]
    own_rows = pl.multiple_of((tm * (own_ref.shape[1] // (sources * ROWS)) + chunk) * ROWS, ROWS)
    copies = []
    for behind in range(sources):
        block = come_refs[behind - 1] if behind else own_ref.at[:, pl.ds(own_rows, ROWS), :]
        slot = lax.rem(tm - behind + sources, sources)
        copies.append(pltpu.make_async_copy(block, x_ref.at[slot], sems.at[behind]))
    for copy in copies:
        copy.start()
    for copy in copies:
        copy.wait()
    spectra = sources * frames
    length = taps_ref.shape[1]
    taps = taps_ref.shape[0]
    depth = RADIX * spectra
    z_refs = (zr_ref, zi_ref)

    @pl.loop(0, RADIX)
    def _(section):
        at = pl.multiple_of(section * LANES, LANES)
        weights = [taps_ref[pl.ds(m, 1), pl.ds(at, LANES)] for m in range(taps)]
        for part in range(2):
            blocks = []
            for t in range(spectra):
                lane = pl.multiple_of((t % frames) * length + section * LANES, LANES)
                blocks.append(x_ref[t // frames, part, :, pl.ds(lane, LANES)].astype(jnp.float32))
            for t in range(spectra):
                total = weights[0] * blocks[t]
                for m in range(1, min(t + 1, taps)):
                    total = total + weights[m] * blocks[t - m]
                fil_ref[section, t, part] = total

    @pl.loop(0, spectra)
    def _(t):
        for half in range(ROWS // 8):
            values = [
                tuple(fil_ref[section, t, part, pl.ds(half * 8, 8), :] for part in range(2))
                for section in range(RADIX)
            ]
            for low, (re, im) in enumerate(butterflies(values)):
                if low:
                    cos = twiddle_ref[0, pl.ds(low, 1), :]
                    sin = twiddle_ref[1, pl.ds(low, 1), :]
                    re, im = re * cos + im * sin, im * cos - re * sin
                rows = pl.ds(half * 8 * depth + low * spectra + t, 8, stride=depth)
                zr_ref[rows, :] = re
                zi_ref[rows, :] = im

    form = (((1,), (1,)), ((), ()))
    high_matrix, low_matrix = matrix_ref[0], matrix_ref[1]
    halves = depth // LANES

    @pl.loop(0, ROWS)
    def _(station):
        rows = pl.ds(pl.multiple_of(station * depth, depth), depth)
        value = jnp.concatenate([ref[rows, :] for ref in z_refs], axis=1)
        high = value.astype(jnp.bfloat16)
        rest = (value - high.astype(jnp.float32)).astype(jnp.bfloat16)
        total = lax.dot_general(high_matrix, high, form, preferred_element_type=jnp.float32)
        total += lax.dot_general(high_matrix, rest, form, preferred_element_type=jnp.float32)
        total += lax.dot_general(low_matrix, high, form, preferred_element_type=jnp.float32)
        for half in range(halves):
            for part in range(2):
                rows = pl.ds((half * 2 + part) * ROWS + station, LANES, stride=halves * 2 * ROWS)
                w_ref[rows, :] = total[
                    part * LANES : (part + 1) * LANES, half * LANES : (half + 1) * LANES
                ]

    share = w_ref.shape[0] // (columns * sources)
    band_rows = 2 * ROWS
    piece = 4 * band_rows
    for blocks, out_ref in zip(plan, out_refs):
        at = 0
        for across, along, start, stop in blocks:
            owner = lax.rem(chan + across, columns) * sources + lax.rem(tm + along, sources)
            for row in range(start * band_rows, stop * band_rows, piece):
                rows = pl.ds(pl.multiple_of(owner * share + row, piece), piece)
                out_ref[at : at + piece, :] = w_ref[rows, :].astype(jnp.bfloat16)
                at += piece


def channelise(place, chunk, voltages, come, taps_filter, tables, frames, columns, plan):
    sources = 1 + len(come)
    length = taps_filter.shape[1]
    spectra = sources * frames
    twiddle, matrix = tables
    out_rows = length // AVG * 2 * ROWS
    whole = pl.BlockSpec(memory_space=pltpu.VMEM)
    counts = [sum(stop - start for _, _, start, stop in blocks) for blocks in plan]
    flat = pl.pallas_call(
        lambda *refs: channelise_kernel(frames, chunk, columns, plan, *refs),
        out_shape=[
            jax.ShapeDtypeStruct((count * 2 * ROWS, LANES), jnp.bfloat16) for count in counts
        ],
        in_specs=[pl.BlockSpec(memory_space=pltpu.SMEM)]
        + [pl.BlockSpec(memory_space=pl.ANY)] * sources
        + [whole] * 3,
        out_specs=[whole] * len(plan),
        scratch_shapes=[
            pltpu.VMEM((sources, 2, ROWS, frames * length), jnp.bfloat16),
            pltpu.VMEM((RADIX, spectra, 2, ROWS, LANES), jnp.float32),
            pltpu.VMEM((ROWS * RADIX * spectra, LANES), jnp.float32),
            pltpu.VMEM((ROWS * RADIX * spectra, LANES), jnp.float32),
            pltpu.VMEM((out_rows, LANES), jnp.float32),
            pltpu.SemaphoreType.DMA((sources,)),
        ],
        compiler_params=pltpu.CompilerParams(vmem_limit_bytes=40 * 2**20),
        cost_estimate=pl.CostEstimate(
            flops=9 * 10**9, bytes_accessed=4 * 2**20, transcendentals=0
        ),
        name="channelise",
    )(place, voltages, *come, taps_filter, jnp.asarray(twiddle), jnp.asarray(matrix))
    return [piece.reshape(count, 2, ROWS, LANES) for piece, count in zip(flat, counts)]


def correlate_kernel(places, starts, width, place_ref, sel_ref, weight_ref, *refs):
    x_refs, (out_ref, x_all, rows_all, sems) = refs[: 2 * len(starts)], refs[-4:]
    tiles = out_ref.shape[0]
    band = pl.program_id(0)
    bands = x_all.shape[1]
    spans = [(0, 1), (1, bands)]

    def copies(span):
        first, last = spans[span]
        number = 0
        for index, (start, rows) in enumerate(zip(starts, places)):
            for side in range(2):
                x_ref = x_refs[2 * index + side]
                pol = lax.rem(place_ref[2] + side, 2)
                share = x_ref.shape[0] // len(rows)
                for block, at in enumerate(rows):
                    yield pltpu.make_async_copy(
                        x_ref.at[pl.ds(block * share + start + first, last - first)],
                        x_all.at[pol, pl.ds(first, last - first), :, pl.ds(at, ROWS), :],
                        sems.at[span, number],
                    )
                    number += 1

    @pl.when(band == 0)
    def _():
        for span in range(2):
            for copy in copies(span):
                copy.start()
        for copy in copies(0):
            copy.wait()

    @pl.when(band == 1)
    def _():
        for copy in copies(1):
            copy.wait()

    for pol in range(2):
        lanes = slice(pol * 2 * LANES, (pol + 1) * 2 * LANES)
        value = jnp.concatenate([x_all[pol, band, part] for part in range(2)], axis=1)
        picked = jnp.dot(sel_ref[...], value, preferred_element_type=jnp.float32)
        for tile in range(tiles):
            at = tile * 2 * width
            left = picked[at : at + width] * weight_ref[pl.ds(tile, 1), :]
            right = picked[at + width : at + 2 * width]
            rows_all[at : at + width, lanes] = left.astype(jnp.bfloat16)
            rows_all[at + width : at + 2 * width, lanes] = right.astype(jnp.bfloat16)
    form = (((1,), (1,)), ((), ()))
    for tile in range(tiles):
        at = tile * 2 * width
        left = jnp.concatenate(
            [rows_all[at : at + width, pol * 2 * LANES : (pol + 1) * 2 * LANES] for pol in range(2)]
        )
        at += width
        right = jnp.concatenate(
            [rows_all[at : at + width, pol * 2 * LANES : (pol + 1) * 2 * LANES] for pol in range(2)]
        )
        turned = jnp.concatenate([left[:, LANES:], -left[:, :LANES]], axis=1)
        both = jnp.concatenate([left, turned])
        result = lax.dot_general(both, right, form, preferred_element_type=jnp.float32)
        out_ref[tile, 0] = result.reshape(2, 2, width, 2 * width)


def correlate_tiles(
    place, select, weight, pieces, places, starts, width, first, count, bands, earlier
):
    tiles = weight.shape[0]
    whole = pl.BlockSpec(memory_space=pltpu.VMEM)
    more = [] if earlier is None else [earlier]
    blocks = 2 * sum(len(rows) for rows in places)
    return pl.pallas_call(
        lambda *refs: correlate_kernel(places, starts, width, *refs),
        grid=(count,),
        out_shape=jax.ShapeDtypeStruct((tiles, bands, 2, 2, width, 2 * width), jnp.float32),
        in_specs=[pl.BlockSpec(memory_space=pltpu.SMEM)]
        + [whole] * 2
        + [pl.BlockSpec(memory_space=pl.ANY)] * (len(pieces) + len(more)),
        out_specs=pl.BlockSpec(
            (tiles, 1, 2, 2, width, 2 * width), lambda g: (0, g + first, 0, 0, 0, 0)
        ),
        scratch_shapes=[
            pltpu.VMEM((2, count, 2, select.shape[1], LANES), jnp.bfloat16),
            pltpu.VMEM((tiles * 2 * width, 4 * LANES), jnp.bfloat16),
            pltpu.SemaphoreType.DMA((2, blocks)),
        ],
        input_output_aliases={3 + len(pieces): 0} if more else {},
        compiler_params=pltpu.CompilerParams(vmem_limit_bytes=32 * 2**20),
        cost_estimate=pl.CostEstimate(
            flops=13 * 10**9 * count // bands,
            bytes_accessed=42 * 2**20 * count // bands,
            transcendentals=0,
        ),
        name="correlate",
    )(place, select, weight, *pieces, *more)


def tile_tables(tile_a, tile_b, tile_owner, tile_flags, row_of):
    tiles = tile_owner.shape[0]
    held = tile_owner == lax.axis_index("pol")
    order = jnp.arange(tiles, dtype=jnp.int32)
    rank = jnp.sum((held[None, :] & (order[None, :] < order[:, None])).astype(jnp.int32), axis=1)
    slots = jnp.arange(CAP, dtype=jnp.int32)
    pick = (held[None, :] & (rank[None, :] == slots[:, None])).astype(jnp.int32)
    sides = jnp.stack([row_of(tile_a), row_of(tile_b)], axis=1) + 1
    rows = jnp.sum(pick[:, :, None, None] * sides[None], axis=1) - 1
    flags = jnp.sum(pick[:, :, None] * tile_flags[None], axis=1).astype(jnp.float32)
    return rows, flags


def on_device_chunks(voltages, taps_filter, tile_a, tile_b, tile_owner, tile_flags):
    length = taps_filter.shape[1]
    stations = voltages.shape[2]
    frames = voltages.shape[3] // length
    chan_count, time_count = lax.axis_size("chan"), lax.axis_size("tm")
    owners = chan_count * time_count
    chunk_count = stations // (time_count * ROWS)
    width = tile_a.shape[1]
    bands = length // AVG // owners
    tables = fourier_tables(length)

    chan, tm = lax.axis_index("chan"), lax.axis_index("tm")
    place = jnp.stack([chan, tm, lax.axis_index("pol")]).astype(jnp.int32)

    def row_of(station):
        column, rest = station // stations, station % stations
        block, inside = rest // (chunk_count * ROWS), rest % (chunk_count * ROWS)
        across = (chan - column) % chan_count
        behind = (tm - block) % time_count
        piece = across * time_count + behind
        return ((inside // ROWS) * owners + piece) * ROWS + inside % ROWS

    rows, flags = tile_tables(tile_a, tile_b, tile_owner, tile_flags, row_of)
    total_rows = chunk_count * owners * ROWS
    select = (rows[..., None] == jnp.arange(total_rows, dtype=jnp.int32)).astype(jnp.bfloat16)
    select = select.reshape(CAP * 2 * width, total_rows)
    depth = AVG * time_count * frames
    weight = jnp.tile(flags * (1.0 / depth), (1, 2 * AVG))

    samples = voltages.reshape(2, stations, frames * length)

    def travel(value, axes, distances):
        sizes = [lax.axis_size(axis) for axis in axes]
        pairs = []
        for index in np.ndindex(*sizes):
            target = [(i + d) % n for i, d, n in zip(index, distances, sizes)]
            pairs.append(tuple(int(np.ravel_multi_index(x, sizes)) for x in (index, target)))
        return lax.ppermute(value, axes, pairs)

    def after(values, earlier):
        return lax.optimization_barrier((list(values), list(earlier)))

    def block_for(values, chunk, distance):
        first = ((tm + distance) % time_count * chunk_count + chunk) * ROWS
        return lax.dynamic_slice(values, (0, first, 0), (2, ROWS, frames * length))

    def turn_time(blocks, distances):
        return [travel(block, ("tm",), (d,)) for d, block in zip(distances, blocks)]

    def filtered(chunk, arrived, plan):
        arrived = [arrived[distances.index(d)] for d in range(1, time_count)]
        return channelise(
            place, chunk, samples, arrived, taps_filter, tables, frames, chan_count, plan
        )

    def across(values):
        return [travel(v, ("chan",), (1,)) for v in values]

    distances = [2, 1, 3]
    spare = 1
    cuts = [0, bands * 3 // 8, bands * 3 // 4, bands]
    spans = list(zip(cuts[:-1], cuts[1:]))

    head, (again,) = after([block_for(samples, 0, distances[0])], [samples])
    first = turn_time(head, distances[:1])
    blocks, (again,) = after([block_for(again, 0, d) for d in distances[1:]], [again])
    first += turn_time(blocks, distances[1:])
    blocks, held = after([block_for(again, 1, d) for d in distances[1:]], first[:-spare])
    first[:-spare] = held
    second = turn_time(blocks, distances[1:])
    blocks, held = after([block_for(again, 1, distances[0])], second[:1])
    second[:1] = held
    second = turn_time(blocks, distances[:1]) + second

    def parts_of(spans):
        return [
            [(x, z, *span) for z in [0] + distances] for span in spans for x in range(chan_count)
        ]

    def columns(spans, near, far):
        mixed = []
        for (start, stop), near_part, far_part in zip(spans, near, far):
            shape = (time_count, stop - start, 2, ROWS, LANES)
            near_part, far_part = near_part.reshape(shape), far_part.reshape(shape)
            mixed.append([jnp.stack([near_part[z], far_part[z]]) for z in range(time_count)])
        return mixed

    def part_of(value, group, span):
        value = value.reshape((time_count, group[1] - group[0]) + value.shape[1:])
        return value[:, span[0] - group[0] : span[1] - group[0]]

    whole = [(0, bands)]
    spectra = filtered(0, first, parts_of(whole))
    far, second[1:] = after(spectra[1::2], second[1:])
    (mixed,) = columns(whole, spectra[0::2], across(far))
    blocks, held = after(mixed[1:], second[:1] + [select, weight])
    second[:1], (select, weight) = held[:1], held[1:]
    moved = turn_time(blocks, distances)

    groups = [spans[0], (spans[0][1], bands)]
    spectra = filtered(1, second, parts_of(groups))
    far, moved[:1] = after(spectra[1::2], moved[:1])
    early = [mixed[0]] + moved
    far = across(far)
    near = [part_of(spectra[0], groups[0], spans[0])]
    near += [part_of(spectra[2], groups[1], span) for span in spans[1:]]
    far = [part_of(far[0], groups[0], spans[0])] + [
        part_of(far[1], groups[1], span) for span in spans[1:]
    ]
    mixed = columns(spans, near, far)

    def with_other(values):
        values = [v.reshape((-1,) + v.shape[-3:]) for v in values]
        return [side for v in values for side in (v, travel(v, ("pol",), (1,)))]

    def row(chunk, x, z):
        return ((chunk * chan_count + x) * time_count + z) * ROWS

    blocks, held = after(mixed[0][1:], early[1:-spare])
    early[1:-spare] = held
    late = [[mixed[0][0]] + turn_time(blocks, distances)]
    early = with_other([jnp.stack(early)])
    order = [0] + distances
    early_places = [[row(0, x, z) for z in order for x in range(chan_count)]]
    late_places = [[row(1, x, z) for x in range(chan_count)] for z in order]

    visibility = None
    for number, (start, stop) in enumerate(spans):
        pieces, places = late[number], late_places
        if visibility is not None:
            pieces, (visibility,) = after(pieces, [visibility])
        if number + 1 < len(spans):
            held = pieces[1:-spare] + (early[1:] if number == 0 else [])
            blocks, held = after(mixed[number + 1][1:], held)
            pieces[1:-spare] = held[: time_count - 1 - spare]
            if number == 0:
                early[1:] = held[time_count - 1 - spare :]
            late.append([mixed[number + 1][0]] + turn_time(blocks, distances))
            pieces, places = [jnp.stack(pieces)], [sum(late_places, [])]
        visibility = correlate_tiles(
            place, select, weight, early + with_other(pieces), early_places + places,
            [start] + [0] * len(places), width, start, stop - start, bands, visibility,
        )
    return visibility


def on_device(voltages, taps_filter, tile_a, tile_b, tile_owner, tile_flags):
    taps, length = taps_filter.shape
    frames = voltages.shape[3] // length
    time_count = lax.axis_size("tm")
    fits = (
        length == RADIX * LANES
        and AVG * time_count * frames == LANES
        and 2 * tile_a.shape[1] == LANES
        and voltages.shape[2] == 2 * time_count * ROWS
        and (lax.axis_size("chan"), time_count) == (2, 4)
    )
    form = on_device_chunks if fits else on_device_any
    return form(voltages, taps_filter, tile_a, tile_b, tile_owner, tile_flags)


def solution(mesh):
    return jax.shard_map(
        on_device,
        mesh=mesh,
        in_specs=(P("grp", "pol", "chan", "tm"), P(), P(), P(), P(), P()),
        out_specs=P("pol", ("chan", "tm"), "grp", None, None, None),
        check_vma=False,
    )
```

```python
import math

import jax
import jax.numpy as jnp
import numpy as np
from jax import lax
from jax.experimental import pallas as pl
from jax.experimental.pallas import tpu as pltpu
from jax.sharding import PartitionSpec as P

AVG = 8
CAP = 8
RADIX = 16
LANES = 128
ROWS = 16


radix_first = 32


def from_behind(value, axis, steps):
    count = lax.axis_size(axis)
    first, last = (max(0, -steps), min(count, count - steps))
    return lax.ppermute(value, axis, [(source, source + steps) for source in range(first, last)])


def fourier(filtered):
    length = filtered.shape[-1]
    second = length // radix_first
    exact_mode = lax.Precision.HIGHEST
    grid = filtered.reshape(filtered.shape[:-1] + (radix_first, second))
    outer = jnp.arange(radix_first, dtype=jnp.int32)
    inner = jnp.arange(second, dtype=jnp.int32)
    phase_one = (
        2.0
        * math.pi
        / radix_first
        * (outer[:, None] * outer[None, :] % radix_first).astype(jnp.float32)
    )
    phase_twist = 2.0 * math.pi / length * (outer[:, None] * inner[None, :]).astype(jnp.float32)
    phase_two = (
        2.0 * math.pi / second * (inner[:, None] * inner[None, :] % second).astype(jnp.float32)
    )
    cos_one, sin_one = (jnp.cos(phase_one), jnp.sin(phase_one))
    cos_twist, sin_twist = (jnp.cos(phase_twist), jnp.sin(phase_twist))
    cos_two, sin_two = (jnp.cos(phase_two), jnp.sin(phase_two))
    first_form = "fk,stkj->stfj"
    section_re = jnp.einsum(first_form, cos_one, grid[0], precision=exact_mode) + jnp.einsum(
        first_form, sin_one, grid[1], precision=exact_mode
    )
    section_im = jnp.einsum(first_form, cos_one, grid[1], precision=exact_mode) - jnp.einsum(
        first_form, sin_one, grid[0], precision=exact_mode
    )
    turned_re = section_re * cos_twist + section_im * sin_twist
    turned_im = section_im * cos_twist - section_re * sin_twist
    second_form = "gj,stfj->stgf"
    final_re = jnp.einsum(second_form, cos_two, turned_re, precision=exact_mode) + jnp.einsum(
        second_form, sin_two, turned_im, precision=exact_mode
    )
    final_im = jnp.einsum(second_form, cos_two, turned_im, precision=exact_mode) - jnp.einsum(
        second_form, sin_two, turned_re, precision=exact_mode
    )
    joined = jnp.stack([final_re, final_im]).reshape(filtered.shape)
    return joined * (1.0 / math.sqrt(length))


def correlate(full, rows_a, rows_b, flags, group_count):
    depth = full.shape[4]
    weight = jnp.tile(flags.astype(jnp.bfloat16), depth // flags.shape[0])
    left_rows = jnp.take(full, rows_a, axis=2) * weight
    right_rows = jnp.take(full, rows_b, axis=2)
    stacked_left = jnp.stack(
        [
            jnp.concatenate([left_rows[0], left_rows[1]], axis=-1),
            jnp.concatenate([left_rows[1], -left_rows[0]], axis=-1),
        ]
    )
    joined_right = jnp.concatenate([right_rows[0], right_rows[1]], axis=-1)
    result = jnp.einsum(
        "rpank,qbnk->nrpaqb", stacked_left, joined_right, preferred_element_type=jnp.float32
    )
    width = rows_a.shape[0]
    return result.reshape(group_count, 2, 2, width, 2 * width) * (1.0 / depth)


def on_device_any(voltages, taps_filter, tile_a, tile_b, tile_owner, tile_flags):
    history = taps_filter.shape[0] - 1
    length = taps_filter.shape[1]
    stations = voltages.shape[2]
    frames = voltages.shape[3] // length
    local_blocks = voltages.reshape(2, stations, frames, length)
    hop_count = -(-history // frames)
    sending = local_blocks
    extended = local_blocks
    for hop_index in range(hop_count):
        sending = from_behind(sending, "tm", 1)
        extended = jnp.concatenate([sending, extended], axis=2)
    extended = extended[:, :, extended.shape[2] - history - frames :]
    filtered = jnp.zeros((2, stations, frames, length), jnp.float32)
    for tap_index in range(history + 1):
        start = history - tap_index
        filtered = filtered + taps_filter[tap_index] * extended[
            :, :, start : start + frames
        ].astype(jnp.float32)
    spectra = fourier(filtered).astype(jnp.bfloat16)
    chan_count = lax.axis_size("chan")
    time_count = lax.axis_size("tm")
    narrow = length // (chan_count * time_count)
    outgoing = spectra.reshape(2, stations, frames, chan_count, time_count, narrow)
    outgoing = outgoing.transpose(0, 3, 4, 5, 1, 2)
    flat = outgoing.reshape(2, chan_count * time_count, narrow, stations * frames)
    moved = lax.all_to_all(flat, ("chan", "tm"), split_axis=1, concat_axis=1, tiled=True)
    moved = moved.reshape(2, chan_count, time_count, narrow, stations, frames)
    bands = narrow // AVG
    every_station = chan_count * stations
    spectra_count = time_count * frames
    arranged = moved.transpose(0, 1, 4, 3, 2, 5).reshape(
        2, 1, every_station, bands, AVG * spectra_count
    )
    full = lax.all_gather(arranged, "pol", axis=1, tiled=True)
    position = lax.axis_index("pol")
    width = tile_a.shape[1]
    capacity = CAP
    held = tile_owner == position
    listed = jnp.nonzero(held, size=capacity, fill_value=0)[0].astype(jnp.int32)
    tally = jnp.sum(held.astype(jnp.int32))
    initial = jnp.zeros((capacity, bands, 2, 2, width, 2 * width), jnp.float32)

    def fill_slot(slot, results):
        chosen_tile = listed[slot]
        return results.at[slot].set(
            correlate(
                full, tile_a[chosen_tile], tile_b[chosen_tile], tile_flags[chosen_tile], bands
            )
        )

    visibility = lax.fori_loop(0, tally, fill_slot, initial)
    return visibility


def fourier_tables(length):
    low = np.arange(RADIX)
    lane = np.arange(LANES)
    turn = 2.0 * np.pi / length * np.outer(low, lane)
    twiddle = np.stack([np.cos(turn), np.sin(turn)]).astype(np.float32)
    angle = 2.0 * np.pi / LANES * (np.outer(lane, lane) % LANES)
    cos, sin = np.cos(angle) / math.sqrt(length), np.sin(angle) / math.sqrt(length)
    matrix = np.block([[cos, sin], [-sin, cos]]).astype(np.float32)
    high = matrix.astype(jnp.bfloat16)
    rest = (matrix - high.astype(np.float32)).astype(jnp.bfloat16)
    return twiddle, np.stack([high, rest])


def butterflies(values):
    count = len(values)
    if count == 1:
        return values
    even, odd = butterflies(values[0::2]), butterflies(values[1::2])
    first, second = [], []
    for index in range(count // 2):
        (a, b), (c, d) = even[index], odd[index]
        if index == 0:
            e, f = c, d
        elif 4 * index == count:
            e, f = d, -c
        elif 8 * index == count:
            root = math.sqrt(0.5)
            e, f = (c + d) * root, (d - c) * root
        elif 8 * index == 3 * count:
            root = math.sqrt(0.5)
            e, f = (d - c) * root, -(c + d) * root
        else:
            turn = 2.0 * math.pi * index / count
            cos, sin = math.cos(turn), math.sin(turn)
            e, f = c * cos + d * sin, d * cos - c * sin
        first.append((a + e, b + f))
        second.append((a - e, b - f))
    return first + second


def channelise_kernel(frames, chunk, columns, plan, place_ref, own_ref, *refs):
    sources = refs[-6].shape[0]
    come_refs = refs[: sources - 1]
    taps_ref, twiddle_ref, matrix_ref = refs[sources - 1 : sources + 2]
    out_refs = refs[sources + 2 : -6]
    x_ref, fil_ref, zr_ref, zi_ref, w_ref, sems = refs[-6:]
    chan, tm = place_ref[0], place_ref[1]
    own_rows = pl.multiple_of((tm * (own_ref.shape[1] // (sources * ROWS)) + chunk) * ROWS, ROWS)
    copies = []
    for behind in range(sources):
        block = come_refs[behind - 1] if behind else own_ref.at[:, pl.ds(own_rows, ROWS), :]
        slot = lax.rem(tm - behind + sources, sources)
        copies.append(pltpu.make_async_copy(block, x_ref.at[slot], sems.at[behind]))
    for copy in copies:
        copy.start()
    for copy in copies:
        copy.wait()
    spectra = sources * frames
    length = taps_ref.shape[1]
    taps = taps_ref.shape[0]
    depth = RADIX * spectra
    z_refs = (zr_ref, zi_ref)

    @pl.loop(0, RADIX)
    def _(section):
        at = pl.multiple_of(section * LANES, LANES)
        weights = [taps_ref[pl.ds(m, 1), pl.ds(at, LANES)] for m in range(taps)]
        for part in range(2):
            blocks = []
            for t in range(spectra):
                lane = pl.multiple_of((t % frames) * length + section * LANES, LANES)
                blocks.append(x_ref[t // frames, part, :, pl.ds(lane, LANES)].astype(jnp.float32))
            for t in range(spectra):
                total = weights[0] * blocks[t]
                for m in range(1, min(t + 1, taps)):
                    total = total + weights[m] * blocks[t - m]
                fil_ref[section, t, part] = total

    @pl.loop(0, spectra)
    def _(t):
        for half in range(ROWS // 8):
            values = [
                tuple(fil_ref[section, t, part, pl.ds(half * 8, 8), :] for part in range(2))
                for section in range(RADIX)
            ]
            for low, (re, im) in enumerate(butterflies(values)):
                if low:
                    cos = twiddle_ref[0, pl.ds(low, 1), :]
                    sin = twiddle_ref[1, pl.ds(low, 1), :]
                    re, im = re * cos + im * sin, im * cos - re * sin
                rows = pl.ds(half * 8 * depth + low * spectra + t, 8, stride=depth)
                zr_ref[rows, :] = re
                zi_ref[rows, :] = im

    form = (((1,), (1,)), ((), ()))
    high_matrix, low_matrix = matrix_ref[0], matrix_ref[1]
    halves = depth // LANES

    @pl.loop(0, ROWS)
    def _(station):
        rows = pl.ds(pl.multiple_of(station * depth, depth), depth)
        value = jnp.concatenate([ref[rows, :] for ref in z_refs], axis=1)
        high = value.astype(jnp.bfloat16)
        rest = (value - high.astype(jnp.float32)).astype(jnp.bfloat16)
        total = lax.dot_general(high_matrix, high, form, preferred_element_type=jnp.float32)
        total += lax.dot_general(high_matrix, rest, form, preferred_element_type=jnp.float32)
        total += lax.dot_general(low_matrix, high, form, preferred_element_type=jnp.float32)
        for half in range(halves):
            for part in range(2):
                rows = pl.ds((half * 2 + part) * ROWS + station, LANES, stride=halves * 2 * ROWS)
                w_ref[rows, :] = total[
                    part * LANES : (part + 1) * LANES, half * LANES : (half + 1) * LANES
                ]

    share = w_ref.shape[0] // (columns * sources)
    band_rows = 2 * ROWS
    piece = 4 * band_rows
    for blocks, out_ref in zip(plan, out_refs):
        at = 0
        for across, along, start, stop in blocks:
            owner = lax.rem(chan + across, columns) * sources + lax.rem(tm + along, sources)
            for row in range(start * band_rows, stop * band_rows, piece):
                rows = pl.ds(pl.multiple_of(owner * share + row, piece), piece)
                out_ref[at : at + piece, :] = w_ref[rows, :].astype(jnp.bfloat16)
                at += piece


def channelise(place, chunk, voltages, come, taps_filter, tables, frames, columns, plan):
    sources = 1 + len(come)
    length = taps_filter.shape[1]
    spectra = sources * frames
    twiddle, matrix = tables
    out_rows = length // AVG * 2 * ROWS
    whole = pl.BlockSpec(memory_space=pltpu.VMEM)
    counts = [sum(stop - start for _, _, start, stop in blocks) for blocks in plan]
    flat = pl.pallas_call(
        lambda *refs: channelise_kernel(frames, chunk, columns, plan, *refs),
        out_shape=[
            jax.ShapeDtypeStruct((count * 2 * ROWS, LANES), jnp.bfloat16) for count in counts
        ],
        in_specs=[pl.BlockSpec(memory_space=pltpu.SMEM)]
        + [pl.BlockSpec(memory_space=pl.ANY)] * sources
        + [whole] * 3,
        out_specs=[whole] * len(plan),
        scratch_shapes=[
            pltpu.VMEM((sources, 2, ROWS, frames * length), jnp.bfloat16),
            pltpu.VMEM((RADIX, spectra, 2, ROWS, LANES), jnp.float32),
            pltpu.VMEM((ROWS * RADIX * spectra, LANES), jnp.float32),
            pltpu.VMEM((ROWS * RADIX * spectra, LANES), jnp.float32),
            pltpu.VMEM((out_rows, LANES), jnp.float32),
            pltpu.SemaphoreType.DMA((sources,)),
        ],
        compiler_params=pltpu.CompilerParams(vmem_limit_bytes=40 * 2**20),
        cost_estimate=pl.CostEstimate(
            flops=9 * 10**9, bytes_accessed=4 * 2**20, transcendentals=0
        ),
        name="channelise",
    )(place, voltages, *come, taps_filter, jnp.asarray(twiddle), jnp.asarray(matrix))
    return [piece.reshape(count, 2, ROWS, LANES) for piece, count in zip(flat, counts)]


def correlate_kernel(starts, width, place_ref, sel_ref, weight_ref, *refs):
    x_refs, (out_ref, x_all, even_rows, odd_rows, sems) = refs[: 2 * len(starts)], refs[-5:]
    tiles = out_ref.shape[0]
    step = pl.program_id(0)
    bands = x_all.shape[2]
    spans = [(0, 2), (2, bands)]

    def copies(span):
        first, last = spans[span]
        block = 0
        for index, start in enumerate(starts):
            blocks = x_refs[2 * index].shape[0]
            for side in range(2):
                yield pltpu.make_async_copy(
                    x_refs[2 * index + side].at[:, pl.ds(start + first, last - first)],
                    x_all.at[
                        lax.rem(place_ref[2] + side, 2),
                        pl.ds(block, blocks),
                        pl.ds(first, last - first),
                    ],
                    sems.at[span, 2 * index + side],
                )
            block += blocks

    def gather(band, rows_ref):
        for pol in range(2):
            lanes = slice(pol * 2 * LANES, (pol + 1) * 2 * LANES)
            value = jnp.concatenate(
                [
                    jnp.concatenate([x_all[pol, block, band, part] for part in range(2)], axis=1)
                    for block in range(x_all.shape[1])
                ]
            )
            picked = jnp.dot(sel_ref[...], value, preferred_element_type=jnp.float32)
            for tile in range(tiles):
                at = tile * 2 * width
                left = picked[at : at + width] * weight_ref[pl.ds(tile, 1), :]
                right = picked[at + width : at + 2 * width]
                rows_ref[at : at + width, lanes] = left.astype(jnp.bfloat16)
                rows_ref[at + width : at + 2 * width, lanes] = right.astype(jnp.bfloat16)

    form = (((1,), (1,)), ((), ()))

    def multiply(number, rows_ref):
        for tile in range(tiles):
            at = tile * 2 * width
            left, right = (
                jnp.concatenate(
                    [
                        rows_ref[at + first : at + first + width, lanes : lanes + 2 * LANES]
                        for lanes in (0, 2 * LANES)
                    ]
                )
                for first in (0, width)
            )
            turned = jnp.concatenate([left[:, LANES:], -left[:, :LANES]], axis=1)
            both = jnp.concatenate([left, turned])
            result = lax.dot_general(both, right, form, preferred_element_type=jnp.float32)
            out_ref[tile, number] = result.reshape(2, 2, width, 2 * width)

    @pl.when(step == 0)
    def _():
        for span in range(2):
            for copy in copies(span):
                copy.start()
        for copy in copies(0):
            copy.wait()
        gather(0, even_rows)
        for copy in copies(1):
            copy.wait()

    gather(2 * step + 1, odd_rows)
    multiply(0, even_rows)
    gather(jnp.minimum(2 * step + 2, bands - 1), even_rows)
    multiply(1, odd_rows)


def correlate_tiles(place, select, weight, pieces, starts, width, first, count, bands, earlier):
    tiles = weight.shape[0]
    whole = pl.BlockSpec(memory_space=pltpu.VMEM)
    more = [] if earlier is None else [earlier]
    rows = pltpu.VMEM((tiles * 2 * width, 4 * LANES), jnp.bfloat16)
    return pl.pallas_call(
        lambda *refs: correlate_kernel(starts, width, *refs),
        grid=(count // 2,),
        out_shape=jax.ShapeDtypeStruct((tiles, bands, 2, 2, width, 2 * width), jnp.float32),
        in_specs=[pl.BlockSpec(memory_space=pltpu.SMEM)]
        + [whole] * 2
        + [pl.BlockSpec(memory_space=pl.ANY)] * (len(pieces) + len(more)),
        out_specs=pl.BlockSpec(
            (tiles, 2, 2, 2, width, 2 * width), lambda g: (0, g + first // 2, 0, 0, 0, 0)
        ),
        scratch_shapes=[
            pltpu.VMEM((2, select.shape[1] // ROWS, count, 2, ROWS, LANES), jnp.bfloat16),
            rows,
            rows,
            pltpu.SemaphoreType.DMA((2, len(pieces))),
        ],
        input_output_aliases={3 + len(pieces): 0} if more else {},
        compiler_params=pltpu.CompilerParams(vmem_limit_bytes=32 * 2**20),
        cost_estimate=pl.CostEstimate(
            flops=13 * 10**9 * count // bands,
            bytes_accessed=42 * 2**20 * count // bands,
            transcendentals=0,
        ),
        name="correlate",
    )(place, select, weight, *pieces, *more)


def tile_tables(tile_a, tile_b, tile_owner, tile_flags, row_of):
    tiles = tile_owner.shape[0]
    held = tile_owner == lax.axis_index("pol")
    order = jnp.arange(tiles, dtype=jnp.int32)
    rank = jnp.sum((held[None, :] & (order[None, :] < order[:, None])).astype(jnp.int32), axis=1)
    slots = jnp.arange(CAP, dtype=jnp.int32)
    pick = (held[None, :] & (rank[None, :] == slots[:, None])).astype(jnp.int32)
    sides = jnp.stack([row_of(tile_a), row_of(tile_b)], axis=1) + 1
    rows = jnp.sum(pick[:, :, None, None] * sides[None], axis=1) - 1
    flags = jnp.sum(pick[:, :, None] * tile_flags[None], axis=1).astype(jnp.float32)
    return rows, flags


def on_device_chunks(voltages, taps_filter, tile_a, tile_b, tile_owner, tile_flags):
    length = taps_filter.shape[1]
    stations = voltages.shape[2]
    frames = voltages.shape[3] // length
    chan_count, time_count = lax.axis_size("chan"), lax.axis_size("tm")
    owners = chan_count * time_count
    chunk_count = stations // (time_count * ROWS)
    width = tile_a.shape[1]
    bands = length // AVG // owners
    tables = fourier_tables(length)

    chan, tm = lax.axis_index("chan"), lax.axis_index("tm")
    place = jnp.stack([chan, tm, lax.axis_index("pol")]).astype(jnp.int32)

    def row_of(station):
        column, rest = station // stations, station % stations
        block, inside = rest // (chunk_count * ROWS), rest % (chunk_count * ROWS)
        across = (chan - column) % chan_count
        behind = (tm - block) % time_count
        piece = behind * chan_count + across
        return ((inside // ROWS) * owners + piece) * ROWS + inside % ROWS

    rows, flags = tile_tables(tile_a, tile_b, tile_owner, tile_flags, row_of)
    total_rows = chunk_count * owners * ROWS
    select = (rows[..., None] == jnp.arange(total_rows, dtype=jnp.int32)).astype(jnp.bfloat16)
    select = select.reshape(CAP * 2 * width, total_rows)
    depth = AVG * time_count * frames
    weight = jnp.tile(flags * (1.0 / depth), (1, 2 * AVG))

    samples = voltages.reshape(2, stations, frames * length)

    def travel(value, axes, distances):
        sizes = [lax.axis_size(axis) for axis in axes]
        pairs = []
        for index in np.ndindex(*sizes):
            target = [(i + d) % n for i, d, n in zip(index, distances, sizes)]
            pairs.append(tuple(int(np.ravel_multi_index(x, sizes)) for x in (index, target)))
        return lax.ppermute(value, axes, pairs)

    def after(values, earlier):
        return lax.optimization_barrier((list(values), list(earlier)))

    def block_for(values, chunk, distance):
        first = ((tm + distance) % time_count * chunk_count + chunk) * ROWS
        return lax.dynamic_slice(values, (0, first, 0), (2, ROWS, frames * length))

    def filtered(chunk, arrived, plan):
        return channelise(
            place, chunk, samples, arrived, taps_filter, tables, frames, chan_count, plan
        )

    sent = []

    def over_tm(value, distance, guard):
        if guard <= len(sent):
            (value,), sent[-guard : len(sent) - guard + 1] = after([value], [sent[-guard]])
        sent.append(travel(value, ("tm",), (distance,)))

    def over_chan(values, guard):
        values, sent[guard : guard + 1] = after(values, [sent[guard]])
        return [travel(v, ("chan",), (1,)) for v in values]

    def columns(near, far):
        return jnp.stack([near, far])

    hops = range(1, time_count)
    half = bands // 2
    spans = [(0, half), (half, bands)]

    values = samples
    for distance in hops:
        block = block_for(values, 0, distance)
        over_tm(block, distance, 2)
        if distance == 1:
            (block,), (values,) = after([block], [samples])
    for distance in hops:
        over_tm(block_for(values, 1, distance), distance, 2)

    order = [1, 2, 3, 0]
    plan = [[(x, z, 0, bands) for z in order] for x in range(chan_count)]
    plan = plan[:1] + [plan[1][:2], plan[1][2:]]
    near, *far = filtered(0, sent[:3], plan)
    near = near.reshape(time_count, bands, 2, ROWS, LANES)
    far = over_chan(far[:1], 3) + over_chan(far[1:], 4)
    far = [v.reshape(2, bands, 2, ROWS, LANES) for v in far]
    mixed = {z: columns(near[i], far[i // 2][i % 2]) for i, z in enumerate(order)}
    sent[4:5], (select, weight) = after([sent[4]], [select, weight])
    for distance in hops:
        over_tm(mixed[distance], distance, 2)
    home = mixed[0]

    plan = [[(x, z, *span) for z in range(time_count)] for span in spans for x in range(2)]
    low, far_low, high, far_high = filtered(1, sent[3:6], plan)
    far = over_chan([far_low], 6) + over_chan([far_high], 7)
    shape = (time_count, half, 2, ROWS, LANES)
    low, high, far_low, far_high = (v.reshape(shape) for v in (low, high, *far))
    low = [columns(low[z], far_low[z]) for z in range(time_count)]
    high = [columns(high[z], far_high[z]) for z in range(time_count)]
    for distance in hops:
        over_tm(low[distance], distance, 2)

    def flat(values):
        return jnp.stack(values).reshape((-1,) + values[0].shape[1:])

    def with_other(values):
        return [side for v in values for side in (v, travel(v, ("pol",), (1,)))]

    early = with_other([flat([home] + sent[6:9])])
    blocks, held = after(high[1:], sent[10:12] + early[1:])
    sent[10:12], early[1:] = held[:2], held[2:]
    for distance, block in zip(hops, blocks):
        over_tm(block, distance, len(sent) + 1)
    visibility = correlate_tiles(
        place, select, weight, early + with_other([flat([low[0]] + sent[9:12])]),
        [0, 0], width, 0, half, bands, None,
    )
    last, (visibility,) = after([high[0]] + sent[12:15], [visibility])
    return correlate_tiles(
        place, select, weight, early + with_other(last),
        [half] + [0] * 4, width, half, half, bands, visibility,
    )


def on_device(voltages, taps_filter, tile_a, tile_b, tile_owner, tile_flags):
    taps, length = taps_filter.shape
    frames = voltages.shape[3] // length
    time_count = lax.axis_size("tm")
    fits = (
        length == RADIX * LANES
        and AVG * time_count * frames == LANES
        and 2 * tile_a.shape[1] == LANES
        and voltages.shape[2] == 2 * time_count * ROWS
        and (lax.axis_size("chan"), time_count) == (2, 4)
    )
    form = on_device_chunks if fits else on_device_any
    return form(voltages, taps_filter, tile_a, tile_b, tile_owner, tile_flags)


def solution(mesh):
    return jax.shard_map(
        on_device,
        mesh=mesh,
        in_specs=(P("grp", "pol", "chan", "tm"), P(), P(), P(), P(), P()),
        out_specs=P("pol", ("chan", "tm"), "grp", None, None, None),
        check_vma=False,
    )
```

```python
import math

import jax
import jax.numpy as jnp
import numpy as np
from jax import lax
from jax.experimental import pallas as pl
from jax.experimental.pallas import tpu as pltpu
from jax.sharding import PartitionSpec as P

AVG = 8
CAP = 8
RADIX = 16
LANES = 128
ROWS = 16


radix_first = 32


def from_behind(value, axis, steps):
    count = lax.axis_size(axis)
    first, last = (max(0, -steps), min(count, count - steps))
    return lax.ppermute(value, axis, [(source, source + steps) for source in range(first, last)])


def fourier(filtered):
    length = filtered.shape[-1]
    second = length // radix_first
    exact_mode = lax.Precision.HIGHEST
    grid = filtered.reshape(filtered.shape[:-1] + (radix_first, second))
    outer = jnp.arange(radix_first, dtype=jnp.int32)
    inner = jnp.arange(second, dtype=jnp.int32)
    phase_one = (
        2.0
        * math.pi
        / radix_first
        * (outer[:, None] * outer[None, :] % radix_first).astype(jnp.float32)
    )
    phase_twist = 2.0 * math.pi / length * (outer[:, None] * inner[None, :]).astype(jnp.float32)
    phase_two = (
        2.0 * math.pi / second * (inner[:, None] * inner[None, :] % second).astype(jnp.float32)
    )
    cos_one, sin_one = (jnp.cos(phase_one), jnp.sin(phase_one))
    cos_twist, sin_twist = (jnp.cos(phase_twist), jnp.sin(phase_twist))
    cos_two, sin_two = (jnp.cos(phase_two), jnp.sin(phase_two))
    first_form = "fk,stkj->stfj"
    section_re = jnp.einsum(first_form, cos_one, grid[0], precision=exact_mode) + jnp.einsum(
        first_form, sin_one, grid[1], precision=exact_mode
    )
    section_im = jnp.einsum(first_form, cos_one, grid[1], precision=exact_mode) - jnp.einsum(
        first_form, sin_one, grid[0], precision=exact_mode
    )
    turned_re = section_re * cos_twist + section_im * sin_twist
    turned_im = section_im * cos_twist - section_re * sin_twist
    second_form = "gj,stfj->stgf"
    final_re = jnp.einsum(second_form, cos_two, turned_re, precision=exact_mode) + jnp.einsum(
        second_form, sin_two, turned_im, precision=exact_mode
    )
    final_im = jnp.einsum(second_form, cos_two, turned_im, precision=exact_mode) - jnp.einsum(
        second_form, sin_two, turned_re, precision=exact_mode
    )
    joined = jnp.stack([final_re, final_im]).reshape(filtered.shape)
    return joined * (1.0 / math.sqrt(length))


def correlate(full, rows_a, rows_b, flags, group_count):
    depth = full.shape[4]
    weight = jnp.tile(flags.astype(jnp.bfloat16), depth // flags.shape[0])
    left_rows = jnp.take(full, rows_a, axis=2) * weight
    right_rows = jnp.take(full, rows_b, axis=2)
    stacked_left = jnp.stack(
        [
            jnp.concatenate([left_rows[0], left_rows[1]], axis=-1),
            jnp.concatenate([left_rows[1], -left_rows[0]], axis=-1),
        ]
    )
    joined_right = jnp.concatenate([right_rows[0], right_rows[1]], axis=-1)
    result = jnp.einsum(
        "rpank,qbnk->nrpaqb", stacked_left, joined_right, preferred_element_type=jnp.float32
    )
    width = rows_a.shape[0]
    return result.reshape(group_count, 2, 2, width, 2 * width) * (1.0 / depth)


def on_device_any(voltages, taps_filter, tile_a, tile_b, tile_owner, tile_flags):
    history = taps_filter.shape[0] - 1
    length = taps_filter.shape[1]
    stations = voltages.shape[2]
    frames = voltages.shape[3] // length
    local_blocks = voltages.reshape(2, stations, frames, length)
    hop_count = -(-history // frames)
    sending = local_blocks
    extended = local_blocks
    for hop_index in range(hop_count):
        sending = from_behind(sending, "tm", 1)
        extended = jnp.concatenate([sending, extended], axis=2)
    extended = extended[:, :, extended.shape[2] - history - frames :]
    filtered = jnp.zeros((2, stations, frames, length), jnp.float32)
    for tap_index in range(history + 1):
        start = history - tap_index
        filtered = filtered + taps_filter[tap_index] * extended[
            :, :, start : start + frames
        ].astype(jnp.float32)
    spectra = fourier(filtered).astype(jnp.bfloat16)
    chan_count = lax.axis_size("chan")
    time_count = lax.axis_size("tm")
    narrow = length // (chan_count * time_count)
    outgoing = spectra.reshape(2, stations, frames, chan_count, time_count, narrow)
    outgoing = outgoing.transpose(0, 3, 4, 5, 1, 2)
    flat = outgoing.reshape(2, chan_count * time_count, narrow, stations * frames)
    moved = lax.all_to_all(flat, ("chan", "tm"), split_axis=1, concat_axis=1, tiled=True)
    moved = moved.reshape(2, chan_count, time_count, narrow, stations, frames)
    bands = narrow // AVG
    every_station = chan_count * stations
    spectra_count = time_count * frames
    arranged = moved.transpose(0, 1, 4, 3, 2, 5).reshape(
        2, 1, every_station, bands, AVG * spectra_count
    )
    full = lax.all_gather(arranged, "pol", axis=1, tiled=True)
    position = lax.axis_index("pol")
    width = tile_a.shape[1]
    capacity = CAP
    held = tile_owner == position
    listed = jnp.nonzero(held, size=capacity, fill_value=0)[0].astype(jnp.int32)
    tally = jnp.sum(held.astype(jnp.int32))
    initial = jnp.zeros((capacity, bands, 2, 2, width, 2 * width), jnp.float32)

    def fill_slot(slot, results):
        chosen_tile = listed[slot]
        return results.at[slot].set(
            correlate(
                full, tile_a[chosen_tile], tile_b[chosen_tile], tile_flags[chosen_tile], bands
            )
        )

    visibility = lax.fori_loop(0, tally, fill_slot, initial)
    return visibility


def fourier_tables(length):
    low = np.arange(RADIX)
    lane = np.arange(LANES)
    turn = 2.0 * np.pi / length * np.outer(low, lane)
    twiddle = np.stack([np.cos(turn), np.sin(turn)]).astype(np.float32)
    angle = 2.0 * np.pi / LANES * (np.outer(lane, lane) % LANES)
    cos, sin = np.cos(angle) / math.sqrt(length), np.sin(angle) / math.sqrt(length)
    matrix = np.block([[cos, sin], [-sin, cos]]).astype(np.float32)
    high = matrix.astype(jnp.bfloat16)
    rest = (matrix - high.astype(np.float32)).astype(jnp.bfloat16)
    return twiddle, np.stack([high, rest])


def butterflies(values):
    count = len(values)
    if count == 1:
        return values
    even, odd = butterflies(values[0::2]), butterflies(values[1::2])
    first, second = [], []
    for index in range(count // 2):
        (a, b), (c, d) = even[index], odd[index]
        if index == 0:
            e, f = c, d
        elif 4 * index == count:
            e, f = d, -c
        elif 8 * index == count:
            root = math.sqrt(0.5)
            e, f = (c + d) * root, (d - c) * root
        elif 8 * index == 3 * count:
            root = math.sqrt(0.5)
            e, f = (d - c) * root, -(c + d) * root
        else:
            turn = 2.0 * math.pi * index / count
            cos, sin = math.cos(turn), math.sin(turn)
            e, f = c * cos + d * sin, d * cos - c * sin
        first.append((a + e, b + f))
        second.append((a - e, b - f))
    return first + second


def channelise_kernel(frames, chunk, columns, plan, place_ref, own_ref, *refs):
    sources = refs[-6].shape[0]
    come_refs = refs[: sources - 1]
    taps_ref, twiddle_ref, matrix_ref = refs[sources - 1 : sources + 2]
    out_refs = refs[sources + 2 : -6]
    x_ref, fil_ref, zr_ref, zi_ref, w_ref, sems = refs[-6:]
    chan, tm = place_ref[0], place_ref[1]
    own_rows = pl.multiple_of((tm * (own_ref.shape[1] // (sources * ROWS)) + chunk) * ROWS, ROWS)
    copies = []
    for behind in range(sources):
        block = come_refs[behind - 1] if behind else own_ref.at[:, pl.ds(own_rows, ROWS), :]
        slot = lax.rem(tm - behind + sources, sources)
        copies.append(pltpu.make_async_copy(block, x_ref.at[slot], sems.at[behind]))
    for copy in copies:
        copy.start()
    for copy in copies:
        copy.wait()
    spectra = sources * frames
    length = taps_ref.shape[1]
    taps = taps_ref.shape[0]
    depth = RADIX * spectra
    z_refs = (zr_ref, zi_ref)

    @pl.loop(0, RADIX)
    def _(section):
        at = pl.multiple_of(section * LANES, LANES)
        weights = [taps_ref[pl.ds(m, 1), pl.ds(at, LANES)] for m in range(taps)]
        for part in range(2):
            blocks = []
            for t in range(spectra):
                lane = pl.multiple_of((t % frames) * length + section * LANES, LANES)
                blocks.append(x_ref[t // frames, part, :, pl.ds(lane, LANES)].astype(jnp.float32))
            for t in range(spectra):
                total = weights[0] * blocks[t]
                for m in range(1, min(t + 1, taps)):
                    total = total + weights[m] * blocks[t - m]
                fil_ref[section, t, part] = total

    @pl.loop(0, spectra)
    def _(t):
        for half in range(ROWS // 8):
            values = [
                tuple(fil_ref[section, t, part, pl.ds(half * 8, 8), :] for part in range(2))
                for section in range(RADIX)
            ]
            for low, (re, im) in enumerate(butterflies(values)):
                if low:
                    cos = twiddle_ref[0, pl.ds(low, 1), :]
                    sin = twiddle_ref[1, pl.ds(low, 1), :]
                    re, im = re * cos + im * sin, im * cos - re * sin
                rows = pl.ds(half * 8 * depth + low * spectra + t, 8, stride=depth)
                zr_ref[rows, :] = re
                zi_ref[rows, :] = im

    form = (((1,), (1,)), ((), ()))
    high_matrix, low_matrix = matrix_ref[0], matrix_ref[1]
    halves = depth // LANES

    @pl.loop(0, ROWS)
    def _(station):
        rows = pl.ds(pl.multiple_of(station * depth, depth), depth)
        value = jnp.concatenate([ref[rows, :] for ref in z_refs], axis=1)
        high = value.astype(jnp.bfloat16)
        rest = (value - high.astype(jnp.float32)).astype(jnp.bfloat16)
        total = lax.dot_general(high_matrix, high, form, preferred_element_type=jnp.float32)
        total += lax.dot_general(high_matrix, rest, form, preferred_element_type=jnp.float32)
        total += lax.dot_general(low_matrix, high, form, preferred_element_type=jnp.float32)
        for half in range(halves):
            for part in range(2):
                rows = pl.ds((half * 2 + part) * ROWS + station, LANES, stride=halves * 2 * ROWS)
                w_ref[rows, :] = total[
                    part * LANES : (part + 1) * LANES, half * LANES : (half + 1) * LANES
                ]

    share = w_ref.shape[0] // (columns * sources)
    band_rows = 2 * ROWS
    piece = 4 * band_rows
    for blocks, out_ref in zip(plan, out_refs):
        at = 0
        for across, along, start, stop in blocks:
            owner = lax.rem(chan + across, columns) * sources + lax.rem(tm + along, sources)
            for row in range(start * band_rows, stop * band_rows, piece):
                rows = pl.ds(pl.multiple_of(owner * share + row, piece), piece)
                out_ref[at : at + piece, :] = w_ref[rows, :].astype(jnp.bfloat16)
                at += piece


def channelise(place, chunk, voltages, come, taps_filter, tables, frames, columns, plan):
    sources = 1 + len(come)
    length = taps_filter.shape[1]
    spectra = sources * frames
    twiddle, matrix = tables
    out_rows = length // AVG * 2 * ROWS
    whole = pl.BlockSpec(memory_space=pltpu.VMEM)
    counts = [sum(stop - start for _, _, start, stop in blocks) for blocks in plan]
    flat = pl.pallas_call(
        lambda *refs: channelise_kernel(frames, chunk, columns, plan, *refs),
        out_shape=[
            jax.ShapeDtypeStruct((count * 2 * ROWS, LANES), jnp.bfloat16) for count in counts
        ],
        in_specs=[pl.BlockSpec(memory_space=pltpu.SMEM)]
        + [pl.BlockSpec(memory_space=pl.ANY)] * sources
        + [whole] * 3,
        out_specs=[whole] * len(plan),
        scratch_shapes=[
            pltpu.VMEM((sources, 2, ROWS, frames * length), jnp.bfloat16),
            pltpu.VMEM((RADIX, spectra, 2, ROWS, LANES), jnp.float32),
            pltpu.VMEM((ROWS * RADIX * spectra, LANES), jnp.float32),
            pltpu.VMEM((ROWS * RADIX * spectra, LANES), jnp.float32),
            pltpu.VMEM((out_rows, LANES), jnp.float32),
            pltpu.SemaphoreType.DMA((sources,)),
        ],
        compiler_params=pltpu.CompilerParams(vmem_limit_bytes=40 * 2**20),
        cost_estimate=pl.CostEstimate(
            flops=9 * 10**9, bytes_accessed=4 * 2**20, transcendentals=0
        ),
        name="channelise",
    )(place, voltages, *come, taps_filter, jnp.asarray(twiddle), jnp.asarray(matrix))
    return [piece.reshape(count, 2, ROWS, LANES) for piece, count in zip(flat, counts)]


def correlate_kernel(starts, width, place_ref, sel_ref, weight_ref, *refs):
    x_refs, (out_ref, x_all, even_rows, odd_rows, sems) = refs[: 2 * len(starts)], refs[-5:]
    tiles = out_ref.shape[0]
    step = pl.program_id(0)
    bands = x_all.shape[2]
    spans = [(0, 2), (2, bands)]

    def copies(span):
        first, last = spans[span]
        block = 0
        for index, start in enumerate(starts):
            blocks = x_refs[2 * index].shape[0]
            for side in range(2):
                yield pltpu.make_async_copy(
                    x_refs[2 * index + side].at[:, pl.ds(start + first, last - first)],
                    x_all.at[
                        lax.rem(place_ref[2] + side, 2),
                        pl.ds(block, blocks),
                        pl.ds(first, last - first),
                    ],
                    sems.at[span, 2 * index + side],
                )
            block += blocks

    def gather(band, rows_ref):
        for pol in range(2):
            lanes = slice(pol * 2 * LANES, (pol + 1) * 2 * LANES)
            value = jnp.concatenate(
                [
                    jnp.concatenate([x_all[pol, block, band, part] for part in range(2)], axis=1)
                    for block in range(x_all.shape[1])
                ]
            )
            picked = jnp.dot(sel_ref[...], value, preferred_element_type=jnp.float32)
            for tile in range(tiles):
                at = tile * 2 * width
                left = picked[at : at + width] * weight_ref[pl.ds(tile, 1), :]
                right = picked[at + width : at + 2 * width]
                rows_ref[at : at + width, lanes] = left.astype(jnp.bfloat16)
                rows_ref[at + width : at + 2 * width, lanes] = right.astype(jnp.bfloat16)

    form = (((1,), (1,)), ((), ()))

    def multiply(number, rows_ref):
        for tile in range(tiles):
            at = tile * 2 * width
            left, right = (
                jnp.concatenate(
                    [
                        rows_ref[at + first : at + first + width, lanes : lanes + 2 * LANES]
                        for lanes in (0, 2 * LANES)
                    ]
                )
                for first in (0, width)
            )
            turned = jnp.concatenate([left[:, LANES:], -left[:, :LANES]], axis=1)
            both = jnp.concatenate([left, turned])
            result = lax.dot_general(both, right, form, preferred_element_type=jnp.float32)
            out_ref[tile, number] = result.reshape(2, 2, width, 2 * width)

    @pl.when(step == 0)
    def _():
        for span in range(2):
            for copy in copies(span):
                copy.start()
        for copy in copies(0):
            copy.wait()
        gather(0, even_rows)
        for copy in copies(1):
            copy.wait()

    gather(2 * step + 1, odd_rows)
    multiply(0, even_rows)
    gather(jnp.minimum(2 * step + 2, bands - 1), even_rows)
    multiply(1, odd_rows)


def correlate_tiles(place, select, weight, pieces, starts, width, first, count, bands, earlier):
    tiles = weight.shape[0]
    whole = pl.BlockSpec(memory_space=pltpu.VMEM)
    more = [] if earlier is None else [earlier]
    rows = pltpu.VMEM((tiles * 2 * width, 4 * LANES), jnp.bfloat16)
    return pl.pallas_call(
        lambda *refs: correlate_kernel(starts, width, *refs),
        grid=(count // 2,),
        out_shape=jax.ShapeDtypeStruct((tiles, bands, 2, 2, width, 2 * width), jnp.float32),
        in_specs=[pl.BlockSpec(memory_space=pltpu.SMEM)]
        + [whole] * 2
        + [pl.BlockSpec(memory_space=pl.ANY)] * (len(pieces) + len(more)),
        out_specs=pl.BlockSpec(
            (tiles, 2, 2, 2, width, 2 * width), lambda g: (0, g + first // 2, 0, 0, 0, 0)
        ),
        scratch_shapes=[
            pltpu.VMEM((2, select.shape[1] // ROWS, count, 2, ROWS, LANES), jnp.bfloat16),
            rows,
            rows,
            pltpu.SemaphoreType.DMA((2, len(pieces))),
        ],
        input_output_aliases={3 + len(pieces): 0} if more else {},
        compiler_params=pltpu.CompilerParams(vmem_limit_bytes=32 * 2**20),
        cost_estimate=pl.CostEstimate(
            flops=13 * 10**9 * count // bands,
            bytes_accessed=42 * 2**20 * count // bands,
            transcendentals=0,
        ),
        name="correlate",
    )(place, select, weight, *pieces, *more)


def tile_tables(tile_a, tile_b, tile_owner, tile_flags, row_of):
    tiles = tile_owner.shape[0]
    held = tile_owner == lax.axis_index("pol")
    order = jnp.arange(tiles, dtype=jnp.int32)
    rank = jnp.sum((held[None, :] & (order[None, :] < order[:, None])).astype(jnp.int32), axis=1)
    slots = jnp.arange(CAP, dtype=jnp.int32)
    pick = (held[None, :] & (rank[None, :] == slots[:, None])).astype(jnp.int32)
    sides = jnp.stack([row_of(tile_a), row_of(tile_b)], axis=1) + 1
    rows = jnp.sum(pick[:, :, None, None] * sides[None], axis=1) - 1
    flags = jnp.sum(pick[:, :, None] * tile_flags[None], axis=1).astype(jnp.float32)
    return rows, flags


def on_device_chunks(voltages, taps_filter, tile_a, tile_b, tile_owner, tile_flags):
    length = taps_filter.shape[1]
    stations = voltages.shape[2]
    frames = voltages.shape[3] // length
    chan_count, time_count = lax.axis_size("chan"), lax.axis_size("tm")
    owners = chan_count * time_count
    chunk_count = stations // (time_count * ROWS)
    width = tile_a.shape[1]
    bands = length // AVG // owners
    tables = fourier_tables(length)

    chan, tm = lax.axis_index("chan"), lax.axis_index("tm")
    place = jnp.stack([chan, tm, lax.axis_index("pol")]).astype(jnp.int32)

    def row_of(station):
        column, rest = station // stations, station % stations
        block, inside = rest // (chunk_count * ROWS), rest % (chunk_count * ROWS)
        across = (chan - column) % chan_count
        behind = (tm - block) % time_count
        piece = behind * chan_count + across
        return ((inside // ROWS) * owners + piece) * ROWS + inside % ROWS

    rows, flags = tile_tables(tile_a, tile_b, tile_owner, tile_flags, row_of)
    total_rows = chunk_count * owners * ROWS
    select = (rows[..., None] == jnp.arange(total_rows, dtype=jnp.int32)).astype(jnp.bfloat16)
    select = select.reshape(CAP * 2 * width, total_rows)
    depth = AVG * time_count * frames
    weight = jnp.tile(flags * (1.0 / depth), (1, 2 * AVG))

    samples = voltages.reshape(2, stations, frames * length)

    def travel(value, axes, distances):
        sizes = [lax.axis_size(axis) for axis in axes]
        pairs = []
        for index in np.ndindex(*sizes):
            target = [(i + d) % n for i, d, n in zip(index, distances, sizes)]
            pairs.append(tuple(int(np.ravel_multi_index(x, sizes)) for x in (index, target)))
        return lax.ppermute(value, axes, pairs)

    def after(values, earlier):
        return lax.optimization_barrier((list(values), list(earlier)))

    def block_for(values, chunk, distance):
        first = ((tm + distance) % time_count * chunk_count + chunk) * ROWS
        return lax.dynamic_slice(values, (0, first, 0), (2, ROWS, frames * length))

    def filtered(chunk, arrived, plan):
        return channelise(
            place, chunk, samples, arrived, taps_filter, tables, frames, chan_count, plan
        )

    def over(value, across, along):
        return travel(value, ("chan", "tm"), (across, along))

    def columns(near, far):
        return jnp.stack([near, far])

    half = bands // 2
    pairs = [(x, z) for z in range(time_count) for x in range(chan_count)]
    early_pairs = [(x, z) for z in (1, 3) for x in range(2)] + [(1, 0)]
    late_pairs = [(0, 2), (1, 2)]

    (one,), (values,) = after([block_for(samples, 0, 1)], [samples])
    two, three = (block_for(values, 0, distance) for distance in (2, 3))
    one, two = over(one, 0, 1), over(two, 0, 2)
    (three,), (one,) = after([three], [one])
    first = [one, two, over(three, 0, 3)]
    blocks = [block_for(values, 1, distance) for distance in (1, 2, 3)]
    (one, two, three), first = after(blocks, first)
    one, three = over(one, 0, 1), over(three, 0, 3)
    (two,), (one,) = after([two], [one])
    second = [one, over(two, 0, 2), three]

    plan = [[(x, z, 0, bands)] for x, z in pairs]
    early = dict(zip(pairs, filtered(0, first, plan)))
    blocks, held = after([early[p] for p in early_pairs], [second[1], select, weight])
    second[1], select, weight = held
    early.update((p, over(block, *p)) for p, block in zip(early_pairs, blocks))
    blocks, held = after([early[p] for p in late_pairs], [early[p] for p in early_pairs[:2]])
    early.update(zip(early_pairs[:2], held))
    early.update((p, over(block, *p)) for p, block in zip(late_pairs, blocks))

    plan = [[(x, z, 0, half)] for x, z in pairs]
    plan += [[(x, z, half, bands) for z in range(time_count)] for x in range(chan_count)]
    *low, near, far = filtered(1, second, plan)
    low = dict(zip(pairs, low))
    blocks, held = after([low[p] for p in early_pairs] + [far], [early[p] for p in late_pairs[:1]])
    early.update(zip(late_pairs[:1], held))
    low.update((p, over(block, *p)) for p, block in zip(early_pairs, blocks))
    far = over(blocks[-1], 1, 0)
    blocks, held = after([low[p] for p in late_pairs], [low[p] for p in early_pairs[:2]])
    low.update(zip(early_pairs[:2], held))
    low.update((p, over(block, *p)) for p, block in zip(late_pairs, blocks))
    near, far = (v.reshape(time_count, half, 2, ROWS, LANES) for v in (near, far))
    high = [columns(near[z], far[z]) for z in range(time_count)]

    def with_other(values):
        return [side for v in values for side in (v, travel(v, ("pol",), (1,)))]

    early = with_other([jnp.stack([early[p] for p in pairs])])
    blocks, held = after(high[1:], [low[late_pairs[0]], early[1]])
    low[late_pairs[0]], early[1] = held
    high[1:] = [over(block, 0, z) for z, block in zip((1, 2, 3), blocks)]
    visibility = correlate_tiles(
        place, select, weight, early + with_other([jnp.stack([low[p] for p in pairs])]),
        [0, 0], width, 0, half, bands, None,
    )
    high, (visibility,) = after(high, [visibility])
    return correlate_tiles(
        place, select, weight, early + with_other(high),
        [half] + [0] * 4, width, half, half, bands, visibility,
    )


def on_device(voltages, taps_filter, tile_a, tile_b, tile_owner, tile_flags):
    taps, length = taps_filter.shape
    frames = voltages.shape[3] // length
    time_count = lax.axis_size("tm")
    fits = (
        length == RADIX * LANES
        and AVG * time_count * frames == LANES
        and 2 * tile_a.shape[1] == LANES
        and voltages.shape[2] == 2 * time_count * ROWS
        and (lax.axis_size("chan"), time_count) == (2, 4)
    )
    form = on_device_chunks if fits else on_device_any
    return form(voltages, taps_filter, tile_a, tile_b, tile_owner, tile_flags)


def solution(mesh):
    return jax.shard_map(
        on_device,
        mesh=mesh,
        in_specs=(P("grp", "pol", "chan", "tm"), P(), P(), P(), P(), P()),
        out_specs=P("pol", ("chan", "tm"), "grp", None, None, None),
        check_vma=False,
    )
```

```python
import math

import jax
import jax.numpy as jnp
import numpy as np
from jax import lax
from jax.experimental import pallas as pl
from jax.experimental.pallas import tpu as pltpu
from jax.sharding import PartitionSpec as P

AVG = 8
CAP = 8
RADIX = 16
LANES = 128
ROWS = 16


radix_first = 32


def from_behind(value, axis, steps):
    count = lax.axis_size(axis)
    first, last = (max(0, -steps), min(count, count - steps))
    return lax.ppermute(value, axis, [(source, source + steps) for source in range(first, last)])


def fourier(filtered):
    length = filtered.shape[-1]
    second = length // radix_first
    exact_mode = lax.Precision.HIGHEST
    grid = filtered.reshape(filtered.shape[:-1] + (radix_first, second))
    outer = jnp.arange(radix_first, dtype=jnp.int32)
    inner = jnp.arange(second, dtype=jnp.int32)
    phase_one = (
        2.0
        * math.pi
        / radix_first
        * (outer[:, None] * outer[None, :] % radix_first).astype(jnp.float32)
    )
    phase_twist = 2.0 * math.pi / length * (outer[:, None] * inner[None, :]).astype(jnp.float32)
    phase_two = (
        2.0 * math.pi / second * (inner[:, None] * inner[None, :] % second).astype(jnp.float32)
    )
    cos_one, sin_one = (jnp.cos(phase_one), jnp.sin(phase_one))
    cos_twist, sin_twist = (jnp.cos(phase_twist), jnp.sin(phase_twist))
    cos_two, sin_two = (jnp.cos(phase_two), jnp.sin(phase_two))
    first_form = "fk,stkj->stfj"
    section_re = jnp.einsum(first_form, cos_one, grid[0], precision=exact_mode) + jnp.einsum(
        first_form, sin_one, grid[1], precision=exact_mode
    )
    section_im = jnp.einsum(first_form, cos_one, grid[1], precision=exact_mode) - jnp.einsum(
        first_form, sin_one, grid[0], precision=exact_mode
    )
    turned_re = section_re * cos_twist + section_im * sin_twist
    turned_im = section_im * cos_twist - section_re * sin_twist
    second_form = "gj,stfj->stgf"
    final_re = jnp.einsum(second_form, cos_two, turned_re, precision=exact_mode) + jnp.einsum(
        second_form, sin_two, turned_im, precision=exact_mode
    )
    final_im = jnp.einsum(second_form, cos_two, turned_im, precision=exact_mode) - jnp.einsum(
        second_form, sin_two, turned_re, precision=exact_mode
    )
    joined = jnp.stack([final_re, final_im]).reshape(filtered.shape)
    return joined * (1.0 / math.sqrt(length))


def correlate(full, rows_a, rows_b, flags, group_count):
    depth = full.shape[4]
    weight = jnp.tile(flags.astype(jnp.bfloat16), depth // flags.shape[0])
    left_rows = jnp.take(full, rows_a, axis=2) * weight
    right_rows = jnp.take(full, rows_b, axis=2)
    stacked_left = jnp.stack(
        [
            jnp.concatenate([left_rows[0], left_rows[1]], axis=-1),
            jnp.concatenate([left_rows[1], -left_rows[0]], axis=-1),
        ]
    )
    joined_right = jnp.concatenate([right_rows[0], right_rows[1]], axis=-1)
    result = jnp.einsum(
        "rpank,qbnk->nrpaqb", stacked_left, joined_right, preferred_element_type=jnp.float32
    )
    width = rows_a.shape[0]
    return result.reshape(group_count, 2, 2, width, 2 * width) * (1.0 / depth)


def on_device_any(voltages, taps_filter, tile_a, tile_b, tile_owner, tile_flags):
    history = taps_filter.shape[0] - 1
    length = taps_filter.shape[1]
    stations = voltages.shape[2]
    frames = voltages.shape[3] // length
    local_blocks = voltages.reshape(2, stations, frames, length)
    hop_count = -(-history // frames)
    sending = local_blocks
    extended = local_blocks
    for hop_index in range(hop_count):
        sending = from_behind(sending, "tm", 1)
        extended = jnp.concatenate([sending, extended], axis=2)
    extended = extended[:, :, extended.shape[2] - history - frames :]
    filtered = jnp.zeros((2, stations, frames, length), jnp.float32)
    for tap_index in range(history + 1):
        start = history - tap_index
        filtered = filtered + taps_filter[tap_index] * extended[
            :, :, start : start + frames
        ].astype(jnp.float32)
    spectra = fourier(filtered).astype(jnp.bfloat16)
    chan_count = lax.axis_size("chan")
    time_count = lax.axis_size("tm")
    narrow = length // (chan_count * time_count)
    outgoing = spectra.reshape(2, stations, frames, chan_count, time_count, narrow)
    outgoing = outgoing.transpose(0, 3, 4, 5, 1, 2)
    flat = outgoing.reshape(2, chan_count * time_count, narrow, stations * frames)
    moved = lax.all_to_all(flat, ("chan", "tm"), split_axis=1, concat_axis=1, tiled=True)
    moved = moved.reshape(2, chan_count, time_count, narrow, stations, frames)
    bands = narrow // AVG
    every_station = chan_count * stations
    spectra_count = time_count * frames
    arranged = moved.transpose(0, 1, 4, 3, 2, 5).reshape(
        2, 1, every_station, bands, AVG * spectra_count
    )
    full = lax.all_gather(arranged, "pol", axis=1, tiled=True)
    position = lax.axis_index("pol")
    width = tile_a.shape[1]
    capacity = CAP
    held = tile_owner == position
    listed = jnp.nonzero(held, size=capacity, fill_value=0)[0].astype(jnp.int32)
    tally = jnp.sum(held.astype(jnp.int32))
    initial = jnp.zeros((capacity, bands, 2, 2, width, 2 * width), jnp.float32)

    def fill_slot(slot, results):
        chosen_tile = listed[slot]
        return results.at[slot].set(
            correlate(
                full, tile_a[chosen_tile], tile_b[chosen_tile], tile_flags[chosen_tile], bands
            )
        )

    visibility = lax.fori_loop(0, tally, fill_slot, initial)
    return visibility


def fourier_tables(length):
    low = np.arange(RADIX)
    lane = np.arange(LANES)
    turn = 2.0 * np.pi / length * np.outer(low, lane)
    twiddle = np.stack([np.cos(turn), np.sin(turn)]).astype(np.float32)
    angle = 2.0 * np.pi / LANES * (np.outer(lane, lane) % LANES)
    cos, sin = np.cos(angle) / math.sqrt(length), np.sin(angle) / math.sqrt(length)
    matrix = np.block([[cos, sin], [-sin, cos]]).astype(np.float32)
    high = matrix.astype(jnp.bfloat16)
    rest = (matrix - high.astype(np.float32)).astype(jnp.bfloat16)
    return twiddle, np.stack([high, rest])


def butterflies(values):
    count = len(values)
    if count == 1:
        return values
    even, odd = butterflies(values[0::2]), butterflies(values[1::2])
    first, second = [], []
    for index in range(count // 2):
        (a, b), (c, d) = even[index], odd[index]
        if index == 0:
            e, f = c, d
        elif 4 * index == count:
            e, f = d, -c
        elif 8 * index == count:
            root = math.sqrt(0.5)
            e, f = (c + d) * root, (d - c) * root
        elif 8 * index == 3 * count:
            root = math.sqrt(0.5)
            e, f = (d - c) * root, -(c + d) * root
        else:
            turn = 2.0 * math.pi * index / count
            cos, sin = math.cos(turn), math.sin(turn)
            e, f = c * cos + d * sin, d * cos - c * sin
        first.append((a + e, b + f))
        second.append((a - e, b - f))
    return first + second


def channelise_kernel(frames, chunk, columns, plan, place_ref, own_ref, *refs):
    sources = refs[-6].shape[0]
    come_refs = refs[: sources - 1]
    taps_ref, twiddle_ref, matrix_ref = refs[sources - 1 : sources + 2]
    out_refs = refs[sources + 2 : -6]
    x_ref, fil_ref, zr_ref, zi_ref, w_ref, sems = refs[-6:]
    chan, tm = place_ref[0], place_ref[1]
    own_rows = pl.multiple_of((tm * (own_ref.shape[1] // (sources * ROWS)) + chunk) * ROWS, ROWS)
    copies = []
    for behind in range(sources):
        block = come_refs[behind - 1] if behind else own_ref.at[:, pl.ds(own_rows, ROWS), :]
        slot = lax.rem(tm - behind + sources, sources)
        copies.append(pltpu.make_async_copy(block, x_ref.at[slot], sems.at[behind]))
    for copy in copies:
        copy.start()
    for copy in copies:
        copy.wait()
    spectra = sources * frames
    length = taps_ref.shape[1]
    taps = taps_ref.shape[0]
    depth = RADIX * spectra
    z_refs = (zr_ref, zi_ref)

    @pl.loop(0, RADIX)
    def _(section):
        at = pl.multiple_of(section * LANES, LANES)
        weights = [taps_ref[pl.ds(m, 1), pl.ds(at, LANES)] for m in range(taps)]
        for part in range(2):
            blocks = []
            for t in range(spectra):
                lane = pl.multiple_of((t % frames) * length + section * LANES, LANES)
                blocks.append(x_ref[t // frames, part, :, pl.ds(lane, LANES)].astype(jnp.float32))
            for t in range(spectra):
                total = weights[0] * blocks[t]
                for m in range(1, min(t + 1, taps)):
                    total = total + weights[m] * blocks[t - m]
                fil_ref[section, t, part] = total

    @pl.loop(0, spectra)
    def _(t):
        for half in range(ROWS // 8):
            values = [
                tuple(fil_ref[section, t, part, pl.ds(half * 8, 8), :] for part in range(2))
                for section in range(RADIX)
            ]
            for low, (re, im) in enumerate(butterflies(values)):
                if low:
                    cos = twiddle_ref[0, pl.ds(low, 1), :]
                    sin = twiddle_ref[1, pl.ds(low, 1), :]
                    re, im = re * cos + im * sin, im * cos - re * sin
                rows = pl.ds(half * 8 * depth + low * spectra + t, 8, stride=depth)
                zr_ref[rows, :] = re
                zi_ref[rows, :] = im

    form = (((1,), (1,)), ((), ()))
    high_matrix, low_matrix = matrix_ref[0], matrix_ref[1]
    halves = depth // LANES

    @pl.loop(0, ROWS)
    def _(station):
        rows = pl.ds(pl.multiple_of(station * depth, depth), depth)
        value = jnp.concatenate([ref[rows, :] for ref in z_refs], axis=1)
        high = value.astype(jnp.bfloat16)
        rest = (value - high.astype(jnp.float32)).astype(jnp.bfloat16)
        total = lax.dot_general(high_matrix, high, form, preferred_element_type=jnp.float32)
        total += lax.dot_general(high_matrix, rest, form, preferred_element_type=jnp.float32)
        total += lax.dot_general(low_matrix, high, form, preferred_element_type=jnp.float32)
        for half in range(halves):
            for part in range(2):
                rows = pl.ds((half * 2 + part) * ROWS + station, LANES, stride=halves * 2 * ROWS)
                w_ref[rows, :] = total[
                    part * LANES : (part + 1) * LANES, half * LANES : (half + 1) * LANES
                ]

    share = w_ref.shape[0] // (columns * sources)
    band_rows = 2 * ROWS
    piece = 4 * band_rows
    for blocks, out_ref in zip(plan, out_refs):
        at = 0
        for across, along, start, stop in blocks:
            owner = lax.rem(chan + across, columns) * sources + lax.rem(tm + along, sources)
            for row in range(start * band_rows, stop * band_rows, piece):
                rows = pl.ds(pl.multiple_of(owner * share + row, piece), piece)
                out_ref[at : at + piece, :] = w_ref[rows, :].astype(jnp.bfloat16)
                at += piece


def channelise(place, chunk, voltages, come, taps_filter, tables, frames, columns, plan):
    sources = 1 + len(come)
    length = taps_filter.shape[1]
    spectra = sources * frames
    twiddle, matrix = tables
    out_rows = length // AVG * 2 * ROWS
    whole = pl.BlockSpec(memory_space=pltpu.VMEM)
    counts = [sum(stop - start for _, _, start, stop in blocks) for blocks in plan]
    flat = pl.pallas_call(
        lambda *refs: channelise_kernel(frames, chunk, columns, plan, *refs),
        out_shape=[
            jax.ShapeDtypeStruct((count * 2 * ROWS, LANES), jnp.bfloat16) for count in counts
        ],
        in_specs=[pl.BlockSpec(memory_space=pltpu.SMEM)]
        + [pl.BlockSpec(memory_space=pl.ANY)] * sources
        + [whole] * 3,
        out_specs=[whole] * len(plan),
        scratch_shapes=[
            pltpu.VMEM((sources, 2, ROWS, frames * length), jnp.bfloat16),
            pltpu.VMEM((RADIX, spectra, 2, ROWS, LANES), jnp.float32),
            pltpu.VMEM((ROWS * RADIX * spectra, LANES), jnp.float32),
            pltpu.VMEM((ROWS * RADIX * spectra, LANES), jnp.float32),
            pltpu.VMEM((out_rows, LANES), jnp.float32),
            pltpu.SemaphoreType.DMA((sources,)),
        ],
        compiler_params=pltpu.CompilerParams(vmem_limit_bytes=40 * 2**20),
        cost_estimate=pl.CostEstimate(
            flops=9 * 10**9, bytes_accessed=4 * 2**20, transcendentals=0
        ),
        name="channelise",
    )(place, voltages, *come, taps_filter, jnp.asarray(twiddle), jnp.asarray(matrix))
    return [piece.reshape(count, 2, ROWS, LANES) for piece, count in zip(flat, counts)]


def correlate_kernel(starts, width, place_ref, left_sel_ref, right_sel_ref, weight_ref, *refs):
    x_refs, (out_ref, x_all, *rows_refs, sems) = refs[: 2 * len(starts)], refs[-7:]
    tiles = out_ref.shape[0]
    step = pl.program_id(0)
    bands = x_all.shape[2]
    spans = [(0, 2), (2, bands)]

    def copies(span):
        first, last = spans[span]
        block = 0
        for index, start in enumerate(starts):
            blocks = x_refs[2 * index].shape[0]
            for side in range(2):
                yield pltpu.make_async_copy(
                    x_refs[2 * index + side].at[:, pl.ds(start + first, last - first)],
                    x_all.at[
                        lax.rem(place_ref[2] + side, 2),
                        pl.ds(block, blocks),
                        pl.ds(first, last - first),
                    ],
                    sems.at[span, 2 * index + side],
                )
            block += blocks

    lower = lax.broadcasted_iota(jnp.int32, (1, 2 * width), 1) < width

    def gather(band, left_ref, right_ref):
        right = []
        for pol in range(2):
            lanes = slice(pol * 2 * LANES, (pol + 1) * 2 * LANES)
            value = jnp.concatenate(
                [
                    jnp.concatenate([x_all[pol, block, band, part] for part in range(2)], axis=1)
                    for block in range(x_all.shape[1])
                ]
            )
            left = jnp.dot(left_sel_ref[...], value, preferred_element_type=jnp.float32)
            for tile in range(tiles):
                rows = slice(tile * width, (tile + 1) * width)
                scaled = left[rows] * weight_ref[pl.ds(tile, 1), :]
                left_ref[rows, lanes] = scaled.astype(jnp.bfloat16)
            right.append(
                lax.dot_general(
                    value,
                    right_sel_ref[pol],
                    (((0,), (0,)), ((), ())),
                    preferred_element_type=jnp.float32,
                )
            )
        for pair in range(tiles // 2):
            first, second = (v[:, pair * 2 * width : (pair + 1) * 2 * width] for v in right)
            even = jnp.where(lower, first, second)
            odd = pltpu.roll(jnp.where(lower, second, first), width, 1)
            right_ref[2 * pair] = even.astype(jnp.bfloat16)
            right_ref[2 * pair + 1] = odd.astype(jnp.bfloat16)

    def multiply(number, left_ref, right_ref):
        for tile in range(tiles):
            rows = slice(tile * width, (tile + 1) * width)
            left = jnp.concatenate(
                [left_ref[rows, lanes : lanes + 2 * LANES] for lanes in (0, 2 * LANES)]
            )
            right = right_ref[tile]
            turned = jnp.concatenate([-right[LANES:], right[:LANES]])
            both = jnp.concatenate([right, turned], axis=1)
            result = jnp.dot(left, both, preferred_element_type=jnp.float32)
            for part in range(2):
                out_ref[tile, number, part] = result[
                    :, part * 2 * width : (part + 1) * 2 * width
                ].reshape(2, width, 2 * width)

    even, odd = rows_refs[:2], rows_refs[2:]

    @pl.when(step == 0)
    def _():
        for span in range(2):
            for copy in copies(span):
                copy.start()
        for copy in copies(0):
            copy.wait()
        gather(0, *even)
        for copy in copies(1):
            copy.wait()

    gather(2 * step + 1, *odd)
    multiply(0, *even)
    gather(jnp.minimum(2 * step + 2, bands - 1), *even)
    multiply(1, *odd)


def correlate_tiles(place, tables, pieces, starts, width, first, count, bands, earlier):
    left_select, _, weight = tables
    tiles = weight.shape[0]
    whole = pl.BlockSpec(memory_space=pltpu.VMEM)
    more = [] if earlier is None else [earlier]
    rows = [
        pltpu.VMEM((tiles * width, 4 * LANES), jnp.bfloat16),
        pltpu.VMEM((tiles, 2 * LANES, 2 * width), jnp.bfloat16),
    ]
    return pl.pallas_call(
        lambda *refs: correlate_kernel(starts, width, *refs),
        grid=(count // 2,),
        out_shape=jax.ShapeDtypeStruct((tiles, bands, 2, 2, width, 2 * width), jnp.float32),
        in_specs=[pl.BlockSpec(memory_space=pltpu.SMEM)]
        + [whole] * len(tables)
        + [pl.BlockSpec(memory_space=pl.ANY)] * (len(pieces) + len(more)),
        out_specs=pl.BlockSpec(
            (tiles, 2, 2, 2, width, 2 * width), lambda g: (0, g + first // 2, 0, 0, 0, 0)
        ),
        scratch_shapes=[
            pltpu.VMEM((2, left_select.shape[1] // ROWS, count, 2, ROWS, LANES), jnp.bfloat16),
            *rows,
            *rows,
            pltpu.SemaphoreType.DMA((2, len(pieces))),
        ],
        input_output_aliases={1 + len(tables) + len(pieces): 0} if more else {},
        compiler_params=pltpu.CompilerParams(vmem_limit_bytes=32 * 2**20),
        cost_estimate=pl.CostEstimate(
            flops=13 * 10**9 * count // bands,
            bytes_accessed=42 * 2**20 * count // bands,
            transcendentals=0,
        ),
        name="correlate",
    )(place, *tables, *pieces, *more)


def tile_tables(tile_a, tile_b, tile_owner, tile_flags, row_of):
    tiles = tile_owner.shape[0]
    held = tile_owner == lax.axis_index("pol")
    order = jnp.arange(tiles, dtype=jnp.int32)
    rank = jnp.sum((held[None, :] & (order[None, :] < order[:, None])).astype(jnp.int32), axis=1)
    slots = jnp.arange(CAP, dtype=jnp.int32)
    pick = (held[None, :] & (rank[None, :] == slots[:, None])).astype(jnp.int32)
    sides = jnp.stack([row_of(tile_a), row_of(tile_b)], axis=1) + 1
    rows = jnp.sum(pick[:, :, None, None] * sides[None], axis=1) - 1
    flags = jnp.sum(pick[:, :, None] * tile_flags[None], axis=1).astype(jnp.float32)
    return rows, flags


def on_device_chunks(voltages, taps_filter, tile_a, tile_b, tile_owner, tile_flags):
    length = taps_filter.shape[1]
    stations = voltages.shape[2]
    frames = voltages.shape[3] // length
    chan_count, time_count = lax.axis_size("chan"), lax.axis_size("tm")
    owners = chan_count * time_count
    chunk_count = stations // (time_count * ROWS)
    width = tile_a.shape[1]
    bands = length // AVG // owners
    tables = fourier_tables(length)

    chan, tm = lax.axis_index("chan"), lax.axis_index("tm")
    place = jnp.stack([chan, tm, lax.axis_index("pol")]).astype(jnp.int32)

    def row_of(station):
        column, rest = station // stations, station % stations
        block, inside = rest // (chunk_count * ROWS), rest % (chunk_count * ROWS)
        across = (chan - column) % chan_count
        behind = (tm - block) % time_count
        piece = behind * chan_count + across
        return ((inside // ROWS) * owners + piece) * ROWS + inside % ROWS

    rows, flags = tile_tables(tile_a, tile_b, tile_owner, tile_flags, row_of)
    total_rows = chunk_count * owners * ROWS
    station_rows = jnp.arange(total_rows, dtype=jnp.int32)
    left_rows = rows[:, 0].reshape(-1)
    left_select = (left_rows[:, None] == station_rows).astype(jnp.bfloat16)
    right_rows = rows[:, 1].reshape(CAP // 2, 2, width)
    right_rows = jnp.stack([right_rows, right_rows[:, ::-1]]).reshape(2, 1, -1)
    right_select = (right_rows == station_rows[:, None]).astype(jnp.bfloat16)
    depth = AVG * time_count * frames
    weight = jnp.tile(flags * (1.0 / depth), (1, 2 * AVG))
    tables_of_tiles = [left_select, right_select, weight]

    samples = voltages.reshape(2, stations, frames * length)

    def travel(value, axes, distances):
        sizes = [lax.axis_size(axis) for axis in axes]
        pairs = []
        for index in np.ndindex(*sizes):
            target = [(i + d) % n for i, d, n in zip(index, distances, sizes)]
            pairs.append(tuple(int(np.ravel_multi_index(x, sizes)) for x in (index, target)))
        return lax.ppermute(value, axes, pairs)

    def after(values, earlier):
        return lax.optimization_barrier((list(values), list(earlier)))

    def block_for(values, chunk, distance):
        first = ((tm + distance) % time_count * chunk_count + chunk) * ROWS
        return lax.dynamic_slice(values, (0, first, 0), (2, ROWS, frames * length))

    def filtered(chunk, arrived, plan):
        return channelise(
            place, chunk, samples, arrived, taps_filter, tables, frames, chan_count, plan
        )

    def over(value, across, along):
        return travel(value, ("chan", "tm"), (across, along))

    def columns(near, far):
        return jnp.stack([near, far])

    half = bands // 2
    pairs = [(x, z) for z in range(time_count) for x in range(chan_count)]
    early_pairs = [(x, z) for z in (1, 3) for x in range(2)] + [(1, 0)]
    late_pairs = [(0, 2), (1, 2)]

    (one,), (values,) = after([block_for(samples, 0, 1)], [samples])
    two, three = (block_for(values, 0, distance) for distance in (2, 3))
    one, two = over(one, 0, 1), over(two, 0, 2)
    (three,), (one,) = after([three], [one])
    three = over(three, 0, 3)
    blocks = [block_for(values, 1, distance) for distance in (1, 2, 3)]
    blocks[:1], (two,) = after(blocks[:1], [two])
    blocks[2:], (three,) = after(blocks[2:], [three])
    first = [one, two, three]
    one, three = over(blocks[0], 0, 1), over(blocks[2], 0, 3)
    (two,), (one,) = after(blocks[1:2], [one])
    second = [one, over(two, 0, 2), three]

    plan = [[(x, z, 0, bands)] for x, z in pairs]
    early = dict(zip(pairs, filtered(0, first, plan)))
    blocks, held = after([early[p] for p in early_pairs], [second[1], *tables_of_tiles])
    second[1], tables_of_tiles = held[0], held[1:]
    early.update((p, over(block, *p)) for p, block in zip(early_pairs, blocks))
    blocks, held = after([early[p] for p in late_pairs], [early[p] for p in early_pairs[:2]])
    early.update(zip(early_pairs[:2], held))
    early.update((p, over(block, *p)) for p, block in zip(late_pairs, blocks))

    plan = [
        [(x, z, start, start + half) for start in (0, half) for z in range(time_count)]
        for x in range(chan_count)
    ]
    near, far = filtered(1, second, plan)
    (far,), held = after([far], [early[p] for p in early_pairs[:2]])
    early.update(zip(early_pairs[:2], held))
    far = over(far, 1, 0)
    shape = (2, time_count, half, 2, ROWS, LANES)
    (near, high), (far, far_high) = (v.reshape(shape) for v in (near, far))
    low = [columns(near[z], far[z]) for z in range(time_count)]
    high = [columns(high[z], far_high[z]) for z in range(time_count)]
    blocks, held = after(low[1:], [early[p] for p in late_pairs[:1]])
    early.update(zip(late_pairs[:1], held))
    moved = {z: over(blocks[z - 1], 0, z) for z in (2, 1, 3)}
    low = [low[0]] + [moved[z] for z in (1, 2, 3)]

    def with_other(values):
        return [side for v in values for side in (v, travel(v, ("pol",), (1,)))]

    early = with_other([jnp.stack([early[p] for p in pairs])])
    blocks, held = after(high[1:], [low[2], low[1], early[1]])
    low[2], low[1], early[1] = held
    moved = {z: over(blocks[z - 1], 0, z) for z in (2, 1, 3)}
    high = [high[0]] + [moved[z] for z in (1, 2, 3)]
    low = jnp.stack(low).reshape(2 * time_count, half, 2, ROWS, LANES)
    visibility = correlate_tiles(
        place, tables_of_tiles, early + with_other([low]),
        [0, 0], width, 0, half, bands, None,
    )
    high, (visibility,) = after(high, [visibility])
    return correlate_tiles(
        place, tables_of_tiles, early + with_other(high),
        [half] + [0] * 4, width, half, half, bands, visibility,
    )


def on_device(voltages, taps_filter, tile_a, tile_b, tile_owner, tile_flags):
    taps, length = taps_filter.shape
    frames = voltages.shape[3] // length
    time_count = lax.axis_size("tm")
    fits = (
        length == RADIX * LANES
        and AVG * time_count * frames == LANES
        and 2 * tile_a.shape[1] == LANES
        and voltages.shape[2] == 2 * time_count * ROWS
        and (lax.axis_size("chan"), time_count) == (2, 4)
    )
    form = on_device_chunks if fits else on_device_any
    return form(voltages, taps_filter, tile_a, tile_b, tile_owner, tile_flags)


def solution(mesh):
    return jax.shard_map(
        on_device,
        mesh=mesh,
        in_specs=(P("grp", "pol", "chan", "tm"), P(), P(), P(), P(), P()),
        out_specs=P("pol", ("chan", "tm"), "grp", None, None, None),
        check_vma=False,
    )
```

```python
import math

import jax
import jax.numpy as jnp
import numpy as np
from jax import lax
from jax.experimental import pallas as pl
from jax.experimental.pallas import tpu as pltpu
from jax.sharding import PartitionSpec as P

AVG = 8
CAP = 8
RADIX = 16
LANES = 128
ROWS = 16


radix_first = 32


def from_behind(value, axis, steps):
    count = lax.axis_size(axis)
    first, last = (max(0, -steps), min(count, count - steps))
    return lax.ppermute(value, axis, [(source, source + steps) for source in range(first, last)])


def fourier(filtered):
    length = filtered.shape[-1]
    second = length // radix_first
    exact_mode = lax.Precision.HIGHEST
    grid = filtered.reshape(filtered.shape[:-1] + (radix_first, second))
    outer = jnp.arange(radix_first, dtype=jnp.int32)
    inner = jnp.arange(second, dtype=jnp.int32)
    phase_one = (
        2.0
        * math.pi
        / radix_first
        * (outer[:, None] * outer[None, :] % radix_first).astype(jnp.float32)
    )
    phase_twist = 2.0 * math.pi / length * (outer[:, None] * inner[None, :]).astype(jnp.float32)
    phase_two = (
        2.0 * math.pi / second * (inner[:, None] * inner[None, :] % second).astype(jnp.float32)
    )
    cos_one, sin_one = (jnp.cos(phase_one), jnp.sin(phase_one))
    cos_twist, sin_twist = (jnp.cos(phase_twist), jnp.sin(phase_twist))
    cos_two, sin_two = (jnp.cos(phase_two), jnp.sin(phase_two))
    first_form = "fk,stkj->stfj"
    section_re = jnp.einsum(first_form, cos_one, grid[0], precision=exact_mode) + jnp.einsum(
        first_form, sin_one, grid[1], precision=exact_mode
    )
    section_im = jnp.einsum(first_form, cos_one, grid[1], precision=exact_mode) - jnp.einsum(
        first_form, sin_one, grid[0], precision=exact_mode
    )
    turned_re = section_re * cos_twist + section_im * sin_twist
    turned_im = section_im * cos_twist - section_re * sin_twist
    second_form = "gj,stfj->stgf"
    final_re = jnp.einsum(second_form, cos_two, turned_re, precision=exact_mode) + jnp.einsum(
        second_form, sin_two, turned_im, precision=exact_mode
    )
    final_im = jnp.einsum(second_form, cos_two, turned_im, precision=exact_mode) - jnp.einsum(
        second_form, sin_two, turned_re, precision=exact_mode
    )
    joined = jnp.stack([final_re, final_im]).reshape(filtered.shape)
    return joined * (1.0 / math.sqrt(length))


def correlate(full, rows_a, rows_b, flags, group_count):
    depth = full.shape[4]
    weight = jnp.tile(flags.astype(jnp.bfloat16), depth // flags.shape[0])
    left_rows = jnp.take(full, rows_a, axis=2) * weight
    right_rows = jnp.take(full, rows_b, axis=2)
    stacked_left = jnp.stack(
        [
            jnp.concatenate([left_rows[0], left_rows[1]], axis=-1),
            jnp.concatenate([left_rows[1], -left_rows[0]], axis=-1),
        ]
    )
    joined_right = jnp.concatenate([right_rows[0], right_rows[1]], axis=-1)
    result = jnp.einsum(
        "rpank,qbnk->nrpaqb", stacked_left, joined_right, preferred_element_type=jnp.float32
    )
    width = rows_a.shape[0]
    return result.reshape(group_count, 2, 2, width, 2 * width) * (1.0 / depth)


def on_device_any(voltages, taps_filter, tile_a, tile_b, tile_owner, tile_flags):
    history = taps_filter.shape[0] - 1
    length = taps_filter.shape[1]
    stations = voltages.shape[2]
    frames = voltages.shape[3] // length
    local_blocks = voltages.reshape(2, stations, frames, length)
    hop_count = -(-history // frames)
    sending = local_blocks
    extended = local_blocks
    for hop_index in range(hop_count):
        sending = from_behind(sending, "tm", 1)
        extended = jnp.concatenate([sending, extended], axis=2)
    extended = extended[:, :, extended.shape[2] - history - frames :]
    filtered = jnp.zeros((2, stations, frames, length), jnp.float32)
    for tap_index in range(history + 1):
        start = history - tap_index
        filtered = filtered + taps_filter[tap_index] * extended[
            :, :, start : start + frames
        ].astype(jnp.float32)
    spectra = fourier(filtered).astype(jnp.bfloat16)
    chan_count = lax.axis_size("chan")
    time_count = lax.axis_size("tm")
    narrow = length // (chan_count * time_count)
    outgoing = spectra.reshape(2, stations, frames, chan_count, time_count, narrow)
    outgoing = outgoing.transpose(0, 3, 4, 5, 1, 2)
    flat = outgoing.reshape(2, chan_count * time_count, narrow, stations * frames)
    moved = lax.all_to_all(flat, ("chan", "tm"), split_axis=1, concat_axis=1, tiled=True)
    moved = moved.reshape(2, chan_count, time_count, narrow, stations, frames)
    bands = narrow // AVG
    every_station = chan_count * stations
    spectra_count = time_count * frames
    arranged = moved.transpose(0, 1, 4, 3, 2, 5).reshape(
        2, 1, every_station, bands, AVG * spectra_count
    )
    full = lax.all_gather(arranged, "pol", axis=1, tiled=True)
    position = lax.axis_index("pol")
    width = tile_a.shape[1]
    capacity = CAP
    held = tile_owner == position
    listed = jnp.nonzero(held, size=capacity, fill_value=0)[0].astype(jnp.int32)
    tally = jnp.sum(held.astype(jnp.int32))
    initial = jnp.zeros((capacity, bands, 2, 2, width, 2 * width), jnp.float32)

    def fill_slot(slot, results):
        chosen_tile = listed[slot]
        return results.at[slot].set(
            correlate(
                full, tile_a[chosen_tile], tile_b[chosen_tile], tile_flags[chosen_tile], bands
            )
        )

    visibility = lax.fori_loop(0, tally, fill_slot, initial)
    return visibility


def fourier_tables(length):
    low = np.arange(RADIX)
    lane = np.arange(LANES)
    turn = 2.0 * np.pi / length * np.outer(low, lane)
    twiddle = np.stack([np.cos(turn), np.sin(turn)]).astype(np.float32)
    angle = 2.0 * np.pi / LANES * (np.outer(lane, lane) % LANES)
    cos, sin = np.cos(angle) / math.sqrt(length), np.sin(angle) / math.sqrt(length)
    matrix = np.block([[cos, sin], [-sin, cos]]).astype(np.float32)
    high = matrix.astype(jnp.bfloat16)
    rest = (matrix - high.astype(np.float32)).astype(jnp.bfloat16)
    return twiddle, np.stack([high, rest])


def butterflies(values):
    count = len(values)
    if count == 1:
        return values
    even, odd = butterflies(values[0::2]), butterflies(values[1::2])
    first, second = [], []
    for index in range(count // 2):
        (a, b), (c, d) = even[index], odd[index]
        if index == 0:
            e, f = c, d
        elif 4 * index == count:
            e, f = d, -c
        elif 8 * index == count:
            root = math.sqrt(0.5)
            e, f = (c + d) * root, (d - c) * root
        elif 8 * index == 3 * count:
            root = math.sqrt(0.5)
            e, f = (d - c) * root, -(c + d) * root
        else:
            turn = 2.0 * math.pi * index / count
            cos, sin = math.cos(turn), math.sin(turn)
            e, f = c * cos + d * sin, d * cos - c * sin
        first.append((a + e, b + f))
        second.append((a - e, b - f))
    return first + second


def channelise_kernel(frames, chunk, columns, plan, place_ref, own_ref, *refs):
    sources = refs[-6].shape[0]
    come_refs = refs[: sources - 1]
    taps_ref, twiddle_ref, matrix_ref = refs[sources - 1 : sources + 2]
    out_refs = refs[sources + 2 : -6]
    x_ref, fil_ref, zr_ref, zi_ref, w_ref, sems = refs[-6:]
    chan, tm = place_ref[0], place_ref[1]
    own_rows = pl.multiple_of((tm * (own_ref.shape[1] // (sources * ROWS)) + chunk) * ROWS, ROWS)
    copies = []
    for behind in range(sources):
        block = come_refs[behind - 1] if behind else own_ref.at[:, pl.ds(own_rows, ROWS), :]
        slot = lax.rem(tm - behind + sources, sources)
        copies.append(pltpu.make_async_copy(block, x_ref.at[slot], sems.at[behind]))
    for copy in copies:
        copy.start()
    for copy in copies:
        copy.wait()
    spectra = sources * frames
    length = taps_ref.shape[1]
    taps = taps_ref.shape[0]
    depth = RADIX * spectra
    z_refs = (zr_ref, zi_ref)

    @pl.loop(0, RADIX)
    def _(section):
        at = pl.multiple_of(section * LANES, LANES)
        weights = [taps_ref[pl.ds(m, 1), pl.ds(at, LANES)] for m in range(taps)]
        for part in range(2):
            blocks = []
            for t in range(spectra):
                lane = pl.multiple_of((t % frames) * length + section * LANES, LANES)
                blocks.append(x_ref[t // frames, part, :, pl.ds(lane, LANES)].astype(jnp.float32))
            for t in range(spectra):
                total = weights[0] * blocks[t]
                for m in range(1, min(t + 1, taps)):
                    total = total + weights[m] * blocks[t - m]
                fil_ref[section, t, part] = total

    @pl.loop(0, spectra)
    def _(t):
        for half in range(ROWS // 8):
            values = [
                tuple(fil_ref[section, t, part, pl.ds(half * 8, 8), :] for part in range(2))
                for section in range(RADIX)
            ]
            for low, (re, im) in enumerate(butterflies(values)):
                if low:
                    cos = twiddle_ref[0, pl.ds(low, 1), :]
                    sin = twiddle_ref[1, pl.ds(low, 1), :]
                    re, im = re * cos + im * sin, im * cos - re * sin
                rows = pl.ds(half * 8 * depth + low * spectra + t, 8, stride=depth)
                zr_ref[rows, :] = re
                zi_ref[rows, :] = im

    form = (((1,), (1,)), ((), ()))
    high_matrix, low_matrix = matrix_ref[0], matrix_ref[1]
    halves = depth // LANES

    @pl.loop(0, ROWS)
    def _(station):
        rows = pl.ds(pl.multiple_of(station * depth, depth), depth)
        value = jnp.concatenate([ref[rows, :] for ref in z_refs], axis=1)
        high = value.astype(jnp.bfloat16)
        rest = (value - high.astype(jnp.float32)).astype(jnp.bfloat16)
        total = lax.dot_general(high_matrix, high, form, preferred_element_type=jnp.float32)
        total += lax.dot_general(high_matrix, rest, form, preferred_element_type=jnp.float32)
        total += lax.dot_general(low_matrix, high, form, preferred_element_type=jnp.float32)
        for half in range(halves):
            for part in range(2):
                rows = pl.ds((half * 2 + part) * ROWS + station, LANES, stride=halves * 2 * ROWS)
                w_ref[rows, :] = total[
                    part * LANES : (part + 1) * LANES, half * LANES : (half + 1) * LANES
                ]

    share = w_ref.shape[0] // (columns * sources)
    band_rows = 2 * ROWS
    piece = 4 * band_rows
    for blocks, out_ref in zip(plan, out_refs):
        at = 0
        for across, along, start, stop in blocks:
            owner = lax.rem(chan + across, columns) * sources + lax.rem(tm + along, sources)
            for row in range(start * band_rows, stop * band_rows, piece):
                rows = pl.ds(pl.multiple_of(owner * share + row, piece), piece)
                out_ref[at : at + piece, :] = w_ref[rows, :].astype(jnp.bfloat16)
                at += piece


def channelise(place, chunk, voltages, come, taps_filter, tables, frames, columns, plan):
    sources = 1 + len(come)
    length = taps_filter.shape[1]
    spectra = sources * frames
    twiddle, matrix = tables
    out_rows = length // AVG * 2 * ROWS
    whole = pl.BlockSpec(memory_space=pltpu.VMEM)
    counts = [sum(stop - start for _, _, start, stop in blocks) for blocks in plan]
    flat = pl.pallas_call(
        lambda *refs: channelise_kernel(frames, chunk, columns, plan, *refs),
        out_shape=[
            jax.ShapeDtypeStruct((count * 2 * ROWS, LANES), jnp.bfloat16) for count in counts
        ],
        in_specs=[pl.BlockSpec(memory_space=pltpu.SMEM)]
        + [pl.BlockSpec(memory_space=pl.ANY)] * sources
        + [whole] * 3,
        out_specs=[whole] * len(plan),
        scratch_shapes=[
            pltpu.VMEM((sources, 2, ROWS, frames * length), jnp.bfloat16),
            pltpu.VMEM((RADIX, spectra, 2, ROWS, LANES), jnp.float32),
            pltpu.VMEM((ROWS * RADIX * spectra, LANES), jnp.float32),
            pltpu.VMEM((ROWS * RADIX * spectra, LANES), jnp.float32),
            pltpu.VMEM((out_rows, LANES), jnp.float32),
            pltpu.SemaphoreType.DMA((sources,)),
        ],
        compiler_params=pltpu.CompilerParams(vmem_limit_bytes=40 * 2**20),
        cost_estimate=pl.CostEstimate(
            flops=9 * 10**9, bytes_accessed=4 * 2**20, transcendentals=0
        ),
        name="channelise",
    )(place, voltages, *come, taps_filter, jnp.asarray(twiddle), jnp.asarray(matrix))
    return [piece.reshape(count, 2, ROWS, LANES) for piece, count in zip(flat, counts)]


def correlate_kernel(starts, width, place_ref, left_sel_ref, right_sel_ref, weight_ref, *refs):
    x_refs, (out_ref, x_all, *rows_refs, sems) = refs[: 2 * len(starts)], refs[-7:]
    tiles = out_ref.shape[0]
    step = pl.program_id(0)
    bands = x_all.shape[2]
    spans = [(0, 2), (2, bands)]

    def copies(span):
        first, last = spans[span]
        block = 0
        for index, start in enumerate(starts):
            blocks = x_refs[2 * index].shape[0]
            for side in range(2):
                yield pltpu.make_async_copy(
                    x_refs[2 * index + side].at[:, pl.ds(start + first, last - first)],
                    x_all.at[
                        lax.rem(place_ref[2] + side, 2),
                        pl.ds(block, blocks),
                        pl.ds(first, last - first),
                    ],
                    sems.at[span, 2 * index + side],
                )
            block += blocks

    lower = lax.broadcasted_iota(jnp.int32, (1, 2 * width), 1) < width

    def gather(band, left_ref, right_ref):
        right = []
        for pol in range(2):
            lanes = slice(pol * 2 * LANES, (pol + 1) * 2 * LANES)
            value = jnp.concatenate(
                [
                    jnp.concatenate([x_all[pol, block, band, part] for part in range(2)], axis=1)
                    for block in range(x_all.shape[1])
                ]
            )
            left = jnp.dot(left_sel_ref[...], value, preferred_element_type=jnp.float32)
            for tile in range(tiles):
                rows = slice(tile * width, (tile + 1) * width)
                scaled = left[rows] * weight_ref[pl.ds(tile, 1), :]
                left_ref[rows, lanes] = scaled.astype(jnp.bfloat16)
            right.append(
                lax.dot_general(
                    value,
                    right_sel_ref[pol],
                    (((0,), (0,)), ((), ())),
                    preferred_element_type=jnp.float32,
                )
            )
        for pair in range(tiles // 2):
            first, second = (v[:, pair * 2 * width : (pair + 1) * 2 * width] for v in right)
            even = jnp.where(lower, first, second)
            odd = pltpu.roll(jnp.where(lower, second, first), width, 1)
            right_ref[2 * pair] = even.astype(jnp.bfloat16)
            right_ref[2 * pair + 1] = odd.astype(jnp.bfloat16)

    def multiply(number, left_ref, right_ref):
        for tile in range(tiles):
            rows = slice(tile * width, (tile + 1) * width)
            left = jnp.concatenate(
                [left_ref[rows, lanes : lanes + 2 * LANES] for lanes in (0, 2 * LANES)]
            )
            right = right_ref[tile]
            turned = jnp.concatenate([-right[LANES:], right[:LANES]])
            both = jnp.concatenate([right, turned], axis=1)
            result = jnp.dot(left, both, preferred_element_type=jnp.float32)
            for part in range(2):
                out_ref[tile, number, part] = result[
                    :, part * 2 * width : (part + 1) * 2 * width
                ].reshape(2, width, 2 * width)

    even, odd = rows_refs[:2], rows_refs[2:]

    @pl.when(step == 0)
    def _():
        for span in range(2):
            for copy in copies(span):
                copy.start()
        for copy in copies(0):
            copy.wait()
        gather(0, *even)
        for copy in copies(1):
            copy.wait()

    gather(2 * step + 1, *odd)
    multiply(0, *even)
    gather(jnp.minimum(2 * step + 2, bands - 1), *even)
    multiply(1, *odd)


def correlate_tiles(place, tables, pieces, starts, width, first, count, bands, earlier):
    left_select, _, weight = tables
    tiles = weight.shape[0]
    whole = pl.BlockSpec(memory_space=pltpu.VMEM)
    more = [] if earlier is None else [earlier]
    rows = [
        pltpu.VMEM((tiles * width, 4 * LANES), jnp.bfloat16),
        pltpu.VMEM((tiles, 2 * LANES, 2 * width), jnp.bfloat16),
    ]
    return pl.pallas_call(
        lambda *refs: correlate_kernel(starts, width, *refs),
        grid=(count // 2,),
        out_shape=jax.ShapeDtypeStruct((tiles, bands, 2, 2, width, 2 * width), jnp.float32),
        in_specs=[pl.BlockSpec(memory_space=pltpu.SMEM)]
        + [whole] * len(tables)
        + [pl.BlockSpec(memory_space=pl.ANY)] * (len(pieces) + len(more)),
        out_specs=pl.BlockSpec(
            (tiles, 2, 2, 2, width, 2 * width), lambda g: (0, g + first // 2, 0, 0, 0, 0)
        ),
        scratch_shapes=[
            pltpu.VMEM((2, left_select.shape[1] // ROWS, count, 2, ROWS, LANES), jnp.bfloat16),
            *rows,
            *rows,
            pltpu.SemaphoreType.DMA((2, len(pieces))),
        ],
        input_output_aliases={1 + len(tables) + len(pieces): 0} if more else {},
        compiler_params=pltpu.CompilerParams(vmem_limit_bytes=32 * 2**20),
        cost_estimate=pl.CostEstimate(
            flops=13 * 10**9 * count // bands,
            bytes_accessed=42 * 2**20 * count // bands,
            transcendentals=0,
        ),
        name="correlate",
    )(place, *tables, *pieces, *more)


def tile_tables(tile_a, tile_b, tile_owner, tile_flags, row_of):
    tiles = tile_owner.shape[0]
    held = tile_owner == lax.axis_index("pol")
    order = jnp.arange(tiles, dtype=jnp.int32)
    rank = jnp.sum((held[None, :] & (order[None, :] < order[:, None])).astype(jnp.int32), axis=1)
    slots = jnp.arange(CAP, dtype=jnp.int32)
    pick = (held[None, :] & (rank[None, :] == slots[:, None])).astype(jnp.int32)
    sides = jnp.stack([row_of(tile_a), row_of(tile_b)], axis=1) + 1
    rows = jnp.sum(pick[:, :, None, None] * sides[None], axis=1) - 1
    flags = jnp.sum(pick[:, :, None] * tile_flags[None], axis=1).astype(jnp.float32)
    return rows, flags


def on_device_chunks(voltages, taps_filter, tile_a, tile_b, tile_owner, tile_flags):
    length = taps_filter.shape[1]
    stations = voltages.shape[2]
    frames = voltages.shape[3] // length
    chan_count, time_count = lax.axis_size("chan"), lax.axis_size("tm")
    owners = chan_count * time_count
    chunk_count = stations // (time_count * ROWS)
    width = tile_a.shape[1]
    bands = length // AVG // owners
    tables = fourier_tables(length)

    chan, tm = lax.axis_index("chan"), lax.axis_index("tm")
    place = jnp.stack([chan, tm, lax.axis_index("pol")]).astype(jnp.int32)

    def row_of(station):
        column, rest = station // stations, station % stations
        block, inside = rest // (chunk_count * ROWS), rest % (chunk_count * ROWS)
        across = (chan - column) % chan_count
        behind = (tm - block) % time_count
        piece = behind * chan_count + across
        return ((inside // ROWS) * owners + piece) * ROWS + inside % ROWS

    rows, flags = tile_tables(tile_a, tile_b, tile_owner, tile_flags, row_of)
    total_rows = chunk_count * owners * ROWS
    station_rows = jnp.arange(total_rows, dtype=jnp.int32)
    left_rows = rows[:, 0].reshape(-1)
    left_select = (left_rows[:, None] == station_rows).astype(jnp.bfloat16)
    right_rows = rows[:, 1].reshape(CAP // 2, 2, width)
    right_rows = jnp.stack([right_rows, right_rows[:, ::-1]]).reshape(2, 1, -1)
    right_select = (right_rows == station_rows[:, None]).astype(jnp.bfloat16)
    depth = AVG * time_count * frames
    weight = jnp.tile(flags * (1.0 / depth), (1, 2 * AVG))
    tables_of_tiles = [left_select, right_select, weight]

    samples = voltages.reshape(2, stations, frames * length)

    def travel(value, axes, distances):
        sizes = [lax.axis_size(axis) for axis in axes]
        pairs = []
        for index in np.ndindex(*sizes):
            target = [(i + d) % n for i, d, n in zip(index, distances, sizes)]
            pairs.append(tuple(int(np.ravel_multi_index(x, sizes)) for x in (index, target)))
        return lax.ppermute(value, axes, pairs)

    def after(values, earlier):
        return lax.optimization_barrier((list(values), list(earlier)))

    def block_for(values, chunk, distance):
        first = ((tm + distance) % time_count * chunk_count + chunk) * ROWS
        return lax.dynamic_slice(values, (0, first, 0), (2, ROWS, frames * length))

    def filtered(chunk, arrived, plan):
        return channelise(
            place, chunk, samples, arrived, taps_filter, tables, frames, chan_count, plan
        )

    def over(value, across, along):
        return travel(value, ("chan", "tm"), (across, along))

    def columns(near, far):
        return jnp.stack([near, far])

    cut = bands * 5 // 8
    rest = bands - cut
    pairs = [(x, z) for z in range(time_count) for x in range(chan_count)]
    early_pairs = [(x, z) for z in (1, 3) for x in range(2)] + [(1, 0)]
    late_pairs = [(0, 2), (1, 2)]

    (one,), (values,) = after([block_for(samples, 0, 1)], [samples])
    two, three = (block_for(values, 0, distance) for distance in (2, 3))
    one, two = over(one, 0, 1), over(two, 0, 2)
    (three,), (one,) = after([three], [one])
    three = over(three, 0, 3)
    blocks = [block_for(values, 1, distance) for distance in (1, 2, 3)]
    blocks[:1], (two,) = after(blocks[:1], [two])
    blocks[2:], (three,) = after(blocks[2:], [three])
    first = [one, two, three]
    one, three = over(blocks[0], 0, 1), over(blocks[2], 0, 3)
    (two,), (one,) = after(blocks[1:2], [one])
    second = [one, over(two, 0, 2), three]

    plan = [[(x, z, 0, bands)] for x, z in pairs]
    early = dict(zip(pairs, filtered(0, first, plan)))
    blocks, held = after([early[p] for p in early_pairs], [second[1], *tables_of_tiles])
    second[1], tables_of_tiles = held[0], held[1:]
    early.update((p, over(block, *p)) for p, block in zip(early_pairs, blocks))
    blocks, held = after([early[p] for p in late_pairs], [early[p] for p in early_pairs[:2]])
    early.update(zip(early_pairs[:2], held))
    early.update((p, over(block, *p)) for p, block in zip(late_pairs, blocks))

    plan = [
        [(x, z, *span) for span in ((0, cut), (cut, bands)) for z in range(time_count)]
        for x in range(chan_count)
    ]
    near, far = filtered(1, second, plan)
    (far,), held = after([far], [early[p] for p in early_pairs[:4]])
    early.update(zip(early_pairs[:4], held))
    far = over(far, 1, 0)
    low, high = [], []
    for z in range(time_count):
        for mixed, first, count in ((low, z * cut, cut), (high, time_count * cut + z * rest, rest)):
            mixed.append(columns(near[first : first + count], far[first : first + count]))
    blocks, held = after(low[1:], [early[p] for p in late_pairs[:1]])
    early.update(zip(late_pairs[:1], held))
    moved = {z: over(blocks[z - 1], 0, z) for z in (2, 1, 3)}
    low = [low[0]] + [moved[z] for z in (1, 2, 3)]

    def with_other(values):
        return [side for v in values for side in (v, travel(v, ("pol",), (1,)))]

    early = with_other([jnp.stack([early[p] for p in pairs])])
    blocks, held = after(high[1:], [low[2], low[1], early[1]])
    low[2], low[1], early[1] = held
    moved = {z: over(blocks[z - 1], 0, z) for z in (2, 1, 3)}
    high = [high[0]] + [moved[z] for z in (1, 2, 3)]
    low = jnp.stack(low).reshape(2 * time_count, cut, 2, ROWS, LANES)
    visibility = correlate_tiles(
        place, tables_of_tiles, early + with_other([low]),
        [0, 0], width, 0, cut, bands, None,
    )
    home = with_other(high[:1])
    high, (visibility,) = after(high[1:], [visibility])
    return correlate_tiles(
        place, tables_of_tiles, early + home + with_other(high),
        [cut] + [0] * 4, width, cut, rest, bands, visibility,
    )


def on_device(voltages, taps_filter, tile_a, tile_b, tile_owner, tile_flags):
    taps, length = taps_filter.shape
    frames = voltages.shape[3] // length
    time_count = lax.axis_size("tm")
    fits = (
        length == RADIX * LANES
        and AVG * time_count * frames == LANES
        and 2 * tile_a.shape[1] == LANES
        and voltages.shape[2] == 2 * time_count * ROWS
        and (lax.axis_size("chan"), time_count) == (2, 4)
    )
    form = on_device_chunks if fits else on_device_any
    return form(voltages, taps_filter, tile_a, tile_b, tile_owner, tile_flags)


def solution(mesh):
    return jax.shard_map(
        on_device,
        mesh=mesh,
        in_specs=(P("grp", "pol", "chan", "tm"), P(), P(), P(), P(), P()),
        out_specs=P("pol", ("chan", "tm"), "grp", None, None, None),
        check_vma=False,
    )
```

```python
import math

import jax
import jax.numpy as jnp
import numpy as np
from jax import lax
from jax.experimental import pallas as pl
from jax.experimental.pallas import tpu as pltpu
from jax.sharding import PartitionSpec as P

AVG = 8
CAP = 8
RADIX = 16
LANES = 128
ROWS = 16


radix_first = 32


def from_behind(value, axis, steps):
    count = lax.axis_size(axis)
    first, last = (max(0, -steps), min(count, count - steps))
    return lax.ppermute(value, axis, [(source, source + steps) for source in range(first, last)])


def fourier(filtered):
    length = filtered.shape[-1]
    second = length // radix_first
    exact_mode = lax.Precision.HIGHEST
    grid = filtered.reshape(filtered.shape[:-1] + (radix_first, second))
    outer = jnp.arange(radix_first, dtype=jnp.int32)
    inner = jnp.arange(second, dtype=jnp.int32)
    phase_one = (
        2.0
        * math.pi
        / radix_first
        * (outer[:, None] * outer[None, :] % radix_first).astype(jnp.float32)
    )
    phase_twist = 2.0 * math.pi / length * (outer[:, None] * inner[None, :]).astype(jnp.float32)
    phase_two = (
        2.0 * math.pi / second * (inner[:, None] * inner[None, :] % second).astype(jnp.float32)
    )
    cos_one, sin_one = (jnp.cos(phase_one), jnp.sin(phase_one))
    cos_twist, sin_twist = (jnp.cos(phase_twist), jnp.sin(phase_twist))
    cos_two, sin_two = (jnp.cos(phase_two), jnp.sin(phase_two))
    first_form = "fk,stkj->stfj"
    section_re = jnp.einsum(first_form, cos_one, grid[0], precision=exact_mode) + jnp.einsum(
        first_form, sin_one, grid[1], precision=exact_mode
    )
    section_im = jnp.einsum(first_form, cos_one, grid[1], precision=exact_mode) - jnp.einsum(
        first_form, sin_one, grid[0], precision=exact_mode
    )
    turned_re = section_re * cos_twist + section_im * sin_twist
    turned_im = section_im * cos_twist - section_re * sin_twist
    second_form = "gj,stfj->stgf"
    final_re = jnp.einsum(second_form, cos_two, turned_re, precision=exact_mode) + jnp.einsum(
        second_form, sin_two, turned_im, precision=exact_mode
    )
    final_im = jnp.einsum(second_form, cos_two, turned_im, precision=exact_mode) - jnp.einsum(
        second_form, sin_two, turned_re, precision=exact_mode
    )
    joined = jnp.stack([final_re, final_im]).reshape(filtered.shape)
    return joined * (1.0 / math.sqrt(length))


def correlate(full, rows_a, rows_b, flags, group_count):
    depth = full.shape[4]
    weight = jnp.tile(flags.astype(jnp.bfloat16), depth // flags.shape[0])
    left_rows = jnp.take(full, rows_a, axis=2) * weight
    right_rows = jnp.take(full, rows_b, axis=2)
    stacked_left = jnp.stack(
        [
            jnp.concatenate([left_rows[0], left_rows[1]], axis=-1),
            jnp.concatenate([left_rows[1], -left_rows[0]], axis=-1),
        ]
    )
    joined_right = jnp.concatenate([right_rows[0], right_rows[1]], axis=-1)
    result = jnp.einsum(
        "rpank,qbnk->nrpaqb", stacked_left, joined_right, preferred_element_type=jnp.float32
    )
    width = rows_a.shape[0]
    return result.reshape(group_count, 2, 2, width, 2 * width) * (1.0 / depth)


def on_device_any(voltages, taps_filter, tile_a, tile_b, tile_owner, tile_flags):
    history = taps_filter.shape[0] - 1
    length = taps_filter.shape[1]
    stations = voltages.shape[2]
    frames = voltages.shape[3] // length
    local_blocks = voltages.reshape(2, stations, frames, length)
    hop_count = -(-history // frames)
    sending = local_blocks
    extended = local_blocks
    for hop_index in range(hop_count):
        sending = from_behind(sending, "tm", 1)
        extended = jnp.concatenate([sending, extended], axis=2)
    extended = extended[:, :, extended.shape[2] - history - frames :]
    filtered = jnp.zeros((2, stations, frames, length), jnp.float32)
    for tap_index in range(history + 1):
        start = history - tap_index
        filtered = filtered + taps_filter[tap_index] * extended[
            :, :, start : start + frames
        ].astype(jnp.float32)
    spectra = fourier(filtered).astype(jnp.bfloat16)
    chan_count = lax.axis_size("chan")
    time_count = lax.axis_size("tm")
    narrow = length // (chan_count * time_count)
    outgoing = spectra.reshape(2, stations, frames, chan_count, time_count, narrow)
    outgoing = outgoing.transpose(0, 3, 4, 5, 1, 2)
    flat = outgoing.reshape(2, chan_count * time_count, narrow, stations * frames)
    moved = lax.all_to_all(flat, ("chan", "tm"), split_axis=1, concat_axis=1, tiled=True)
    moved = moved.reshape(2, chan_count, time_count, narrow, stations, frames)
    bands = narrow // AVG
    every_station = chan_count * stations
    spectra_count = time_count * frames
    arranged = moved.transpose(0, 1, 4, 3, 2, 5).reshape(
        2, 1, every_station, bands, AVG * spectra_count
    )
    full = lax.all_gather(arranged, "pol", axis=1, tiled=True)
    position = lax.axis_index("pol")
    width = tile_a.shape[1]
    capacity = CAP
    held = tile_owner == position
    listed = jnp.nonzero(held, size=capacity, fill_value=0)[0].astype(jnp.int32)
    tally = jnp.sum(held.astype(jnp.int32))
    initial = jnp.zeros((capacity, bands, 2, 2, width, 2 * width), jnp.float32)

    def fill_slot(slot, results):
        chosen_tile = listed[slot]
        return results.at[slot].set(
            correlate(
                full, tile_a[chosen_tile], tile_b[chosen_tile], tile_flags[chosen_tile], bands
            )
        )

    visibility = lax.fori_loop(0, tally, fill_slot, initial)
    return visibility


def fourier_tables(length):
    low = np.arange(RADIX)
    lane = np.arange(LANES)
    turn = 2.0 * np.pi / length * np.outer(low, lane)
    twiddle = np.stack([np.cos(turn), np.sin(turn)]).astype(np.float32)
    angle = 2.0 * np.pi / LANES * (np.outer(lane, lane) % LANES)
    cos, sin = np.cos(angle) / math.sqrt(length), np.sin(angle) / math.sqrt(length)
    matrix = np.block([[cos, sin], [-sin, cos]]).astype(np.float32)
    high = matrix.astype(jnp.bfloat16)
    rest = (matrix - high.astype(np.float32)).astype(jnp.bfloat16)
    return twiddle, np.stack([high, rest])


def butterflies(values):
    count = len(values)
    if count == 1:
        return values
    even, odd = butterflies(values[0::2]), butterflies(values[1::2])
    first, second = [], []
    for index in range(count // 2):
        (a, b), (c, d) = even[index], odd[index]
        if index == 0:
            e, f = c, d
        elif 4 * index == count:
            e, f = d, -c
        elif 8 * index == count:
            root = math.sqrt(0.5)
            e, f = (c + d) * root, (d - c) * root
        elif 8 * index == 3 * count:
            root = math.sqrt(0.5)
            e, f = (d - c) * root, -(c + d) * root
        else:
            turn = 2.0 * math.pi * index / count
            cos, sin = math.cos(turn), math.sin(turn)
            e, f = c * cos + d * sin, d * cos - c * sin
        first.append((a + e, b + f))
        second.append((a - e, b - f))
    return first + second


def channelise_kernel(frames, chunk, columns, plan, place_ref, own_ref, *refs):
    sources = refs[-6].shape[0]
    come_refs = refs[: sources - 1]
    taps_ref, twiddle_ref, matrix_ref = refs[sources - 1 : sources + 2]
    out_refs = refs[sources + 2 : -6]
    x_ref, fil_ref, zr_ref, zi_ref, w_ref, sems = refs[-6:]
    chan, tm = place_ref[0], place_ref[1]
    own_rows = pl.multiple_of((tm * (own_ref.shape[1] // (sources * ROWS)) + chunk) * ROWS, ROWS)
    copies = []
    for behind in range(sources):
        block = come_refs[behind - 1] if behind else own_ref.at[:, pl.ds(own_rows, ROWS), :]
        slot = lax.rem(tm - behind + sources, sources)
        copies.append(pltpu.make_async_copy(block, x_ref.at[slot], sems.at[behind]))
    for copy in copies:
        copy.start()
    for copy in copies:
        copy.wait()
    spectra = sources * frames
    length = taps_ref.shape[1]
    taps = taps_ref.shape[0]
    depth = RADIX * spectra
    z_refs = (zr_ref, zi_ref)

    @pl.loop(0, RADIX)
    def _(section):
        at = pl.multiple_of(section * LANES, LANES)
        weights = [taps_ref[pl.ds(m, 1), pl.ds(at, LANES)] for m in range(taps)]
        for part in range(2):
            blocks = []
            for t in range(spectra):
                lane = pl.multiple_of((t % frames) * length + section * LANES, LANES)
                blocks.append(x_ref[t // frames, part, :, pl.ds(lane, LANES)].astype(jnp.float32))
            for t in range(spectra):
                total = weights[0] * blocks[t]
                for m in range(1, min(t + 1, taps)):
                    total = total + weights[m] * blocks[t - m]
                fil_ref[section, t, part] = total

    @pl.loop(0, spectra)
    def _(t):
        for half in range(ROWS // 8):
            values = [
                tuple(fil_ref[section, t, part, pl.ds(half * 8, 8), :] for part in range(2))
                for section in range(RADIX)
            ]
            for low, (re, im) in enumerate(butterflies(values)):
                if low:
                    cos = twiddle_ref[0, pl.ds(low, 1), :]
                    sin = twiddle_ref[1, pl.ds(low, 1), :]
                    re, im = re * cos + im * sin, im * cos - re * sin
                rows = pl.ds(half * 8 * depth + low * spectra + t, 8, stride=depth)
                zr_ref[rows, :] = re
                zi_ref[rows, :] = im

    form = (((1,), (1,)), ((), ()))
    high_matrix, low_matrix = matrix_ref[0], matrix_ref[1]
    halves = depth // LANES

    @pl.loop(0, ROWS)
    def _(station):
        rows = pl.ds(pl.multiple_of(station * depth, depth), depth)
        value = jnp.concatenate([ref[rows, :] for ref in z_refs], axis=1)
        high = value.astype(jnp.bfloat16)
        rest = (value - high.astype(jnp.float32)).astype(jnp.bfloat16)
        total = lax.dot_general(high_matrix, high, form, preferred_element_type=jnp.float32)
        total += lax.dot_general(high_matrix, rest, form, preferred_element_type=jnp.float32)
        total += lax.dot_general(low_matrix, high, form, preferred_element_type=jnp.float32)
        for half in range(halves):
            for part in range(2):
                rows = pl.ds((half * 2 + part) * ROWS + station, LANES, stride=halves * 2 * ROWS)
                w_ref[rows, :] = total[
                    part * LANES : (part + 1) * LANES, half * LANES : (half + 1) * LANES
                ]

    share = w_ref.shape[0] // (columns * sources)
    band_rows = 2 * ROWS
    piece = 4 * band_rows
    for blocks, out_ref in zip(plan, out_refs):
        at = 0
        for across, along, start, stop in blocks:
            owner = lax.rem(chan + across, columns) * sources + lax.rem(tm + along, sources)
            for row in range(start * band_rows, stop * band_rows, piece):
                rows = pl.ds(pl.multiple_of(owner * share + row, piece), piece)
                out_ref[at : at + piece, :] = w_ref[rows, :].astype(jnp.bfloat16)
                at += piece


def channelise(place, chunk, voltages, come, taps_filter, tables, frames, columns, plan):
    sources = 1 + len(come)
    length = taps_filter.shape[1]
    spectra = sources * frames
    twiddle, matrix = tables
    out_rows = length // AVG * 2 * ROWS
    whole = pl.BlockSpec(memory_space=pltpu.VMEM)
    counts = [sum(stop - start for _, _, start, stop in blocks) for blocks in plan]
    flat = pl.pallas_call(
        lambda *refs: channelise_kernel(frames, chunk, columns, plan, *refs),
        out_shape=[
            jax.ShapeDtypeStruct((count * 2 * ROWS, LANES), jnp.bfloat16) for count in counts
        ],
        in_specs=[pl.BlockSpec(memory_space=pltpu.SMEM)]
        + [pl.BlockSpec(memory_space=pl.ANY)] * sources
        + [whole] * 3,
        out_specs=[whole] * len(plan),
        scratch_shapes=[
            pltpu.VMEM((sources, 2, ROWS, frames * length), jnp.bfloat16),
            pltpu.VMEM((RADIX, spectra, 2, ROWS, LANES), jnp.float32),
            pltpu.VMEM((ROWS * RADIX * spectra, LANES), jnp.float32),
            pltpu.VMEM((ROWS * RADIX * spectra, LANES), jnp.float32),
            pltpu.VMEM((out_rows, LANES), jnp.float32),
            pltpu.SemaphoreType.DMA((sources,)),
        ],
        compiler_params=pltpu.CompilerParams(vmem_limit_bytes=40 * 2**20),
        cost_estimate=pl.CostEstimate(
            flops=9 * 10**9, bytes_accessed=4 * 2**20, transcendentals=0
        ),
        name="channelise",
    )(place, voltages, *come, taps_filter, jnp.asarray(twiddle), jnp.asarray(matrix))
    return [piece.reshape(count, 2, ROWS, LANES) for piece, count in zip(flat, counts)]


def correlate_kernel(starts, width, place_ref, left_sel_ref, right_sel_ref, weight_ref, *refs):
    x_refs, (out_ref, x_all, *rows_refs, sems) = refs[: 2 * len(starts)], refs[-7:]
    tiles = out_ref.shape[0]
    step = pl.program_id(0)
    bands = x_all.shape[2]
    spans = [(0, 2), (2, bands)]

    def copies(span):
        first, last = spans[span]
        block = 0
        for index, start in enumerate(starts):
            blocks = x_refs[2 * index].shape[0]
            for side in range(2):
                yield pltpu.make_async_copy(
                    x_refs[2 * index + side].at[:, pl.ds(start + first, last - first)],
                    x_all.at[
                        lax.rem(place_ref[2] + side, 2),
                        pl.ds(block, blocks),
                        pl.ds(first, last - first),
                    ],
                    sems.at[span, 2 * index + side],
                )
            block += blocks

    lower = lax.broadcasted_iota(jnp.int32, (1, 2 * width), 1) < width

    def gather(band, left_ref, right_ref):
        right = []
        for pol in range(2):
            lanes = slice(pol * 2 * LANES, (pol + 1) * 2 * LANES)
            value = jnp.concatenate(
                [
                    jnp.concatenate([x_all[pol, block, band, part] for part in range(2)], axis=1)
                    for block in range(x_all.shape[1])
                ]
            )
            left = jnp.dot(left_sel_ref[...], value, preferred_element_type=jnp.float32)
            for tile in range(tiles):
                rows = slice(tile * width, (tile + 1) * width)
                scaled = left[rows] * weight_ref[pl.ds(tile, 1), :]
                left_ref[rows, lanes] = scaled.astype(jnp.bfloat16)
            right.append(
                lax.dot_general(
                    value,
                    right_sel_ref[pol],
                    (((0,), (0,)), ((), ())),
                    preferred_element_type=jnp.float32,
                )
            )
        for pair in range(tiles // 2):
            first, second = (v[:, pair * 2 * width : (pair + 1) * 2 * width] for v in right)
            even = jnp.where(lower, first, second)
            odd = pltpu.roll(jnp.where(lower, second, first), width, 1)
            right_ref[2 * pair] = even.astype(jnp.bfloat16)
            right_ref[2 * pair + 1] = odd.astype(jnp.bfloat16)

    def multiply(number, left_ref, right_ref):
        for tile in range(tiles):
            rows = slice(tile * width, (tile + 1) * width)
            left = jnp.concatenate(
                [left_ref[rows, lanes : lanes + 2 * LANES] for lanes in (0, 2 * LANES)]
            )
            right = right_ref[tile]
            turned = jnp.concatenate([-right[LANES:], right[:LANES]])
            both = jnp.concatenate([right, turned], axis=1)
            result = jnp.dot(left, both, preferred_element_type=jnp.float32)
            for part in range(2):
                out_ref[tile, number, part] = result[
                    :, part * 2 * width : (part + 1) * 2 * width
                ].reshape(2, width, 2 * width)

    even, odd = rows_refs[:2], rows_refs[2:]

    @pl.when(step == 0)
    def _():
        for span in range(2):
            for copy in copies(span):
                copy.start()
        for copy in copies(0):
            copy.wait()
        gather(0, *even)
        for copy in copies(1):
            copy.wait()

    gather(2 * step + 1, *odd)
    multiply(0, *even)
    gather(jnp.minimum(2 * step + 2, bands - 1), *even)
    multiply(1, *odd)


def correlate_tiles(place, tables, pieces, starts, width, first, count, bands, earlier):
    left_select, _, weight = tables
    tiles = weight.shape[0]
    whole = pl.BlockSpec(memory_space=pltpu.VMEM)
    more = [] if earlier is None else [earlier]
    rows = [
        pltpu.VMEM((tiles * width, 4 * LANES), jnp.bfloat16),
        pltpu.VMEM((tiles, 2 * LANES, 2 * width), jnp.bfloat16),
    ]
    return pl.pallas_call(
        lambda *refs: correlate_kernel(starts, width, *refs),
        grid=(count // 2,),
        out_shape=jax.ShapeDtypeStruct((tiles, bands, 2, 2, width, 2 * width), jnp.float32),
        in_specs=[pl.BlockSpec(memory_space=pltpu.SMEM)]
        + [whole] * len(tables)
        + [pl.BlockSpec(memory_space=pl.ANY)] * (len(pieces) + len(more)),
        out_specs=pl.BlockSpec(
            (tiles, 2, 2, 2, width, 2 * width), lambda g: (0, g + first // 2, 0, 0, 0, 0)
        ),
        scratch_shapes=[
            pltpu.VMEM((2, left_select.shape[1] // ROWS, count, 2, ROWS, LANES), jnp.bfloat16),
            *rows,
            *rows,
            pltpu.SemaphoreType.DMA((2, len(pieces))),
        ],
        input_output_aliases={1 + len(tables) + len(pieces): 0} if more else {},
        compiler_params=pltpu.CompilerParams(vmem_limit_bytes=32 * 2**20),
        cost_estimate=pl.CostEstimate(
            flops=13 * 10**9 * count // bands,
            bytes_accessed=42 * 2**20 * count // bands,
            transcendentals=0,
        ),
        name="correlate",
    )(place, *tables, *pieces, *more)


def tile_tables(tile_a, tile_b, tile_owner, tile_flags, row_of):
    tiles = tile_owner.shape[0]
    held = tile_owner == lax.axis_index("pol")
    order = jnp.arange(tiles, dtype=jnp.int32)
    rank = jnp.sum((held[None, :] & (order[None, :] < order[:, None])).astype(jnp.int32), axis=1)
    slots = jnp.arange(CAP, dtype=jnp.int32)
    pick = (held[None, :] & (rank[None, :] == slots[:, None])).astype(jnp.int32)
    sides = jnp.stack([row_of(tile_a), row_of(tile_b)], axis=1) + 1
    rows = jnp.sum(pick[:, :, None, None] * sides[None], axis=1) - 1
    flags = jnp.sum(pick[:, :, None] * tile_flags[None], axis=1).astype(jnp.float32)
    return rows, flags


def on_device_chunks(voltages, taps_filter, tile_a, tile_b, tile_owner, tile_flags):
    length = taps_filter.shape[1]
    stations = voltages.shape[2]
    frames = voltages.shape[3] // length
    chan_count, time_count = lax.axis_size("chan"), lax.axis_size("tm")
    owners = chan_count * time_count
    chunk_count = stations // (time_count * ROWS)
    width = tile_a.shape[1]
    bands = length // AVG // owners
    tables = fourier_tables(length)

    chan, tm = lax.axis_index("chan"), lax.axis_index("tm")
    place = jnp.stack([chan, tm, lax.axis_index("pol")]).astype(jnp.int32)

    def row_of(station):
        column, rest = station // stations, station % stations
        block, inside = rest // (chunk_count * ROWS), rest % (chunk_count * ROWS)
        across = (chan - column) % chan_count
        behind = (tm - block) % time_count
        piece = behind * chan_count + across
        return ((inside // ROWS) * owners + piece) * ROWS + inside % ROWS

    rows, flags = tile_tables(tile_a, tile_b, tile_owner, tile_flags, row_of)
    total_rows = chunk_count * owners * ROWS
    station_rows = jnp.arange(total_rows, dtype=jnp.int32)
    left_rows = rows[:, 0].reshape(-1)
    left_select = (left_rows[:, None] == station_rows).astype(jnp.bfloat16)
    right_rows = rows[:, 1].reshape(CAP // 2, 2, width)
    right_rows = jnp.stack([right_rows, right_rows[:, ::-1]]).reshape(2, 1, -1)
    right_select = (right_rows == station_rows[:, None]).astype(jnp.bfloat16)
    depth = AVG * time_count * frames
    weight = jnp.tile(flags * (1.0 / depth), (1, 2 * AVG))
    tables_of_tiles = [left_select, right_select, weight]

    samples = voltages.reshape(2, stations, frames * length)

    def travel(value, axes, distances):
        sizes = [lax.axis_size(axis) for axis in axes]
        pairs = []
        for index in np.ndindex(*sizes):
            target = [(i + d) % n for i, d, n in zip(index, distances, sizes)]
            pairs.append(tuple(int(np.ravel_multi_index(x, sizes)) for x in (index, target)))
        return lax.ppermute(value, axes, pairs)

    def after(values, earlier):
        return lax.optimization_barrier((list(values), list(earlier)))

    def block_for(values, chunk, distance):
        first = ((tm + distance) % time_count * chunk_count + chunk) * ROWS
        return lax.dynamic_slice(values, (0, first, 0), (2, ROWS, frames * length))

    def filtered(chunk, arrived, plan):
        return channelise(
            place, chunk, samples, arrived, taps_filter, tables, frames, chan_count, plan
        )

    def over(value, across, along):
        return travel(value, ("chan", "tm"), (across, along))

    def columns(near, far):
        return jnp.stack([near, far])

    cut = bands // 2
    rest = bands - cut
    pairs = [(x, z) for z in range(time_count) for x in range(chan_count)]
    early_pairs = [(x, z) for z in (1, 3) for x in range(2)]
    late_pairs = [(0, 2), (1, 2), (1, 0)]

    (one,), (values,) = after([block_for(samples, 0, 1)], [samples])
    two, three = (block_for(values, 0, distance) for distance in (2, 3))
    one, two = over(one, 0, 1), over(two, 0, 2)
    (three,), (one,) = after([three], [one])
    three = over(three, 0, 3)
    blocks = [block_for(values, 1, distance) for distance in (1, 2, 3)]
    blocks[:1], (two,) = after(blocks[:1], [two])
    blocks[2:], (three,) = after(blocks[2:], [three])
    first = [one, two, three]
    one, three = over(blocks[0], 0, 1), over(blocks[2], 0, 3)
    (two,), (one,) = after(blocks[1:2], [one])
    second = [one, over(two, 0, 2), three]

    plan = [[(x, z, 0, bands)] for x, z in pairs]
    early = dict(zip(pairs, filtered(0, first, plan)))
    blocks, held = after([early[p] for p in early_pairs], [second[1], *tables_of_tiles])
    second[1], tables_of_tiles = held[0], held[1:]
    early.update((p, over(block, *p)) for p, block in zip(early_pairs, blocks))
    blocks, held = after([early[p] for p in late_pairs], [early[p] for p in early_pairs[:2]])
    early.update(zip(early_pairs[:2], held))
    early.update((p, over(block, *p)) for p, block in zip(late_pairs, blocks))

    spans = [(0, cut), (cut, bands)]
    hops = [1, 2, 3]
    plan = [[(0, z, *span) for span in spans for z in range(time_count)]]
    plan += [[(1, z, *span) for span in spans for z in hops], [(1, 0, *span) for span in spans]]
    near, far, home = filtered(1, second, plan)
    (far,), held = after([far], [early[p] for p in early_pairs[:4]])
    early.update(zip(early_pairs[:4], held))
    far = over(far, 1, 0)
    (home,), (far,) = after([home], [far])
    home = over(home, 1, 0)
    near = near.reshape(2, time_count, cut, 2, ROWS, LANES)
    far = far.reshape(2, len(hops), cut, 2, ROWS, LANES)
    home = home.reshape(2, 1, cut, 2, ROWS, LANES)
    low, high = (
        [columns(near[part, z], far[part, z - 1] if z else home[part, 0]) for z in range(4)]
        for part in range(2)
    )
    blocks, held = after(low[1:], [early[p] for p in late_pairs[:1]])
    early.update(zip(late_pairs[:1], held))
    moved = {z: over(blocks[z - 1], 0, z) for z in (2, 1, 3)}
    low = [low[0]] + [moved[z] for z in (1, 2, 3)]

    def with_other(values):
        return [side for v in values for side in (v, travel(v, ("pol",), (1,)))]

    early = with_other([jnp.stack([early[p] for p in pairs])])
    blocks, held = after(high[1:], [low[2], low[1], early[1]])
    low[2], low[1], early[1] = held
    moved = {z: over(blocks[z - 1], 0, z) for z in (2, 1, 3)}
    high = [high[0]] + [moved[z] for z in (1, 2, 3)]
    low = jnp.stack(low).reshape(2 * time_count, cut, 2, ROWS, LANES)
    visibility = correlate_tiles(
        place, tables_of_tiles, early + with_other([low]),
        [0, 0], width, 0, cut, bands, None,
    )
    home = with_other(high[:1])
    high, (visibility,) = after(high[1:], [visibility])
    return correlate_tiles(
        place, tables_of_tiles, early + home + with_other(high),
        [cut] + [0] * 4, width, cut, rest, bands, visibility,
    )


def on_device(voltages, taps_filter, tile_a, tile_b, tile_owner, tile_flags):
    taps, length = taps_filter.shape
    frames = voltages.shape[3] // length
    time_count = lax.axis_size("tm")
    fits = (
        length == RADIX * LANES
        and AVG * time_count * frames == LANES
        and 2 * tile_a.shape[1] == LANES
        and voltages.shape[2] == 2 * time_count * ROWS
        and (lax.axis_size("chan"), time_count) == (2, 4)
    )
    form = on_device_chunks if fits else on_device_any
    return form(voltages, taps_filter, tile_a, tile_b, tile_owner, tile_flags)


def solution(mesh):
    return jax.shard_map(
        on_device,
        mesh=mesh,
        in_specs=(P("grp", "pol", "chan", "tm"), P(), P(), P(), P(), P()),
        out_specs=P("pol", ("chan", "tm"), "grp", None, None, None),
        check_vma=False,
    )
```

```python
import math

import jax
import jax.numpy as jnp
import numpy as np
from jax import lax
from jax.experimental import pallas as pl
from jax.experimental.pallas import tpu as pltpu
from jax.sharding import PartitionSpec as P

AVG = 8
CAP = 8
RADIX = 16
LANES = 128
ROWS = 16


radix_first = 32


def from_behind(value, axis, steps):
    count = lax.axis_size(axis)
    first, last = (max(0, -steps), min(count, count - steps))
    return lax.ppermute(value, axis, [(source, source + steps) for source in range(first, last)])


def fourier(filtered):
    length = filtered.shape[-1]
    second = length // radix_first
    exact_mode = lax.Precision.HIGHEST
    grid = filtered.reshape(filtered.shape[:-1] + (radix_first, second))
    outer = jnp.arange(radix_first, dtype=jnp.int32)
    inner = jnp.arange(second, dtype=jnp.int32)
    phase_one = (
        2.0
        * math.pi
        / radix_first
        * (outer[:, None] * outer[None, :] % radix_first).astype(jnp.float32)
    )
    phase_twist = 2.0 * math.pi / length * (outer[:, None] * inner[None, :]).astype(jnp.float32)
    phase_two = (
        2.0 * math.pi / second * (inner[:, None] * inner[None, :] % second).astype(jnp.float32)
    )
    cos_one, sin_one = (jnp.cos(phase_one), jnp.sin(phase_one))
    cos_twist, sin_twist = (jnp.cos(phase_twist), jnp.sin(phase_twist))
    cos_two, sin_two = (jnp.cos(phase_two), jnp.sin(phase_two))
    first_form = "fk,stkj->stfj"
    section_re = jnp.einsum(first_form, cos_one, grid[0], precision=exact_mode) + jnp.einsum(
        first_form, sin_one, grid[1], precision=exact_mode
    )
    section_im = jnp.einsum(first_form, cos_one, grid[1], precision=exact_mode) - jnp.einsum(
        first_form, sin_one, grid[0], precision=exact_mode
    )
    turned_re = section_re * cos_twist + section_im * sin_twist
    turned_im = section_im * cos_twist - section_re * sin_twist
    second_form = "gj,stfj->stgf"
    final_re = jnp.einsum(second_form, cos_two, turned_re, precision=exact_mode) + jnp.einsum(
        second_form, sin_two, turned_im, precision=exact_mode
    )
    final_im = jnp.einsum(second_form, cos_two, turned_im, precision=exact_mode) - jnp.einsum(
        second_form, sin_two, turned_re, precision=exact_mode
    )
    joined = jnp.stack([final_re, final_im]).reshape(filtered.shape)
    return joined * (1.0 / math.sqrt(length))


def correlate(full, rows_a, rows_b, flags, group_count):
    depth = full.shape[4]
    weight = jnp.tile(flags.astype(jnp.bfloat16), depth // flags.shape[0])
    left_rows = jnp.take(full, rows_a, axis=2) * weight
    right_rows = jnp.take(full, rows_b, axis=2)
    stacked_left = jnp.stack(
        [
            jnp.concatenate([left_rows[0], left_rows[1]], axis=-1),
            jnp.concatenate([left_rows[1], -left_rows[0]], axis=-1),
        ]
    )
    joined_right = jnp.concatenate([right_rows[0], right_rows[1]], axis=-1)
    result = jnp.einsum(
        "rpank,qbnk->nrpaqb", stacked_left, joined_right, preferred_element_type=jnp.float32
    )
    width = rows_a.shape[0]
    return result.reshape(group_count, 2, 2, width, 2 * width) * (1.0 / depth)


def on_device_any(voltages, taps_filter, tile_a, tile_b, tile_owner, tile_flags):
    history = taps_filter.shape[0] - 1
    length = taps_filter.shape[1]
    stations = voltages.shape[2]
    frames = voltages.shape[3] // length
    local_blocks = voltages.reshape(2, stations, frames, length)
    hop_count = -(-history // frames)
    sending = local_blocks
    extended = local_blocks
    for hop_index in range(hop_count):
        sending = from_behind(sending, "tm", 1)
        extended = jnp.concatenate([sending, extended], axis=2)
    extended = extended[:, :, extended.shape[2] - history - frames :]
    filtered = jnp.zeros((2, stations, frames, length), jnp.float32)
    for tap_index in range(history + 1):
        start = history - tap_index
        filtered = filtered + taps_filter[tap_index] * extended[
            :, :, start : start + frames
        ].astype(jnp.float32)
    spectra = fourier(filtered).astype(jnp.bfloat16)
    chan_count = lax.axis_size("chan")
    time_count = lax.axis_size("tm")
    narrow = length // (chan_count * time_count)
    outgoing = spectra.reshape(2, stations, frames, chan_count, time_count, narrow)
    outgoing = outgoing.transpose(0, 3, 4, 5, 1, 2)
    flat = outgoing.reshape(2, chan_count * time_count, narrow, stations * frames)
    moved = lax.all_to_all(flat, ("chan", "tm"), split_axis=1, concat_axis=1, tiled=True)
    moved = moved.reshape(2, chan_count, time_count, narrow, stations, frames)
    bands = narrow // AVG
    every_station = chan_count * stations
    spectra_count = time_count * frames
    arranged = moved.transpose(0, 1, 4, 3, 2, 5).reshape(
        2, 1, every_station, bands, AVG * spectra_count
    )
    full = lax.all_gather(arranged, "pol", axis=1, tiled=True)
    position = lax.axis_index("pol")
    width = tile_a.shape[1]
    capacity = CAP
    held = tile_owner == position
    listed = jnp.nonzero(held, size=capacity, fill_value=0)[0].astype(jnp.int32)
    tally = jnp.sum(held.astype(jnp.int32))
    initial = jnp.zeros((capacity, bands, 2, 2, width, 2 * width), jnp.float32)

    def fill_slot(slot, results):
        chosen_tile = listed[slot]
        return results.at[slot].set(
            correlate(
                full, tile_a[chosen_tile], tile_b[chosen_tile], tile_flags[chosen_tile], bands
            )
        )

    visibility = lax.fori_loop(0, tally, fill_slot, initial)
    return visibility


def fourier_tables(length):
    low = np.arange(RADIX)
    lane = np.arange(LANES)
    turn = 2.0 * np.pi / length * np.outer(low, lane)
    twiddle = np.stack([np.cos(turn), np.sin(turn)]).astype(np.float32)
    angle = 2.0 * np.pi / LANES * (np.outer(lane, lane) % LANES)
    cos, sin = np.cos(angle) / math.sqrt(length), np.sin(angle) / math.sqrt(length)
    matrix = np.block([[cos, sin], [-sin, cos]]).astype(np.float32)
    high = matrix.astype(jnp.bfloat16)
    rest = (matrix - high.astype(np.float32)).astype(jnp.bfloat16)
    return twiddle, np.stack([high, rest])


def butterflies(values):
    count = len(values)
    if count == 1:
        return values
    even, odd = butterflies(values[0::2]), butterflies(values[1::2])
    first, second = [], []
    for index in range(count // 2):
        (a, b), (c, d) = even[index], odd[index]
        if index == 0:
            e, f = c, d
        elif 4 * index == count:
            e, f = d, -c
        elif 8 * index == count:
            root = math.sqrt(0.5)
            e, f = (c + d) * root, (d - c) * root
        elif 8 * index == 3 * count:
            root = math.sqrt(0.5)
            e, f = (d - c) * root, -(c + d) * root
        else:
            turn = 2.0 * math.pi * index / count
            cos, sin = math.cos(turn), math.sin(turn)
            e, f = c * cos + d * sin, d * cos - c * sin
        first.append((a + e, b + f))
        second.append((a - e, b - f))
    return first + second


def channelise_kernel(frames, chunk, columns, plan, place_ref, own_ref, *refs):
    sources = refs[-6].shape[0]
    come_refs = refs[: sources - 1]
    taps_ref, twiddle_ref, matrix_ref = refs[sources - 1 : sources + 2]
    out_refs = refs[sources + 2 : -6]
    x_ref, fil_ref, zr_ref, zi_ref, w_ref, sems = refs[-6:]
    chan, tm = place_ref[0], place_ref[1]
    own_rows = pl.multiple_of((tm * (own_ref.shape[1] // (sources * ROWS)) + chunk) * ROWS, ROWS)
    copies = []
    for behind in range(sources):
        block = come_refs[behind - 1] if behind else own_ref.at[:, pl.ds(own_rows, ROWS), :]
        slot = lax.rem(tm - behind + sources, sources)
        copies.append(pltpu.make_async_copy(block, x_ref.at[slot], sems.at[behind]))
    for copy in copies:
        copy.start()
    for copy in copies:
        copy.wait()
    spectra = sources * frames
    length = taps_ref.shape[1]
    taps = taps_ref.shape[0]
    depth = RADIX * spectra
    z_refs = (zr_ref, zi_ref)

    @pl.loop(0, RADIX)
    def _(section):
        at = pl.multiple_of(section * LANES, LANES)
        weights = [taps_ref[pl.ds(m, 1), pl.ds(at, LANES)] for m in range(taps)]
        for part in range(2):
            blocks = []
            for t in range(spectra):
                lane = pl.multiple_of((t % frames) * length + section * LANES, LANES)
                blocks.append(x_ref[t // frames, part, :, pl.ds(lane, LANES)].astype(jnp.float32))
            for t in range(spectra):
                total = weights[0] * blocks[t]
                for m in range(1, min(t + 1, taps)):
                    total = total + weights[m] * blocks[t - m]
                fil_ref[section, t, part] = total

    @pl.loop(0, spectra)
    def _(t):
        for half in range(ROWS // 8):
            values = [
                tuple(fil_ref[section, t, part, pl.ds(half * 8, 8), :] for part in range(2))
                for section in range(RADIX)
            ]
            for low, (re, im) in enumerate(butterflies(values)):
                if low:
                    cos = twiddle_ref[0, pl.ds(low, 1), :]
                    sin = twiddle_ref[1, pl.ds(low, 1), :]
                    re, im = re * cos + im * sin, im * cos - re * sin
                rows = pl.ds(half * 8 * depth + low * spectra + t, 8, stride=depth)
                zr_ref[rows, :] = re
                zi_ref[rows, :] = im

    form = (((1,), (1,)), ((), ()))
    high_matrix, low_matrix = matrix_ref[0], matrix_ref[1]
    halves = depth // LANES

    @pl.loop(0, ROWS)
    def _(station):
        rows = pl.ds(pl.multiple_of(station * depth, depth), depth)
        value = jnp.concatenate([ref[rows, :] for ref in z_refs], axis=1)
        high = value.astype(jnp.bfloat16)
        rest = (value - high.astype(jnp.float32)).astype(jnp.bfloat16)
        total = lax.dot_general(high_matrix, high, form, preferred_element_type=jnp.float32)
        total += lax.dot_general(high_matrix, rest, form, preferred_element_type=jnp.float32)
        total += lax.dot_general(low_matrix, high, form, preferred_element_type=jnp.float32)
        for half in range(halves):
            for part in range(2):
                rows = pl.ds((half * 2 + part) * ROWS + station, LANES, stride=halves * 2 * ROWS)
                w_ref[rows, :] = total[
                    part * LANES : (part + 1) * LANES, half * LANES : (half + 1) * LANES
                ]

    share = w_ref.shape[0] // (columns * sources)
    band_rows = 2 * ROWS
    piece = 4 * band_rows
    for blocks, out_ref in zip(plan, out_refs):
        at = 0
        for across, along, start, stop in blocks:
            owner = lax.rem(chan + across, columns) * sources + lax.rem(tm + along, sources)
            for row in range(start * band_rows, stop * band_rows, piece):
                rows = pl.ds(pl.multiple_of(owner * share + row, piece), piece)
                out_ref[at : at + piece, :] = w_ref[rows, :].astype(jnp.bfloat16)
                at += piece


def channelise(place, chunk, voltages, come, taps_filter, tables, frames, columns, plan):
    sources = 1 + len(come)
    length = taps_filter.shape[1]
    spectra = sources * frames
    twiddle, matrix = tables
    out_rows = length // AVG * 2 * ROWS
    whole = pl.BlockSpec(memory_space=pltpu.VMEM)
    counts = [sum(stop - start for _, _, start, stop in blocks) for blocks in plan]
    flat = pl.pallas_call(
        lambda *refs: channelise_kernel(frames, chunk, columns, plan, *refs),
        out_shape=[
            jax.ShapeDtypeStruct((count * 2 * ROWS, LANES), jnp.bfloat16) for count in counts
        ],
        in_specs=[pl.BlockSpec(memory_space=pltpu.SMEM)]
        + [pl.BlockSpec(memory_space=pl.ANY)] * sources
        + [whole] * 3,
        out_specs=[whole] * len(plan),
        scratch_shapes=[
            pltpu.VMEM((sources, 2, ROWS, frames * length), jnp.bfloat16),
            pltpu.VMEM((RADIX, spectra, 2, ROWS, LANES), jnp.float32),
            pltpu.VMEM((ROWS * RADIX * spectra, LANES), jnp.float32),
            pltpu.VMEM((ROWS * RADIX * spectra, LANES), jnp.float32),
            pltpu.VMEM((out_rows, LANES), jnp.float32),
            pltpu.SemaphoreType.DMA((sources,)),
        ],
        compiler_params=pltpu.CompilerParams(vmem_limit_bytes=40 * 2**20),
        cost_estimate=pl.CostEstimate(
            flops=9 * 10**9, bytes_accessed=4 * 2**20, transcendentals=0
        ),
        name="channelise",
    )(place, voltages, *come, taps_filter, jnp.asarray(twiddle), jnp.asarray(matrix))
    return [piece.reshape(count, 2, ROWS, LANES) for piece, count in zip(flat, counts)]


def correlate_kernel(starts, width, place_ref, left_sel_ref, right_sel_ref, weight_ref, *refs):
    x_refs, (out_ref, x_all, *rows_refs, sems) = refs[: 2 * len(starts)], refs[-7:]
    tiles = out_ref.shape[0]
    step = pl.program_id(0)
    bands = x_all.shape[2]
    spans = [(0, 2), (2, bands)]

    def copies(span):
        first, last = spans[span]
        block = 0
        for index, start in enumerate(starts):
            blocks = x_refs[2 * index].shape[0]
            for side in range(2):
                yield pltpu.make_async_copy(
                    x_refs[2 * index + side].at[:, pl.ds(start + first, last - first)],
                    x_all.at[
                        lax.rem(place_ref[2] + side, 2),
                        pl.ds(block, blocks),
                        pl.ds(first, last - first),
                    ],
                    sems.at[span, 2 * index + side],
                )
            block += blocks

    lower = lax.broadcasted_iota(jnp.int32, (1, 2 * width), 1) < width

    def gather(band, left_ref, right_ref):
        right = []
        for pol in range(2):
            lanes = slice(pol * 2 * LANES, (pol + 1) * 2 * LANES)
            value = jnp.concatenate(
                [
                    jnp.concatenate([x_all[pol, block, band, part] for part in range(2)], axis=1)
                    for block in range(x_all.shape[1])
                ]
            )
            left = jnp.dot(left_sel_ref[...], value, preferred_element_type=jnp.float32)
            for tile in range(tiles):
                rows = slice(tile * width, (tile + 1) * width)
                scaled = left[rows] * weight_ref[pl.ds(tile, 1), :]
                left_ref[rows, lanes] = scaled.astype(jnp.bfloat16)
            right.append(
                lax.dot_general(
                    value,
                    right_sel_ref[pol],
                    (((0,), (0,)), ((), ())),
                    preferred_element_type=jnp.float32,
                )
            )
        for pair in range(tiles // 2):
            first, second = (v[:, pair * 2 * width : (pair + 1) * 2 * width] for v in right)
            even = jnp.where(lower, first, second)
            odd = pltpu.roll(jnp.where(lower, second, first), width, 1)
            right_ref[2 * pair] = even.astype(jnp.bfloat16)
            right_ref[2 * pair + 1] = odd.astype(jnp.bfloat16)

    def multiply(number, left_ref, right_ref):
        for tile in range(tiles):
            rows = slice(tile * width, (tile + 1) * width)
            left = jnp.concatenate(
                [left_ref[rows, lanes : lanes + 2 * LANES] for lanes in (0, 2 * LANES)]
            )
            right = right_ref[tile]
            turned = jnp.concatenate([-right[LANES:], right[:LANES]])
            both = jnp.concatenate([right, turned], axis=1)
            result = jnp.dot(left, both, preferred_element_type=jnp.float32)
            for part in range(2):
                out_ref[tile, number, part] = result[
                    :, part * 2 * width : (part + 1) * 2 * width
                ].reshape(2, width, 2 * width)

    even, odd = rows_refs[:2], rows_refs[2:]

    @pl.when(step == 0)
    def _():
        for span in range(2):
            for copy in copies(span):
                copy.start()
        for copy in copies(0):
            copy.wait()
        gather(0, *even)
        for copy in copies(1):
            copy.wait()

    gather(2 * step + 1, *odd)
    multiply(0, *even)
    gather(jnp.minimum(2 * step + 2, bands - 1), *even)
    multiply(1, *odd)


def correlate_tiles(place, tables, pieces, starts, width, first, count, bands, earlier):
    left_select, _, weight = tables
    tiles = weight.shape[0]
    whole = pl.BlockSpec(memory_space=pltpu.VMEM)
    more = [] if earlier is None else [earlier]
    rows = [
        pltpu.VMEM((tiles * width, 4 * LANES), jnp.bfloat16),
        pltpu.VMEM((tiles, 2 * LANES, 2 * width), jnp.bfloat16),
    ]
    return pl.pallas_call(
        lambda *refs: correlate_kernel(starts, width, *refs),
        grid=(count // 2,),
        out_shape=jax.ShapeDtypeStruct((tiles, bands, 2, 2, width, 2 * width), jnp.float32),
        in_specs=[pl.BlockSpec(memory_space=pltpu.SMEM)]
        + [whole] * len(tables)
        + [pl.BlockSpec(memory_space=pl.ANY)] * (len(pieces) + len(more)),
        out_specs=pl.BlockSpec(
            (tiles, 2, 2, 2, width, 2 * width), lambda g: (0, g + first // 2, 0, 0, 0, 0)
        ),
        scratch_shapes=[
            pltpu.VMEM((2, left_select.shape[1] // ROWS, count, 2, ROWS, LANES), jnp.bfloat16),
            *rows,
            *rows,
            pltpu.SemaphoreType.DMA((2, len(pieces))),
        ],
        input_output_aliases={1 + len(tables) + len(pieces): 0} if more else {},
        compiler_params=pltpu.CompilerParams(vmem_limit_bytes=32 * 2**20),
        cost_estimate=pl.CostEstimate(
            flops=13 * 10**9 * count // bands,
            bytes_accessed=42 * 2**20 * count // bands,
            transcendentals=0,
        ),
        name="correlate",
    )(place, *tables, *pieces, *more)


def tile_tables(tile_a, tile_b, tile_owner, tile_flags, row_of):
    tiles = tile_owner.shape[0]
    held = tile_owner == lax.axis_index("pol")
    order = jnp.arange(tiles, dtype=jnp.int32)
    rank = jnp.sum((held[None, :] & (order[None, :] < order[:, None])).astype(jnp.int32), axis=1)
    slots = jnp.arange(CAP, dtype=jnp.int32)
    pick = (held[None, :] & (rank[None, :] == slots[:, None])).astype(jnp.int32)
    sides = jnp.stack([row_of(tile_a), row_of(tile_b)], axis=1) + 1
    rows = jnp.sum(pick[:, :, None, None] * sides[None], axis=1) - 1
    flags = jnp.sum(pick[:, :, None] * tile_flags[None], axis=1).astype(jnp.float32)
    return rows, flags


def on_device_chunks(voltages, taps_filter, tile_a, tile_b, tile_owner, tile_flags):
    length = taps_filter.shape[1]
    stations = voltages.shape[2]
    frames = voltages.shape[3] // length
    chan_count, time_count = lax.axis_size("chan"), lax.axis_size("tm")
    owners = chan_count * time_count
    chunk_count = stations // (time_count * ROWS)
    width = tile_a.shape[1]
    bands = length // AVG // owners
    tables = fourier_tables(length)

    chan, tm = lax.axis_index("chan"), lax.axis_index("tm")
    place = jnp.stack([chan, tm, lax.axis_index("pol")]).astype(jnp.int32)

    def row_of(station):
        column, rest = station // stations, station % stations
        block, inside = rest // (chunk_count * ROWS), rest % (chunk_count * ROWS)
        across = (chan - column) % chan_count
        behind = (tm - block) % time_count
        piece = behind * chan_count + across
        return ((inside // ROWS) * owners + piece) * ROWS + inside % ROWS

    rows, flags = tile_tables(tile_a, tile_b, tile_owner, tile_flags, row_of)
    total_rows = chunk_count * owners * ROWS
    station_rows = jnp.arange(total_rows, dtype=jnp.int32)
    left_rows = rows[:, 0].reshape(-1)
    left_select = (left_rows[:, None] == station_rows).astype(jnp.bfloat16)
    right_rows = rows[:, 1].reshape(CAP // 2, 2, width)
    right_rows = jnp.stack([right_rows, right_rows[:, ::-1]]).reshape(2, 1, -1)
    right_select = (right_rows == station_rows[:, None]).astype(jnp.bfloat16)
    depth = AVG * time_count * frames
    weight = jnp.tile(flags * (1.0 / depth), (1, 2 * AVG))
    tables_of_tiles = [left_select, right_select, weight]

    samples = voltages.reshape(2, stations, frames * length)

    def travel(value, axes, distances):
        sizes = [lax.axis_size(axis) for axis in axes]
        pairs = []
        for index in np.ndindex(*sizes):
            target = [(i + d) % n for i, d, n in zip(index, distances, sizes)]
            pairs.append(tuple(int(np.ravel_multi_index(x, sizes)) for x in (index, target)))
        return lax.ppermute(value, axes, pairs)

    def after(values, earlier):
        return lax.optimization_barrier((list(values), list(earlier)))

    def block_for(values, chunk, distance):
        first = ((tm + distance) % time_count * chunk_count + chunk) * ROWS
        return lax.dynamic_slice(values, (0, first, 0), (2, ROWS, frames * length))

    def filtered(chunk, arrived, plan):
        return channelise(
            place, chunk, samples, arrived, taps_filter, tables, frames, chan_count, plan
        )

    def over(value, across, along):
        return travel(value, ("chan", "tm"), (across, along))

    def columns(near, far):
        return jnp.stack([near, far])

    cut = bands // 2
    rest = bands - cut
    pairs = [(x, z) for z in range(time_count) for x in range(chan_count)]
    early_pairs = [(x, z) for z in (1, 3) for x in range(2)]
    late_pairs = [(0, 2), (1, 2), (1, 0)]

    (one,), (values,) = after([block_for(samples, 0, 1)], [samples])
    two, three = (block_for(values, 0, distance) for distance in (2, 3))
    one, two = over(one, 0, 1), over(two, 0, 2)
    (three,), (one,) = after([three], [one])
    three = over(three, 0, 3)
    blocks = [block_for(values, 1, distance) for distance in (1, 2, 3)]
    blocks[:1], (two,) = after(blocks[:1], [two])
    blocks[2:], (three,) = after(blocks[2:], [three])
    first = [one, two, three]
    one, three = over(blocks[0], 0, 1), over(blocks[2], 0, 3)
    (two,), (one,) = after(blocks[1:2], [one])
    second = [one, over(two, 0, 2), three]

    plan = [[(x, z, 0, bands)] for x, z in pairs]
    early = dict(zip(pairs, filtered(0, first, plan)))
    blocks, held = after([early[p] for p in early_pairs], [second[1], *tables_of_tiles])
    second[1], tables_of_tiles = held[0], held[1:]
    early.update((p, over(block, *p)) for p, block in zip(early_pairs, blocks))
    spans = [(0, cut), (cut, bands)]
    hops = [1, 2, 3]
    plan = [[(0, z, *span) for span in spans for z in range(time_count)]]
    plan += [[(1, z, *span) for span in spans for z in hops], [(1, 0, *span) for span in spans]]
    near, far, home = filtered(1, second, plan)
    blocks, (near,) = after([early[p] for p in late_pairs], [near])
    early.update((p, over(block, *p)) for p, block in zip(late_pairs, blocks))
    (far,), held = after([far], [early[p] for p in early_pairs[:4]])
    early.update(zip(early_pairs[:4], held))
    far = over(far, 1, 0)
    (home,), (far,) = after([home], [far])
    home = over(home, 1, 0)
    near = near.reshape(2, time_count, cut, 2, ROWS, LANES)
    far = far.reshape(2, len(hops), cut, 2, ROWS, LANES)
    home = home.reshape(2, 1, cut, 2, ROWS, LANES)
    low, high = (
        [columns(near[part, z], far[part, z - 1] if z else home[part, 0]) for z in range(4)]
        for part in range(2)
    )
    blocks, held = after(low[1:], [early[p] for p in late_pairs[:1]])
    early.update(zip(late_pairs[:1], held))
    moved = {z: over(blocks[z - 1], 0, z) for z in (2, 1, 3)}
    low = [low[0]] + [moved[z] for z in (1, 2, 3)]

    def with_other(values):
        return [side for v in values for side in (v, travel(v, ("pol",), (1,)))]

    early = with_other([jnp.stack([early[p] for p in pairs])])
    blocks, held = after(high[1:], [low[2], low[1], early[1]])
    low[2], low[1], early[1] = held
    moved = {z: over(blocks[z - 1], 0, z) for z in (2, 1, 3)}
    high = [high[0]] + [moved[z] for z in (1, 2, 3)]
    low = jnp.stack(low).reshape(2 * time_count, cut, 2, ROWS, LANES)
    visibility = correlate_tiles(
        place, tables_of_tiles, early + with_other([low]),
        [0, 0], width, 0, cut, bands, None,
    )
    home = with_other(high[:1])
    high, (visibility,) = after(high[1:], [visibility])
    return correlate_tiles(
        place, tables_of_tiles, early + home + with_other(high),
        [cut] + [0] * 4, width, cut, rest, bands, visibility,
    )


def on_device(voltages, taps_filter, tile_a, tile_b, tile_owner, tile_flags):
    taps, length = taps_filter.shape
    frames = voltages.shape[3] // length
    time_count = lax.axis_size("tm")
    fits = (
        length == RADIX * LANES
        and AVG * time_count * frames == LANES
        and 2 * tile_a.shape[1] == LANES
        and voltages.shape[2] == 2 * time_count * ROWS
        and (lax.axis_size("chan"), time_count) == (2, 4)
    )
    form = on_device_chunks if fits else on_device_any
    return form(voltages, taps_filter, tile_a, tile_b, tile_owner, tile_flags)


def solution(mesh):
    return jax.shard_map(
        on_device,
        mesh=mesh,
        in_specs=(P("grp", "pol", "chan", "tm"), P(), P(), P(), P(), P()),
        out_specs=P("pol", ("chan", "tm"), "grp", None, None, None),
        check_vma=False,
    )
```

```python
import math

import jax
import jax.numpy as jnp
import numpy as np
from jax import lax
from jax.experimental import pallas as pl
from jax.experimental.pallas import tpu as pltpu
from jax.sharding import PartitionSpec as P

AVG = 8
CAP = 8
RADIX = 16
LANES = 128
ROWS = 16


radix_first = 32


def from_behind(value, axis, steps):
    count = lax.axis_size(axis)
    first, last = (max(0, -steps), min(count, count - steps))
    return lax.ppermute(value, axis, [(source, source + steps) for source in range(first, last)])


def fourier(filtered):
    length = filtered.shape[-1]
    second = length // radix_first
    exact_mode = lax.Precision.HIGHEST
    grid = filtered.reshape(filtered.shape[:-1] + (radix_first, second))
    outer = jnp.arange(radix_first, dtype=jnp.int32)
    inner = jnp.arange(second, dtype=jnp.int32)
    phase_one = (
        2.0
        * math.pi
        / radix_first
        * (outer[:, None] * outer[None, :] % radix_first).astype(jnp.float32)
    )
    phase_twist = 2.0 * math.pi / length * (outer[:, None] * inner[None, :]).astype(jnp.float32)
    phase_two = (
        2.0 * math.pi / second * (inner[:, None] * inner[None, :] % second).astype(jnp.float32)
    )
    cos_one, sin_one = (jnp.cos(phase_one), jnp.sin(phase_one))
    cos_twist, sin_twist = (jnp.cos(phase_twist), jnp.sin(phase_twist))
    cos_two, sin_two = (jnp.cos(phase_two), jnp.sin(phase_two))
    first_form = "fk,stkj->stfj"
    section_re = jnp.einsum(first_form, cos_one, grid[0], precision=exact_mode) + jnp.einsum(
        first_form, sin_one, grid[1], precision=exact_mode
    )
    section_im = jnp.einsum(first_form, cos_one, grid[1], precision=exact_mode) - jnp.einsum(
        first_form, sin_one, grid[0], precision=exact_mode
    )
    turned_re = section_re * cos_twist + section_im * sin_twist
    turned_im = section_im * cos_twist - section_re * sin_twist
    second_form = "gj,stfj->stgf"
    final_re = jnp.einsum(second_form, cos_two, turned_re, precision=exact_mode) + jnp.einsum(
        second_form, sin_two, turned_im, precision=exact_mode
    )
    final_im = jnp.einsum(second_form, cos_two, turned_im, precision=exact_mode) - jnp.einsum(
        second_form, sin_two, turned_re, precision=exact_mode
    )
    joined = jnp.stack([final_re, final_im]).reshape(filtered.shape)
    return joined * (1.0 / math.sqrt(length))


def correlate(full, rows_a, rows_b, flags, group_count):
    depth = full.shape[4]
    weight = jnp.tile(flags.astype(jnp.bfloat16), depth // flags.shape[0])
    left_rows = jnp.take(full, rows_a, axis=2) * weight
    right_rows = jnp.take(full, rows_b, axis=2)
    stacked_left = jnp.stack(
        [
            jnp.concatenate([left_rows[0], left_rows[1]], axis=-1),
            jnp.concatenate([left_rows[1], -left_rows[0]], axis=-1),
        ]
    )
    joined_right = jnp.concatenate([right_rows[0], right_rows[1]], axis=-1)
    result = jnp.einsum(
        "rpank,qbnk->nrpaqb", stacked_left, joined_right, preferred_element_type=jnp.float32
    )
    width = rows_a.shape[0]
    return result.reshape(group_count, 2, 2, width, 2 * width) * (1.0 / depth)


def on_device_any(voltages, taps_filter, tile_a, tile_b, tile_owner, tile_flags):
    history = taps_filter.shape[0] - 1
    length = taps_filter.shape[1]
    stations = voltages.shape[2]
    frames = voltages.shape[3] // length
    local_blocks = voltages.reshape(2, stations, frames, length)
    hop_count = -(-history // frames)
    sending = local_blocks
    extended = local_blocks
    for hop_index in range(hop_count):
        sending = from_behind(sending, "tm", 1)
        extended = jnp.concatenate([sending, extended], axis=2)
    extended = extended[:, :, extended.shape[2] - history - frames :]
    filtered = jnp.zeros((2, stations, frames, length), jnp.float32)
    for tap_index in range(history + 1):
        start = history - tap_index
        filtered = filtered + taps_filter[tap_index] * extended[
            :, :, start : start + frames
        ].astype(jnp.float32)
    spectra = fourier(filtered).astype(jnp.bfloat16)
    chan_count = lax.axis_size("chan")
    time_count = lax.axis_size("tm")
    narrow = length // (chan_count * time_count)
    outgoing = spectra.reshape(2, stations, frames, chan_count, time_count, narrow)
    outgoing = outgoing.transpose(0, 3, 4, 5, 1, 2)
    flat = outgoing.reshape(2, chan_count * time_count, narrow, stations * frames)
    moved = lax.all_to_all(flat, ("chan", "tm"), split_axis=1, concat_axis=1, tiled=True)
    moved = moved.reshape(2, chan_count, time_count, narrow, stations, frames)
    bands = narrow // AVG
    every_station = chan_count * stations
    spectra_count = time_count * frames
    arranged = moved.transpose(0, 1, 4, 3, 2, 5).reshape(
        2, 1, every_station, bands, AVG * spectra_count
    )
    full = lax.all_gather(arranged, "pol", axis=1, tiled=True)
    position = lax.axis_index("pol")
    width = tile_a.shape[1]
    capacity = CAP
    held = tile_owner == position
    listed = jnp.nonzero(held, size=capacity, fill_value=0)[0].astype(jnp.int32)
    tally = jnp.sum(held.astype(jnp.int32))
    initial = jnp.zeros((capacity, bands, 2, 2, width, 2 * width), jnp.float32)

    def fill_slot(slot, results):
        chosen_tile = listed[slot]
        return results.at[slot].set(
            correlate(
                full, tile_a[chosen_tile], tile_b[chosen_tile], tile_flags[chosen_tile], bands
            )
        )

    visibility = lax.fori_loop(0, tally, fill_slot, initial)
    return visibility


def fourier_tables(length):
    low = np.arange(RADIX)
    lane = np.arange(LANES)
    turn = 2.0 * np.pi / length * np.outer(low, lane)
    twiddle = np.stack([np.cos(turn), np.sin(turn)]).astype(np.float32)
    angle = 2.0 * np.pi / LANES * (np.outer(lane, lane) % LANES)
    cos, sin = np.cos(angle) / math.sqrt(length), np.sin(angle) / math.sqrt(length)
    matrix = np.block([[cos, sin], [-sin, cos]]).astype(np.float32)
    high = matrix.astype(jnp.bfloat16)
    rest = (matrix - high.astype(np.float32)).astype(jnp.bfloat16)
    return twiddle, np.stack([high, rest])


def butterflies(values):
    count = len(values)
    if count == 1:
        return values
    even, odd = butterflies(values[0::2]), butterflies(values[1::2])
    first, second = [], []
    for index in range(count // 2):
        (a, b), (c, d) = even[index], odd[index]
        if index == 0:
            e, f = c, d
        elif 4 * index == count:
            e, f = d, -c
        elif 8 * index == count:
            root = math.sqrt(0.5)
            e, f = (c + d) * root, (d - c) * root
        elif 8 * index == 3 * count:
            root = math.sqrt(0.5)
            e, f = (d - c) * root, -(c + d) * root
        else:
            turn = 2.0 * math.pi * index / count
            cos, sin = math.cos(turn), math.sin(turn)
            e, f = c * cos + d * sin, d * cos - c * sin
        first.append((a + e, b + f))
        second.append((a - e, b - f))
    return first + second


def channelise_kernel(frames, chunk, columns, plan, place_ref, own_ref, *refs):
    sources = refs[-6].shape[0]
    come_refs = refs[: sources - 1]
    taps_ref, twiddle_ref, matrix_ref = refs[sources - 1 : sources + 2]
    out_refs = refs[sources + 2 : -6]
    x_ref, fil_ref, zr_ref, zi_ref, w_ref, sems = refs[-6:]
    chan, tm = place_ref[0], place_ref[1]
    own_rows = pl.multiple_of((tm * (own_ref.shape[1] // (sources * ROWS)) + chunk) * ROWS, ROWS)
    copies = []
    for behind in range(sources):
        block = come_refs[behind - 1] if behind else own_ref.at[:, pl.ds(own_rows, ROWS), :]
        slot = lax.rem(tm - behind + sources, sources)
        copies.append(pltpu.make_async_copy(block, x_ref.at[slot], sems.at[behind]))
    for copy in copies:
        copy.start()
    for copy in copies:
        copy.wait()
    spectra = sources * frames
    length = taps_ref.shape[1]
    taps = taps_ref.shape[0]
    depth = RADIX * spectra
    z_refs = (zr_ref, zi_ref)

    @pl.loop(0, RADIX)
    def _(section):
        at = pl.multiple_of(section * LANES, LANES)
        weights = [taps_ref[pl.ds(m, 1), pl.ds(at, LANES)] for m in range(taps)]
        for part in range(2):
            blocks = []
            for t in range(spectra):
                lane = pl.multiple_of((t % frames) * length + section * LANES, LANES)
                blocks.append(x_ref[t // frames, part, :, pl.ds(lane, LANES)].astype(jnp.float32))
            for t in range(spectra):
                total = weights[0] * blocks[t]
                for m in range(1, min(t + 1, taps)):
                    total = total + weights[m] * blocks[t - m]
                fil_ref[section, t, part] = total

    @pl.loop(0, spectra)
    def _(t):
        for half in range(ROWS // 8):
            values = [
                tuple(fil_ref[section, t, part, pl.ds(half * 8, 8), :] for part in range(2))
                for section in range(RADIX)
            ]
            for low, (re, im) in enumerate(butterflies(values)):
                if low:
                    cos = twiddle_ref[0, pl.ds(low, 1), :]
                    sin = twiddle_ref[1, pl.ds(low, 1), :]
                    re, im = re * cos + im * sin, im * cos - re * sin
                rows = pl.ds(half * 8 * depth + low * spectra + t, 8, stride=depth)
                zr_ref[rows, :] = re
                zi_ref[rows, :] = im

    form = (((1,), (1,)), ((), ()))
    high_matrix, low_matrix = matrix_ref[0], matrix_ref[1]
    halves = depth // LANES

    @pl.loop(0, ROWS)
    def _(station):
        rows = pl.ds(pl.multiple_of(station * depth, depth), depth)
        value = jnp.concatenate([ref[rows, :] for ref in z_refs], axis=1)
        high = value.astype(jnp.bfloat16)
        rest = (value - high.astype(jnp.float32)).astype(jnp.bfloat16)
        total = lax.dot_general(high_matrix, high, form, preferred_element_type=jnp.float32)
        total += lax.dot_general(high_matrix, rest, form, preferred_element_type=jnp.float32)
        total += lax.dot_general(low_matrix, high, form, preferred_element_type=jnp.float32)
        for half in range(halves):
            for part in range(2):
                rows = pl.ds((half * 2 + part) * ROWS + station, LANES, stride=halves * 2 * ROWS)
                w_ref[rows, :] = total[
                    part * LANES : (part + 1) * LANES, half * LANES : (half + 1) * LANES
                ]

    share = w_ref.shape[0] // (columns * sources)
    band_rows = 2 * ROWS
    piece = 4 * band_rows
    for blocks, out_ref in zip(plan, out_refs):
        at = 0
        for across, along, start, stop in blocks:
            owner = lax.rem(chan + across, columns) * sources + lax.rem(tm + along, sources)
            for row in range(start * band_rows, stop * band_rows, piece):
                rows = pl.ds(pl.multiple_of(owner * share + row, piece), piece)
                out_ref[at : at + piece, :] = w_ref[rows, :].astype(jnp.bfloat16)
                at += piece


def channelise(place, chunk, voltages, come, taps_filter, tables, frames, columns, plan):
    sources = 1 + len(come)
    length = taps_filter.shape[1]
    spectra = sources * frames
    twiddle, matrix = tables
    out_rows = length // AVG * 2 * ROWS
    whole = pl.BlockSpec(memory_space=pltpu.VMEM)
    counts = [sum(stop - start for _, _, start, stop in blocks) for blocks in plan]
    flat = pl.pallas_call(
        lambda *refs: channelise_kernel(frames, chunk, columns, plan, *refs),
        out_shape=[
            jax.ShapeDtypeStruct((count * 2 * ROWS, LANES), jnp.bfloat16) for count in counts
        ],
        in_specs=[pl.BlockSpec(memory_space=pltpu.SMEM)]
        + [pl.BlockSpec(memory_space=pl.ANY)] * sources
        + [whole] * 3,
        out_specs=[whole] * len(plan),
        scratch_shapes=[
            pltpu.VMEM((sources, 2, ROWS, frames * length), jnp.bfloat16),
            pltpu.VMEM((RADIX, spectra, 2, ROWS, LANES), jnp.float32),
            pltpu.VMEM((ROWS * RADIX * spectra, LANES), jnp.float32),
            pltpu.VMEM((ROWS * RADIX * spectra, LANES), jnp.float32),
            pltpu.VMEM((out_rows, LANES), jnp.float32),
            pltpu.SemaphoreType.DMA((sources,)),
        ],
        compiler_params=pltpu.CompilerParams(vmem_limit_bytes=40 * 2**20),
        cost_estimate=pl.CostEstimate(
            flops=9 * 10**9, bytes_accessed=4 * 2**20, transcendentals=0
        ),
        name="channelise",
    )(place, voltages, *come, taps_filter, jnp.asarray(twiddle), jnp.asarray(matrix))
    return [piece.reshape(count, 2, ROWS, LANES) for piece, count in zip(flat, counts)]


def correlate_kernel(starts, width, place_ref, left_sel_ref, right_sel_ref, weight_ref, *refs):
    x_refs, (out_ref, x_all, *rows_refs, sems) = refs[: 2 * len(starts)], refs[-7:]
    tiles = out_ref.shape[0]
    step = pl.program_id(0)
    bands = x_all.shape[2]
    spans = [(0, 2), (2, bands)]

    def copies(span):
        first, last = spans[span]
        block = 0
        for index, start in enumerate(starts):
            blocks = x_refs[2 * index].shape[0]
            for side in range(2):
                yield pltpu.make_async_copy(
                    x_refs[2 * index + side].at[:, pl.ds(start + first, last - first)],
                    x_all.at[
                        lax.rem(place_ref[2] + side, 2),
                        pl.ds(block, blocks),
                        pl.ds(first, last - first),
                    ],
                    sems.at[span, 2 * index + side],
                )
            block += blocks

    lower = lax.broadcasted_iota(jnp.int32, (1, 2 * width), 1) < width

    def gather(band, left_ref, right_ref):
        right = []
        for pol in range(2):
            lanes = slice(pol * 2 * LANES, (pol + 1) * 2 * LANES)
            value = jnp.concatenate(
                [
                    jnp.concatenate([x_all[pol, block, band, part] for part in range(2)], axis=1)
                    for block in range(x_all.shape[1])
                ]
            )
            left = jnp.dot(left_sel_ref[...], value, preferred_element_type=jnp.float32)
            for tile in range(tiles):
                rows = slice(tile * width, (tile + 1) * width)
                scaled = left[rows] * weight_ref[pl.ds(tile, 1), :]
                left_ref[rows, lanes] = scaled.astype(jnp.bfloat16)
            right.append(
                lax.dot_general(
                    value,
                    right_sel_ref[pol],
                    (((0,), (0,)), ((), ())),
                    preferred_element_type=jnp.float32,
                )
            )
        for pair in range(tiles // 2):
            first, second = (v[:, pair * 2 * width : (pair + 1) * 2 * width] for v in right)
            even = jnp.where(lower, first, second)
            odd = pltpu.roll(jnp.where(lower, second, first), width, 1)
            right_ref[2 * pair] = even.astype(jnp.bfloat16)
            right_ref[2 * pair + 1] = odd.astype(jnp.bfloat16)

    def multiply(number, left_ref, right_ref):
        for tile in range(tiles):
            rows = slice(tile * width, (tile + 1) * width)
            left = jnp.concatenate(
                [left_ref[rows, lanes : lanes + 2 * LANES] for lanes in (0, 2 * LANES)]
            )
            right = right_ref[tile]
            turned = jnp.concatenate([-right[LANES:], right[:LANES]])
            both = jnp.concatenate([right, turned], axis=1)
            result = jnp.dot(left, both, preferred_element_type=jnp.float32)
            for part in range(2):
                out_ref[tile, number, part] = result[
                    :, part * 2 * width : (part + 1) * 2 * width
                ].reshape(2, width, 2 * width)

    even, odd = rows_refs[:2], rows_refs[2:]

    @pl.when(step == 0)
    def _():
        for span in range(2):
            for copy in copies(span):
                copy.start()
        for copy in copies(0):
            copy.wait()
        gather(0, *even)
        for copy in copies(1):
            copy.wait()

    gather(2 * step + 1, *odd)
    multiply(0, *even)
    gather(jnp.minimum(2 * step + 2, bands - 1), *even)
    multiply(1, *odd)


def correlate_tiles(place, tables, pieces, starts, width, first, count, bands, earlier):
    left_select, _, weight = tables
    tiles = weight.shape[0]
    whole = pl.BlockSpec(memory_space=pltpu.VMEM)
    more = [] if earlier is None else [earlier]
    rows = [
        pltpu.VMEM((tiles * width, 4 * LANES), jnp.bfloat16),
        pltpu.VMEM((tiles, 2 * LANES, 2 * width), jnp.bfloat16),
    ]
    return pl.pallas_call(
        lambda *refs: correlate_kernel(starts, width, *refs),
        grid=(count // 2,),
        out_shape=jax.ShapeDtypeStruct((tiles, bands, 2, 2, width, 2 * width), jnp.float32),
        in_specs=[pl.BlockSpec(memory_space=pltpu.SMEM)]
        + [whole] * len(tables)
        + [pl.BlockSpec(memory_space=pl.ANY)] * (len(pieces) + len(more)),
        out_specs=pl.BlockSpec(
            (tiles, 2, 2, 2, width, 2 * width), lambda g: (0, g + first // 2, 0, 0, 0, 0)
        ),
        scratch_shapes=[
            pltpu.VMEM((2, left_select.shape[1] // ROWS, count, 2, ROWS, LANES), jnp.bfloat16),
            *rows,
            *rows,
            pltpu.SemaphoreType.DMA((2, len(pieces))),
        ],
        input_output_aliases={1 + len(tables) + len(pieces): 0} if more else {},
        compiler_params=pltpu.CompilerParams(vmem_limit_bytes=32 * 2**20),
        cost_estimate=pl.CostEstimate(
            flops=13 * 10**9 * count // bands,
            bytes_accessed=42 * 2**20 * count // bands,
            transcendentals=0,
        ),
        name="correlate",
    )(place, *tables, *pieces, *more)


def tile_tables(tile_a, tile_b, tile_owner, tile_flags, row_of):
    tiles = tile_owner.shape[0]
    held = tile_owner == lax.axis_index("pol")
    order = jnp.arange(tiles, dtype=jnp.int32)
    rank = jnp.sum((held[None, :] & (order[None, :] < order[:, None])).astype(jnp.int32), axis=1)
    slots = jnp.arange(CAP, dtype=jnp.int32)
    pick = (held[None, :] & (rank[None, :] == slots[:, None])).astype(jnp.int32)
    sides = jnp.stack([row_of(tile_a), row_of(tile_b)], axis=1) + 1
    rows = jnp.sum(pick[:, :, None, None] * sides[None], axis=1) - 1
    flags = jnp.sum(pick[:, :, None] * tile_flags[None], axis=1).astype(jnp.float32)
    return rows, flags


def on_device_chunks(voltages, taps_filter, tile_a, tile_b, tile_owner, tile_flags):
    length = taps_filter.shape[1]
    stations = voltages.shape[2]
    frames = voltages.shape[3] // length
    chan_count, time_count = lax.axis_size("chan"), lax.axis_size("tm")
    owners = chan_count * time_count
    chunk_count = stations // (time_count * ROWS)
    width = tile_a.shape[1]
    bands = length // AVG // owners
    tables = fourier_tables(length)

    chan, tm = lax.axis_index("chan"), lax.axis_index("tm")
    place = jnp.stack([chan, tm, lax.axis_index("pol")]).astype(jnp.int32)

    pairs = [(0, 2), (1, 2), (0, 1), (1, 1), (0, 3), (1, 3), (1, 0), (0, 0)]

    def row_of(station):
        column, rest = station // stations, station % stations
        block, inside = rest // (chunk_count * ROWS), rest % (chunk_count * ROWS)
        across = (chan - column) % chan_count
        behind = (tm - block) % time_count
        piece = sum(i * ((across == x) & (behind == z)) for i, (x, z) in enumerate(pairs))
        return ((inside // ROWS) * owners + piece) * ROWS + inside % ROWS

    rows, flags = tile_tables(tile_a, tile_b, tile_owner, tile_flags, row_of)
    total_rows = chunk_count * owners * ROWS
    station_rows = jnp.arange(total_rows, dtype=jnp.int32)
    left_rows = rows[:, 0].reshape(-1)
    left_select = (left_rows[:, None] == station_rows).astype(jnp.bfloat16)
    right_rows = rows[:, 1].reshape(CAP // 2, 2, width)
    right_rows = jnp.stack([right_rows, right_rows[:, ::-1]]).reshape(2, 1, -1)
    right_select = (right_rows == station_rows[:, None]).astype(jnp.bfloat16)
    depth = AVG * time_count * frames
    weight = jnp.tile(flags * (1.0 / depth), (1, 2 * AVG))
    tables_of_tiles = [left_select, right_select, weight]

    samples = voltages.reshape(2, stations, frames * length)

    def travel(value, axes, distances):
        sizes = [lax.axis_size(axis) for axis in axes]
        pairs = []
        for index in np.ndindex(*sizes):
            target = [(i + d) % n for i, d, n in zip(index, distances, sizes)]
            pairs.append(tuple(int(np.ravel_multi_index(x, sizes)) for x in (index, target)))
        return lax.ppermute(value, axes, pairs)

    def after(values, earlier):
        return lax.optimization_barrier((list(values), list(earlier)))

    def block_for(values, chunk, distance):
        first = ((tm + distance) % time_count * chunk_count + chunk) * ROWS
        return lax.dynamic_slice(values, (0, first, 0), (2, ROWS, frames * length))

    def filtered(chunk, arrived, plan):
        return channelise(
            place, chunk, samples, arrived, taps_filter, tables, frames, chan_count, plan
        )

    def over(value, across, along):
        return travel(value, ("chan", "tm"), (across, along))

    def columns(near, far):
        return jnp.stack([near, far])

    cut = bands // 2
    sooner, later = pairs[:4], pairs[4:7]

    def start(pieces, chosen, guards):
        blocks, guards = after([pieces[p] for p in chosen], guards)
        pieces.update((p, over(block, *p)) for p, block in zip(chosen, blocks))
        return guards

    (one,), (values,) = after([block_for(samples, 0, 1)], [samples])
    first = {1: over(one, 0, 1), 3: over(block_for(values, 0, 3), 0, 3)}
    (two,), (first[1],) = after([block_for(values, 0, 2)], [first[1]])
    first[2] = over(two, 0, 2)
    blocks = {distance: block_for(values, 1, distance) for distance in (1, 2, 3)}
    (one,), (first[3],) = after([blocks[1]], [first[3]])
    (three,), (first[2],) = after([blocks[3]], [first[2]])
    second = {1: over(one, 0, 1), 3: over(three, 0, 3)}
    (two,), (second[1],) = after([blocks[2]], [second[1]])
    second[2] = over(two, 0, 2)

    plan = [[(x, z, 0, bands)] for x, z in pairs]
    early = dict(zip(pairs, filtered(0, [first[z] for z in (1, 2, 3)], plan)))
    second[2], *tables_of_tiles = start(early, sooner, [second[2], *tables_of_tiles])

    plan = [[(x, z, *span)] for span in ((0, cut), (cut, bands)) for x, z in pairs]
    spectra = filtered(1, [second[z] for z in (1, 2, 3)], plan)
    low, high = dict(zip(pairs, spectra[: len(pairs)])), dict(zip(pairs, spectra[len(pairs) :]))
    guards = start(early, later, [low[0, 0]] + [early[p] for p in sooner])
    low[0, 0] = guards[0]
    early.update(zip(sooner, guards[1:]))
    (early[0, 3],) = start(low, sooner, [early[0, 3]])
    (low[0, 2],) = start(low, later, [low[0, 2]])
    (low[0, 3],) = start(high, sooner, [low[0, 3]])

    def with_other(values):
        return [side for v in values for side in (v, travel(v, ("pol",), (1,)))]

    def in_fours(pieces):
        return [jnp.stack([pieces[p] for p in chosen]) for chosen in (pairs[:4], pairs[4:])]

    early = with_other(in_fours(early))
    home = with_other([high[0, 0][None]])
    visibility = correlate_tiles(
        place, tables_of_tiles, early + with_other(in_fours(low)),
        [0] * 4, width, 0, cut, bands, None,
    )
    guards, (visibility,) = after([high[p] for p in sooner], [visibility])
    high.update(zip(sooner, guards))
    (visibility,) = start(high, later, [visibility])
    late = with_other([jnp.stack(guards)] + [high[p][None] for p in later]) + home
    return correlate_tiles(
        place, tables_of_tiles, early + late,
        [cut] * 2 + [0] * 5, width, cut, bands - cut, bands, visibility,
    )


def on_device(voltages, taps_filter, tile_a, tile_b, tile_owner, tile_flags):
    taps, length = taps_filter.shape
    frames = voltages.shape[3] // length
    time_count = lax.axis_size("tm")
    fits = (
        length == RADIX * LANES
        and AVG * time_count * frames == LANES
        and 2 * tile_a.shape[1] == LANES
        and voltages.shape[2] == 2 * time_count * ROWS
        and (lax.axis_size("chan"), time_count) == (2, 4)
    )
    form = on_device_chunks if fits else on_device_any
    return form(voltages, taps_filter, tile_a, tile_b, tile_owner, tile_flags)


def solution(mesh):
    return jax.shard_map(
        on_device,
        mesh=mesh,
        in_specs=(P("grp", "pol", "chan", "tm"), P(), P(), P(), P(), P()),
        out_specs=P("pol", ("chan", "tm"), "grp", None, None, None),
        check_vma=False,
    )
```

```python
import math

import jax
import jax.numpy as jnp
import numpy as np
from jax import lax
from jax.experimental import pallas as pl
from jax.experimental.pallas import tpu as pltpu
from jax.sharding import PartitionSpec as P

AVG = 8
CAP = 8
RADIX = 16
LANES = 128
ROWS = 16


radix_first = 32


def from_behind(value, axis, steps):
    count = lax.axis_size(axis)
    first, last = (max(0, -steps), min(count, count - steps))
    return lax.ppermute(value, axis, [(source, source + steps) for source in range(first, last)])


def fourier(filtered):
    length = filtered.shape[-1]
    second = length // radix_first
    exact_mode = lax.Precision.HIGHEST
    grid = filtered.reshape(filtered.shape[:-1] + (radix_first, second))
    outer = jnp.arange(radix_first, dtype=jnp.int32)
    inner = jnp.arange(second, dtype=jnp.int32)
    phase_one = (
        2.0
        * math.pi
        / radix_first
        * (outer[:, None] * outer[None, :] % radix_first).astype(jnp.float32)
    )
    phase_twist = 2.0 * math.pi / length * (outer[:, None] * inner[None, :]).astype(jnp.float32)
    phase_two = (
        2.0 * math.pi / second * (inner[:, None] * inner[None, :] % second).astype(jnp.float32)
    )
    cos_one, sin_one = (jnp.cos(phase_one), jnp.sin(phase_one))
    cos_twist, sin_twist = (jnp.cos(phase_twist), jnp.sin(phase_twist))
    cos_two, sin_two = (jnp.cos(phase_two), jnp.sin(phase_two))
    first_form = "fk,stkj->stfj"
    section_re = jnp.einsum(first_form, cos_one, grid[0], precision=exact_mode) + jnp.einsum(
        first_form, sin_one, grid[1], precision=exact_mode
    )
    section_im = jnp.einsum(first_form, cos_one, grid[1], precision=exact_mode) - jnp.einsum(
        first_form, sin_one, grid[0], precision=exact_mode
    )
    turned_re = section_re * cos_twist + section_im * sin_twist
    turned_im = section_im * cos_twist - section_re * sin_twist
    second_form = "gj,stfj->stgf"
    final_re = jnp.einsum(second_form, cos_two, turned_re, precision=exact_mode) + jnp.einsum(
        second_form, sin_two, turned_im, precision=exact_mode
    )
    final_im = jnp.einsum(second_form, cos_two, turned_im, precision=exact_mode) - jnp.einsum(
        second_form, sin_two, turned_re, precision=exact_mode
    )
    joined = jnp.stack([final_re, final_im]).reshape(filtered.shape)
    return joined * (1.0 / math.sqrt(length))


def correlate(full, rows_a, rows_b, flags, group_count):
    depth = full.shape[4]
    weight = jnp.tile(flags.astype(jnp.bfloat16), depth // flags.shape[0])
    left_rows = jnp.take(full, rows_a, axis=2) * weight
    right_rows = jnp.take(full, rows_b, axis=2)
    stacked_left = jnp.stack(
        [
            jnp.concatenate([left_rows[0], left_rows[1]], axis=-1),
            jnp.concatenate([left_rows[1], -left_rows[0]], axis=-1),
        ]
    )
    joined_right = jnp.concatenate([right_rows[0], right_rows[1]], axis=-1)
    result = jnp.einsum(
        "rpank,qbnk->nrpaqb", stacked_left, joined_right, preferred_element_type=jnp.float32
    )
    width = rows_a.shape[0]
    return result.reshape(group_count, 2, 2, width, 2 * width) * (1.0 / depth)


def on_device_any(voltages, taps_filter, tile_a, tile_b, tile_owner, tile_flags):
    history = taps_filter.shape[0] - 1
    length = taps_filter.shape[1]
    stations = voltages.shape[2]
    frames = voltages.shape[3] // length
    local_blocks = voltages.reshape(2, stations, frames, length)
    hop_count = -(-history // frames)
    sending = local_blocks
    extended = local_blocks
    for hop_index in range(hop_count):
        sending = from_behind(sending, "tm", 1)
        extended = jnp.concatenate([sending, extended], axis=2)
    extended = extended[:, :, extended.shape[2] - history - frames :]
    filtered = jnp.zeros((2, stations, frames, length), jnp.float32)
    for tap_index in range(history + 1):
        start = history - tap_index
        filtered = filtered + taps_filter[tap_index] * extended[
            :, :, start : start + frames
        ].astype(jnp.float32)
    spectra = fourier(filtered).astype(jnp.bfloat16)
    chan_count = lax.axis_size("chan")
    time_count = lax.axis_size("tm")
    narrow = length // (chan_count * time_count)
    outgoing = spectra.reshape(2, stations, frames, chan_count, time_count, narrow)
    outgoing = outgoing.transpose(0, 3, 4, 5, 1, 2)
    flat = outgoing.reshape(2, chan_count * time_count, narrow, stations * frames)
    moved = lax.all_to_all(flat, ("chan", "tm"), split_axis=1, concat_axis=1, tiled=True)
    moved = moved.reshape(2, chan_count, time_count, narrow, stations, frames)
    bands = narrow // AVG
    every_station = chan_count * stations
    spectra_count = time_count * frames
    arranged = moved.transpose(0, 1, 4, 3, 2, 5).reshape(
        2, 1, every_station, bands, AVG * spectra_count
    )
    full = lax.all_gather(arranged, "pol", axis=1, tiled=True)
    position = lax.axis_index("pol")
    width = tile_a.shape[1]
    capacity = CAP
    held = tile_owner == position
    listed = jnp.nonzero(held, size=capacity, fill_value=0)[0].astype(jnp.int32)
    tally = jnp.sum(held.astype(jnp.int32))
    initial = jnp.zeros((capacity, bands, 2, 2, width, 2 * width), jnp.float32)

    def fill_slot(slot, results):
        chosen_tile = listed[slot]
        return results.at[slot].set(
            correlate(
                full, tile_a[chosen_tile], tile_b[chosen_tile], tile_flags[chosen_tile], bands
            )
        )

    visibility = lax.fori_loop(0, tally, fill_slot, initial)
    return visibility


def fourier_tables(length):
    low = np.arange(RADIX)
    lane = np.arange(LANES)
    turn = 2.0 * np.pi / length * np.outer(low, lane)
    twiddle = np.stack([np.cos(turn), np.sin(turn)]).astype(np.float32)
    angle = 2.0 * np.pi / LANES * (np.outer(lane, lane) % LANES)
    cos, sin = np.cos(angle) / math.sqrt(length), np.sin(angle) / math.sqrt(length)
    matrix = np.block([[cos, sin], [-sin, cos]]).astype(np.float32)
    high = matrix.astype(jnp.bfloat16)
    rest = (matrix - high.astype(np.float32)).astype(jnp.bfloat16)
    return twiddle, np.stack([high, rest])


def butterflies(values):
    count = len(values)
    if count == 1:
        return values
    even, odd = butterflies(values[0::2]), butterflies(values[1::2])
    first, second = [], []
    for index in range(count // 2):
        (a, b), (c, d) = even[index], odd[index]
        if index == 0:
            e, f = c, d
        elif 4 * index == count:
            e, f = d, -c
        elif 8 * index == count:
            root = math.sqrt(0.5)
            e, f = (c + d) * root, (d - c) * root
        elif 8 * index == 3 * count:
            root = math.sqrt(0.5)
            e, f = (d - c) * root, -(c + d) * root
        else:
            turn = 2.0 * math.pi * index / count
            cos, sin = math.cos(turn), math.sin(turn)
            e, f = c * cos + d * sin, d * cos - c * sin
        first.append((a + e, b + f))
        second.append((a - e, b - f))
    return first + second


def channelise_kernel(frames, chunk, columns, plan, place_ref, own_ref, *refs):
    sources = refs[-6].shape[0]
    come_refs = refs[: sources - 1]
    taps_ref, twiddle_ref, matrix_ref = refs[sources - 1 : sources + 2]
    out_refs = refs[sources + 2 : -6]
    x_ref, fil_ref, zr_ref, zi_ref, w_ref, sems = refs[-6:]
    chan, tm = place_ref[0], place_ref[1]
    own_rows = pl.multiple_of((tm * (own_ref.shape[1] // (sources * ROWS)) + chunk) * ROWS, ROWS)
    copies = []
    for behind in range(sources):
        block = come_refs[behind - 1] if behind else own_ref.at[:, pl.ds(own_rows, ROWS), :]
        slot = lax.rem(tm - behind + sources, sources)
        copies.append(pltpu.make_async_copy(block, x_ref.at[slot], sems.at[behind]))
    for copy in copies:
        copy.start()
    for copy in copies:
        copy.wait()
    spectra = sources * frames
    length = taps_ref.shape[1]
    taps = taps_ref.shape[0]
    depth = RADIX * spectra
    z_refs = (zr_ref, zi_ref)

    @pl.loop(0, RADIX)
    def _(section):
        at = pl.multiple_of(section * LANES, LANES)
        weights = [taps_ref[pl.ds(m, 1), pl.ds(at, LANES)] for m in range(taps)]
        for part in range(2):
            blocks = []
            for t in range(spectra):
                lane = pl.multiple_of((t % frames) * length + section * LANES, LANES)
                blocks.append(x_ref[t // frames, part, :, pl.ds(lane, LANES)].astype(jnp.float32))
            for t in range(spectra):
                total = weights[0] * blocks[t]
                for m in range(1, min(t + 1, taps)):
                    total = total + weights[m] * blocks[t - m]
                fil_ref[section, t, part] = total

    @pl.loop(0, spectra)
    def _(t):
        for half in range(ROWS // 8):
            values = [
                tuple(fil_ref[section, t, part, pl.ds(half * 8, 8), :] for part in range(2))
                for section in range(RADIX)
            ]
            for low, (re, im) in enumerate(butterflies(values)):
                if low:
                    cos = twiddle_ref[0, pl.ds(low, 1), :]
                    sin = twiddle_ref[1, pl.ds(low, 1), :]
                    re, im = re * cos + im * sin, im * cos - re * sin
                rows = pl.ds(half * 8 * depth + low * spectra + t, 8, stride=depth)
                zr_ref[rows, :] = re
                zi_ref[rows, :] = im

    form = (((1,), (1,)), ((), ()))
    high_matrix, low_matrix = matrix_ref[0], matrix_ref[1]
    halves = depth // LANES

    @pl.loop(0, ROWS)
    def _(station):
        rows = pl.ds(pl.multiple_of(station * depth, depth), depth)
        value = jnp.concatenate([ref[rows, :] for ref in z_refs], axis=1)
        high = value.astype(jnp.bfloat16)
        rest = (value - high.astype(jnp.float32)).astype(jnp.bfloat16)
        total = lax.dot_general(high_matrix, high, form, preferred_element_type=jnp.float32)
        total += lax.dot_general(high_matrix, rest, form, preferred_element_type=jnp.float32)
        total += lax.dot_general(low_matrix, high, form, preferred_element_type=jnp.float32)
        for half in range(halves):
            for part in range(2):
                rows = pl.ds((half * 2 + part) * ROWS + station, LANES, stride=halves * 2 * ROWS)
                w_ref[rows, :] = total[
                    part * LANES : (part + 1) * LANES, half * LANES : (half + 1) * LANES
                ]

    share = w_ref.shape[0] // (columns * sources)
    band_rows = 2 * ROWS
    piece = 4 * band_rows
    for blocks, out_ref in zip(plan, out_refs):
        at = 0
        for across, along, start, stop in blocks:
            owner = lax.rem(chan + across, columns) * sources + lax.rem(tm + along, sources)
            for row in range(start * band_rows, stop * band_rows, piece):
                rows = pl.ds(pl.multiple_of(owner * share + row, piece), piece)
                out_ref[at : at + piece, :] = w_ref[rows, :].astype(jnp.bfloat16)
                at += piece


def channelise(place, chunk, voltages, come, taps_filter, tables, frames, columns, plan):
    sources = 1 + len(come)
    length = taps_filter.shape[1]
    spectra = sources * frames
    twiddle, matrix = tables
    out_rows = length // AVG * 2 * ROWS
    whole = pl.BlockSpec(memory_space=pltpu.VMEM)
    counts = [sum(stop - start for _, _, start, stop in blocks) for blocks in plan]
    flat = pl.pallas_call(
        lambda *refs: channelise_kernel(frames, chunk, columns, plan, *refs),
        out_shape=[
            jax.ShapeDtypeStruct((count * 2 * ROWS, LANES), jnp.bfloat16) for count in counts
        ],
        in_specs=[pl.BlockSpec(memory_space=pltpu.SMEM)]
        + [pl.BlockSpec(memory_space=pl.ANY)] * sources
        + [whole] * 3,
        out_specs=[whole] * len(plan),
        scratch_shapes=[
            pltpu.VMEM((sources, 2, ROWS, frames * length), jnp.bfloat16),
            pltpu.VMEM((RADIX, spectra, 2, ROWS, LANES), jnp.float32),
            pltpu.VMEM((ROWS * RADIX * spectra, LANES), jnp.float32),
            pltpu.VMEM((ROWS * RADIX * spectra, LANES), jnp.float32),
            pltpu.VMEM((out_rows, LANES), jnp.float32),
            pltpu.SemaphoreType.DMA((sources,)),
        ],
        compiler_params=pltpu.CompilerParams(vmem_limit_bytes=40 * 2**20),
        cost_estimate=pl.CostEstimate(
            flops=9 * 10**9, bytes_accessed=4 * 2**20, transcendentals=0
        ),
        name="channelise",
    )(place, voltages, *come, taps_filter, jnp.asarray(twiddle), jnp.asarray(matrix))
    return [piece.reshape(count, 2, ROWS, LANES) for piece, count in zip(flat, counts)]


def correlate_kernel(starts, width, place_ref, left_sel_ref, right_sel_ref, weight_ref, *refs):
    x_refs, (out_ref, x_all, *rows_refs, sems) = refs[: 2 * len(starts)], refs[-7:]
    tiles = out_ref.shape[0]
    step = pl.program_id(0)
    bands = x_all.shape[2]
    spans = [(0, 2), (2, bands)]

    def copies(span):
        first, last = spans[span]
        block = 0
        for index, start in enumerate(starts):
            blocks = x_refs[2 * index].shape[0]
            for side in range(2):
                yield pltpu.make_async_copy(
                    x_refs[2 * index + side].at[:, pl.ds(start + first, last - first)],
                    x_all.at[
                        lax.rem(place_ref[2] + side, 2),
                        pl.ds(block, blocks),
                        pl.ds(first, last - first),
                    ],
                    sems.at[span, 2 * index + side],
                )
            block += blocks

    lower = lax.broadcasted_iota(jnp.int32, (1, 2 * width), 1) < width

    def gather(band, left_ref, right_ref):
        right = []
        for pol in range(2):
            lanes = slice(pol * 2 * LANES, (pol + 1) * 2 * LANES)
            value = jnp.concatenate(
                [
                    jnp.concatenate([x_all[pol, block, band, part] for part in range(2)], axis=1)
                    for block in range(x_all.shape[1])
                ]
            )
            left = jnp.dot(left_sel_ref[...], value, preferred_element_type=jnp.float32)
            for tile in range(tiles):
                rows = slice(tile * width, (tile + 1) * width)
                scaled = left[rows] * weight_ref[pl.ds(tile, 1), :]
                left_ref[rows, lanes] = scaled.astype(jnp.bfloat16)
            right.append(
                lax.dot_general(
                    value,
                    right_sel_ref[pol],
                    (((0,), (0,)), ((), ())),
                    preferred_element_type=jnp.float32,
                )
            )
        for pair in range(tiles // 2):
            first, second = (v[:, pair * 2 * width : (pair + 1) * 2 * width] for v in right)
            even = jnp.where(lower, first, second)
            odd = pltpu.roll(jnp.where(lower, second, first), width, 1)
            right_ref[2 * pair] = even.astype(jnp.bfloat16)
            right_ref[2 * pair + 1] = odd.astype(jnp.bfloat16)

    def multiply(number, left_ref, right_ref):
        for tile in range(tiles):
            rows = slice(tile * width, (tile + 1) * width)
            left = jnp.concatenate(
                [left_ref[rows, lanes : lanes + 2 * LANES] for lanes in (0, 2 * LANES)]
            )
            right = right_ref[tile]
            turned = jnp.concatenate([-right[LANES:], right[:LANES]])
            both = jnp.concatenate([right, turned], axis=1)
            result = jnp.dot(left, both, preferred_element_type=jnp.float32)
            for part in range(2):
                out_ref[tile, number, part] = result[
                    :, part * 2 * width : (part + 1) * 2 * width
                ].reshape(2, width, 2 * width)

    even, odd = rows_refs[:2], rows_refs[2:]

    @pl.when(step == 0)
    def _():
        for span in range(2):
            for copy in copies(span):
                copy.start()
        for copy in copies(0):
            copy.wait()
        gather(0, *even)
        for copy in copies(1):
            copy.wait()

    gather(2 * step + 1, *odd)
    multiply(0, *even)
    gather(jnp.minimum(2 * step + 2, bands - 1), *even)
    multiply(1, *odd)


def correlate_tiles(place, tables, pieces, starts, width, first, count, bands, earlier):
    left_select, _, weight = tables
    tiles = weight.shape[0]
    whole = pl.BlockSpec(memory_space=pltpu.VMEM)
    more = [] if earlier is None else [earlier]
    rows = [
        pltpu.VMEM((tiles * width, 4 * LANES), jnp.bfloat16),
        pltpu.VMEM((tiles, 2 * LANES, 2 * width), jnp.bfloat16),
    ]
    return pl.pallas_call(
        lambda *refs: correlate_kernel(starts, width, *refs),
        grid=(count // 2,),
        out_shape=jax.ShapeDtypeStruct((tiles, bands, 2, 2, width, 2 * width), jnp.float32),
        in_specs=[pl.BlockSpec(memory_space=pltpu.SMEM)]
        + [whole] * len(tables)
        + [pl.BlockSpec(memory_space=pl.ANY)] * (len(pieces) + len(more)),
        out_specs=pl.BlockSpec(
            (tiles, 2, 2, 2, width, 2 * width), lambda g: (0, g + first // 2, 0, 0, 0, 0)
        ),
        scratch_shapes=[
            pltpu.VMEM((2, left_select.shape[1] // ROWS, count, 2, ROWS, LANES), jnp.bfloat16),
            *rows,
            *rows,
            pltpu.SemaphoreType.DMA((2, len(pieces))),
        ],
        input_output_aliases={1 + len(tables) + len(pieces): 0} if more else {},
        compiler_params=pltpu.CompilerParams(vmem_limit_bytes=32 * 2**20),
        cost_estimate=pl.CostEstimate(
            flops=13 * 10**9 * count // bands,
            bytes_accessed=42 * 2**20 * count // bands,
            transcendentals=0,
        ),
        name="correlate",
    )(place, *tables, *pieces, *more)


def tile_tables(tile_a, tile_b, tile_owner, tile_flags, row_of):
    tiles = tile_owner.shape[0]
    held = tile_owner == lax.axis_index("pol")
    order = jnp.arange(tiles, dtype=jnp.int32)
    rank = jnp.sum((held[None, :] & (order[None, :] < order[:, None])).astype(jnp.int32), axis=1)
    slots = jnp.arange(CAP, dtype=jnp.int32)
    pick = (held[None, :] & (rank[None, :] == slots[:, None])).astype(jnp.int32)
    sides = jnp.stack([row_of(tile_a), row_of(tile_b)], axis=1) + 1
    rows = jnp.sum(pick[:, :, None, None] * sides[None], axis=1) - 1
    flags = jnp.sum(pick[:, :, None] * tile_flags[None], axis=1).astype(jnp.float32)
    return rows, flags


def on_device_chunks(voltages, taps_filter, tile_a, tile_b, tile_owner, tile_flags):
    length = taps_filter.shape[1]
    stations = voltages.shape[2]
    frames = voltages.shape[3] // length
    chan_count, time_count = lax.axis_size("chan"), lax.axis_size("tm")
    owners = chan_count * time_count
    chunk_count = stations // (time_count * ROWS)
    width = tile_a.shape[1]
    bands = length // AVG // owners
    tables = fourier_tables(length)

    chan, tm = lax.axis_index("chan"), lax.axis_index("tm")
    place = jnp.stack([chan, tm, lax.axis_index("pol")]).astype(jnp.int32)

    def row_of(station):
        column, rest = station // stations, station % stations
        block, inside = rest // (chunk_count * ROWS), rest % (chunk_count * ROWS)
        across = (chan - column) % chan_count
        behind = (tm - block) % time_count
        piece = behind * chan_count + across
        return ((inside // ROWS) * owners + piece) * ROWS + inside % ROWS

    rows, flags = tile_tables(tile_a, tile_b, tile_owner, tile_flags, row_of)
    total_rows = chunk_count * owners * ROWS
    station_rows = jnp.arange(total_rows, dtype=jnp.int32)
    left_rows = rows[:, 0].reshape(-1)
    left_select = (left_rows[:, None] == station_rows).astype(jnp.bfloat16)
    right_rows = rows[:, 1].reshape(CAP // 2, 2, width)
    right_rows = jnp.stack([right_rows, right_rows[:, ::-1]]).reshape(2, 1, -1)
    right_select = (right_rows == station_rows[:, None]).astype(jnp.bfloat16)
    depth = AVG * time_count * frames
    weight = jnp.tile(flags * (1.0 / depth), (1, 2 * AVG))
    tables_of_tiles = [left_select, right_select, weight]

    samples = voltages.reshape(2, stations, frames * length)

    def travel(value, axes, distances):
        sizes = [lax.axis_size(axis) for axis in axes]
        pairs = []
        for index in np.ndindex(*sizes):
            target = [(i + d) % n for i, d, n in zip(index, distances, sizes)]
            pairs.append(tuple(int(np.ravel_multi_index(x, sizes)) for x in (index, target)))
        return lax.ppermute(value, axes, pairs)

    def after(values, earlier):
        return lax.optimization_barrier((list(values), list(earlier)))

    def block_for(values, chunk, distance):
        first = ((tm + distance) % time_count * chunk_count + chunk) * ROWS
        return lax.dynamic_slice(values, (0, first, 0), (2, ROWS, frames * length))

    def filtered(chunk, arrived, plan):
        return channelise(
            place, chunk, samples, arrived, taps_filter, tables, frames, chan_count, plan
        )

    def over(value, across, along):
        return travel(value, ("chan", "tm"), (across, along))

    def columns(near, far):
        return jnp.stack([near, far])

    cut = bands // 2
    rest = bands - cut
    (one,), (values,) = after([block_for(samples, 0, 1)], [samples])
    two, three = (block_for(values, 0, distance) for distance in (2, 3))
    one, two = over(one, 0, 1), over(two, 0, 2)
    (three,), (one,) = after([three], [one])
    three = over(three, 0, 3)
    blocks = [block_for(values, 1, distance) for distance in (1, 2, 3)]
    blocks[:1], (two,) = after(blocks[:1], [two])
    blocks[2:], (three,) = after(blocks[2:], [three])
    first = [one, two, three]
    one, three = over(blocks[0], 0, 1), over(blocks[2], 0, 3)
    (two,), (one,) = after(blocks[1:2], [one])
    second = [one, over(two, 0, 2), three]

    def over_tm(blocks, order):
        return {z: over(blocks[z], 0, z) for z in order}

    hops = [2, 3, 1, 0]
    plan = [[(0, z, 0, bands) for z in hops]]
    plan += [[(1, z, 0, bands) for z in part] for part in (hops[:2], hops[2:])]
    near, far, others = filtered(0, first, plan)
    (far,), (second[2],) = after([far], [second[2]])
    far = over(far, 1, 0)
    near = dict(zip(hops, near.reshape(4, bands, 2, ROWS, LANES)))
    far = far.reshape(2, bands, 2, ROWS, LANES)
    mixed = [columns(near[z], far[i]) for i, z in enumerate(hops[:2])]
    mixed, (second[1], *tables_of_tiles) = after(mixed, [second[1], *tables_of_tiles])
    early = over_tm(dict(zip(hops, mixed)), hops[:2])
    (others,), (second[1],) = after([others], [second[1]])
    others = over(others, 1, 0)

    spans = [(0, cut), (cut, bands)]
    plan = [[(x, z, *span) for z in range(time_count)] for span in spans for x in range(2)]
    spectra = filtered(1, second, plan)
    (far_low,), (early[2], others) = after([spectra[1]], [early[2], others])
    far_low = over(far_low, 1, 0)
    one, home = others.reshape(2, bands, 2, ROWS, LANES)
    (one,), (early[3],) = after([columns(near[1], one)], [early[3]])
    early.update(over_tm({1: one}, [1]))
    early[0] = columns(near[0], home)
    (far_high,), (far_low,) = after([spectra[3]], [far_low])
    spectra = [spectra[0], far_low, spectra[2], over(far_high, 1, 0)]
    spectra = [v.reshape(time_count, cut, 2, ROWS, LANES) for v in spectra]
    low, high = (
        [columns(near[z], far[z]) for z in range(time_count)]
        for near, far in (spectra[:2], spectra[2:])
    )
    blocks, (early[3], high[1]) = after(low[1:], [early[3], high[1]])
    moved = over_tm(dict(zip((1, 2, 3), blocks)), (2, 1, 3))
    low = [low[0]] + [moved[z] for z in (1, 2, 3)]

    def with_other(values):
        return [side for v in values for side in (v, travel(v, ("pol",), (1,)))]

    early = jnp.stack([early[z] for z in range(time_count)])
    early = with_other([early.reshape(2 * time_count, bands, 2, ROWS, LANES)])
    blocks, held = after(high[1:], [low[2], low[1], early[1]])
    low[2], low[1], early[1] = held
    moved = {z: over(blocks[z - 1], 0, z) for z in (2, 1, 3)}
    high = [high[0]] + [moved[z] for z in (1, 2, 3)]
    low = jnp.stack(low).reshape(2 * time_count, cut, 2, ROWS, LANES)
    visibility = correlate_tiles(
        place, tables_of_tiles, early + with_other([low]),
        [0, 0], width, 0, cut, bands, None,
    )
    home = with_other(high[:1])
    high, (visibility,) = after(high[1:], [visibility])
    return correlate_tiles(
        place, tables_of_tiles, early + home + with_other(high),
        [cut] + [0] * 4, width, cut, rest, bands, visibility,
    )


def on_device(voltages, taps_filter, tile_a, tile_b, tile_owner, tile_flags):
    taps, length = taps_filter.shape
    frames = voltages.shape[3] // length
    time_count = lax.axis_size("tm")
    fits = (
        length == RADIX * LANES
        and AVG * time_count * frames == LANES
        and 2 * tile_a.shape[1] == LANES
        and voltages.shape[2] == 2 * time_count * ROWS
        and (lax.axis_size("chan"), time_count) == (2, 4)
    )
    form = on_device_chunks if fits else on_device_any
    return form(voltages, taps_filter, tile_a, tile_b, tile_owner, tile_flags)


def solution(mesh):
    return jax.shard_map(
        on_device,
        mesh=mesh,
        in_specs=(P("grp", "pol", "chan", "tm"), P(), P(), P(), P(), P()),
        out_specs=P("pol", ("chan", "tm"), "grp", None, None, None),
        check_vma=False,
    )
```

```python
import math

import jax
import jax.numpy as jnp
import numpy as np
from jax import lax
from jax.experimental import pallas as pl
from jax.experimental.pallas import tpu as pltpu
from jax.sharding import PartitionSpec as P

AVG = 8
CAP = 8
RADIX = 16
LANES = 128
ROWS = 16


radix_first = 32


def from_behind(value, axis, steps):
    count = lax.axis_size(axis)
    first, last = (max(0, -steps), min(count, count - steps))
    return lax.ppermute(value, axis, [(source, source + steps) for source in range(first, last)])


def fourier(filtered):
    length = filtered.shape[-1]
    second = length // radix_first
    exact_mode = lax.Precision.HIGHEST
    grid = filtered.reshape(filtered.shape[:-1] + (radix_first, second))
    outer = jnp.arange(radix_first, dtype=jnp.int32)
    inner = jnp.arange(second, dtype=jnp.int32)
    phase_one = (
        2.0
        * math.pi
        / radix_first
        * (outer[:, None] * outer[None, :] % radix_first).astype(jnp.float32)
    )
    phase_twist = 2.0 * math.pi / length * (outer[:, None] * inner[None, :]).astype(jnp.float32)
    phase_two = (
        2.0 * math.pi / second * (inner[:, None] * inner[None, :] % second).astype(jnp.float32)
    )
    cos_one, sin_one = (jnp.cos(phase_one), jnp.sin(phase_one))
    cos_twist, sin_twist = (jnp.cos(phase_twist), jnp.sin(phase_twist))
    cos_two, sin_two = (jnp.cos(phase_two), jnp.sin(phase_two))
    first_form = "fk,stkj->stfj"
    section_re = jnp.einsum(first_form, cos_one, grid[0], precision=exact_mode) + jnp.einsum(
        first_form, sin_one, grid[1], precision=exact_mode
    )
    section_im = jnp.einsum(first_form, cos_one, grid[1], precision=exact_mode) - jnp.einsum(
        first_form, sin_one, grid[0], precision=exact_mode
    )
    turned_re = section_re * cos_twist + section_im * sin_twist
    turned_im = section_im * cos_twist - section_re * sin_twist
    second_form = "gj,stfj->stgf"
    final_re = jnp.einsum(second_form, cos_two, turned_re, precision=exact_mode) + jnp.einsum(
        second_form, sin_two, turned_im, precision=exact_mode
    )
    final_im = jnp.einsum(second_form, cos_two, turned_im, precision=exact_mode) - jnp.einsum(
        second_form, sin_two, turned_re, precision=exact_mode
    )
    joined = jnp.stack([final_re, final_im]).reshape(filtered.shape)
    return joined * (1.0 / math.sqrt(length))


def correlate(full, rows_a, rows_b, flags, group_count):
    depth = full.shape[4]
    weight = jnp.tile(flags.astype(jnp.bfloat16), depth // flags.shape[0])
    left_rows = jnp.take(full, rows_a, axis=2) * weight
    right_rows = jnp.take(full, rows_b, axis=2)
    stacked_left = jnp.stack(
        [
            jnp.concatenate([left_rows[0], left_rows[1]], axis=-1),
            jnp.concatenate([left_rows[1], -left_rows[0]], axis=-1),
        ]
    )
    joined_right = jnp.concatenate([right_rows[0], right_rows[1]], axis=-1)
    result = jnp.einsum(
        "rpank,qbnk->nrpaqb", stacked_left, joined_right, preferred_element_type=jnp.float32
    )
    width = rows_a.shape[0]
    return result.reshape(group_count, 2, 2, width, 2 * width) * (1.0 / depth)


def on_device_any(voltages, taps_filter, tile_a, tile_b, tile_owner, tile_flags):
    history = taps_filter.shape[0] - 1
    length = taps_filter.shape[1]
    stations = voltages.shape[2]
    frames = voltages.shape[3] // length
    local_blocks = voltages.reshape(2, stations, frames, length)
    hop_count = -(-history // frames)
    sending = local_blocks
    extended = local_blocks
    for hop_index in range(hop_count):
        sending = from_behind(sending, "tm", 1)
        extended = jnp.concatenate([sending, extended], axis=2)
    extended = extended[:, :, extended.shape[2] - history - frames :]
    filtered = jnp.zeros((2, stations, frames, length), jnp.float32)
    for tap_index in range(history + 1):
        start = history - tap_index
        filtered = filtered + taps_filter[tap_index] * extended[
            :, :, start : start + frames
        ].astype(jnp.float32)
    spectra = fourier(filtered).astype(jnp.bfloat16)
    chan_count = lax.axis_size("chan")
    time_count = lax.axis_size("tm")
    narrow = length // (chan_count * time_count)
    outgoing = spectra.reshape(2, stations, frames, chan_count, time_count, narrow)
    outgoing = outgoing.transpose(0, 3, 4, 5, 1, 2)
    flat = outgoing.reshape(2, chan_count * time_count, narrow, stations * frames)
    moved = lax.all_to_all(flat, ("chan", "tm"), split_axis=1, concat_axis=1, tiled=True)
    moved = moved.reshape(2, chan_count, time_count, narrow, stations, frames)
    bands = narrow // AVG
    every_station = chan_count * stations
    spectra_count = time_count * frames
    arranged = moved.transpose(0, 1, 4, 3, 2, 5).reshape(
        2, 1, every_station, bands, AVG * spectra_count
    )
    full = lax.all_gather(arranged, "pol", axis=1, tiled=True)
    position = lax.axis_index("pol")
    width = tile_a.shape[1]
    capacity = CAP
    held = tile_owner == position
    listed = jnp.nonzero(held, size=capacity, fill_value=0)[0].astype(jnp.int32)
    tally = jnp.sum(held.astype(jnp.int32))
    initial = jnp.zeros((capacity, bands, 2, 2, width, 2 * width), jnp.float32)

    def fill_slot(slot, results):
        chosen_tile = listed[slot]
        return results.at[slot].set(
            correlate(
                full, tile_a[chosen_tile], tile_b[chosen_tile], tile_flags[chosen_tile], bands
            )
        )

    visibility = lax.fori_loop(0, tally, fill_slot, initial)
    return visibility


def fourier_tables(length):
    low = np.arange(RADIX)
    lane = np.arange(LANES)
    turn = 2.0 * np.pi / length * np.outer(low, lane)
    twiddle = np.stack([np.cos(turn), np.sin(turn)]).astype(np.float32)
    angle = 2.0 * np.pi / LANES * (np.outer(lane, lane) % LANES)
    cos, sin = np.cos(angle) / math.sqrt(length), np.sin(angle) / math.sqrt(length)
    matrix = np.block([[cos, sin], [-sin, cos]]).astype(np.float32)
    high = matrix.astype(jnp.bfloat16)
    rest = (matrix - high.astype(np.float32)).astype(jnp.bfloat16)
    return twiddle, np.stack([high, rest])


def butterflies(values):
    count = len(values)
    if count == 1:
        return values
    even, odd = butterflies(values[0::2]), butterflies(values[1::2])
    first, second = [], []
    for index in range(count // 2):
        (a, b), (c, d) = even[index], odd[index]
        if index == 0:
            e, f = c, d
        elif 4 * index == count:
            e, f = d, -c
        elif 8 * index == count:
            root = math.sqrt(0.5)
            e, f = (c + d) * root, (d - c) * root
        elif 8 * index == 3 * count:
            root = math.sqrt(0.5)
            e, f = (d - c) * root, -(c + d) * root
        else:
            turn = 2.0 * math.pi * index / count
            cos, sin = math.cos(turn), math.sin(turn)
            e, f = c * cos + d * sin, d * cos - c * sin
        first.append((a + e, b + f))
        second.append((a - e, b - f))
    return first + second


def channelise_kernel(frames, chunk, columns, plan, place_ref, own_ref, *refs):
    sources = refs[-6].shape[0]
    come_refs = refs[: sources - 1]
    taps_ref, twiddle_ref, matrix_ref = refs[sources - 1 : sources + 2]
    out_refs = refs[sources + 2 : -6]
    x_ref, fil_ref, zr_ref, zi_ref, w_ref, sems = refs[-6:]
    chan, tm = place_ref[0], place_ref[1]
    own_rows = pl.multiple_of((tm * (own_ref.shape[1] // (sources * ROWS)) + chunk) * ROWS, ROWS)
    copies = []
    for behind in range(sources):
        block = come_refs[behind - 1] if behind else own_ref.at[:, pl.ds(own_rows, ROWS), :]
        slot = lax.rem(tm - behind + sources, sources)
        copies.append(pltpu.make_async_copy(block, x_ref.at[slot], sems.at[behind]))
    for copy in copies:
        copy.start()
    for copy in copies:
        copy.wait()
    spectra = sources * frames
    length = taps_ref.shape[1]
    taps = taps_ref.shape[0]
    depth = RADIX * spectra
    z_refs = (zr_ref, zi_ref)

    @pl.loop(0, RADIX)
    def _(section):
        at = pl.multiple_of(section * LANES, LANES)
        weights = [taps_ref[pl.ds(m, 1), pl.ds(at, LANES)] for m in range(taps)]
        for part in range(2):
            blocks = []
            for t in range(spectra):
                lane = pl.multiple_of((t % frames) * length + section * LANES, LANES)
                blocks.append(x_ref[t // frames, part, :, pl.ds(lane, LANES)].astype(jnp.float32))
            for t in range(spectra):
                total = weights[0] * blocks[t]
                for m in range(1, min(t + 1, taps)):
                    total = total + weights[m] * blocks[t - m]
                fil_ref[section, t, part] = total

    @pl.loop(0, spectra)
    def _(t):
        for half in range(ROWS // 8):
            values = [
                tuple(fil_ref[section, t, part, pl.ds(half * 8, 8), :] for part in range(2))
                for section in range(RADIX)
            ]
            for low, (re, im) in enumerate(butterflies(values)):
                if low:
                    cos = twiddle_ref[0, pl.ds(low, 1), :]
                    sin = twiddle_ref[1, pl.ds(low, 1), :]
                    re, im = re * cos + im * sin, im * cos - re * sin
                rows = pl.ds(half * 8 * depth + low * spectra + t, 8, stride=depth)
                zr_ref[rows, :] = re
                zi_ref[rows, :] = im

    form = (((1,), (1,)), ((), ()))
    high_matrix, low_matrix = matrix_ref[0], matrix_ref[1]
    halves = depth // LANES

    @pl.loop(0, ROWS)
    def _(station):
        rows = pl.ds(pl.multiple_of(station * depth, depth), depth)
        value = jnp.concatenate([ref[rows, :] for ref in z_refs], axis=1)
        high = value.astype(jnp.bfloat16)
        rest = (value - high.astype(jnp.float32)).astype(jnp.bfloat16)
        total = lax.dot_general(high_matrix, high, form, preferred_element_type=jnp.float32)
        total += lax.dot_general(high_matrix, rest, form, preferred_element_type=jnp.float32)
        total += lax.dot_general(low_matrix, high, form, preferred_element_type=jnp.float32)
        for half in range(halves):
            for part in range(2):
                rows = pl.ds((half * 2 + part) * ROWS + station, LANES, stride=halves * 2 * ROWS)
                w_ref[rows, :] = total[
                    part * LANES : (part + 1) * LANES, half * LANES : (half + 1) * LANES
                ]

    share = w_ref.shape[0] // (columns * sources)
    band_rows = 2 * ROWS
    piece = 4 * band_rows
    for blocks, out_ref in zip(plan, out_refs):
        at = 0
        for across, along, start, stop in blocks:
            owner = lax.rem(chan + across, columns) * sources + lax.rem(tm + along, sources)
            for row in range(start * band_rows, stop * band_rows, piece):
                rows = pl.ds(pl.multiple_of(owner * share + row, piece), piece)
                out_ref[at : at + piece, :] = w_ref[rows, :].astype(jnp.bfloat16)
                at += piece


def channelise(place, chunk, voltages, come, taps_filter, tables, frames, columns, plan):
    sources = 1 + len(come)
    length = taps_filter.shape[1]
    spectra = sources * frames
    twiddle, matrix = tables
    out_rows = length // AVG * 2 * ROWS
    whole = pl.BlockSpec(memory_space=pltpu.VMEM)
    counts = [sum(stop - start for _, _, start, stop in blocks) for blocks in plan]
    flat = pl.pallas_call(
        lambda *refs: channelise_kernel(frames, chunk, columns, plan, *refs),
        out_shape=[
            jax.ShapeDtypeStruct((count * 2 * ROWS, LANES), jnp.bfloat16) for count in counts
        ],
        in_specs=[pl.BlockSpec(memory_space=pltpu.SMEM)]
        + [pl.BlockSpec(memory_space=pl.ANY)] * sources
        + [whole] * 3,
        out_specs=[whole] * len(plan),
        scratch_shapes=[
            pltpu.VMEM((sources, 2, ROWS, frames * length), jnp.bfloat16),
            pltpu.VMEM((RADIX, spectra, 2, ROWS, LANES), jnp.float32),
            pltpu.VMEM((ROWS * RADIX * spectra, LANES), jnp.float32),
            pltpu.VMEM((ROWS * RADIX * spectra, LANES), jnp.float32),
            pltpu.VMEM((out_rows, LANES), jnp.float32),
            pltpu.SemaphoreType.DMA((sources,)),
        ],
        compiler_params=pltpu.CompilerParams(vmem_limit_bytes=40 * 2**20),
        cost_estimate=pl.CostEstimate(
            flops=9 * 10**9, bytes_accessed=4 * 2**20, transcendentals=0
        ),
        name="channelise",
    )(place, voltages, *come, taps_filter, jnp.asarray(twiddle), jnp.asarray(matrix))
    return [piece.reshape(count, 2, ROWS, LANES) for piece, count in zip(flat, counts)]


def correlate_kernel(starts, width, place_ref, left_sel_ref, right_sel_ref, weight_ref, *refs):
    x_refs, (out_ref, x_all, *rows_refs, sems) = refs[: 2 * len(starts)], refs[-7:]
    tiles = out_ref.shape[0]
    step = pl.program_id(0)
    bands = x_all.shape[2]
    spans = [(0, 2), (2, bands)]

    def copies(span):
        first, last = spans[span]
        block = 0
        for index, start in enumerate(starts):
            blocks = x_refs[2 * index].shape[0]
            for side in range(2):
                yield pltpu.make_async_copy(
                    x_refs[2 * index + side].at[:, pl.ds(start + first, last - first)],
                    x_all.at[
                        lax.rem(place_ref[2] + side, 2),
                        pl.ds(block, blocks),
                        pl.ds(first, last - first),
                    ],
                    sems.at[span, 2 * index + side],
                )
            block += blocks

    lower = lax.broadcasted_iota(jnp.int32, (1, 2 * width), 1) < width

    def gather(band, left_ref, right_ref):
        right = []
        for pol in range(2):
            lanes = slice(pol * 2 * LANES, (pol + 1) * 2 * LANES)
            value = jnp.concatenate(
                [
                    jnp.concatenate([x_all[pol, block, band, part] for part in range(2)], axis=1)
                    for block in range(x_all.shape[1])
                ]
            )
            left = jnp.dot(left_sel_ref[...], value, preferred_element_type=jnp.float32)
            for tile in range(tiles):
                rows = slice(tile * width, (tile + 1) * width)
                scaled = left[rows] * weight_ref[pl.ds(tile, 1), :]
                left_ref[rows, lanes] = scaled.astype(jnp.bfloat16)
            right.append(
                lax.dot_general(
                    value,
                    right_sel_ref[pol],
                    (((0,), (0,)), ((), ())),
                    preferred_element_type=jnp.float32,
                )
            )
        for pair in range(tiles // 2):
            first, second = (v[:, pair * 2 * width : (pair + 1) * 2 * width] for v in right)
            even = jnp.where(lower, first, second)
            odd = pltpu.roll(jnp.where(lower, second, first), width, 1)
            right_ref[2 * pair] = even.astype(jnp.bfloat16)
            right_ref[2 * pair + 1] = odd.astype(jnp.bfloat16)

    def multiply(number, left_ref, right_ref):
        for tile in range(tiles):
            rows = slice(tile * width, (tile + 1) * width)
            left = jnp.concatenate(
                [left_ref[rows, lanes : lanes + 2 * LANES] for lanes in (0, 2 * LANES)]
            )
            right = right_ref[tile]
            turned = jnp.concatenate([-right[LANES:], right[:LANES]])
            both = jnp.concatenate([right, turned], axis=1)
            result = jnp.dot(left, both, preferred_element_type=jnp.float32)
            for part in range(2):
                out_ref[tile, number, part] = result[
                    :, part * 2 * width : (part + 1) * 2 * width
                ].reshape(2, width, 2 * width)

    even, odd = rows_refs[:2], rows_refs[2:]

    @pl.when(step == 0)
    def _():
        for span in range(2):
            for copy in copies(span):
                copy.start()
        for copy in copies(0):
            copy.wait()
        gather(0, *even)
        for copy in copies(1):
            copy.wait()

    gather(2 * step + 1, *odd)
    multiply(0, *even)
    gather(jnp.minimum(2 * step + 2, bands - 1), *even)
    multiply(1, *odd)


def correlate_tiles(place, tables, pieces, starts, width, first, count, bands, earlier):
    left_select, _, weight = tables
    tiles = weight.shape[0]
    whole = pl.BlockSpec(memory_space=pltpu.VMEM)
    more = [] if earlier is None else [earlier]
    rows = [
        pltpu.VMEM((tiles * width, 4 * LANES), jnp.bfloat16),
        pltpu.VMEM((tiles, 2 * LANES, 2 * width), jnp.bfloat16),
    ]
    return pl.pallas_call(
        lambda *refs: correlate_kernel(starts, width, *refs),
        grid=(count // 2,),
        out_shape=jax.ShapeDtypeStruct((tiles, bands, 2, 2, width, 2 * width), jnp.float32),
        in_specs=[pl.BlockSpec(memory_space=pltpu.SMEM)]
        + [whole] * len(tables)
        + [pl.BlockSpec(memory_space=pl.ANY)] * (len(pieces) + len(more)),
        out_specs=pl.BlockSpec(
            (tiles, 2, 2, 2, width, 2 * width), lambda g: (0, g + first // 2, 0, 0, 0, 0)
        ),
        scratch_shapes=[
            pltpu.VMEM((2, left_select.shape[1] // ROWS, count, 2, ROWS, LANES), jnp.bfloat16),
            *rows,
            *rows,
            pltpu.SemaphoreType.DMA((2, len(pieces))),
        ],
        input_output_aliases={1 + len(tables) + len(pieces): 0} if more else {},
        compiler_params=pltpu.CompilerParams(vmem_limit_bytes=32 * 2**20),
        cost_estimate=pl.CostEstimate(
            flops=13 * 10**9 * count // bands,
            bytes_accessed=42 * 2**20 * count // bands,
            transcendentals=0,
        ),
        name="correlate",
    )(place, *tables, *pieces, *more)


def tile_tables(tile_a, tile_b, tile_owner, tile_flags, row_of):
    tiles = tile_owner.shape[0]
    held = tile_owner == lax.axis_index("pol")
    order = jnp.arange(tiles, dtype=jnp.int32)
    rank = jnp.sum((held[None, :] & (order[None, :] < order[:, None])).astype(jnp.int32), axis=1)
    slots = jnp.arange(CAP, dtype=jnp.int32)
    pick = (held[None, :] & (rank[None, :] == slots[:, None])).astype(jnp.int32)
    sides = jnp.stack([row_of(tile_a), row_of(tile_b)], axis=1) + 1
    rows = jnp.sum(pick[:, :, None, None] * sides[None], axis=1) - 1
    flags = jnp.sum(pick[:, :, None] * tile_flags[None], axis=1).astype(jnp.float32)
    return rows, flags


def on_device_chunks(voltages, taps_filter, tile_a, tile_b, tile_owner, tile_flags):
    length = taps_filter.shape[1]
    stations = voltages.shape[2]
    frames = voltages.shape[3] // length
    chan_count, time_count = lax.axis_size("chan"), lax.axis_size("tm")
    owners = chan_count * time_count
    chunk_count = stations // (time_count * ROWS)
    width = tile_a.shape[1]
    bands = length // AVG // owners
    tables = fourier_tables(length)

    chan, tm = lax.axis_index("chan"), lax.axis_index("tm")
    place = jnp.stack([chan, tm, lax.axis_index("pol")]).astype(jnp.int32)

    pairs = [(0, 2), (1, 2), (0, 1), (1, 1), (0, 3), (1, 3), (1, 0), (0, 0)]

    def row_of(station):
        column, rest = station // stations, station % stations
        block, inside = rest // (chunk_count * ROWS), rest % (chunk_count * ROWS)
        across = (chan - column) % chan_count
        behind = (tm - block) % time_count
        piece = sum(i * ((across == x) & (behind == z)) for i, (x, z) in enumerate(pairs))
        return ((inside // ROWS) * owners + piece) * ROWS + inside % ROWS

    rows, flags = tile_tables(tile_a, tile_b, tile_owner, tile_flags, row_of)
    total_rows = chunk_count * owners * ROWS
    station_rows = jnp.arange(total_rows, dtype=jnp.int32)
    left_rows = rows[:, 0].reshape(-1)
    left_select = (left_rows[:, None] == station_rows).astype(jnp.bfloat16)
    right_rows = rows[:, 1].reshape(CAP // 2, 2, width)
    right_rows = jnp.stack([right_rows, right_rows[:, ::-1]]).reshape(2, 1, -1)
    right_select = (right_rows == station_rows[:, None]).astype(jnp.bfloat16)
    depth = AVG * time_count * frames
    weight = jnp.tile(flags * (1.0 / depth), (1, 2 * AVG))
    tables_of_tiles = [left_select, right_select, weight]

    samples = voltages.reshape(2, stations, frames * length)

    def travel(value, axes, distances):
        sizes = [lax.axis_size(axis) for axis in axes]
        pairs = []
        for index in np.ndindex(*sizes):
            target = [(i + d) % n for i, d, n in zip(index, distances, sizes)]
            pairs.append(tuple(int(np.ravel_multi_index(x, sizes)) for x in (index, target)))
        return lax.ppermute(value, axes, pairs)

    def after(values, earlier):
        return lax.optimization_barrier((list(values), list(earlier)))

    def block_for(values, chunk, distance):
        first = ((tm + distance) % time_count * chunk_count + chunk) * ROWS
        return lax.dynamic_slice(values, (0, first, 0), (2, ROWS, frames * length))

    def filtered(chunk, arrived, plan):
        return channelise(
            place, chunk, samples, arrived, taps_filter, tables, frames, chan_count, plan
        )

    def over(value, across, along):
        return travel(value, ("chan", "tm"), (across, along))

    def columns(near, far):
        return jnp.stack([near, far])

    cut = bands // 2
    sooner, later = pairs[:4], pairs[4:7]

    def start(pieces, chosen, guards):
        blocks, guards = after([pieces[p] for p in chosen], guards)
        pieces.update((p, over(block, *p)) for p, block in zip(chosen, blocks))
        return guards

    (one,), (values,) = after([block_for(samples, 0, 1)], [samples])
    two, three = (block_for(values, 0, distance) for distance in (2, 3))
    one, two = over(one, 0, 1), over(two, 0, 2)
    (three,), (one,) = after([three], [one])
    three = over(three, 0, 3)
    blocks = [block_for(values, 1, distance) for distance in (1, 2, 3)]
    blocks[:1], (two,) = after(blocks[:1], [two])
    blocks[2:], (three,) = after(blocks[2:], [three])
    first = [one, two, three]
    one, three = over(blocks[0], 0, 1), over(blocks[2], 0, 3)
    (two,), (one,) = after(blocks[1:2], [one])
    second = [one, over(two, 0, 2), three]

    plan = [[(x, z, 0, bands)] for x, z in pairs]
    early = dict(zip(pairs, filtered(0, first, plan)))
    second[1], *tables_of_tiles = start(early, sooner, [second[1], *tables_of_tiles])

    def with_other(values):
        return [side for v in values for side in (v, travel(v, ("pol",), (1,)))]

    def in_fours(pieces):
        return [jnp.stack([pieces[p] for p in chosen]) for chosen in (pairs[:4], pairs[4:])]

    plan = [[(x, z, *span)] for span in ((0, cut), (cut, bands)) for x, z in pairs]
    spectra = filtered(1, second, plan)
    low, high = dict(zip(pairs, spectra[: len(pairs)])), dict(zip(pairs, spectra[len(pairs) :]))
    guards = start(early, later, [low[0, 0]] + [early[p] for p in sooner])
    low[0, 0] = guards[0]
    early.update(zip(sooner, guards[1:]))
    both = with_other(in_fours(early))
    both[1], early[0, 3] = start(low, sooner, [both[1], early[0, 3]])
    low[0, 2], both[3] = start(low, later, [low[0, 2], both[3]])
    high[1, 0] = over(high[1, 0], 1, 0)
    (low[0, 3],) = start(high, pairs[:5], [low[0, 3]])
    home = with_other([jnp.stack([high[1, 0], high[0, 0]])])
    lows = in_fours(low)
    lows[1:], home = after(lows[1:], home)
    visibility = correlate_tiles(
        place, tables_of_tiles, both + with_other(lows),
        [0] * 4, width, 0, cut, bands, None,
    )
    high[0, 2], visibility = start(high, [(1, 3)], [high[0, 2], visibility])
    pieces, _ = after([high[p] for p in pairs[:6]], [visibility])
    late = [jnp.stack(pieces[:4]), pieces[4][None], pieces[5][None]]
    return correlate_tiles(
        place, tables_of_tiles, both + with_other(late) + home,
        [cut] * 2 + [0] * 4, width, cut, bands - cut, bands, visibility,
    )


def on_device(voltages, taps_filter, tile_a, tile_b, tile_owner, tile_flags):
    taps, length = taps_filter.shape
    frames = voltages.shape[3] // length
    time_count = lax.axis_size("tm")
    fits = (
        length == RADIX * LANES
        and AVG * time_count * frames == LANES
        and 2 * tile_a.shape[1] == LANES
        and voltages.shape[2] == 2 * time_count * ROWS
        and (lax.axis_size("chan"), time_count) == (2, 4)
    )
    form = on_device_chunks if fits else on_device_any
    return form(voltages, taps_filter, tile_a, tile_b, tile_owner, tile_flags)


def solution(mesh):
    return jax.shard_map(
        on_device,
        mesh=mesh,
        in_specs=(P("grp", "pol", "chan", "tm"), P(), P(), P(), P(), P()),
        out_specs=P("pol", ("chan", "tm"), "grp", None, None, None),
        check_vma=False,
    )
```

```python
import math

import jax
import jax.numpy as jnp
import numpy as np
from jax import lax
from jax.experimental import pallas as pl
from jax.experimental.pallas import tpu as pltpu
from jax.sharding import PartitionSpec as P

AVG = 8
CAP = 8
RADIX = 16
LANES = 128
ROWS = 16


radix_first = 32


def from_behind(value, axis, steps):
    count = lax.axis_size(axis)
    first, last = (max(0, -steps), min(count, count - steps))
    return lax.ppermute(value, axis, [(source, source + steps) for source in range(first, last)])


def fourier(filtered):
    length = filtered.shape[-1]
    second = length // radix_first
    exact_mode = lax.Precision.HIGHEST
    grid = filtered.reshape(filtered.shape[:-1] + (radix_first, second))
    outer = jnp.arange(radix_first, dtype=jnp.int32)
    inner = jnp.arange(second, dtype=jnp.int32)
    phase_one = (
        2.0
        * math.pi
        / radix_first
        * (outer[:, None] * outer[None, :] % radix_first).astype(jnp.float32)
    )
    phase_twist = 2.0 * math.pi / length * (outer[:, None] * inner[None, :]).astype(jnp.float32)
    phase_two = (
        2.0 * math.pi / second * (inner[:, None] * inner[None, :] % second).astype(jnp.float32)
    )
    cos_one, sin_one = (jnp.cos(phase_one), jnp.sin(phase_one))
    cos_twist, sin_twist = (jnp.cos(phase_twist), jnp.sin(phase_twist))
    cos_two, sin_two = (jnp.cos(phase_two), jnp.sin(phase_two))
    first_form = "fk,stkj->stfj"
    section_re = jnp.einsum(first_form, cos_one, grid[0], precision=exact_mode) + jnp.einsum(
        first_form, sin_one, grid[1], precision=exact_mode
    )
    section_im = jnp.einsum(first_form, cos_one, grid[1], precision=exact_mode) - jnp.einsum(
        first_form, sin_one, grid[0], precision=exact_mode
    )
    turned_re = section_re * cos_twist + section_im * sin_twist
    turned_im = section_im * cos_twist - section_re * sin_twist
    second_form = "gj,stfj->stgf"
    final_re = jnp.einsum(second_form, cos_two, turned_re, precision=exact_mode) + jnp.einsum(
        second_form, sin_two, turned_im, precision=exact_mode
    )
    final_im = jnp.einsum(second_form, cos_two, turned_im, precision=exact_mode) - jnp.einsum(
        second_form, sin_two, turned_re, precision=exact_mode
    )
    joined = jnp.stack([final_re, final_im]).reshape(filtered.shape)
    return joined * (1.0 / math.sqrt(length))


def correlate(full, rows_a, rows_b, flags, group_count):
    depth = full.shape[4]
    weight = jnp.tile(flags.astype(jnp.bfloat16), depth // flags.shape[0])
    left_rows = jnp.take(full, rows_a, axis=2) * weight
    right_rows = jnp.take(full, rows_b, axis=2)
    stacked_left = jnp.stack(
        [
            jnp.concatenate([left_rows[0], left_rows[1]], axis=-1),
            jnp.concatenate([left_rows[1], -left_rows[0]], axis=-1),
        ]
    )
    joined_right = jnp.concatenate([right_rows[0], right_rows[1]], axis=-1)
    result = jnp.einsum(
        "rpank,qbnk->nrpaqb", stacked_left, joined_right, preferred_element_type=jnp.float32
    )
    width = rows_a.shape[0]
    return result.reshape(group_count, 2, 2, width, 2 * width) * (1.0 / depth)


def on_device_any(voltages, taps_filter, tile_a, tile_b, tile_owner, tile_flags):
    history = taps_filter.shape[0] - 1
    length = taps_filter.shape[1]
    stations = voltages.shape[2]
    frames = voltages.shape[3] // length
    local_blocks = voltages.reshape(2, stations, frames, length)
    hop_count = -(-history // frames)
    sending = local_blocks
    extended = local_blocks
    for hop_index in range(hop_count):
        sending = from_behind(sending, "tm", 1)
        extended = jnp.concatenate([sending, extended], axis=2)
    extended = extended[:, :, extended.shape[2] - history - frames :]
    filtered = jnp.zeros((2, stations, frames, length), jnp.float32)
    for tap_index in range(history + 1):
        start = history - tap_index
        filtered = filtered + taps_filter[tap_index] * extended[
            :, :, start : start + frames
        ].astype(jnp.float32)
    spectra = fourier(filtered).astype(jnp.bfloat16)
    chan_count = lax.axis_size("chan")
    time_count = lax.axis_size("tm")
    narrow = length // (chan_count * time_count)
    outgoing = spectra.reshape(2, stations, frames, chan_count, time_count, narrow)
    outgoing = outgoing.transpose(0, 3, 4, 5, 1, 2)
    flat = outgoing.reshape(2, chan_count * time_count, narrow, stations * frames)
    moved = lax.all_to_all(flat, ("chan", "tm"), split_axis=1, concat_axis=1, tiled=True)
    moved = moved.reshape(2, chan_count, time_count, narrow, stations, frames)
    bands = narrow // AVG
    every_station = chan_count * stations
    spectra_count = time_count * frames
    arranged = moved.transpose(0, 1, 4, 3, 2, 5).reshape(
        2, 1, every_station, bands, AVG * spectra_count
    )
    full = lax.all_gather(arranged, "pol", axis=1, tiled=True)
    position = lax.axis_index("pol")
    width = tile_a.shape[1]
    capacity = CAP
    held = tile_owner == position
    listed = jnp.nonzero(held, size=capacity, fill_value=0)[0].astype(jnp.int32)
    tally = jnp.sum(held.astype(jnp.int32))
    initial = jnp.zeros((capacity, bands, 2, 2, width, 2 * width), jnp.float32)

    def fill_slot(slot, results):
        chosen_tile = listed[slot]
        return results.at[slot].set(
            correlate(
                full, tile_a[chosen_tile], tile_b[chosen_tile], tile_flags[chosen_tile], bands
            )
        )

    visibility = lax.fori_loop(0, tally, fill_slot, initial)
    return visibility


def fourier_tables(length):
    low = np.arange(RADIX)
    lane = np.arange(LANES)
    turn = 2.0 * np.pi / length * np.outer(low, lane)
    twiddle = np.stack([np.cos(turn), np.sin(turn)]).astype(np.float32)
    angle = 2.0 * np.pi / LANES * (np.outer(lane, lane) % LANES)
    cos, sin = np.cos(angle) / math.sqrt(length), np.sin(angle) / math.sqrt(length)
    matrix = np.block([[cos, sin], [-sin, cos]]).astype(np.float32)
    high = matrix.astype(jnp.bfloat16)
    rest = (matrix - high.astype(np.float32)).astype(jnp.bfloat16)
    return twiddle, np.stack([high, rest])


def butterflies(values):
    count = len(values)
    if count == 1:
        return values
    even, odd = butterflies(values[0::2]), butterflies(values[1::2])
    first, second = [], []
    for index in range(count // 2):
        (a, b), (c, d) = even[index], odd[index]
        if index == 0:
            e, f = c, d
        elif 4 * index == count:
            e, f = d, -c
        elif 8 * index == count:
            root = math.sqrt(0.5)
            e, f = (c + d) * root, (d - c) * root
        elif 8 * index == 3 * count:
            root = math.sqrt(0.5)
            e, f = (d - c) * root, -(c + d) * root
        else:
            turn = 2.0 * math.pi * index / count
            cos, sin = math.cos(turn), math.sin(turn)
            e, f = c * cos + d * sin, d * cos - c * sin
        first.append((a + e, b + f))
        second.append((a - e, b - f))
    return first + second


def channelise_kernel(frames, chunk, columns, plan, place_ref, own_ref, *refs):
    sources = refs[-6].shape[0]
    come_refs = refs[: sources - 1]
    taps_ref, twiddle_ref, matrix_ref = refs[sources - 1 : sources + 2]
    out_refs = refs[sources + 2 : -6]
    x_ref, fil_ref, zr_ref, zi_ref, w_ref, sems = refs[-6:]
    chan, tm = place_ref[0], place_ref[1]
    own_rows = pl.multiple_of((tm * (own_ref.shape[1] // (sources * ROWS)) + chunk) * ROWS, ROWS)
    copies = []
    for behind in range(sources):
        block = come_refs[behind - 1] if behind else own_ref.at[:, pl.ds(own_rows, ROWS), :]
        slot = lax.rem(tm - behind + sources, sources)
        copies.append(pltpu.make_async_copy(block, x_ref.at[slot], sems.at[behind]))
    for copy in copies:
        copy.start()
    for copy in copies:
        copy.wait()
    spectra = sources * frames
    length = taps_ref.shape[1]
    taps = taps_ref.shape[0]
    depth = RADIX * spectra
    z_refs = (zr_ref, zi_ref)

    @pl.loop(0, RADIX)
    def _(section):
        at = pl.multiple_of(section * LANES, LANES)
        weights = [taps_ref[pl.ds(m, 1), pl.ds(at, LANES)] for m in range(taps)]
        for part in range(2):
            blocks = []
            for t in range(spectra):
                lane = pl.multiple_of((t % frames) * length + section * LANES, LANES)
                blocks.append(x_ref[t // frames, part, :, pl.ds(lane, LANES)].astype(jnp.float32))
            for t in range(spectra):
                total = weights[0] * blocks[t]
                for m in range(1, min(t + 1, taps)):
                    total = total + weights[m] * blocks[t - m]
                fil_ref[section, t, part] = total

    @pl.loop(0, spectra)
    def _(t):
        for half in range(ROWS // 8):
            values = [
                tuple(fil_ref[section, t, part, pl.ds(half * 8, 8), :] for part in range(2))
                for section in range(RADIX)
            ]
            for low, (re, im) in enumerate(butterflies(values)):
                if low:
                    cos = twiddle_ref[0, pl.ds(low, 1), :]
                    sin = twiddle_ref[1, pl.ds(low, 1), :]
                    re, im = re * cos + im * sin, im * cos - re * sin
                rows = pl.ds(half * 8 * depth + low * spectra + t, 8, stride=depth)
                zr_ref[rows, :] = re
                zi_ref[rows, :] = im

    form = (((1,), (1,)), ((), ()))
    high_matrix, low_matrix = matrix_ref[0], matrix_ref[1]
    halves = depth // LANES

    @pl.loop(0, ROWS)
    def _(station):
        rows = pl.ds(pl.multiple_of(station * depth, depth), depth)
        value = jnp.concatenate([ref[rows, :] for ref in z_refs], axis=1)
        high = value.astype(jnp.bfloat16)
        rest = (value - high.astype(jnp.float32)).astype(jnp.bfloat16)
        total = lax.dot_general(high_matrix, high, form, preferred_element_type=jnp.float32)
        total += lax.dot_general(high_matrix, rest, form, preferred_element_type=jnp.float32)
        total += lax.dot_general(low_matrix, high, form, preferred_element_type=jnp.float32)
        for half in range(halves):
            for part in range(2):
                rows = pl.ds((half * 2 + part) * ROWS + station, LANES, stride=halves * 2 * ROWS)
                w_ref[rows, :] = total[
                    part * LANES : (part + 1) * LANES, half * LANES : (half + 1) * LANES
                ]

    share = w_ref.shape[0] // (columns * sources)
    band_rows = 2 * ROWS
    piece = 4 * band_rows
    for blocks, out_ref in zip(plan, out_refs):
        at = 0
        for across, along, start, stop in blocks:
            owner = lax.rem(chan + across, columns) * sources + lax.rem(tm + along, sources)
            for row in range(start * band_rows, stop * band_rows, piece):
                rows = pl.ds(pl.multiple_of(owner * share + row, piece), piece)
                out_ref[at : at + piece, :] = w_ref[rows, :].astype(jnp.bfloat16)
                at += piece


def channelise(place, chunk, voltages, come, taps_filter, tables, frames, columns, plan):
    sources = 1 + len(come)
    length = taps_filter.shape[1]
    spectra = sources * frames
    twiddle, matrix = tables
    out_rows = length // AVG * 2 * ROWS
    whole = pl.BlockSpec(memory_space=pltpu.VMEM)
    counts = [sum(stop - start for _, _, start, stop in blocks) for blocks in plan]
    flat = pl.pallas_call(
        lambda *refs: channelise_kernel(frames, chunk, columns, plan, *refs),
        out_shape=[
            jax.ShapeDtypeStruct((count * 2 * ROWS, LANES), jnp.bfloat16) for count in counts
        ],
        in_specs=[pl.BlockSpec(memory_space=pltpu.SMEM)]
        + [pl.BlockSpec(memory_space=pl.ANY)] * sources
        + [whole] * 3,
        out_specs=[whole] * len(plan),
        scratch_shapes=[
            pltpu.VMEM((sources, 2, ROWS, frames * length), jnp.bfloat16),
            pltpu.VMEM((RADIX, spectra, 2, ROWS, LANES), jnp.float32),
            pltpu.VMEM((ROWS * RADIX * spectra, LANES), jnp.float32),
            pltpu.VMEM((ROWS * RADIX * spectra, LANES), jnp.float32),
            pltpu.VMEM((out_rows, LANES), jnp.float32),
            pltpu.SemaphoreType.DMA((sources,)),
        ],
        compiler_params=pltpu.CompilerParams(vmem_limit_bytes=40 * 2**20),
        cost_estimate=pl.CostEstimate(
            flops=9 * 10**9, bytes_accessed=4 * 2**20, transcendentals=0
        ),
        name="channelise",
    )(place, voltages, *come, taps_filter, jnp.asarray(twiddle), jnp.asarray(matrix))
    return [piece.reshape(count, 2, ROWS, LANES) for piece, count in zip(flat, counts)]


def correlate_kernel(starts, width, place_ref, left_sel_ref, right_sel_ref, weight_ref, *refs):
    x_refs, (out_ref, x_all, *rows_refs, sems) = refs[: 2 * len(starts)], refs[-7:]
    tiles = out_ref.shape[0]
    step = pl.program_id(0)
    bands = x_all.shape[2]
    spans = [(0, 2), (2, bands)]

    def copies(span):
        first, last = spans[span]
        block = 0
        for index, start in enumerate(starts):
            blocks = x_refs[2 * index].shape[0]
            for side in range(2):
                yield pltpu.make_async_copy(
                    x_refs[2 * index + side].at[:, pl.ds(start + first, last - first)],
                    x_all.at[
                        lax.rem(place_ref[2] + side, 2),
                        pl.ds(block, blocks),
                        pl.ds(first, last - first),
                    ],
                    sems.at[span, 2 * index + side],
                )
            block += blocks

    lower = lax.broadcasted_iota(jnp.int32, (1, 2 * width), 1) < width

    def gather(band, left_ref, right_ref):
        right = []
        for pol in range(2):
            lanes = slice(pol * 2 * LANES, (pol + 1) * 2 * LANES)
            value = jnp.concatenate(
                [
                    jnp.concatenate([x_all[pol, block, band, part] for part in range(2)], axis=1)
                    for block in range(x_all.shape[1])
                ]
            )
            left = jnp.dot(left_sel_ref[...], value, preferred_element_type=jnp.float32)
            for tile in range(tiles):
                rows = slice(tile * width, (tile + 1) * width)
                scaled = left[rows] * weight_ref[pl.ds(tile, 1), :]
                left_ref[rows, lanes] = scaled.astype(jnp.bfloat16)
            right.append(
                lax.dot_general(
                    value,
                    right_sel_ref[pol],
                    (((0,), (0,)), ((), ())),
                    preferred_element_type=jnp.float32,
                )
            )
        for pair in range(tiles // 2):
            first, second = (v[:, pair * 2 * width : (pair + 1) * 2 * width] for v in right)
            even = jnp.where(lower, first, second)
            odd = pltpu.roll(jnp.where(lower, second, first), width, 1)
            right_ref[2 * pair] = even.astype(jnp.bfloat16)
            right_ref[2 * pair + 1] = odd.astype(jnp.bfloat16)

    def multiply(number, left_ref, right_ref):
        for tile in range(tiles):
            rows = slice(tile * width, (tile + 1) * width)
            left = jnp.concatenate(
                [left_ref[rows, lanes : lanes + 2 * LANES] for lanes in (0, 2 * LANES)]
            )
            right = right_ref[tile]
            turned = jnp.concatenate([-right[LANES:], right[:LANES]])
            both = jnp.concatenate([right, turned], axis=1)
            result = jnp.dot(left, both, preferred_element_type=jnp.float32)
            for part in range(2):
                out_ref[tile, number, part] = result[
                    :, part * 2 * width : (part + 1) * 2 * width
                ].reshape(2, width, 2 * width)

    even, odd = rows_refs[:2], rows_refs[2:]

    @pl.when(step == 0)
    def _():
        for span in range(2):
            for copy in copies(span):
                copy.start()
        for copy in copies(0):
            copy.wait()
        gather(0, *even)
        for copy in copies(1):
            copy.wait()

    gather(2 * step + 1, *odd)
    multiply(0, *even)
    gather(jnp.minimum(2 * step + 2, bands - 1), *even)
    multiply(1, *odd)


def correlate_tiles(place, tables, pieces, starts, width, first, count, bands, earlier):
    left_select, _, weight = tables
    tiles = weight.shape[0]
    whole = pl.BlockSpec(memory_space=pltpu.VMEM)
    more = [] if earlier is None else [earlier]
    rows = [
        pltpu.VMEM((tiles * width, 4 * LANES), jnp.bfloat16),
        pltpu.VMEM((tiles, 2 * LANES, 2 * width), jnp.bfloat16),
    ]
    return pl.pallas_call(
        lambda *refs: correlate_kernel(starts, width, *refs),
        grid=(count // 2,),
        out_shape=jax.ShapeDtypeStruct((tiles, bands, 2, 2, width, 2 * width), jnp.float32),
        in_specs=[pl.BlockSpec(memory_space=pltpu.SMEM)]
        + [whole] * len(tables)
        + [pl.BlockSpec(memory_space=pl.ANY)] * (len(pieces) + len(more)),
        out_specs=pl.BlockSpec(
            (tiles, 2, 2, 2, width, 2 * width), lambda g: (0, g + first // 2, 0, 0, 0, 0)
        ),
        scratch_shapes=[
            pltpu.VMEM((2, left_select.shape[1] // ROWS, count, 2, ROWS, LANES), jnp.bfloat16),
            *rows,
            *rows,
            pltpu.SemaphoreType.DMA((2, len(pieces))),
        ],
        input_output_aliases={1 + len(tables) + len(pieces): 0} if more else {},
        compiler_params=pltpu.CompilerParams(vmem_limit_bytes=32 * 2**20),
        cost_estimate=pl.CostEstimate(
            flops=13 * 10**9 * count // bands,
            bytes_accessed=42 * 2**20 * count // bands,
            transcendentals=0,
        ),
        name="correlate",
    )(place, *tables, *pieces, *more)


def tile_tables(tile_a, tile_b, tile_owner, tile_flags, row_of):
    tiles = tile_owner.shape[0]
    held = tile_owner == lax.axis_index("pol")
    order = jnp.arange(tiles, dtype=jnp.int32)
    rank = jnp.sum((held[None, :] & (order[None, :] < order[:, None])).astype(jnp.int32), axis=1)
    slots = jnp.arange(CAP, dtype=jnp.int32)
    pick = (held[None, :] & (rank[None, :] == slots[:, None])).astype(jnp.int32)
    sides = jnp.stack([row_of(tile_a), row_of(tile_b)], axis=1) + 1
    rows = jnp.sum(pick[:, :, None, None] * sides[None], axis=1) - 1
    flags = jnp.sum(pick[:, :, None] * tile_flags[None], axis=1).astype(jnp.float32)
    return rows, flags


def on_device_chunks(voltages, taps_filter, tile_a, tile_b, tile_owner, tile_flags):
    length = taps_filter.shape[1]
    stations = voltages.shape[2]
    frames = voltages.shape[3] // length
    chan_count, time_count = lax.axis_size("chan"), lax.axis_size("tm")
    owners = chan_count * time_count
    chunk_count = stations // (time_count * ROWS)
    width = tile_a.shape[1]
    bands = length // AVG // owners
    tables = fourier_tables(length)

    chan, tm = lax.axis_index("chan"), lax.axis_index("tm")
    place = jnp.stack([chan, tm, lax.axis_index("pol")]).astype(jnp.int32)

    def row_of(station):
        column, rest = station // stations, station % stations
        block, inside = rest // (chunk_count * ROWS), rest % (chunk_count * ROWS)
        across = (chan - column) % chan_count
        behind = (tm - block) % time_count
        piece = behind * chan_count + across
        return ((inside // ROWS) * owners + piece) * ROWS + inside % ROWS

    rows, flags = tile_tables(tile_a, tile_b, tile_owner, tile_flags, row_of)
    total_rows = chunk_count * owners * ROWS
    station_rows = jnp.arange(total_rows, dtype=jnp.int32)
    left_rows = rows[:, 0].reshape(-1)
    left_select = (left_rows[:, None] == station_rows).astype(jnp.bfloat16)
    right_rows = rows[:, 1].reshape(CAP // 2, 2, width)
    right_rows = jnp.stack([right_rows, right_rows[:, ::-1]]).reshape(2, 1, -1)
    right_select = (right_rows == station_rows[:, None]).astype(jnp.bfloat16)
    depth = AVG * time_count * frames
    weight = jnp.tile(flags * (1.0 / depth), (1, 2 * AVG))
    tables_of_tiles = [left_select, right_select, weight]

    samples = voltages.reshape(2, stations, frames * length)

    def travel(value, axes, distances):
        sizes = [lax.axis_size(axis) for axis in axes]
        pairs = []
        for index in np.ndindex(*sizes):
            target = [(i + d) % n for i, d, n in zip(index, distances, sizes)]
            pairs.append(tuple(int(np.ravel_multi_index(x, sizes)) for x in (index, target)))
        return lax.ppermute(value, axes, pairs)

    def after(values, earlier):
        return lax.optimization_barrier((list(values), list(earlier)))

    def block_for(values, chunk, distance):
        first = ((tm + distance) % time_count * chunk_count + chunk) * ROWS
        return lax.dynamic_slice(values, (0, first, 0), (2, ROWS, frames * length))

    def filtered(chunk, arrived, plan):
        return channelise(
            place, chunk, samples, arrived, taps_filter, tables, frames, chan_count, plan
        )

    def over(value, across, along):
        return travel(value, ("chan", "tm"), (across, along))

    def columns(near, far):
        return jnp.stack([near, far])

    cut = bands * 5 // 8
    rest = bands - cut
    pairs = [(x, z) for z in range(time_count) for x in range(chan_count)]
    early_pairs = [(x, z) for z in (1, 3) for x in range(2)]
    late_pairs = [(0, 2), (1, 2), (1, 0)]

    (one,), (values,) = after([block_for(samples, 0, 1)], [samples])
    two, three = (block_for(values, 0, distance) for distance in (2, 3))
    one, two = over(one, 0, 1), over(two, 0, 2)
    (three,), (one,) = after([three], [one])
    three = over(three, 0, 3)
    blocks = [block_for(values, 1, distance) for distance in (1, 2, 3)]
    blocks[:1], (two,) = after(blocks[:1], [two])
    blocks[2:], (three,) = after(blocks[2:], [three])
    first = [one, two, three]
    one, three = over(blocks[0], 0, 1), over(blocks[2], 0, 3)
    (two,), (one,) = after(blocks[1:2], [one])
    second = [one, over(two, 0, 2), three]

    plan = [[(x, z, 0, bands)] for x, z in pairs]
    early = dict(zip(pairs, filtered(0, first, plan)))
    blocks, held = after([early[p] for p in early_pairs], [second[1], *tables_of_tiles])
    second[1], tables_of_tiles = held[0], held[1:]
    early.update((p, over(block, *p)) for p, block in zip(early_pairs, blocks))
    spans = [(0, cut), (cut, bands)]
    hops = [1, 2, 3]
    plan = [[(0, z, *span) for span in spans for z in range(time_count)]]
    plan += [[(1, z, *span) for span in spans for z in hops], [(1, 0, *span) for span in spans]]
    near, far, home = filtered(1, second, plan)
    blocks, (near,) = after([early[p] for p in late_pairs], [near])
    early.update((p, over(block, *p)) for p, block in zip(late_pairs, blocks))
    (far,), held = after([far], [early[p] for p in early_pairs[:4]])
    early.update(zip(early_pairs[:4], held))
    far = over(far, 1, 0)
    (home,), (far,) = after([home], [far])
    home = over(home, 1, 0)
    low, high = [], []
    for mixed, (first_band, last_band), part in ((low, spans[0], 0), (high, spans[1], 1)):
        count = last_band - first_band

        def piece(value, index, pieces):
            start = part * pieces * cut + index * count
            return value[start : start + count]

        mixed.append(columns(piece(near, 0, 4), piece(home, 0, 1)))
        mixed += [columns(piece(near, z, 4), piece(far, z - 1, 3)) for z in hops]
    blocks, held = after(low[1:], [early[p] for p in late_pairs[:1]])
    early.update(zip(late_pairs[:1], held))
    moved = {z: over(blocks[z - 1], 0, z) for z in (2, 1, 3)}
    low = [low[0]] + [moved[z] for z in (1, 2, 3)]

    def with_other(values):
        return [side for v in values for side in (v, travel(v, ("pol",), (1,)))]

    early = with_other([jnp.stack([early[p] for p in pairs])])
    blocks, held = after(high[1:], [low[2], low[1], early[1]])
    low[2], low[1], early[1] = held
    moved = {z: over(blocks[z - 1], 0, z) for z in (2, 1, 3)}
    high = [high[0]] + [moved[z] for z in (1, 2, 3)]
    low = jnp.stack(low).reshape(2 * time_count, cut, 2, ROWS, LANES)
    visibility = correlate_tiles(
        place, tables_of_tiles, early + with_other([low]),
        [0, 0], width, 0, cut, bands, None,
    )
    high, (visibility,) = after(high, [visibility])
    high = jnp.stack(high).reshape(2 * time_count, rest, 2, ROWS, LANES)
    return correlate_tiles(
        place, tables_of_tiles, early + with_other([high]),
        [cut, 0], width, cut, rest, bands, visibility,
    )


def on_device(voltages, taps_filter, tile_a, tile_b, tile_owner, tile_flags):
    taps, length = taps_filter.shape
    frames = voltages.shape[3] // length
    time_count = lax.axis_size("tm")
    fits = (
        length == RADIX * LANES
        and AVG * time_count * frames == LANES
        and 2 * tile_a.shape[1] == LANES
        and voltages.shape[2] == 2 * time_count * ROWS
        and (lax.axis_size("chan"), time_count) == (2, 4)
    )
    form = on_device_chunks if fits else on_device_any
    return form(voltages, taps_filter, tile_a, tile_b, tile_owner, tile_flags)


def solution(mesh):
    return jax.shard_map(
        on_device,
        mesh=mesh,
        in_specs=(P("grp", "pol", "chan", "tm"), P(), P(), P(), P(), P()),
        out_specs=P("pol", ("chan", "tm"), "grp", None, None, None),
        check_vma=False,
    )
```

```python
import math

import jax
import jax.numpy as jnp
import numpy as np
from jax import lax
from jax.experimental import pallas as pl
from jax.experimental.pallas import tpu as pltpu
from jax.sharding import PartitionSpec as P

AVG = 8
CAP = 8
RADIX = 16
LANES = 128
ROWS = 16


radix_first = 32


def from_behind(value, axis, steps):
    count = lax.axis_size(axis)
    first, last = (max(0, -steps), min(count, count - steps))
    return lax.ppermute(value, axis, [(source, source + steps) for source in range(first, last)])


def fourier(filtered):
    length = filtered.shape[-1]
    second = length // radix_first
    exact_mode = lax.Precision.HIGHEST
    grid = filtered.reshape(filtered.shape[:-1] + (radix_first, second))
    outer = jnp.arange(radix_first, dtype=jnp.int32)
    inner = jnp.arange(second, dtype=jnp.int32)
    phase_one = (
        2.0
        * math.pi
        / radix_first
        * (outer[:, None] * outer[None, :] % radix_first).astype(jnp.float32)
    )
    phase_twist = 2.0 * math.pi / length * (outer[:, None] * inner[None, :]).astype(jnp.float32)
    phase_two = (
        2.0 * math.pi / second * (inner[:, None] * inner[None, :] % second).astype(jnp.float32)
    )
    cos_one, sin_one = (jnp.cos(phase_one), jnp.sin(phase_one))
    cos_twist, sin_twist = (jnp.cos(phase_twist), jnp.sin(phase_twist))
    cos_two, sin_two = (jnp.cos(phase_two), jnp.sin(phase_two))
    first_form = "fk,stkj->stfj"
    section_re = jnp.einsum(first_form, cos_one, grid[0], precision=exact_mode) + jnp.einsum(
        first_form, sin_one, grid[1], precision=exact_mode
    )
    section_im = jnp.einsum(first_form, cos_one, grid[1], precision=exact_mode) - jnp.einsum(
        first_form, sin_one, grid[0], precision=exact_mode
    )
    turned_re = section_re * cos_twist + section_im * sin_twist
    turned_im = section_im * cos_twist - section_re * sin_twist
    second_form = "gj,stfj->stgf"
    final_re = jnp.einsum(second_form, cos_two, turned_re, precision=exact_mode) + jnp.einsum(
        second_form, sin_two, turned_im, precision=exact_mode
    )
    final_im = jnp.einsum(second_form, cos_two, turned_im, precision=exact_mode) - jnp.einsum(
        second_form, sin_two, turned_re, precision=exact_mode
    )
    joined = jnp.stack([final_re, final_im]).reshape(filtered.shape)
    return joined * (1.0 / math.sqrt(length))


def correlate(full, rows_a, rows_b, flags, group_count):
    depth = full.shape[4]
    weight = jnp.tile(flags.astype(jnp.bfloat16), depth // flags.shape[0])
    left_rows = jnp.take(full, rows_a, axis=2) * weight
    right_rows = jnp.take(full, rows_b, axis=2)
    stacked_left = jnp.stack(
        [
            jnp.concatenate([left_rows[0], left_rows[1]], axis=-1),
            jnp.concatenate([left_rows[1], -left_rows[0]], axis=-1),
        ]
    )
    joined_right = jnp.concatenate([right_rows[0], right_rows[1]], axis=-1)
    result = jnp.einsum(
        "rpank,qbnk->nrpaqb", stacked_left, joined_right, preferred_element_type=jnp.float32
    )
    width = rows_a.shape[0]
    return result.reshape(group_count, 2, 2, width, 2 * width) * (1.0 / depth)


def on_device_any(voltages, taps_filter, tile_a, tile_b, tile_owner, tile_flags):
    history = taps_filter.shape[0] - 1
    length = taps_filter.shape[1]
    stations = voltages.shape[2]
    frames = voltages.shape[3] // length
    local_blocks = voltages.reshape(2, stations, frames, length)
    hop_count = -(-history // frames)
    sending = local_blocks
    extended = local_blocks
    for hop_index in range(hop_count):
        sending = from_behind(sending, "tm", 1)
        extended = jnp.concatenate([sending, extended], axis=2)
    extended = extended[:, :, extended.shape[2] - history - frames :]
    filtered = jnp.zeros((2, stations, frames, length), jnp.float32)
    for tap_index in range(history + 1):
        start = history - tap_index
        filtered = filtered + taps_filter[tap_index] * extended[
            :, :, start : start + frames
        ].astype(jnp.float32)
    spectra = fourier(filtered).astype(jnp.bfloat16)
    chan_count = lax.axis_size("chan")
    time_count = lax.axis_size("tm")
    narrow = length // (chan_count * time_count)
    outgoing = spectra.reshape(2, stations, frames, chan_count, time_count, narrow)
    outgoing = outgoing.transpose(0, 3, 4, 5, 1, 2)
    flat = outgoing.reshape(2, chan_count * time_count, narrow, stations * frames)
    moved = lax.all_to_all(flat, ("chan", "tm"), split_axis=1, concat_axis=1, tiled=True)
    moved = moved.reshape(2, chan_count, time_count, narrow, stations, frames)
    bands = narrow // AVG
    every_station = chan_count * stations
    spectra_count = time_count * frames
    arranged = moved.transpose(0, 1, 4, 3, 2, 5).reshape(
        2, 1, every_station, bands, AVG * spectra_count
    )
    full = lax.all_gather(arranged, "pol", axis=1, tiled=True)
    position = lax.axis_index("pol")
    width = tile_a.shape[1]
    capacity = CAP
    held = tile_owner == position
    listed = jnp.nonzero(held, size=capacity, fill_value=0)[0].astype(jnp.int32)
    tally = jnp.sum(held.astype(jnp.int32))
    initial = jnp.zeros((capacity, bands, 2, 2, width, 2 * width), jnp.float32)

    def fill_slot(slot, results):
        chosen_tile = listed[slot]
        return results.at[slot].set(
            correlate(
                full, tile_a[chosen_tile], tile_b[chosen_tile], tile_flags[chosen_tile], bands
            )
        )

    visibility = lax.fori_loop(0, tally, fill_slot, initial)
    return visibility


def fourier_tables(length):
    low = np.arange(RADIX)
    lane = np.arange(LANES)
    turn = 2.0 * np.pi / length * np.outer(low, lane)
    twiddle = np.stack([np.cos(turn), np.sin(turn)]).astype(np.float32)
    angle = 2.0 * np.pi / LANES * (np.outer(lane, lane) % LANES)
    cos, sin = np.cos(angle) / math.sqrt(length), np.sin(angle) / math.sqrt(length)
    matrix = np.block([[cos, sin], [-sin, cos]]).astype(np.float32)
    high = matrix.astype(jnp.bfloat16)
    rest = (matrix - high.astype(np.float32)).astype(jnp.bfloat16)
    return twiddle, np.stack([high, rest])


def butterflies(values):
    count = len(values)
    if count == 1:
        return values
    even, odd = butterflies(values[0::2]), butterflies(values[1::2])
    first, second = [], []
    for index in range(count // 2):
        (a, b), (c, d) = even[index], odd[index]
        if index == 0:
            e, f = c, d
        elif 4 * index == count:
            e, f = d, -c
        elif 8 * index == count:
            root = math.sqrt(0.5)
            e, f = (c + d) * root, (d - c) * root
        elif 8 * index == 3 * count:
            root = math.sqrt(0.5)
            e, f = (d - c) * root, -(c + d) * root
        else:
            turn = 2.0 * math.pi * index / count
            cos, sin = math.cos(turn), math.sin(turn)
            e, f = c * cos + d * sin, d * cos - c * sin
        first.append((a + e, b + f))
        second.append((a - e, b - f))
    return first + second


def channelise_kernel(frames, chunk, columns, plan, place_ref, own_ref, *refs):
    sources = refs[-6].shape[0]
    come_refs = refs[: sources - 1]
    taps_ref, twiddle_ref, matrix_ref = refs[sources - 1 : sources + 2]
    out_refs = refs[sources + 2 : -6]
    x_ref, fil_ref, zr_ref, zi_ref, w_ref, sems = refs[-6:]
    chan, tm = place_ref[0], place_ref[1]
    own_rows = pl.multiple_of((tm * (own_ref.shape[1] // (sources * ROWS)) + chunk) * ROWS, ROWS)
    copies = []
    for behind in range(sources):
        block = come_refs[behind - 1] if behind else own_ref.at[:, pl.ds(own_rows, ROWS), :]
        slot = lax.rem(tm - behind + sources, sources)
        copies.append(pltpu.make_async_copy(block, x_ref.at[slot], sems.at[behind]))
    for copy in copies:
        copy.start()
    for copy in copies:
        copy.wait()
    spectra = sources * frames
    length = taps_ref.shape[1]
    taps = taps_ref.shape[0]
    depth = RADIX * spectra
    z_refs = (zr_ref, zi_ref)

    @pl.loop(0, RADIX)
    def _(section):
        at = pl.multiple_of(section * LANES, LANES)
        weights = [taps_ref[pl.ds(m, 1), pl.ds(at, LANES)] for m in range(taps)]
        for part in range(2):
            blocks = []
            for t in range(spectra):
                lane = pl.multiple_of((t % frames) * length + section * LANES, LANES)
                blocks.append(x_ref[t // frames, part, :, pl.ds(lane, LANES)].astype(jnp.float32))
            for t in range(spectra):
                total = weights[0] * blocks[t]
                for m in range(1, min(t + 1, taps)):
                    total = total + weights[m] * blocks[t - m]
                fil_ref[section, t, part] = total

    @pl.loop(0, spectra)
    def _(t):
        for half in range(ROWS // 8):
            values = [
                tuple(fil_ref[section, t, part, pl.ds(half * 8, 8), :] for part in range(2))
                for section in range(RADIX)
            ]
            for low, (re, im) in enumerate(butterflies(values)):
                if low:
                    cos = twiddle_ref[0, pl.ds(low, 1), :]
                    sin = twiddle_ref[1, pl.ds(low, 1), :]
                    re, im = re * cos + im * sin, im * cos - re * sin
                rows = pl.ds(half * 8 * depth + low * spectra + t, 8, stride=depth)
                zr_ref[rows, :] = re
                zi_ref[rows, :] = im

    form = (((1,), (1,)), ((), ()))
    high_matrix, low_matrix = matrix_ref[0], matrix_ref[1]
    halves = depth // LANES

    @pl.loop(0, ROWS)
    def _(station):
        rows = pl.ds(pl.multiple_of(station * depth, depth), depth)
        value = jnp.concatenate([ref[rows, :] for ref in z_refs], axis=1)
        high = value.astype(jnp.bfloat16)
        rest = (value - high.astype(jnp.float32)).astype(jnp.bfloat16)
        total = lax.dot_general(high_matrix, high, form, preferred_element_type=jnp.float32)
        total += lax.dot_general(high_matrix, rest, form, preferred_element_type=jnp.float32)
        total += lax.dot_general(low_matrix, high, form, preferred_element_type=jnp.float32)
        for half in range(halves):
            for part in range(2):
                rows = pl.ds((half * 2 + part) * ROWS + station, LANES, stride=halves * 2 * ROWS)
                w_ref[rows, :] = total[
                    part * LANES : (part + 1) * LANES, half * LANES : (half + 1) * LANES
                ]

    share = w_ref.shape[0] // (columns * sources)
    band_rows = 2 * ROWS
    piece = 4 * band_rows
    for blocks, out_ref in zip(plan, out_refs):
        at = 0
        for across, along, start, stop in blocks:
            owner = lax.rem(chan + across, columns) * sources + lax.rem(tm + along, sources)
            for row in range(start * band_rows, stop * band_rows, piece):
                rows = pl.ds(pl.multiple_of(owner * share + row, piece), piece)
                out_ref[at : at + piece, :] = w_ref[rows, :].astype(jnp.bfloat16)
                at += piece


def channelise(place, chunk, voltages, come, taps_filter, tables, frames, columns, plan):
    sources = 1 + len(come)
    length = taps_filter.shape[1]
    spectra = sources * frames
    twiddle, matrix = tables
    out_rows = length // AVG * 2 * ROWS
    whole = pl.BlockSpec(memory_space=pltpu.VMEM)
    counts = [sum(stop - start for _, _, start, stop in blocks) for blocks in plan]
    flat = pl.pallas_call(
        lambda *refs: channelise_kernel(frames, chunk, columns, plan, *refs),
        out_shape=[
            jax.ShapeDtypeStruct((count * 2 * ROWS, LANES), jnp.bfloat16) for count in counts
        ],
        in_specs=[pl.BlockSpec(memory_space=pltpu.SMEM)]
        + [pl.BlockSpec(memory_space=pl.ANY)] * sources
        + [whole] * 3,
        out_specs=[whole] * len(plan),
        scratch_shapes=[
            pltpu.VMEM((sources, 2, ROWS, frames * length), jnp.bfloat16),
            pltpu.VMEM((RADIX, spectra, 2, ROWS, LANES), jnp.float32),
            pltpu.VMEM((ROWS * RADIX * spectra, LANES), jnp.float32),
            pltpu.VMEM((ROWS * RADIX * spectra, LANES), jnp.float32),
            pltpu.VMEM((out_rows, LANES), jnp.float32),
            pltpu.SemaphoreType.DMA((sources,)),
        ],
        compiler_params=pltpu.CompilerParams(vmem_limit_bytes=40 * 2**20),
        cost_estimate=pl.CostEstimate(
            flops=9 * 10**9, bytes_accessed=4 * 2**20, transcendentals=0
        ),
        name="channelise",
    )(place, voltages, *come, taps_filter, jnp.asarray(twiddle), jnp.asarray(matrix))
    return [piece.reshape(count, 2, ROWS, LANES) for piece, count in zip(flat, counts)]


def correlate_kernel(starts, width, place_ref, left_sel_ref, right_sel_ref, weight_ref, *refs):
    x_refs, (out_ref, x_all, *rows_refs, sems) = refs[: 2 * len(starts)], refs[-7:]
    tiles = out_ref.shape[0]
    step = pl.program_id(0)
    bands = x_all.shape[2]
    spans = [(0, 2), (2, bands)]

    def copies(span):
        first, last = spans[span]
        block = 0
        for index, start in enumerate(starts):
            blocks = x_refs[2 * index].shape[0]
            for side in range(2):
                yield pltpu.make_async_copy(
                    x_refs[2 * index + side].at[:, pl.ds(start + first, last - first)],
                    x_all.at[
                        lax.rem(place_ref[2] + side, 2),
                        pl.ds(block, blocks),
                        pl.ds(first, last - first),
                    ],
                    sems.at[span, 2 * index + side],
                )
            block += blocks

    lower = lax.broadcasted_iota(jnp.int32, (1, 2 * width), 1) < width

    def gather(band, left_ref, right_ref):
        right = []
        for pol in range(2):
            lanes = slice(pol * 2 * LANES, (pol + 1) * 2 * LANES)
            value = jnp.concatenate(
                [
                    jnp.concatenate([x_all[pol, block, band, part] for part in range(2)], axis=1)
                    for block in range(x_all.shape[1])
                ]
            )
            left = jnp.dot(left_sel_ref[...], value, preferred_element_type=jnp.float32)
            for tile in range(tiles):
                rows = slice(tile * width, (tile + 1) * width)
                scaled = left[rows] * weight_ref[pl.ds(tile, 1), :]
                left_ref[rows, lanes] = scaled.astype(jnp.bfloat16)
            right.append(
                lax.dot_general(
                    value,
                    right_sel_ref[pol],
                    (((0,), (0,)), ((), ())),
                    preferred_element_type=jnp.float32,
                )
            )
        for pair in range(tiles // 2):
            first, second = (v[:, pair * 2 * width : (pair + 1) * 2 * width] for v in right)
            even = jnp.where(lower, first, second)
            odd = pltpu.roll(jnp.where(lower, second, first), width, 1)
            right_ref[2 * pair] = even.astype(jnp.bfloat16)
            right_ref[2 * pair + 1] = odd.astype(jnp.bfloat16)

    def multiply(number, left_ref, right_ref):
        for tile in range(tiles):
            rows = slice(tile * width, (tile + 1) * width)
            left = jnp.concatenate(
                [left_ref[rows, lanes : lanes + 2 * LANES] for lanes in (0, 2 * LANES)]
            )
            right = right_ref[tile]
            turned = jnp.concatenate([-right[LANES:], right[:LANES]])
            both = jnp.concatenate([right, turned], axis=1)
            result = jnp.dot(left, both, preferred_element_type=jnp.float32)
            for part in range(2):
                out_ref[tile, number, part] = result[
                    :, part * 2 * width : (part + 1) * 2 * width
                ].reshape(2, width, 2 * width)

    even, odd = rows_refs[:2], rows_refs[2:]

    @pl.when(step == 0)
    def _():
        for span in range(2):
            for copy in copies(span):
                copy.start()
        for copy in copies(0):
            copy.wait()
        gather(0, *even)
        for copy in copies(1):
            copy.wait()

    gather(2 * step + 1, *odd)
    multiply(0, *even)
    gather(jnp.minimum(2 * step + 2, bands - 1), *even)
    multiply(1, *odd)


def correlate_tiles(place, tables, pieces, starts, width, first, count, bands, earlier):
    left_select, _, weight = tables
    tiles = weight.shape[0]
    whole = pl.BlockSpec(memory_space=pltpu.VMEM)
    more = [] if earlier is None else [earlier]
    rows = [
        pltpu.VMEM((tiles * width, 4 * LANES), jnp.bfloat16),
        pltpu.VMEM((tiles, 2 * LANES, 2 * width), jnp.bfloat16),
    ]
    return pl.pallas_call(
        lambda *refs: correlate_kernel(starts, width, *refs),
        grid=(count // 2,),
        out_shape=jax.ShapeDtypeStruct((tiles, bands, 2, 2, width, 2 * width), jnp.float32),
        in_specs=[pl.BlockSpec(memory_space=pltpu.SMEM)]
        + [whole] * len(tables)
        + [pl.BlockSpec(memory_space=pl.ANY)] * (len(pieces) + len(more)),
        out_specs=pl.BlockSpec(
            (tiles, 2, 2, 2, width, 2 * width), lambda g: (0, g + first // 2, 0, 0, 0, 0)
        ),
        scratch_shapes=[
            pltpu.VMEM((2, left_select.shape[1] // ROWS, count, 2, ROWS, LANES), jnp.bfloat16),
            *rows,
            *rows,
            pltpu.SemaphoreType.DMA((2, len(pieces))),
        ],
        input_output_aliases={1 + len(tables) + len(pieces): 0} if more else {},
        compiler_params=pltpu.CompilerParams(vmem_limit_bytes=32 * 2**20),
        cost_estimate=pl.CostEstimate(
            flops=13 * 10**9 * count // bands,
            bytes_accessed=42 * 2**20 * count // bands,
            transcendentals=0,
        ),
        name="correlate",
    )(place, *tables, *pieces, *more)


def tile_tables(tile_a, tile_b, tile_owner, tile_flags, row_of):
    tiles = tile_owner.shape[0]
    held = tile_owner == lax.axis_index("pol")
    order = jnp.arange(tiles, dtype=jnp.int32)
    rank = jnp.sum((held[None, :] & (order[None, :] < order[:, None])).astype(jnp.int32), axis=1)
    slots = jnp.arange(CAP, dtype=jnp.int32)
    pick = (held[None, :] & (rank[None, :] == slots[:, None])).astype(jnp.int32)
    sides = jnp.stack([row_of(tile_a), row_of(tile_b)], axis=1) + 1
    rows = jnp.sum(pick[:, :, None, None] * sides[None], axis=1) - 1
    flags = jnp.sum(pick[:, :, None] * tile_flags[None], axis=1).astype(jnp.float32)
    return rows, flags


def on_device_chunks(voltages, taps_filter, tile_a, tile_b, tile_owner, tile_flags):
    length = taps_filter.shape[1]
    stations = voltages.shape[2]
    frames = voltages.shape[3] // length
    chan_count, time_count = lax.axis_size("chan"), lax.axis_size("tm")
    owners = chan_count * time_count
    chunk_count = stations // (time_count * ROWS)
    width = tile_a.shape[1]
    bands = length // AVG // owners
    tables = fourier_tables(length)

    chan, tm = lax.axis_index("chan"), lax.axis_index("tm")
    place = jnp.stack([chan, tm, lax.axis_index("pol")]).astype(jnp.int32)

    def row_of(station):
        column, rest = station // stations, station % stations
        block, inside = rest // (chunk_count * ROWS), rest % (chunk_count * ROWS)
        across = (chan - column) % chan_count
        behind = (tm - block) % time_count
        piece = behind * chan_count + across
        return ((inside // ROWS) * owners + piece) * ROWS + inside % ROWS

    rows, flags = tile_tables(tile_a, tile_b, tile_owner, tile_flags, row_of)
    total_rows = chunk_count * owners * ROWS
    station_rows = jnp.arange(total_rows, dtype=jnp.int32)
    left_rows = rows[:, 0].reshape(-1)
    left_select = (left_rows[:, None] == station_rows).astype(jnp.bfloat16)
    right_rows = rows[:, 1].reshape(CAP // 2, 2, width)
    right_rows = jnp.stack([right_rows, right_rows[:, ::-1]]).reshape(2, 1, -1)
    right_select = (right_rows == station_rows[:, None]).astype(jnp.bfloat16)
    depth = AVG * time_count * frames
    weight = jnp.tile(flags * (1.0 / depth), (1, 2 * AVG))
    tables_of_tiles = [left_select, right_select, weight]

    samples = voltages.reshape(2, stations, frames * length)

    def travel(value, axes, distances):
        sizes = [lax.axis_size(axis) for axis in axes]
        pairs = []
        for index in np.ndindex(*sizes):
            target = [(i + d) % n for i, d, n in zip(index, distances, sizes)]
            pairs.append(tuple(int(np.ravel_multi_index(x, sizes)) for x in (index, target)))
        return lax.ppermute(value, axes, pairs)

    def after(values, earlier):
        return lax.optimization_barrier((list(values), list(earlier)))

    def block_for(values, chunk, distance):
        first = ((tm + distance) % time_count * chunk_count + chunk) * ROWS
        return lax.dynamic_slice(values, (0, first, 0), (2, ROWS, frames * length))

    def filtered(chunk, arrived, plan):
        return channelise(
            place, chunk, samples, arrived, taps_filter, tables, frames, chan_count, plan
        )

    def over(value, across, along):
        return travel(value, ("chan", "tm"), (across, along))

    def columns(near, far):
        return jnp.stack([near, far])

    cut = bands * 5 // 8
    rest = bands - cut
    pairs = [(x, z) for z in range(time_count) for x in range(chan_count)]
    early_pairs = [(x, z) for z in (1, 3) for x in range(2)]
    late_pairs = [(0, 2), (1, 2), (1, 0)]

    (one,), (values,) = after([block_for(samples, 0, 1)], [samples])
    two, three = (block_for(values, 0, distance) for distance in (2, 3))
    one, two = over(one, 0, 1), over(two, 0, 2)
    (three,), (one,) = after([three], [one])
    three = over(three, 0, 3)
    blocks = [block_for(values, 1, distance) for distance in (1, 2, 3)]
    blocks[:1], (two,) = after(blocks[:1], [two])
    blocks[2:], (three,) = after(blocks[2:], [three])
    first = [one, two, three]
    one, three = over(blocks[0], 0, 1), over(blocks[2], 0, 3)
    (two,), (one,) = after(blocks[1:2], [one])
    second = [one, over(two, 0, 2), three]

    plan = [[(x, z, 0, bands)] for x, z in pairs]
    early = dict(zip(pairs, filtered(0, first, plan)))
    blocks, held = after([early[p] for p in early_pairs], [second[1], *tables_of_tiles])
    second[1], tables_of_tiles = held[0], held[1:]
    early.update((p, over(block, *p)) for p, block in zip(early_pairs, blocks))
    spans = [(0, cut), (cut, bands)]
    hops = [1, 2, 3]
    plan = [[(0, z, *span) for span in spans for z in range(time_count)]]
    plan += [[(1, z, *span) for span in spans for z in hops], [(1, 0, *span) for span in spans]]
    near, far, home = filtered(1, second, plan)
    blocks, (near,) = after([early[p] for p in late_pairs], [near])
    early.update((p, over(block, *p)) for p, block in zip(late_pairs, blocks))
    (far,), held = after([far], [early[p] for p in early_pairs[:4]])
    early.update(zip(early_pairs[:4], held))
    far = over(far, 1, 0)
    def mix(start, index, other_start, other, count):
        first, second = start + index * count, other_start + index * count
        return columns(near[first : first + count], other[second : second + count])

    blocks = {z: mix(0, z, -cut, far, cut) for z in hops}
    (blocks[1], blocks[3]), held = after([blocks[1], blocks[3]], [early[p] for p in late_pairs[:1]])
    early.update(zip(late_pairs[:1], held))
    one, three = over(blocks[1], 0, 1), over(blocks[3], 0, 3)
    (block,), (one,) = after([blocks[2]], [one])
    two = over(block, 0, 2)
    (home,), (three,) = after([home], [three])
    home = over(home, 1, 0)
    low = [mix(0, 0, 0, home, cut), one, two, three]
    high = [mix(time_count * cut, 0, cut, home, rest)]
    high += [mix(time_count * cut, z, 3 * cut - rest, far, rest) for z in hops]

    def with_other(values):
        return [side for v in values for side in (v, travel(v, ("pol",), (1,)))]

    early = with_other([jnp.stack([early[p] for p in pairs])])
    blocks, held = after(high[1:], [low[2], low[1], early[1]])
    low[2], low[1], early[1] = held
    moved = {z: over(blocks[z - 1], 0, z) for z in (2, 1, 3)}
    high = [high[0]] + [moved[z] for z in (1, 2, 3)]
    low = jnp.stack(low).reshape(2 * time_count, cut, 2, ROWS, LANES)
    visibility = correlate_tiles(
        place, tables_of_tiles, early + with_other([low]),
        [0, 0], width, 0, cut, bands, None,
    )
    high, (visibility,) = after(high, [visibility])
    high = jnp.stack(high).reshape(2 * time_count, rest, 2, ROWS, LANES)
    return correlate_tiles(
        place, tables_of_tiles, early + with_other([high]),
        [cut, 0], width, cut, rest, bands, visibility,
    )


def on_device(voltages, taps_filter, tile_a, tile_b, tile_owner, tile_flags):
    taps, length = taps_filter.shape
    frames = voltages.shape[3] // length
    time_count = lax.axis_size("tm")
    fits = (
        length == RADIX * LANES
        and AVG * time_count * frames == LANES
        and 2 * tile_a.shape[1] == LANES
        and voltages.shape[2] == 2 * time_count * ROWS
        and (lax.axis_size("chan"), time_count) == (2, 4)
    )
    form = on_device_chunks if fits else on_device_any
    return form(voltages, taps_filter, tile_a, tile_b, tile_owner, tile_flags)


def solution(mesh):
    return jax.shard_map(
        on_device,
        mesh=mesh,
        in_specs=(P("grp", "pol", "chan", "tm"), P(), P(), P(), P(), P()),
        out_specs=P("pol", ("chan", "tm"), "grp", None, None, None),
        check_vma=False,
    )
```

```python
import math

import jax
import jax.numpy as jnp
import numpy as np
from jax import lax
from jax.experimental import pallas as pl
from jax.experimental.pallas import tpu as pltpu
from jax.sharding import PartitionSpec as P

AVG = 8
CAP = 8
RADIX = 16
LANES = 128
ROWS = 16


radix_first = 32


def from_behind(value, axis, steps):
    count = lax.axis_size(axis)
    first, last = (max(0, -steps), min(count, count - steps))
    return lax.ppermute(value, axis, [(source, source + steps) for source in range(first, last)])


def fourier(filtered):
    length = filtered.shape[-1]
    second = length // radix_first
    exact_mode = lax.Precision.HIGHEST
    grid = filtered.reshape(filtered.shape[:-1] + (radix_first, second))
    outer = jnp.arange(radix_first, dtype=jnp.int32)
    inner = jnp.arange(second, dtype=jnp.int32)
    phase_one = (
        2.0
        * math.pi
        / radix_first
        * (outer[:, None] * outer[None, :] % radix_first).astype(jnp.float32)
    )
    phase_twist = 2.0 * math.pi / length * (outer[:, None] * inner[None, :]).astype(jnp.float32)
    phase_two = (
        2.0 * math.pi / second * (inner[:, None] * inner[None, :] % second).astype(jnp.float32)
    )
    cos_one, sin_one = (jnp.cos(phase_one), jnp.sin(phase_one))
    cos_twist, sin_twist = (jnp.cos(phase_twist), jnp.sin(phase_twist))
    cos_two, sin_two = (jnp.cos(phase_two), jnp.sin(phase_two))
    first_form = "fk,stkj->stfj"
    section_re = jnp.einsum(first_form, cos_one, grid[0], precision=exact_mode) + jnp.einsum(
        first_form, sin_one, grid[1], precision=exact_mode
    )
    section_im = jnp.einsum(first_form, cos_one, grid[1], precision=exact_mode) - jnp.einsum(
        first_form, sin_one, grid[0], precision=exact_mode
    )
    turned_re = section_re * cos_twist + section_im * sin_twist
    turned_im = section_im * cos_twist - section_re * sin_twist
    second_form = "gj,stfj->stgf"
    final_re = jnp.einsum(second_form, cos_two, turned_re, precision=exact_mode) + jnp.einsum(
        second_form, sin_two, turned_im, precision=exact_mode
    )
    final_im = jnp.einsum(second_form, cos_two, turned_im, precision=exact_mode) - jnp.einsum(
        second_form, sin_two, turned_re, precision=exact_mode
    )
    joined = jnp.stack([final_re, final_im]).reshape(filtered.shape)
    return joined * (1.0 / math.sqrt(length))


def correlate(full, rows_a, rows_b, flags, group_count):
    depth = full.shape[4]
    weight = jnp.tile(flags.astype(jnp.bfloat16), depth // flags.shape[0])
    left_rows = jnp.take(full, rows_a, axis=2) * weight
    right_rows = jnp.take(full, rows_b, axis=2)
    stacked_left = jnp.stack(
        [
            jnp.concatenate([left_rows[0], left_rows[1]], axis=-1),
            jnp.concatenate([left_rows[1], -left_rows[0]], axis=-1),
        ]
    )
    joined_right = jnp.concatenate([right_rows[0], right_rows[1]], axis=-1)
    result = jnp.einsum(
        "rpank,qbnk->nrpaqb", stacked_left, joined_right, preferred_element_type=jnp.float32
    )
    width = rows_a.shape[0]
    return result.reshape(group_count, 2, 2, width, 2 * width) * (1.0 / depth)


def on_device_any(voltages, taps_filter, tile_a, tile_b, tile_owner, tile_flags):
    history = taps_filter.shape[0] - 1
    length = taps_filter.shape[1]
    stations = voltages.shape[2]
    frames = voltages.shape[3] // length
    local_blocks = voltages.reshape(2, stations, frames, length)
    hop_count = -(-history // frames)
    sending = local_blocks
    extended = local_blocks
    for hop_index in range(hop_count):
        sending = from_behind(sending, "tm", 1)
        extended = jnp.concatenate([sending, extended], axis=2)
    extended = extended[:, :, extended.shape[2] - history - frames :]
    filtered = jnp.zeros((2, stations, frames, length), jnp.float32)
    for tap_index in range(history + 1):
        start = history - tap_index
        filtered = filtered + taps_filter[tap_index] * extended[
            :, :, start : start + frames
        ].astype(jnp.float32)
    spectra = fourier(filtered).astype(jnp.bfloat16)
    chan_count = lax.axis_size("chan")
    time_count = lax.axis_size("tm")
    narrow = length // (chan_count * time_count)
    outgoing = spectra.reshape(2, stations, frames, chan_count, time_count, narrow)
    outgoing = outgoing.transpose(0, 3, 4, 5, 1, 2)
    flat = outgoing.reshape(2, chan_count * time_count, narrow, stations * frames)
    moved = lax.all_to_all(flat, ("chan", "tm"), split_axis=1, concat_axis=1, tiled=True)
    moved = moved.reshape(2, chan_count, time_count, narrow, stations, frames)
    bands = narrow // AVG
    every_station = chan_count * stations
    spectra_count = time_count * frames
    arranged = moved.transpose(0, 1, 4, 3, 2, 5).reshape(
        2, 1, every_station, bands, AVG * spectra_count
    )
    full = lax.all_gather(arranged, "pol", axis=1, tiled=True)
    position = lax.axis_index("pol")
    width = tile_a.shape[1]
    capacity = CAP
    held = tile_owner == position
    listed = jnp.nonzero(held, size=capacity, fill_value=0)[0].astype(jnp.int32)
    tally = jnp.sum(held.astype(jnp.int32))
    initial = jnp.zeros((capacity, bands, 2, 2, width, 2 * width), jnp.float32)

    def fill_slot(slot, results):
        chosen_tile = listed[slot]
        return results.at[slot].set(
            correlate(
                full, tile_a[chosen_tile], tile_b[chosen_tile], tile_flags[chosen_tile], bands
            )
        )

    visibility = lax.fori_loop(0, tally, fill_slot, initial)
    return visibility


def fourier_tables(length):
    low = np.arange(RADIX)
    lane = np.arange(LANES)
    turn = 2.0 * np.pi / length * np.outer(low, lane)
    twiddle = np.stack([np.cos(turn), np.sin(turn)]).astype(np.float32)
    angle = 2.0 * np.pi / LANES * (np.outer(lane, lane) % LANES)
    cos, sin = np.cos(angle) / math.sqrt(length), np.sin(angle) / math.sqrt(length)
    matrix = np.block([[cos, sin], [-sin, cos]]).astype(np.float32)
    high = matrix.astype(jnp.bfloat16)
    rest = (matrix - high.astype(np.float32)).astype(jnp.bfloat16)
    return twiddle, np.stack([high, rest])


def butterflies(values):
    count = len(values)
    if count == 1:
        return values
    even, odd = butterflies(values[0::2]), butterflies(values[1::2])
    first, second = [], []
    for index in range(count // 2):
        (a, b), (c, d) = even[index], odd[index]
        if index == 0:
            e, f = c, d
        elif 4 * index == count:
            e, f = d, -c
        elif 8 * index == count:
            root = math.sqrt(0.5)
            e, f = (c + d) * root, (d - c) * root
        elif 8 * index == 3 * count:
            root = math.sqrt(0.5)
            e, f = (d - c) * root, -(c + d) * root
        else:
            turn = 2.0 * math.pi * index / count
            cos, sin = math.cos(turn), math.sin(turn)
            e, f = c * cos + d * sin, d * cos - c * sin
        first.append((a + e, b + f))
        second.append((a - e, b - f))
    return first + second


def channelise_kernel(frames, chunk, columns, plan, place_ref, own_ref, *refs):
    sources = refs[-6].shape[0]
    come_refs = refs[: sources - 1]
    taps_ref, twiddle_ref, matrix_ref = refs[sources - 1 : sources + 2]
    out_refs = refs[sources + 2 : -6]
    x_ref, fil_ref, zr_ref, zi_ref, w_ref, sems = refs[-6:]
    chan, tm = place_ref[0], place_ref[1]
    own_rows = pl.multiple_of((tm * (own_ref.shape[1] // (sources * ROWS)) + chunk) * ROWS, ROWS)
    copies = []
    for behind in range(sources):
        block = come_refs[behind - 1] if behind else own_ref.at[:, pl.ds(own_rows, ROWS), :]
        slot = lax.rem(tm - behind + sources, sources)
        copies.append(pltpu.make_async_copy(block, x_ref.at[slot], sems.at[behind]))
    for copy in copies:
        copy.start()
    for copy in copies:
        copy.wait()
    spectra = sources * frames
    length = taps_ref.shape[1]
    taps = taps_ref.shape[0]
    depth = RADIX * spectra
    z_refs = (zr_ref, zi_ref)

    @pl.loop(0, RADIX)
    def _(section):
        at = pl.multiple_of(section * LANES, LANES)
        weights = [taps_ref[pl.ds(m, 1), pl.ds(at, LANES)] for m in range(taps)]
        for part in range(2):
            blocks = []
            for t in range(spectra):
                lane = pl.multiple_of((t % frames) * length + section * LANES, LANES)
                blocks.append(x_ref[t // frames, part, :, pl.ds(lane, LANES)].astype(jnp.float32))
            for t in range(spectra):
                total = weights[0] * blocks[t]
                for m in range(1, min(t + 1, taps)):
                    total = total + weights[m] * blocks[t - m]
                fil_ref[section, t, part] = total

    @pl.loop(0, spectra)
    def _(t):
        for half in range(ROWS // 8):
            values = [
                tuple(fil_ref[section, t, part, pl.ds(half * 8, 8), :] for part in range(2))
                for section in range(RADIX)
            ]
            for low, (re, im) in enumerate(butterflies(values)):
                if low:
                    cos = twiddle_ref[0, pl.ds(low, 1), :]
                    sin = twiddle_ref[1, pl.ds(low, 1), :]
                    re, im = re * cos + im * sin, im * cos - re * sin
                rows = pl.ds(half * 8 * depth + low * spectra + t, 8, stride=depth)
                zr_ref[rows, :] = re
                zi_ref[rows, :] = im

    form = (((1,), (1,)), ((), ()))
    high_matrix, low_matrix = matrix_ref[0], matrix_ref[1]
    halves = depth // LANES

    @pl.loop(0, ROWS)
    def _(station):
        rows = pl.ds(pl.multiple_of(station * depth, depth), depth)
        value = jnp.concatenate([ref[rows, :] for ref in z_refs], axis=1)
        high = value.astype(jnp.bfloat16)
        rest = (value - high.astype(jnp.float32)).astype(jnp.bfloat16)
        total = lax.dot_general(high_matrix, high, form, preferred_element_type=jnp.float32)
        total += lax.dot_general(high_matrix, rest, form, preferred_element_type=jnp.float32)
        total += lax.dot_general(low_matrix, high, form, preferred_element_type=jnp.float32)
        for half in range(halves):
            for part in range(2):
                rows = pl.ds((half * 2 + part) * ROWS + station, LANES, stride=halves * 2 * ROWS)
                w_ref[rows, :] = total[
                    part * LANES : (part + 1) * LANES, half * LANES : (half + 1) * LANES
                ]

    share = w_ref.shape[0] // (columns * sources)
    band_rows = 2 * ROWS
    piece = 2 * band_rows
    for blocks, out_ref in zip(plan, out_refs):
        at = 0
        for across, along, start, stop in blocks:
            owner = lax.rem(chan + across, columns) * sources + lax.rem(tm + along, sources)
            for row in range(start * band_rows, stop * band_rows, piece):
                rows = pl.ds(pl.multiple_of(owner * share + row, piece), piece)
                out_ref[at : at + piece, :] = w_ref[rows, :].astype(jnp.bfloat16)
                at += piece


def channelise(place, chunk, voltages, come, taps_filter, tables, frames, columns, plan):
    sources = 1 + len(come)
    length = taps_filter.shape[1]
    spectra = sources * frames
    twiddle, matrix = tables
    out_rows = length // AVG * 2 * ROWS
    whole = pl.BlockSpec(memory_space=pltpu.VMEM)
    counts = [sum(stop - start for _, _, start, stop in blocks) for blocks in plan]
    flat = pl.pallas_call(
        lambda *refs: channelise_kernel(frames, chunk, columns, plan, *refs),
        out_shape=[
            jax.ShapeDtypeStruct((count * 2 * ROWS, LANES), jnp.bfloat16) for count in counts
        ],
        in_specs=[pl.BlockSpec(memory_space=pltpu.SMEM)]
        + [pl.BlockSpec(memory_space=pl.ANY)] * sources
        + [whole] * 3,
        out_specs=[whole] * len(plan),
        scratch_shapes=[
            pltpu.VMEM((sources, 2, ROWS, frames * length), jnp.bfloat16),
            pltpu.VMEM((RADIX, spectra, 2, ROWS, LANES), jnp.float32),
            pltpu.VMEM((ROWS * RADIX * spectra, LANES), jnp.float32),
            pltpu.VMEM((ROWS * RADIX * spectra, LANES), jnp.float32),
            pltpu.VMEM((out_rows, LANES), jnp.float32),
            pltpu.SemaphoreType.DMA((sources,)),
        ],
        compiler_params=pltpu.CompilerParams(vmem_limit_bytes=40 * 2**20),
        cost_estimate=pl.CostEstimate(
            flops=9 * 10**9, bytes_accessed=4 * 2**20, transcendentals=0
        ),
        name="channelise",
    )(place, voltages, *come, taps_filter, jnp.asarray(twiddle), jnp.asarray(matrix))
    return [piece.reshape(count, 2, ROWS, LANES) for piece, count in zip(flat, counts)]


def correlate_kernel(starts, width, place_ref, left_sel_ref, right_sel_ref, weight_ref, *refs):
    x_refs, (out_ref, x_all, *rows_refs, sems) = refs[: 2 * len(starts)], refs[-7:]
    tiles = out_ref.shape[0]
    step = pl.program_id(0)
    bands = x_all.shape[2]
    spans = [(0, 2), (2, bands)]

    def copies(span):
        first, last = spans[span]
        block = 0
        for index, start in enumerate(starts):
            blocks = x_refs[2 * index].shape[0]
            for side in range(2):
                yield pltpu.make_async_copy(
                    x_refs[2 * index + side].at[:, pl.ds(start + first, last - first)],
                    x_all.at[
                        lax.rem(place_ref[2] + side, 2),
                        pl.ds(block, blocks),
                        pl.ds(first, last - first),
                    ],
                    sems.at[span, 2 * index + side],
                )
            block += blocks

    lower = lax.broadcasted_iota(jnp.int32, (1, 2 * width), 1) < width

    def gather(band, left_ref, right_ref):
        right = []
        for pol in range(2):
            lanes = slice(pol * 2 * LANES, (pol + 1) * 2 * LANES)
            value = jnp.concatenate(
                [
                    jnp.concatenate([x_all[pol, block, band, part] for part in range(2)], axis=1)
                    for block in range(x_all.shape[1])
                ]
            )
            left = jnp.dot(left_sel_ref[...], value, preferred_element_type=jnp.float32)
            for tile in range(tiles):
                rows = slice(tile * width, (tile + 1) * width)
                scaled = left[rows] * weight_ref[pl.ds(tile, 1), :]
                left_ref[rows, lanes] = scaled.astype(jnp.bfloat16)
            right.append(
                lax.dot_general(
                    value,
                    right_sel_ref[pol],
                    (((0,), (0,)), ((), ())),
                    preferred_element_type=jnp.float32,
                )
            )
        for pair in range(tiles // 2):
            first, second = (v[:, pair * 2 * width : (pair + 1) * 2 * width] for v in right)
            even = jnp.where(lower, first, second)
            odd = pltpu.roll(jnp.where(lower, second, first), width, 1)
            right_ref[2 * pair] = even.astype(jnp.bfloat16)
            right_ref[2 * pair + 1] = odd.astype(jnp.bfloat16)

    def multiply(number, left_ref, right_ref):
        for tile in range(tiles):
            rows = slice(tile * width, (tile + 1) * width)
            left = jnp.concatenate(
                [left_ref[rows, lanes : lanes + 2 * LANES] for lanes in (0, 2 * LANES)]
            )
            right = right_ref[tile]
            turned = jnp.concatenate([-right[LANES:], right[:LANES]])
            both = jnp.concatenate([right, turned], axis=1)
            result = jnp.dot(left, both, preferred_element_type=jnp.float32)
            for part in range(2):
                out_ref[tile, number, part] = result[
                    :, part * 2 * width : (part + 1) * 2 * width
                ].reshape(2, width, 2 * width)

    even, odd = rows_refs[:2], rows_refs[2:]

    @pl.when(step == 0)
    def _():
        for span in range(2):
            for copy in copies(span):
                copy.start()
        for copy in copies(0):
            copy.wait()
        gather(0, *even)
        for copy in copies(1):
            copy.wait()

    gather(2 * step + 1, *odd)
    multiply(0, *even)
    gather(jnp.minimum(2 * step + 2, bands - 1), *even)
    multiply(1, *odd)


def correlate_tiles(place, tables, pieces, starts, width, first, count, bands, earlier):
    left_select, _, weight = tables
    tiles = weight.shape[0]
    whole = pl.BlockSpec(memory_space=pltpu.VMEM)
    more = [] if earlier is None else [earlier]
    rows = [
        pltpu.VMEM((tiles * width, 4 * LANES), jnp.bfloat16),
        pltpu.VMEM((tiles, 2 * LANES, 2 * width), jnp.bfloat16),
    ]
    return pl.pallas_call(
        lambda *refs: correlate_kernel(starts, width, *refs),
        grid=(count // 2,),
        out_shape=jax.ShapeDtypeStruct((tiles, bands, 2, 2, width, 2 * width), jnp.float32),
        in_specs=[pl.BlockSpec(memory_space=pltpu.SMEM)]
        + [whole] * len(tables)
        + [pl.BlockSpec(memory_space=pl.ANY)] * (len(pieces) + len(more)),
        out_specs=pl.BlockSpec(
            (tiles, 2, 2, 2, width, 2 * width), lambda g: (0, g + first // 2, 0, 0, 0, 0)
        ),
        scratch_shapes=[
            pltpu.VMEM((2, left_select.shape[1] // ROWS, count, 2, ROWS, LANES), jnp.bfloat16),
            *rows,
            *rows,
            pltpu.SemaphoreType.DMA((2, len(pieces))),
        ],
        input_output_aliases={1 + len(tables) + len(pieces): 0} if more else {},
        compiler_params=pltpu.CompilerParams(vmem_limit_bytes=32 * 2**20),
        cost_estimate=pl.CostEstimate(
            flops=13 * 10**9 * count // bands,
            bytes_accessed=42 * 2**20 * count // bands,
            transcendentals=0,
        ),
        name="correlate",
    )(place, *tables, *pieces, *more)


def tile_tables(tile_a, tile_b, tile_owner, tile_flags, row_of):
    tiles = tile_owner.shape[0]
    held = tile_owner == lax.axis_index("pol")
    order = jnp.arange(tiles, dtype=jnp.int32)
    rank = jnp.sum((held[None, :] & (order[None, :] < order[:, None])).astype(jnp.int32), axis=1)
    slots = jnp.arange(CAP, dtype=jnp.int32)
    pick = (held[None, :] & (rank[None, :] == slots[:, None])).astype(jnp.int32)
    sides = jnp.stack([row_of(tile_a), row_of(tile_b)], axis=1) + 1
    rows = jnp.sum(pick[:, :, None, None] * sides[None], axis=1) - 1
    flags = jnp.sum(pick[:, :, None] * tile_flags[None], axis=1).astype(jnp.float32)
    return rows, flags


def on_device_chunks(voltages, taps_filter, tile_a, tile_b, tile_owner, tile_flags):
    length = taps_filter.shape[1]
    stations = voltages.shape[2]
    frames = voltages.shape[3] // length
    chan_count, time_count = lax.axis_size("chan"), lax.axis_size("tm")
    owners = chan_count * time_count
    chunk_count = stations // (time_count * ROWS)
    width = tile_a.shape[1]
    bands = length // AVG // owners
    tables = fourier_tables(length)

    chan, tm = lax.axis_index("chan"), lax.axis_index("tm")
    place = jnp.stack([chan, tm, lax.axis_index("pol")]).astype(jnp.int32)

    def row_of(station):
        column, rest = station // stations, station % stations
        block, inside = rest // (chunk_count * ROWS), rest % (chunk_count * ROWS)
        across = (chan - column) % chan_count
        behind = (tm - block) % time_count
        piece = behind * chan_count + across
        return ((inside // ROWS) * owners + piece) * ROWS + inside % ROWS

    rows, flags = tile_tables(tile_a, tile_b, tile_owner, tile_flags, row_of)
    total_rows = chunk_count * owners * ROWS
    station_rows = jnp.arange(total_rows, dtype=jnp.int32)
    left_rows = rows[:, 0].reshape(-1)
    left_select = (left_rows[:, None] == station_rows).astype(jnp.bfloat16)
    right_rows = rows[:, 1].reshape(CAP // 2, 2, width)
    right_rows = jnp.stack([right_rows, right_rows[:, ::-1]]).reshape(2, 1, -1)
    right_select = (right_rows == station_rows[:, None]).astype(jnp.bfloat16)
    depth = AVG * time_count * frames
    weight = jnp.tile(flags * (1.0 / depth), (1, 2 * AVG))
    tables_of_tiles = [left_select, right_select, weight]

    samples = voltages.reshape(2, stations, frames * length)

    def travel(value, axes, distances):
        sizes = [lax.axis_size(axis) for axis in axes]
        pairs = []
        for index in np.ndindex(*sizes):
            target = [(i + d) % n for i, d, n in zip(index, distances, sizes)]
            pairs.append(tuple(int(np.ravel_multi_index(x, sizes)) for x in (index, target)))
        return lax.ppermute(value, axes, pairs)

    def after(values, earlier):
        return lax.optimization_barrier((list(values), list(earlier)))

    def block_for(values, chunk, distance):
        first = ((tm + distance) % time_count * chunk_count + chunk) * ROWS
        return lax.dynamic_slice(values, (0, first, 0), (2, ROWS, frames * length))

    def filtered(chunk, arrived, plan):
        return channelise(
            place, chunk, samples, arrived, taps_filter, tables, frames, chan_count, plan
        )

    def over(value, across, along):
        return travel(value, ("chan", "tm"), (across, along))

    def columns(near, far):
        return jnp.stack([near, far])

    cut = bands * 9 // 16
    rest = bands - cut
    pairs = [(x, z) for z in range(time_count) for x in range(chan_count)]
    early_pairs = [(x, z) for z in (1, 3) for x in range(2)]
    late_pairs = [(0, 2), (1, 2), (1, 0)]

    (one,), (values,) = after([block_for(samples, 0, 1)], [samples])
    two, three = (block_for(values, 0, distance) for distance in (2, 3))
    one, two = over(one, 0, 1), over(two, 0, 2)
    (three,), (one,) = after([three], [one])
    three = over(three, 0, 3)
    blocks = [block_for(values, 1, distance) for distance in (1, 2, 3)]
    blocks[:1], (two,) = after(blocks[:1], [two])
    blocks[2:], (three,) = after(blocks[2:], [three])
    first = [one, two, three]
    one, three = over(blocks[0], 0, 1), over(blocks[2], 0, 3)
    (two,), (one,) = after(blocks[1:2], [one])
    second = [one, over(two, 0, 2), three]

    plan = [[(x, z, 0, bands)] for x, z in pairs]
    early = dict(zip(pairs, filtered(0, first, plan)))
    blocks, held = after([early[p] for p in early_pairs], [second[1], *tables_of_tiles])
    second[1], tables_of_tiles = held[0], held[1:]
    early.update((p, over(block, *p)) for p, block in zip(early_pairs, blocks))
    spans = [(0, cut), (cut, bands)]
    hops = [1, 2, 3]
    plan = [[(0, z, *span) for span in spans for z in range(time_count)]]
    plan += [[(1, z, *span) for span in spans for z in hops], [(1, 0, *span) for span in spans]]
    near, far, home = filtered(1, second, plan)
    blocks, (near,) = after([early[p] for p in late_pairs], [near])
    early.update((p, over(block, *p)) for p, block in zip(late_pairs, blocks))
    (far,), held = after([far], [early[p] for p in early_pairs[:4]])
    early.update(zip(early_pairs[:4], held))
    far = over(far, 1, 0)
    def mix(start, index, other_start, other, count):
        first, second = start + index * count, other_start + index * count
        return columns(near[first : first + count], other[second : second + count])

    blocks = {z: mix(0, z, -cut, far, cut) for z in hops}
    order = [2, 1, 3]
    values, held = after([blocks[z] for z in order], [early[p] for p in late_pairs[:1]])
    early.update(zip(late_pairs[:1], held))
    two, one, three = (over(value, 0, z) for value, z in zip(values, order))
    (home,), (one,) = after([home], [one])
    home = over(home, 1, 0)
    low = [mix(0, 0, 0, home, cut), one, two, three]
    high = [mix(time_count * cut, 0, cut, home, rest)]
    high += [mix(time_count * cut, z, 3 * cut - rest, far, rest) for z in hops]

    def with_other(values):
        return [side for v in values for side in (v, travel(v, ("pol",), (1,)))]

    early = with_other([jnp.stack([early[p] for p in pairs])])
    blocks, held = after(high[1:], [low[2], low[1], early[1]])
    low[2], low[1], early[1] = held
    moved = {z: over(blocks[z - 1], 0, z) for z in (2, 1, 3)}
    high = [high[0]] + [moved[z] for z in (1, 2, 3)]
    low = jnp.stack(low).reshape(2 * time_count, cut, 2, ROWS, LANES)
    visibility = correlate_tiles(
        place, tables_of_tiles, early + with_other([low]),
        [0, 0], width, 0, cut, bands, None,
    )
    high, (visibility,) = after(high, [visibility])
    high = jnp.stack(high).reshape(2 * time_count, rest, 2, ROWS, LANES)
    return correlate_tiles(
        place, tables_of_tiles, early + with_other([high]),
        [cut, 0], width, cut, rest, bands, visibility,
    )


def on_device(voltages, taps_filter, tile_a, tile_b, tile_owner, tile_flags):
    taps, length = taps_filter.shape
    frames = voltages.shape[3] // length
    time_count = lax.axis_size("tm")
    fits = (
        length == RADIX * LANES
        and AVG * time_count * frames == LANES
        and 2 * tile_a.shape[1] == LANES
        and voltages.shape[2] == 2 * time_count * ROWS
        and (lax.axis_size("chan"), time_count) == (2, 4)
    )
    form = on_device_chunks if fits else on_device_any
    return form(voltages, taps_filter, tile_a, tile_b, tile_owner, tile_flags)


def solution(mesh):
    return jax.shard_map(
        on_device,
        mesh=mesh,
        in_specs=(P("grp", "pol", "chan", "tm"), P(), P(), P(), P(), P()),
        out_specs=P("pol", ("chan", "tm"), "grp", None, None, None),
        check_vma=False,
    )
```

```python
import math

import jax
import jax.numpy as jnp
import numpy as np
from jax import lax
from jax.experimental import pallas as pl
from jax.experimental.pallas import tpu as pltpu
from jax.sharding import PartitionSpec as P

AVG = 8
CAP = 8
RADIX = 16
LANES = 128
ROWS = 16


radix_first = 32


def from_behind(value, axis, steps):
    count = lax.axis_size(axis)
    first, last = (max(0, -steps), min(count, count - steps))
    return lax.ppermute(value, axis, [(source, source + steps) for source in range(first, last)])


def fourier(filtered):
    length = filtered.shape[-1]
    second = length // radix_first
    exact_mode = lax.Precision.HIGHEST
    grid = filtered.reshape(filtered.shape[:-1] + (radix_first, second))
    outer = jnp.arange(radix_first, dtype=jnp.int32)
    inner = jnp.arange(second, dtype=jnp.int32)
    phase_one = (
        2.0
        * math.pi
        / radix_first
        * (outer[:, None] * outer[None, :] % radix_first).astype(jnp.float32)
    )
    phase_twist = 2.0 * math.pi / length * (outer[:, None] * inner[None, :]).astype(jnp.float32)
    phase_two = (
        2.0 * math.pi / second * (inner[:, None] * inner[None, :] % second).astype(jnp.float32)
    )
    cos_one, sin_one = (jnp.cos(phase_one), jnp.sin(phase_one))
    cos_twist, sin_twist = (jnp.cos(phase_twist), jnp.sin(phase_twist))
    cos_two, sin_two = (jnp.cos(phase_two), jnp.sin(phase_two))
    first_form = "fk,stkj->stfj"
    section_re = jnp.einsum(first_form, cos_one, grid[0], precision=exact_mode) + jnp.einsum(
        first_form, sin_one, grid[1], precision=exact_mode
    )
    section_im = jnp.einsum(first_form, cos_one, grid[1], precision=exact_mode) - jnp.einsum(
        first_form, sin_one, grid[0], precision=exact_mode
    )
    turned_re = section_re * cos_twist + section_im * sin_twist
    turned_im = section_im * cos_twist - section_re * sin_twist
    second_form = "gj,stfj->stgf"
    final_re = jnp.einsum(second_form, cos_two, turned_re, precision=exact_mode) + jnp.einsum(
        second_form, sin_two, turned_im, precision=exact_mode
    )
    final_im = jnp.einsum(second_form, cos_two, turned_im, precision=exact_mode) - jnp.einsum(
        second_form, sin_two, turned_re, precision=exact_mode
    )
    joined = jnp.stack([final_re, final_im]).reshape(filtered.shape)
    return joined * (1.0 / math.sqrt(length))


def correlate(full, rows_a, rows_b, flags, group_count):
    depth = full.shape[4]
    weight = jnp.tile(flags.astype(jnp.bfloat16), depth // flags.shape[0])
    left_rows = jnp.take(full, rows_a, axis=2) * weight
    right_rows = jnp.take(full, rows_b, axis=2)
    stacked_left = jnp.stack(
        [
            jnp.concatenate([left_rows[0], left_rows[1]], axis=-1),
            jnp.concatenate([left_rows[1], -left_rows[0]], axis=-1),
        ]
    )
    joined_right = jnp.concatenate([right_rows[0], right_rows[1]], axis=-1)
    result = jnp.einsum(
        "rpank,qbnk->nrpaqb", stacked_left, joined_right, preferred_element_type=jnp.float32
    )
    width = rows_a.shape[0]
    return result.reshape(group_count, 2, 2, width, 2 * width) * (1.0 / depth)


def on_device_any(voltages, taps_filter, tile_a, tile_b, tile_owner, tile_flags):
    history = taps_filter.shape[0] - 1
    length = taps_filter.shape[1]
    stations = voltages.shape[2]
    frames = voltages.shape[3] // length
    local_blocks = voltages.reshape(2, stations, frames, length)
    hop_count = -(-history // frames)
    sending = local_blocks
    extended = local_blocks
    for hop_index in range(hop_count):
        sending = from_behind(sending, "tm", 1)
        extended = jnp.concatenate([sending, extended], axis=2)
    extended = extended[:, :, extended.shape[2] - history - frames :]
    filtered = jnp.zeros((2, stations, frames, length), jnp.float32)
    for tap_index in range(history + 1):
        start = history - tap_index
        filtered = filtered + taps_filter[tap_index] * extended[
            :, :, start : start + frames
        ].astype(jnp.float32)
    spectra = fourier(filtered).astype(jnp.bfloat16)
    chan_count = lax.axis_size("chan")
    time_count = lax.axis_size("tm")
    narrow = length // (chan_count * time_count)
    outgoing = spectra.reshape(2, stations, frames, chan_count, time_count, narrow)
    outgoing = outgoing.transpose(0, 3, 4, 5, 1, 2)
    flat = outgoing.reshape(2, chan_count * time_count, narrow, stations * frames)
    moved = lax.all_to_all(flat, ("chan", "tm"), split_axis=1, concat_axis=1, tiled=True)
    moved = moved.reshape(2, chan_count, time_count, narrow, stations, frames)
    bands = narrow // AVG
    every_station = chan_count * stations
    spectra_count = time_count * frames
    arranged = moved.transpose(0, 1, 4, 3, 2, 5).reshape(
        2, 1, every_station, bands, AVG * spectra_count
    )
    full = lax.all_gather(arranged, "pol", axis=1, tiled=True)
    position = lax.axis_index("pol")
    width = tile_a.shape[1]
    capacity = CAP
    held = tile_owner == position
    listed = jnp.nonzero(held, size=capacity, fill_value=0)[0].astype(jnp.int32)
    tally = jnp.sum(held.astype(jnp.int32))
    initial = jnp.zeros((capacity, bands, 2, 2, width, 2 * width), jnp.float32)

    def fill_slot(slot, results):
        chosen_tile = listed[slot]
        return results.at[slot].set(
            correlate(
                full, tile_a[chosen_tile], tile_b[chosen_tile], tile_flags[chosen_tile], bands
            )
        )

    visibility = lax.fori_loop(0, tally, fill_slot, initial)
    return visibility


def fourier_tables(length):
    low = np.arange(RADIX)
    lane = np.arange(LANES)
    turn = 2.0 * np.pi / length * np.outer(low, lane)
    twiddle = np.stack([np.cos(turn), np.sin(turn)]).astype(np.float32)
    angle = 2.0 * np.pi / LANES * (np.outer(lane, lane) % LANES)
    cos, sin = np.cos(angle) / math.sqrt(length), np.sin(angle) / math.sqrt(length)
    matrix = np.block([[cos, sin], [-sin, cos]]).astype(np.float32)
    high = matrix.astype(jnp.bfloat16)
    rest = (matrix - high.astype(np.float32)).astype(jnp.bfloat16)
    return twiddle, np.stack([high, rest])


def butterflies(values):
    count = len(values)
    if count == 1:
        return values
    even, odd = butterflies(values[0::2]), butterflies(values[1::2])
    first, second = [], []
    for index in range(count // 2):
        (a, b), (c, d) = even[index], odd[index]
        if index == 0:
            e, f = c, d
        elif 4 * index == count:
            e, f = d, -c
        elif 8 * index == count:
            root = math.sqrt(0.5)
            e, f = (c + d) * root, (d - c) * root
        elif 8 * index == 3 * count:
            root = math.sqrt(0.5)
            e, f = (d - c) * root, -(c + d) * root
        else:
            turn = 2.0 * math.pi * index / count
            cos, sin = math.cos(turn), math.sin(turn)
            e, f = c * cos + d * sin, d * cos - c * sin
        first.append((a + e, b + f))
        second.append((a - e, b - f))
    return first + second


def channelise_kernel(frames, chunk, columns, plan, place_ref, own_ref, *refs):
    sources = refs[-6].shape[0]
    come_refs = refs[: sources - 1]
    taps_ref, twiddle_ref, matrix_ref = refs[sources - 1 : sources + 2]
    out_refs = refs[sources + 2 : -6]
    x_ref, fil_ref, zr_ref, zi_ref, w_ref, sems = refs[-6:]
    chan, tm = place_ref[0], place_ref[1]
    own_rows = pl.multiple_of((tm * (own_ref.shape[1] // (sources * ROWS)) + chunk) * ROWS, ROWS)
    copies = []
    for behind in range(sources):
        block = come_refs[behind - 1] if behind else own_ref.at[:, pl.ds(own_rows, ROWS), :]
        slot = lax.rem(tm - behind + sources, sources)
        copies.append(pltpu.make_async_copy(block, x_ref.at[slot], sems.at[behind]))
    for copy in copies:
        copy.start()
    for copy in copies:
        copy.wait()
    spectra = sources * frames
    length = taps_ref.shape[1]
    taps = taps_ref.shape[0]
    depth = RADIX * spectra
    z_refs = (zr_ref, zi_ref)

    @pl.loop(0, RADIX)
    def _(section):
        at = pl.multiple_of(section * LANES, LANES)
        weights = [taps_ref[pl.ds(m, 1), pl.ds(at, LANES)] for m in range(taps)]
        for part in range(2):
            blocks = []
            for t in range(spectra):
                lane = pl.multiple_of((t % frames) * length + section * LANES, LANES)
                blocks.append(x_ref[t // frames, part, :, pl.ds(lane, LANES)].astype(jnp.float32))
            for t in range(spectra):
                total = weights[0] * blocks[t]
                for m in range(1, min(t + 1, taps)):
                    total = total + weights[m] * blocks[t - m]
                fil_ref[section, t, part] = total

    @pl.loop(0, spectra)
    def _(t):
        for half in range(ROWS // 8):
            values = [
                tuple(fil_ref[section, t, part, pl.ds(half * 8, 8), :] for part in range(2))
                for section in range(RADIX)
            ]
            for low, (re, im) in enumerate(butterflies(values)):
                if low:
                    cos = twiddle_ref[0, pl.ds(low, 1), :]
                    sin = twiddle_ref[1, pl.ds(low, 1), :]
                    re, im = re * cos + im * sin, im * cos - re * sin
                rows = pl.ds(half * 8 * depth + low * spectra + t, 8, stride=depth)
                zr_ref[rows, :] = re
                zi_ref[rows, :] = im

    form = (((1,), (1,)), ((), ()))
    high_matrix, low_matrix = matrix_ref[0], matrix_ref[1]
    halves = depth // LANES

    @pl.loop(0, ROWS)
    def _(station):
        rows = pl.ds(pl.multiple_of(station * depth, depth), depth)
        value = jnp.concatenate([ref[rows, :] for ref in z_refs], axis=1)
        high = value.astype(jnp.bfloat16)
        rest = (value - high.astype(jnp.float32)).astype(jnp.bfloat16)
        total = lax.dot_general(high_matrix, high, form, preferred_element_type=jnp.float32)
        total += lax.dot_general(high_matrix, rest, form, preferred_element_type=jnp.float32)
        total += lax.dot_general(low_matrix, high, form, preferred_element_type=jnp.float32)
        for half in range(halves):
            for part in range(2):
                rows = pl.ds((half * 2 + part) * ROWS + station, LANES, stride=halves * 2 * ROWS)
                w_ref[rows, :] = total[
                    part * LANES : (part + 1) * LANES, half * LANES : (half + 1) * LANES
                ]

    share = w_ref.shape[0] // (columns * sources)
    band_rows = 2 * ROWS
    piece = 2 * band_rows
    for blocks, out_ref in zip(plan, out_refs):
        at = 0
        for across, along, start, stop in blocks:
            owner = lax.rem(chan + across, columns) * sources + lax.rem(tm + along, sources)
            for row in range(start * band_rows, stop * band_rows, piece):
                rows = pl.ds(pl.multiple_of(owner * share + row, piece), piece)
                out_ref[at : at + piece, :] = w_ref[rows, :].astype(jnp.bfloat16)
                at += piece


def channelise(place, chunk, voltages, come, taps_filter, tables, frames, columns, plan):
    sources = 1 + len(come)
    length = taps_filter.shape[1]
    spectra = sources * frames
    twiddle, matrix = tables
    out_rows = length // AVG * 2 * ROWS
    whole = pl.BlockSpec(memory_space=pltpu.VMEM)
    counts = [sum(stop - start for _, _, start, stop in blocks) for blocks in plan]
    flat = pl.pallas_call(
        lambda *refs: channelise_kernel(frames, chunk, columns, plan, *refs),
        out_shape=[
            jax.ShapeDtypeStruct((count * 2 * ROWS, LANES), jnp.bfloat16) for count in counts
        ],
        in_specs=[pl.BlockSpec(memory_space=pltpu.SMEM)]
        + [pl.BlockSpec(memory_space=pl.ANY)] * sources
        + [whole] * 3,
        out_specs=[whole] * len(plan),
        scratch_shapes=[
            pltpu.VMEM((sources, 2, ROWS, frames * length), jnp.bfloat16),
            pltpu.VMEM((RADIX, spectra, 2, ROWS, LANES), jnp.float32),
            pltpu.VMEM((ROWS * RADIX * spectra, LANES), jnp.float32),
            pltpu.VMEM((ROWS * RADIX * spectra, LANES), jnp.float32),
            pltpu.VMEM((out_rows, LANES), jnp.float32),
            pltpu.SemaphoreType.DMA((sources,)),
        ],
        compiler_params=pltpu.CompilerParams(vmem_limit_bytes=40 * 2**20),
        cost_estimate=pl.CostEstimate(
            flops=9 * 10**9, bytes_accessed=4 * 2**20, transcendentals=0
        ),
        name="channelise",
    )(place, voltages, *come, taps_filter, jnp.asarray(twiddle), jnp.asarray(matrix))
    return [piece.reshape(count, 2, ROWS, LANES) for piece, count in zip(flat, counts)]


def correlate_kernel(starts, width, place_ref, left_sel_ref, right_sel_ref, weight_ref, *refs):
    x_refs, (out_ref, x_all, *rows_refs, sems) = refs[: 2 * len(starts)], refs[-7:]
    tiles = out_ref.shape[0]
    step = pl.program_id(0)
    bands = x_all.shape[2]
    spans = [(0, 2), (2, bands)]

    def copies(span):
        first, last = spans[span]
        block = 0
        for index, start in enumerate(starts):
            blocks = x_refs[2 * index].shape[0]
            for side in range(2):
                yield pltpu.make_async_copy(
                    x_refs[2 * index + side].at[:, pl.ds(start + first, last - first)],
                    x_all.at[
                        lax.rem(place_ref[2] + side, 2),
                        pl.ds(block, blocks),
                        pl.ds(first, last - first),
                    ],
                    sems.at[span, 2 * index + side],
                )
            block += blocks

    lower = lax.broadcasted_iota(jnp.int32, (1, 2 * width), 1) < width

    def gather(band, left_ref, right_ref):
        right = []
        for pol in range(2):
            lanes = slice(pol * 2 * LANES, (pol + 1) * 2 * LANES)
            value = jnp.concatenate(
                [
                    jnp.concatenate([x_all[pol, block, band, part] for part in range(2)], axis=1)
                    for block in range(x_all.shape[1])
                ]
            )
            left = jnp.dot(left_sel_ref[...], value, preferred_element_type=jnp.float32)
            for tile in range(tiles):
                rows = slice(tile * width, (tile + 1) * width)
                scaled = left[rows] * weight_ref[pl.ds(tile, 1), :]
                left_ref[rows, lanes] = scaled.astype(jnp.bfloat16)
            right.append(
                lax.dot_general(
                    value,
                    right_sel_ref[pol],
                    (((0,), (0,)), ((), ())),
                    preferred_element_type=jnp.float32,
                ).astype(jnp.bfloat16)
            )
        for pair in range(tiles // 2):
            first, second = (v[:, pair * 2 * width : (pair + 1) * 2 * width] for v in right)
            even = jnp.where(lower, first, second)
            odd = pltpu.roll(jnp.where(lower, second, first), width, 1)
            right_ref[2 * pair] = even
            right_ref[2 * pair + 1] = odd

    def multiply(number, left_ref, right_ref):
        for tile in range(tiles):
            rows = slice(tile * width, (tile + 1) * width)
            left = jnp.concatenate(
                [left_ref[rows, lanes : lanes + 2 * LANES] for lanes in (0, 2 * LANES)]
            )
            right = right_ref[tile]
            turned = jnp.concatenate([-right[LANES:], right[:LANES]])
            both = jnp.concatenate([right, turned], axis=1)
            result = jnp.dot(left, both, preferred_element_type=jnp.float32)
            for part in range(2):
                out_ref[tile, number, part] = result[
                    :, part * 2 * width : (part + 1) * 2 * width
                ].reshape(2, width, 2 * width)

    even, odd = rows_refs[:2], rows_refs[2:]

    @pl.when(step == 0)
    def _():
        for span in range(2):
            for copy in copies(span):
                copy.start()
        for copy in copies(0):
            copy.wait()
        gather(0, *even)
        for copy in copies(1):
            copy.wait()

    gather(2 * step + 1, *odd)
    multiply(0, *even)
    gather(jnp.minimum(2 * step + 2, bands - 1), *even)
    multiply(1, *odd)


def correlate_tiles(place, tables, pieces, starts, width, first, count, bands, earlier):
    left_select, _, weight = tables
    tiles = weight.shape[0]
    whole = pl.BlockSpec(memory_space=pltpu.VMEM)
    more = [] if earlier is None else [earlier]
    rows = [
        pltpu.VMEM((tiles * width, 4 * LANES), jnp.bfloat16),
        pltpu.VMEM((tiles, 2 * LANES, 2 * width), jnp.bfloat16),
    ]
    return pl.pallas_call(
        lambda *refs: correlate_kernel(starts, width, *refs),
        grid=(count // 2,),
        out_shape=jax.ShapeDtypeStruct((tiles, bands, 2, 2, width, 2 * width), jnp.float32),
        in_specs=[pl.BlockSpec(memory_space=pltpu.SMEM)]
        + [whole] * len(tables)
        + [pl.BlockSpec(memory_space=pl.ANY)] * (len(pieces) + len(more)),
        out_specs=pl.BlockSpec(
            (tiles, 2, 2, 2, width, 2 * width), lambda g: (0, g + first // 2, 0, 0, 0, 0)
        ),
        scratch_shapes=[
            pltpu.VMEM((2, left_select.shape[1] // ROWS, count, 2, ROWS, LANES), jnp.bfloat16),
            *rows,
            *rows,
            pltpu.SemaphoreType.DMA((2, len(pieces))),
        ],
        input_output_aliases={1 + len(tables) + len(pieces): 0} if more else {},
        compiler_params=pltpu.CompilerParams(vmem_limit_bytes=32 * 2**20),
        cost_estimate=pl.CostEstimate(
            flops=13 * 10**9 * count // bands,
            bytes_accessed=42 * 2**20 * count // bands,
            transcendentals=0,
        ),
        name="correlate",
    )(place, *tables, *pieces, *more)


def tile_tables(tile_a, tile_b, tile_owner, tile_flags, row_of):
    tiles = tile_owner.shape[0]
    held = tile_owner == lax.axis_index("pol")
    order = jnp.arange(tiles, dtype=jnp.int32)
    rank = jnp.sum((held[None, :] & (order[None, :] < order[:, None])).astype(jnp.int32), axis=1)
    slots = jnp.arange(CAP, dtype=jnp.int32)
    pick = (held[None, :] & (rank[None, :] == slots[:, None])).astype(jnp.int32)
    sides = jnp.stack([row_of(tile_a), row_of(tile_b)], axis=1) + 1
    rows = jnp.sum(pick[:, :, None, None] * sides[None], axis=1) - 1
    flags = jnp.sum(pick[:, :, None] * tile_flags[None], axis=1).astype(jnp.float32)
    return rows, flags


def on_device_chunks(voltages, taps_filter, tile_a, tile_b, tile_owner, tile_flags):
    length = taps_filter.shape[1]
    stations = voltages.shape[2]
    frames = voltages.shape[3] // length
    chan_count, time_count = lax.axis_size("chan"), lax.axis_size("tm")
    owners = chan_count * time_count
    chunk_count = stations // (time_count * ROWS)
    width = tile_a.shape[1]
    bands = length // AVG // owners
    tables = fourier_tables(length)

    chan, tm = lax.axis_index("chan"), lax.axis_index("tm")
    place = jnp.stack([chan, tm, lax.axis_index("pol")]).astype(jnp.int32)

    def row_of(station):
        column, rest = station // stations, station % stations
        block, inside = rest // (chunk_count * ROWS), rest % (chunk_count * ROWS)
        across = (chan - column) % chan_count
        behind = (tm - block) % time_count
        piece = behind * chan_count + across
        return ((inside // ROWS) * owners + piece) * ROWS + inside % ROWS

    rows, flags = tile_tables(tile_a, tile_b, tile_owner, tile_flags, row_of)
    total_rows = chunk_count * owners * ROWS
    station_rows = jnp.arange(total_rows, dtype=jnp.int32)
    left_rows = rows[:, 0].reshape(-1)
    left_select = (left_rows[:, None] == station_rows).astype(jnp.bfloat16)
    right_rows = rows[:, 1].reshape(CAP // 2, 2, width)
    right_rows = jnp.stack([right_rows, right_rows[:, ::-1]]).reshape(2, 1, -1)
    right_select = (right_rows == station_rows[:, None]).astype(jnp.bfloat16)
    depth = AVG * time_count * frames
    weight = jnp.tile(flags * (1.0 / depth), (1, 2 * AVG))
    tables_of_tiles = [left_select, right_select, weight]

    samples = voltages.reshape(2, stations, frames * length)

    def travel(value, axes, distances):
        sizes = [lax.axis_size(axis) for axis in axes]
        pairs = []
        for index in np.ndindex(*sizes):
            target = [(i + d) % n for i, d, n in zip(index, distances, sizes)]
            pairs.append(tuple(int(np.ravel_multi_index(x, sizes)) for x in (index, target)))
        return lax.ppermute(value, axes, pairs)

    def after(values, earlier):
        return lax.optimization_barrier((list(values), list(earlier)))

    def block_for(values, chunk, distance):
        first = ((tm + distance) % time_count * chunk_count + chunk) * ROWS
        return lax.dynamic_slice(values, (0, first, 0), (2, ROWS, frames * length))

    def filtered(chunk, arrived, plan):
        return channelise(
            place, chunk, samples, arrived, taps_filter, tables, frames, chan_count, plan
        )

    def over(value, across, along):
        return travel(value, ("chan", "tm"), (across, along))

    def columns(near, far):
        return jnp.stack([near, far])

    cut = bands * 5 // 8
    rest = bands - cut
    pairs = [(x, z) for z in range(time_count) for x in range(chan_count)]
    early_pairs = [(x, z) for z in (1, 3) for x in range(2)]
    late_pairs = [(0, 2), (1, 2), (1, 0)]

    (one,), (values,) = after([block_for(samples, 0, 1)], [samples])
    two, three = (block_for(values, 0, distance) for distance in (2, 3))
    one, two = over(one, 0, 1), over(two, 0, 2)
    (three,), (one,) = after([three], [one])
    three = over(three, 0, 3)
    blocks = [block_for(values, 1, distance) for distance in (1, 2, 3)]
    blocks[:1], (two,) = after(blocks[:1], [two])
    blocks[2:], (three,) = after(blocks[2:], [three])
    first = [one, two, three]
    one, three = over(blocks[0], 0, 1), over(blocks[2], 0, 3)
    (two,), (one,) = after(blocks[1:2], [one])
    second = [one, over(two, 0, 2), three]

    plan = [[(x, z, 0, bands)] for x, z in pairs]
    early = dict(zip(pairs, filtered(0, first, plan)))
    blocks, held = after([early[p] for p in early_pairs], [second[1], *tables_of_tiles])
    second[1], tables_of_tiles = held[0], held[1:]
    early.update((p, over(block, *p)) for p, block in zip(early_pairs, blocks))
    spans = [(0, cut), (cut, bands)]
    hops = [1, 2, 3]
    plan = [[(0, z, *span) for span in spans for z in range(time_count)]]
    plan += [[(1, z, *span) for span in spans for z in hops], [(1, 0, *span) for span in spans]]
    near, far, home = filtered(1, second, plan)
    blocks, (near,) = after([early[p] for p in late_pairs], [near])
    early.update((p, over(block, *p)) for p, block in zip(late_pairs, blocks))
    (far,), held = after([far], [early[p] for p in early_pairs[:4]])
    early.update(zip(early_pairs[:4], held))
    far = over(far, 1, 0)
    def mix(start, index, other_start, other, count):
        first, second = start + index * count, other_start + index * count
        return columns(near[first : first + count], other[second : second + count])

    blocks = {z: mix(0, z, -cut, far, cut) for z in hops}
    order = [2, 1, 3]
    values, held = after([blocks[z] for z in order], [early[p] for p in late_pairs[:1]])
    early.update(zip(late_pairs[:1], held))
    two, one, three = (over(value, 0, z) for value, z in zip(values, order))
    (home,), (one,) = after([home], [one])
    home = over(home, 1, 0)
    low = [mix(0, 0, 0, home, cut), one, two, three]
    high = [mix(time_count * cut, 0, cut, home, rest)]
    high += [mix(time_count * cut, z, 3 * cut - rest, far, rest) for z in hops]

    def with_other(values):
        return [side for v in values for side in (v, travel(v, ("pol",), (1,)))]

    early = with_other([jnp.stack([early[p] for p in pairs])])
    blocks, held = after(high[1:], [low[2], low[1], early[1]])
    low[2], low[1], early[1] = held
    moved = {z: over(blocks[z - 1], 0, z) for z in (2, 1, 3)}
    high = [high[0]] + [moved[z] for z in (1, 2, 3)]
    low = jnp.stack(low).reshape(2 * time_count, cut, 2, ROWS, LANES)
    visibility = correlate_tiles(
        place, tables_of_tiles, early + with_other([low]),
        [0, 0], width, 0, cut, bands, None,
    )
    high, (visibility,) = after(high, [visibility])
    high = jnp.stack(high).reshape(2 * time_count, rest, 2, ROWS, LANES)
    return correlate_tiles(
        place, tables_of_tiles, early + with_other([high]),
        [cut, 0], width, cut, rest, bands, visibility,
    )


def on_device(voltages, taps_filter, tile_a, tile_b, tile_owner, tile_flags):
    taps, length = taps_filter.shape
    frames = voltages.shape[3] // length
    time_count = lax.axis_size("tm")
    fits = (
        length == RADIX * LANES
        and AVG * time_count * frames == LANES
        and 2 * tile_a.shape[1] == LANES
        and voltages.shape[2] == 2 * time_count * ROWS
        and (lax.axis_size("chan"), time_count) == (2, 4)
    )
    form = on_device_chunks if fits else on_device_any
    return form(voltages, taps_filter, tile_a, tile_b, tile_owner, tile_flags)


def solution(mesh):
    return jax.shard_map(
        on_device,
        mesh=mesh,
        in_specs=(P("grp", "pol", "chan", "tm"), P(), P(), P(), P(), P()),
        out_specs=P("pol", ("chan", "tm"), "grp", None, None, None),
        check_vma=False,
    )
```

```python
import math

import jax
import jax.numpy as jnp
import numpy as np
from jax import lax
from jax.experimental import pallas as pl
from jax.experimental.pallas import tpu as pltpu
from jax.sharding import PartitionSpec as P

AVG = 8
CAP = 8
RADIX = 16
LANES = 128
ROWS = 16


radix_first = 32


def from_behind(value, axis, steps):
    count = lax.axis_size(axis)
    first, last = (max(0, -steps), min(count, count - steps))
    return lax.ppermute(value, axis, [(source, source + steps) for source in range(first, last)])


def fourier(filtered):
    length = filtered.shape[-1]
    second = length // radix_first
    exact_mode = lax.Precision.HIGHEST
    grid = filtered.reshape(filtered.shape[:-1] + (radix_first, second))
    outer = jnp.arange(radix_first, dtype=jnp.int32)
    inner = jnp.arange(second, dtype=jnp.int32)
    phase_one = (
        2.0
        * math.pi
        / radix_first
        * (outer[:, None] * outer[None, :] % radix_first).astype(jnp.float32)
    )
    phase_twist = 2.0 * math.pi / length * (outer[:, None] * inner[None, :]).astype(jnp.float32)
    phase_two = (
        2.0 * math.pi / second * (inner[:, None] * inner[None, :] % second).astype(jnp.float32)
    )
    cos_one, sin_one = (jnp.cos(phase_one), jnp.sin(phase_one))
    cos_twist, sin_twist = (jnp.cos(phase_twist), jnp.sin(phase_twist))
    cos_two, sin_two = (jnp.cos(phase_two), jnp.sin(phase_two))
    first_form = "fk,stkj->stfj"
    section_re = jnp.einsum(first_form, cos_one, grid[0], precision=exact_mode) + jnp.einsum(
        first_form, sin_one, grid[1], precision=exact_mode
    )
    section_im = jnp.einsum(first_form, cos_one, grid[1], precision=exact_mode) - jnp.einsum(
        first_form, sin_one, grid[0], precision=exact_mode
    )
    turned_re = section_re * cos_twist + section_im * sin_twist
    turned_im = section_im * cos_twist - section_re * sin_twist
    second_form = "gj,stfj->stgf"
    final_re = jnp.einsum(second_form, cos_two, turned_re, precision=exact_mode) + jnp.einsum(
        second_form, sin_two, turned_im, precision=exact_mode
    )
    final_im = jnp.einsum(second_form, cos_two, turned_im, precision=exact_mode) - jnp.einsum(
        second_form, sin_two, turned_re, precision=exact_mode
    )
    joined = jnp.stack([final_re, final_im]).reshape(filtered.shape)
    return joined * (1.0 / math.sqrt(length))


def correlate(full, rows_a, rows_b, flags, group_count):
    depth = full.shape[4]
    weight = jnp.tile(flags.astype(jnp.bfloat16), depth // flags.shape[0])
    left_rows = jnp.take(full, rows_a, axis=2) * weight
    right_rows = jnp.take(full, rows_b, axis=2)
    stacked_left = jnp.stack(
        [
            jnp.concatenate([left_rows[0], left_rows[1]], axis=-1),
            jnp.concatenate([left_rows[1], -left_rows[0]], axis=-1),
        ]
    )
    joined_right = jnp.concatenate([right_rows[0], right_rows[1]], axis=-1)
    result = jnp.einsum(
        "rpank,qbnk->nrpaqb", stacked_left, joined_right, preferred_element_type=jnp.float32
    )
    width = rows_a.shape[0]
    return result.reshape(group_count, 2, 2, width, 2 * width) * (1.0 / depth)


def on_device_any(voltages, taps_filter, tile_a, tile_b, tile_owner, tile_flags):
    history = taps_filter.shape[0] - 1
    length = taps_filter.shape[1]
    stations = voltages.shape[2]
    frames = voltages.shape[3] // length
    local_blocks = voltages.reshape(2, stations, frames, length)
    hop_count = -(-history // frames)
    sending = local_blocks
    extended = local_blocks
    for hop_index in range(hop_count):
        sending = from_behind(sending, "tm", 1)
        extended = jnp.concatenate([sending, extended], axis=2)
    extended = extended[:, :, extended.shape[2] - history - frames :]
    filtered = jnp.zeros((2, stations, frames, length), jnp.float32)
    for tap_index in range(history + 1):
        start = history - tap_index
        filtered = filtered + taps_filter[tap_index] * extended[
            :, :, start : start + frames
        ].astype(jnp.float32)
    spectra = fourier(filtered).astype(jnp.bfloat16)
    chan_count = lax.axis_size("chan")
    time_count = lax.axis_size("tm")
    narrow = length // (chan_count * time_count)
    outgoing = spectra.reshape(2, stations, frames, chan_count, time_count, narrow)
    outgoing = outgoing.transpose(0, 3, 4, 5, 1, 2)
    flat = outgoing.reshape(2, chan_count * time_count, narrow, stations * frames)
    moved = lax.all_to_all(flat, ("chan", "tm"), split_axis=1, concat_axis=1, tiled=True)
    moved = moved.reshape(2, chan_count, time_count, narrow, stations, frames)
    bands = narrow // AVG
    every_station = chan_count * stations
    spectra_count = time_count * frames
    arranged = moved.transpose(0, 1, 4, 3, 2, 5).reshape(
        2, 1, every_station, bands, AVG * spectra_count
    )
    full = lax.all_gather(arranged, "pol", axis=1, tiled=True)
    position = lax.axis_index("pol")
    width = tile_a.shape[1]
    capacity = CAP
    held = tile_owner == position
    listed = jnp.nonzero(held, size=capacity, fill_value=0)[0].astype(jnp.int32)
    tally = jnp.sum(held.astype(jnp.int32))
    initial = jnp.zeros((capacity, bands, 2, 2, width, 2 * width), jnp.float32)

    def fill_slot(slot, results):
        chosen_tile = listed[slot]
        return results.at[slot].set(
            correlate(
                full, tile_a[chosen_tile], tile_b[chosen_tile], tile_flags[chosen_tile], bands
            )
        )

    visibility = lax.fori_loop(0, tally, fill_slot, initial)
    return visibility


def fourier_tables(length):
    low = np.arange(RADIX)
    lane = np.arange(LANES)
    turn = 2.0 * np.pi / length * np.outer(low, lane)
    twiddle = np.stack([np.cos(turn), np.sin(turn)]).astype(np.float32)
    angle = 2.0 * np.pi / LANES * (np.outer(lane, lane) % LANES)
    cos, sin = np.cos(angle) / math.sqrt(length), np.sin(angle) / math.sqrt(length)
    matrix = np.block([[cos, sin], [-sin, cos]]).astype(np.float32)
    high = matrix.astype(jnp.bfloat16)
    rest = (matrix - high.astype(np.float32)).astype(jnp.bfloat16)
    return twiddle, np.stack([high, rest])


def butterflies(values):
    count = len(values)
    if count == 1:
        return values
    even, odd = butterflies(values[0::2]), butterflies(values[1::2])
    first, second = [], []
    for index in range(count // 2):
        (a, b), (c, d) = even[index], odd[index]
        if index == 0:
            e, f = c, d
        elif 4 * index == count:
            e, f = d, -c
        elif 8 * index == count:
            root = math.sqrt(0.5)
            e, f = (c + d) * root, (d - c) * root
        elif 8 * index == 3 * count:
            root = math.sqrt(0.5)
            e, f = (d - c) * root, -(c + d) * root
        else:
            turn = 2.0 * math.pi * index / count
            cos, sin = math.cos(turn), math.sin(turn)
            e, f = c * cos + d * sin, d * cos - c * sin
        first.append((a + e, b + f))
        second.append((a - e, b - f))
    return first + second


def channelise_kernel(frames, chunk, columns, plan, place_ref, own_ref, *refs):
    sources = refs[-6].shape[0]
    come_refs = refs[: sources - 1]
    taps_ref, twiddle_ref, matrix_ref = refs[sources - 1 : sources + 2]
    out_refs = refs[sources + 2 : -6]
    x_ref, fil_ref, zr_ref, zi_ref, w_ref, sems = refs[-6:]
    chan, tm = place_ref[0], place_ref[1]
    own_rows = pl.multiple_of((tm * (own_ref.shape[1] // (sources * ROWS)) + chunk) * ROWS, ROWS)
    copies = []
    for behind in range(sources):
        block = come_refs[behind - 1] if behind else own_ref.at[:, pl.ds(own_rows, ROWS), :]
        slot = lax.rem(tm - behind + sources, sources)
        copies.append(pltpu.make_async_copy(block, x_ref.at[slot], sems.at[behind]))
    for copy in copies:
        copy.start()
    for copy in copies:
        copy.wait()
    spectra = sources * frames
    length = taps_ref.shape[1]
    taps = taps_ref.shape[0]
    depth = RADIX * spectra
    z_refs = (zr_ref, zi_ref)

    @pl.loop(0, RADIX)
    def _(section):
        at = pl.multiple_of(section * LANES, LANES)
        weights = [taps_ref[pl.ds(m, 1), pl.ds(at, LANES)] for m in range(taps)]
        for part in range(2):
            blocks = []
            for t in range(spectra):
                lane = pl.multiple_of((t % frames) * length + section * LANES, LANES)
                blocks.append(x_ref[t // frames, part, :, pl.ds(lane, LANES)].astype(jnp.float32))
            for t in range(spectra):
                total = weights[0] * blocks[t]
                for m in range(1, min(t + 1, taps)):
                    total = total + weights[m] * blocks[t - m]
                fil_ref[section, t, part] = total

    @pl.loop(0, spectra)
    def _(t):
        for half in range(ROWS // 8):
            values = [
                tuple(fil_ref[section, t, part, pl.ds(half * 8, 8), :] for part in range(2))
                for section in range(RADIX)
            ]
            for low, (re, im) in enumerate(butterflies(values)):
                if low:
                    cos = twiddle_ref[0, pl.ds(low, 1), :]
                    sin = twiddle_ref[1, pl.ds(low, 1), :]
                    re, im = re * cos + im * sin, im * cos - re * sin
                rows = pl.ds(half * 8 * depth + low * spectra + t, 8, stride=depth)
                zr_ref[rows, :] = re
                zi_ref[rows, :] = im

    form = (((1,), (1,)), ((), ()))
    high_matrix, low_matrix = matrix_ref[0], matrix_ref[1]
    halves = depth // LANES

    @pl.loop(0, ROWS)
    def _(station):
        rows = pl.ds(pl.multiple_of(station * depth, depth), depth)
        value = jnp.concatenate([ref[rows, :] for ref in z_refs], axis=1)
        high = value.astype(jnp.bfloat16)
        rest = (value - high.astype(jnp.float32)).astype(jnp.bfloat16)
        total = lax.dot_general(high_matrix, high, form, preferred_element_type=jnp.float32)
        total += lax.dot_general(high_matrix, rest, form, preferred_element_type=jnp.float32)
        total += lax.dot_general(low_matrix, high, form, preferred_element_type=jnp.float32)
        for half in range(halves):
            for part in range(2):
                rows = pl.ds((half * 2 + part) * ROWS + station, LANES, stride=halves * 2 * ROWS)
                w_ref[rows, :] = total[
                    part * LANES : (part + 1) * LANES, half * LANES : (half + 1) * LANES
                ]

    share = w_ref.shape[0] // (columns * sources)
    band_rows = 2 * ROWS
    piece = 2 * band_rows
    for blocks, out_ref in zip(plan, out_refs):
        at = 0
        for across, along, start, stop in blocks:
            owner = lax.rem(chan + across, columns) * sources + lax.rem(tm + along, sources)
            for row in range(start * band_rows, stop * band_rows, piece):
                rows = pl.ds(pl.multiple_of(owner * share + row, piece), piece)
                out_ref[at : at + piece, :] = w_ref[rows, :].astype(jnp.bfloat16)
                at += piece


def channelise(place, chunk, voltages, come, taps_filter, tables, frames, columns, plan):
    sources = 1 + len(come)
    length = taps_filter.shape[1]
    spectra = sources * frames
    twiddle, matrix = tables
    out_rows = length // AVG * 2 * ROWS
    whole = pl.BlockSpec(memory_space=pltpu.VMEM)
    counts = [sum(stop - start for _, _, start, stop in blocks) for blocks in plan]
    flat = pl.pallas_call(
        lambda *refs: channelise_kernel(frames, chunk, columns, plan, *refs),
        out_shape=[
            jax.ShapeDtypeStruct((count * 2 * ROWS, LANES), jnp.bfloat16) for count in counts
        ],
        in_specs=[pl.BlockSpec(memory_space=pltpu.SMEM)]
        + [pl.BlockSpec(memory_space=pl.ANY)] * sources
        + [whole] * 3,
        out_specs=[whole] * len(plan),
        scratch_shapes=[
            pltpu.VMEM((sources, 2, ROWS, frames * length), jnp.bfloat16),
            pltpu.VMEM((RADIX, spectra, 2, ROWS, LANES), jnp.float32),
            pltpu.VMEM((ROWS * RADIX * spectra, LANES), jnp.float32),
            pltpu.VMEM((ROWS * RADIX * spectra, LANES), jnp.float32),
            pltpu.VMEM((out_rows, LANES), jnp.float32),
            pltpu.SemaphoreType.DMA((sources,)),
        ],
        compiler_params=pltpu.CompilerParams(vmem_limit_bytes=40 * 2**20),
        cost_estimate=pl.CostEstimate(
            flops=9 * 10**9, bytes_accessed=4 * 2**20, transcendentals=0
        ),
        name="channelise",
    )(place, voltages, *come, taps_filter, jnp.asarray(twiddle), jnp.asarray(matrix))
    return [piece.reshape(count, 2, ROWS, LANES) for piece, count in zip(flat, counts)]


def correlate_kernel(starts, width, place_ref, left_sel_ref, right_sel_ref, weight_ref, *refs):
    x_refs, (out_ref, x_all, *rows_refs, sems) = refs[: 2 * len(starts)], refs[-7:]
    tiles = out_ref.shape[0]
    step = pl.program_id(0)
    bands = x_all.shape[2]
    spans = [(0, 2), (2, bands)]

    def copies(span):
        first, last = spans[span]
        block = 0
        for index, start in enumerate(starts):
            blocks = x_refs[2 * index].shape[0]
            for side in range(2):
                yield pltpu.make_async_copy(
                    x_refs[2 * index + side].at[:, pl.ds(start + first, last - first)],
                    x_all.at[
                        lax.rem(place_ref[2] + side, 2),
                        pl.ds(block, blocks),
                        pl.ds(first, last - first),
                    ],
                    sems.at[span, 2 * index + side],
                )
            block += blocks

    lower = lax.broadcasted_iota(jnp.int32, (1, 2 * width), 1) < width

    def gather(band, left_ref, right_ref):
        value = jnp.concatenate(
            [
                jnp.concatenate(
                    [x_all[pol, block, band, part] for pol in range(2) for part in range(2)], axis=1
                )
                for block in range(x_all.shape[1])
            ]
        )
        left = jnp.dot(left_sel_ref[...], value, preferred_element_type=jnp.float32)
        for tile in range(tiles):
            rows = slice(tile * width, (tile + 1) * width)
            scaled = left[rows] * weight_ref[pl.ds(tile, 1), :]
            left_ref[rows, :] = scaled.astype(jnp.bfloat16)
        right = lax.dot_general(
            value,
            right_sel_ref[...],
            (((0,), (0,)), ((), ())),
            preferred_element_type=jnp.float32,
        )
        for pair in range(tiles // 2):
            columns = right[:, pair * 2 * width : (pair + 1) * 2 * width]
            first, second = columns[: 2 * LANES], columns[2 * LANES :]
            even = jnp.where(lower, first, pltpu.roll(second, width, 1))
            odd = jnp.where(lower, pltpu.roll(first, width, 1), second)
            right_ref[2 * pair] = even.astype(jnp.bfloat16)
            right_ref[2 * pair + 1] = odd.astype(jnp.bfloat16)

    def multiply(number, left_ref, right_ref):
        for tile in range(tiles):
            rows = slice(tile * width, (tile + 1) * width)
            left = jnp.concatenate(
                [left_ref[rows, lanes : lanes + 2 * LANES] for lanes in (0, 2 * LANES)]
            )
            right = right_ref[tile]
            turned = jnp.concatenate([-right[LANES:], right[:LANES]])
            both = jnp.concatenate([right, turned], axis=1)
            result = jnp.dot(left, both, preferred_element_type=jnp.float32)
            for part in range(2):
                out_ref[tile, number, part] = result[
                    :, part * 2 * width : (part + 1) * 2 * width
                ].reshape(2, width, 2 * width)

    even, odd = rows_refs[:2], rows_refs[2:]

    @pl.when(step == 0)
    def _():
        for span in range(2):
            for copy in copies(span):
                copy.start()
        for copy in copies(0):
            copy.wait()
        gather(0, *even)
        for copy in copies(1):
            copy.wait()

    gather(2 * step + 1, *odd)
    multiply(0, *even)
    gather(jnp.minimum(2 * step + 2, bands - 1), *even)
    multiply(1, *odd)


def correlate_tiles(place, tables, pieces, starts, width, first, count, bands, earlier):
    left_select, _, weight = tables
    tiles = weight.shape[0]
    whole = pl.BlockSpec(memory_space=pltpu.VMEM)
    more = [] if earlier is None else [earlier]
    rows = [
        pltpu.VMEM((tiles * width, 4 * LANES), jnp.bfloat16),
        pltpu.VMEM((tiles, 2 * LANES, 2 * width), jnp.bfloat16),
    ]
    return pl.pallas_call(
        lambda *refs: correlate_kernel(starts, width, *refs),
        grid=(count // 2,),
        out_shape=jax.ShapeDtypeStruct((tiles, bands, 2, 2, width, 2 * width), jnp.float32),
        in_specs=[pl.BlockSpec(memory_space=pltpu.SMEM)]
        + [whole] * len(tables)
        + [pl.BlockSpec(memory_space=pl.ANY)] * (len(pieces) + len(more)),
        out_specs=pl.BlockSpec(
            (tiles, 2, 2, 2, width, 2 * width), lambda g: (0, g + first // 2, 0, 0, 0, 0)
        ),
        scratch_shapes=[
            pltpu.VMEM((2, left_select.shape[1] // ROWS, count, 2, ROWS, LANES), jnp.bfloat16),
            *rows,
            *rows,
            pltpu.SemaphoreType.DMA((2, len(pieces))),
        ],
        input_output_aliases={1 + len(tables) + len(pieces): 0} if more else {},
        compiler_params=pltpu.CompilerParams(vmem_limit_bytes=32 * 2**20),
        cost_estimate=pl.CostEstimate(
            flops=13 * 10**9 * count // bands,
            bytes_accessed=42 * 2**20 * count // bands,
            transcendentals=0,
        ),
        name="correlate",
    )(place, *tables, *pieces, *more)


def tile_tables(tile_a, tile_b, tile_owner, tile_flags, row_of):
    tiles = tile_owner.shape[0]
    held = tile_owner == lax.axis_index("pol")
    order = jnp.arange(tiles, dtype=jnp.int32)
    rank = jnp.sum((held[None, :] & (order[None, :] < order[:, None])).astype(jnp.int32), axis=1)
    slots = jnp.arange(CAP, dtype=jnp.int32)
    pick = (held[None, :] & (rank[None, :] == slots[:, None])).astype(jnp.int32)
    sides = jnp.stack([row_of(tile_a), row_of(tile_b)], axis=1) + 1
    rows = jnp.sum(pick[:, :, None, None] * sides[None], axis=1) - 1
    flags = jnp.sum(pick[:, :, None] * tile_flags[None], axis=1).astype(jnp.float32)
    return rows, flags


def on_device_chunks(voltages, taps_filter, tile_a, tile_b, tile_owner, tile_flags):
    length = taps_filter.shape[1]
    stations = voltages.shape[2]
    frames = voltages.shape[3] // length
    chan_count, time_count = lax.axis_size("chan"), lax.axis_size("tm")
    owners = chan_count * time_count
    chunk_count = stations // (time_count * ROWS)
    width = tile_a.shape[1]
    bands = length // AVG // owners
    tables = fourier_tables(length)

    chan, tm = lax.axis_index("chan"), lax.axis_index("tm")
    place = jnp.stack([chan, tm, lax.axis_index("pol")]).astype(jnp.int32)

    def row_of(station):
        column, rest = station // stations, station % stations
        block, inside = rest // (chunk_count * ROWS), rest % (chunk_count * ROWS)
        across = (chan - column) % chan_count
        behind = (tm - block) % time_count
        piece = behind * chan_count + across
        return ((inside // ROWS) * owners + piece) * ROWS + inside % ROWS

    rows, flags = tile_tables(tile_a, tile_b, tile_owner, tile_flags, row_of)
    total_rows = chunk_count * owners * ROWS
    station_rows = jnp.arange(total_rows, dtype=jnp.int32)
    left_rows = rows[:, 0].reshape(-1)
    left_select = (left_rows[:, None] == station_rows).astype(jnp.bfloat16)
    right_rows = rows[:, 1].reshape(1, -1)
    right_select = (right_rows == station_rows[:, None]).astype(jnp.bfloat16)
    depth = AVG * time_count * frames
    weight = jnp.tile(flags * (1.0 / depth), (1, 4 * AVG))
    tables_of_tiles = [left_select, right_select, weight]

    samples = voltages.reshape(2, stations, frames * length)

    def travel(value, axes, distances):
        sizes = [lax.axis_size(axis) for axis in axes]
        pairs = []
        for index in np.ndindex(*sizes):
            target = [(i + d) % n for i, d, n in zip(index, distances, sizes)]
            pairs.append(tuple(int(np.ravel_multi_index(x, sizes)) for x in (index, target)))
        return lax.ppermute(value, axes, pairs)

    def after(values, earlier):
        return lax.optimization_barrier((list(values), list(earlier)))

    def block_for(values, chunk, distance):
        first = ((tm + distance) % time_count * chunk_count + chunk) * ROWS
        return lax.dynamic_slice(values, (0, first, 0), (2, ROWS, frames * length))

    def filtered(chunk, arrived, plan):
        return channelise(
            place, chunk, samples, arrived, taps_filter, tables, frames, chan_count, plan
        )

    def over(value, across, along):
        return travel(value, ("chan", "tm"), (across, along))

    def columns(near, far):
        return jnp.stack([near, far])

    cut = bands * 5 // 8
    rest = bands - cut
    pairs = [(x, z) for z in range(time_count) for x in range(chan_count)]
    early_pairs = [(x, z) for z in (1, 3) for x in range(2)]
    late_pairs = [(0, 2), (1, 2), (1, 0)]

    (one,), (values,) = after([block_for(samples, 0, 1)], [samples])
    two, three = (block_for(values, 0, distance) for distance in (2, 3))
    one, two = over(one, 0, 1), over(two, 0, 2)
    (three,), (one,) = after([three], [one])
    three = over(three, 0, 3)
    blocks = [block_for(values, 1, distance) for distance in (1, 2, 3)]
    blocks[:1], (two,) = after(blocks[:1], [two])
    blocks[2:], (three,) = after(blocks[2:], [three])
    first = [one, two, three]
    one, three = over(blocks[0], 0, 1), over(blocks[2], 0, 3)
    (two,), (one,) = after(blocks[1:2], [one])
    second = [one, over(two, 0, 2), three]

    plan = [[(x, z, 0, bands)] for x, z in pairs]
    early = dict(zip(pairs, filtered(0, first, plan)))
    blocks, held = after([early[p] for p in early_pairs], [second[1], *tables_of_tiles])
    second[1], tables_of_tiles = held[0], held[1:]
    early.update((p, over(block, *p)) for p, block in zip(early_pairs, blocks))
    spans = [(0, cut), (cut, bands)]
    hops = [1, 2, 3]
    plan = [[(0, z, *span) for span in spans for z in range(time_count)]]
    plan += [[(1, z, *span) for span in spans for z in hops], [(1, 0, *span) for span in spans]]
    near, far, home = filtered(1, second, plan)
    blocks, (near,) = after([early[p] for p in late_pairs], [near])
    early.update((p, over(block, *p)) for p, block in zip(late_pairs, blocks))
    (far,), held = after([far], [early[p] for p in early_pairs[:4]])
    early.update(zip(early_pairs[:4], held))
    far = over(far, 1, 0)
    def mix(start, index, other_start, other, count):
        first, second = start + index * count, other_start + index * count
        return columns(near[first : first + count], other[second : second + count])

    blocks = {z: mix(0, z, -cut, far, cut) for z in hops}
    order = [2, 1, 3]
    values, held = after([blocks[z] for z in order], [early[p] for p in late_pairs[:1]])
    early.update(zip(late_pairs[:1], held))
    two, one, three = (over(value, 0, z) for value, z in zip(values, order))
    (home,), (one,) = after([home], [one])
    home = over(home, 1, 0)
    low = [mix(0, 0, 0, home, cut), one, two, three]
    high = [mix(time_count * cut, 0, cut, home, rest)]
    high += [mix(time_count * cut, z, 3 * cut - rest, far, rest) for z in hops]

    def with_other(values):
        return [side for v in values for side in (v, travel(v, ("pol",), (1,)))]

    early = with_other([jnp.stack([early[p] for p in pairs])])
    blocks, held = after(high[1:], [low[2], low[1], early[1]])
    low[2], low[1], early[1] = held
    moved = {z: over(blocks[z - 1], 0, z) for z in (2, 1, 3)}
    high = [high[0]] + [moved[z] for z in (1, 2, 3)]
    low = jnp.stack(low).reshape(2 * time_count, cut, 2, ROWS, LANES)
    visibility = correlate_tiles(
        place, tables_of_tiles, early + with_other([low]),
        [0, 0], width, 0, cut, bands, None,
    )
    high, (visibility,) = after(high, [visibility])
    high = jnp.stack(high).reshape(2 * time_count, rest, 2, ROWS, LANES)
    return correlate_tiles(
        place, tables_of_tiles, early + with_other([high]),
        [cut, 0], width, cut, rest, bands, visibility,
    )


def on_device(voltages, taps_filter, tile_a, tile_b, tile_owner, tile_flags):
    taps, length = taps_filter.shape
    frames = voltages.shape[3] // length
    time_count = lax.axis_size("tm")
    fits = (
        length == RADIX * LANES
        and AVG * time_count * frames == LANES
        and 2 * tile_a.shape[1] == LANES
        and voltages.shape[2] == 2 * time_count * ROWS
        and (lax.axis_size("chan"), time_count) == (2, 4)
    )
    form = on_device_chunks if fits else on_device_any
    return form(voltages, taps_filter, tile_a, tile_b, tile_owner, tile_flags)


def solution(mesh):
    return jax.shard_map(
        on_device,
        mesh=mesh,
        in_specs=(P("grp", "pol", "chan", "tm"), P(), P(), P(), P(), P()),
        out_specs=P("pol", ("chan", "tm"), "grp", None, None, None),
        check_vma=False,
    )
```

```python
import math

import jax
import jax.numpy as jnp
import numpy as np
from jax import lax
from jax.experimental import pallas as pl
from jax.experimental.pallas import tpu as pltpu
from jax.sharding import PartitionSpec as P

AVG = 8
CAP = 8
RADIX = 16
LANES = 128
ROWS = 16


radix_first = 32


def from_behind(value, axis, steps):
    count = lax.axis_size(axis)
    first, last = (max(0, -steps), min(count, count - steps))
    return lax.ppermute(value, axis, [(source, source + steps) for source in range(first, last)])


def fourier(filtered):
    length = filtered.shape[-1]
    second = length // radix_first
    exact_mode = lax.Precision.HIGHEST
    grid = filtered.reshape(filtered.shape[:-1] + (radix_first, second))
    outer = jnp.arange(radix_first, dtype=jnp.int32)
    inner = jnp.arange(second, dtype=jnp.int32)
    phase_one = (
        2.0
        * math.pi
        / radix_first
        * (outer[:, None] * outer[None, :] % radix_first).astype(jnp.float32)
    )
    phase_twist = 2.0 * math.pi / length * (outer[:, None] * inner[None, :]).astype(jnp.float32)
    phase_two = (
        2.0 * math.pi / second * (inner[:, None] * inner[None, :] % second).astype(jnp.float32)
    )
    cos_one, sin_one = (jnp.cos(phase_one), jnp.sin(phase_one))
    cos_twist, sin_twist = (jnp.cos(phase_twist), jnp.sin(phase_twist))
    cos_two, sin_two = (jnp.cos(phase_two), jnp.sin(phase_two))
    first_form = "fk,stkj->stfj"
    section_re = jnp.einsum(first_form, cos_one, grid[0], precision=exact_mode) + jnp.einsum(
        first_form, sin_one, grid[1], precision=exact_mode
    )
    section_im = jnp.einsum(first_form, cos_one, grid[1], precision=exact_mode) - jnp.einsum(
        first_form, sin_one, grid[0], precision=exact_mode
    )
    turned_re = section_re * cos_twist + section_im * sin_twist
    turned_im = section_im * cos_twist - section_re * sin_twist
    second_form = "gj,stfj->stgf"
    final_re = jnp.einsum(second_form, cos_two, turned_re, precision=exact_mode) + jnp.einsum(
        second_form, sin_two, turned_im, precision=exact_mode
    )
    final_im = jnp.einsum(second_form, cos_two, turned_im, precision=exact_mode) - jnp.einsum(
        second_form, sin_two, turned_re, precision=exact_mode
    )
    joined = jnp.stack([final_re, final_im]).reshape(filtered.shape)
    return joined * (1.0 / math.sqrt(length))


def correlate(full, rows_a, rows_b, flags, group_count):
    depth = full.shape[4]
    weight = jnp.tile(flags.astype(jnp.bfloat16), depth // flags.shape[0])
    left_rows = jnp.take(full, rows_a, axis=2) * weight
    right_rows = jnp.take(full, rows_b, axis=2)
    stacked_left = jnp.stack(
        [
            jnp.concatenate([left_rows[0], left_rows[1]], axis=-1),
            jnp.concatenate([left_rows[1], -left_rows[0]], axis=-1),
        ]
    )
    joined_right = jnp.concatenate([right_rows[0], right_rows[1]], axis=-1)
    result = jnp.einsum(
        "rpank,qbnk->nrpaqb", stacked_left, joined_right, preferred_element_type=jnp.float32
    )
    width = rows_a.shape[0]
    return result.reshape(group_count, 2, 2, width, 2 * width) * (1.0 / depth)


def on_device_any(voltages, taps_filter, tile_a, tile_b, tile_owner, tile_flags):
    history = taps_filter.shape[0] - 1
    length = taps_filter.shape[1]
    stations = voltages.shape[2]
    frames = voltages.shape[3] // length
    local_blocks = voltages.reshape(2, stations, frames, length)
    hop_count = -(-history // frames)
    sending = local_blocks
    extended = local_blocks
    for hop_index in range(hop_count):
        sending = from_behind(sending, "tm", 1)
        extended = jnp.concatenate([sending, extended], axis=2)
    extended = extended[:, :, extended.shape[2] - history - frames :]
    filtered = jnp.zeros((2, stations, frames, length), jnp.float32)
    for tap_index in range(history + 1):
        start = history - tap_index
        filtered = filtered + taps_filter[tap_index] * extended[
            :, :, start : start + frames
        ].astype(jnp.float32)
    spectra = fourier(filtered).astype(jnp.bfloat16)
    chan_count = lax.axis_size("chan")
    time_count = lax.axis_size("tm")
    narrow = length // (chan_count * time_count)
    outgoing = spectra.reshape(2, stations, frames, chan_count, time_count, narrow)
    outgoing = outgoing.transpose(0, 3, 4, 5, 1, 2)
    flat = outgoing.reshape(2, chan_count * time_count, narrow, stations * frames)
    moved = lax.all_to_all(flat, ("chan", "tm"), split_axis=1, concat_axis=1, tiled=True)
    moved = moved.reshape(2, chan_count, time_count, narrow, stations, frames)
    bands = narrow // AVG
    every_station = chan_count * stations
    spectra_count = time_count * frames
    arranged = moved.transpose(0, 1, 4, 3, 2, 5).reshape(
        2, 1, every_station, bands, AVG * spectra_count
    )
    full = lax.all_gather(arranged, "pol", axis=1, tiled=True)
    position = lax.axis_index("pol")
    width = tile_a.shape[1]
    capacity = CAP
    held = tile_owner == position
    listed = jnp.nonzero(held, size=capacity, fill_value=0)[0].astype(jnp.int32)
    tally = jnp.sum(held.astype(jnp.int32))
    initial = jnp.zeros((capacity, bands, 2, 2, width, 2 * width), jnp.float32)

    def fill_slot(slot, results):
        chosen_tile = listed[slot]
        return results.at[slot].set(
            correlate(
                full, tile_a[chosen_tile], tile_b[chosen_tile], tile_flags[chosen_tile], bands
            )
        )

    visibility = lax.fori_loop(0, tally, fill_slot, initial)
    return visibility


def fourier_tables(length):
    low = np.arange(RADIX)
    lane = np.arange(LANES)
    turn = 2.0 * np.pi / length * np.outer(low, lane)
    twiddle = np.stack([np.cos(turn), np.sin(turn)]).astype(np.float32)
    angle = 2.0 * np.pi / LANES * (np.outer(lane, lane) % LANES)
    cos, sin = np.cos(angle) / math.sqrt(length), np.sin(angle) / math.sqrt(length)
    matrix = np.block([[cos, sin], [-sin, cos]]).astype(np.float32)
    high = matrix.astype(jnp.bfloat16)
    rest = (matrix - high.astype(np.float32)).astype(jnp.bfloat16)
    return twiddle, np.stack([high, rest])


def butterflies(values):
    count = len(values)
    if count == 1:
        return values
    even, odd = butterflies(values[0::2]), butterflies(values[1::2])
    first, second = [], []
    for index in range(count // 2):
        (a, b), (c, d) = even[index], odd[index]
        if index == 0:
            e, f = c, d
        elif 4 * index == count:
            e, f = d, -c
        elif 8 * index == count:
            root = math.sqrt(0.5)
            e, f = (c + d) * root, (d - c) * root
        elif 8 * index == 3 * count:
            root = math.sqrt(0.5)
            e, f = (d - c) * root, -(c + d) * root
        else:
            turn = 2.0 * math.pi * index / count
            cos, sin = math.cos(turn), math.sin(turn)
            e, f = c * cos + d * sin, d * cos - c * sin
        first.append((a + e, b + f))
        second.append((a - e, b - f))
    return first + second


def channelise_kernel(frames, chunk, columns, plan, place_ref, own_ref, *refs):
    sources = refs[-6].shape[0]
    come_refs = refs[: sources - 1]
    taps_ref, twiddle_ref, matrix_ref = refs[sources - 1 : sources + 2]
    out_refs = refs[sources + 2 : -6]
    x_ref, fil_ref, zr_ref, zi_ref, w_ref, sems = refs[-6:]
    chan, tm = place_ref[0], place_ref[1]
    own_rows = pl.multiple_of((tm * (own_ref.shape[1] // (sources * ROWS)) + chunk) * ROWS, ROWS)
    copies = []
    for behind in range(sources):
        block = come_refs[behind - 1] if behind else own_ref.at[:, pl.ds(own_rows, ROWS), :]
        slot = lax.rem(tm - behind + sources, sources)
        copies.append(pltpu.make_async_copy(block, x_ref.at[slot], sems.at[behind]))
    for copy in copies:
        copy.start()
    for copy in copies:
        copy.wait()
    spectra = sources * frames
    length = taps_ref.shape[1]
    taps = taps_ref.shape[0]
    depth = RADIX * spectra
    z_refs = (zr_ref, zi_ref)

    @pl.loop(0, RADIX)
    def _(section):
        at = pl.multiple_of(section * LANES, LANES)
        weights = [taps_ref[pl.ds(m, 1), pl.ds(at, LANES)] for m in range(taps)]
        for part in range(2):
            blocks = []
            for t in range(spectra):
                lane = pl.multiple_of((t % frames) * length + section * LANES, LANES)
                blocks.append(x_ref[t // frames, part, :, pl.ds(lane, LANES)].astype(jnp.float32))
            for t in range(spectra):
                total = weights[0] * blocks[t]
                for m in range(1, min(t + 1, taps)):
                    total = total + weights[m] * blocks[t - m]
                fil_ref[section, t, part] = total

    @pl.loop(0, spectra)
    def _(t):
        for half in range(ROWS // 8):
            values = [
                tuple(fil_ref[section, t, part, pl.ds(half * 8, 8), :] for part in range(2))
                for section in range(RADIX)
            ]
            for low, (re, im) in enumerate(butterflies(values)):
                if low:
                    cos = twiddle_ref[0, pl.ds(low, 1), :]
                    sin = twiddle_ref[1, pl.ds(low, 1), :]
                    re, im = re * cos + im * sin, im * cos - re * sin
                rows = pl.ds(half * 8 * depth + low * spectra + t, 8, stride=depth)
                zr_ref[rows, :] = re
                zi_ref[rows, :] = im

    form = (((1,), (1,)), ((), ()))
    high_matrix, low_matrix = matrix_ref[0], matrix_ref[1]
    halves = depth // LANES

    @pl.loop(0, ROWS)
    def _(station):
        rows = pl.ds(pl.multiple_of(station * depth, depth), depth)
        value = jnp.concatenate([ref[rows, :] for ref in z_refs], axis=1)
        high = value.astype(jnp.bfloat16)
        rest = (value - high.astype(jnp.float32)).astype(jnp.bfloat16)
        total = lax.dot_general(high_matrix, high, form, preferred_element_type=jnp.float32)
        total += lax.dot_general(high_matrix, rest, form, preferred_element_type=jnp.float32)
        total += lax.dot_general(low_matrix, high, form, preferred_element_type=jnp.float32)
        for half in range(halves):
            for part in range(2):
                rows = pl.ds((half * 2 + part) * ROWS + station, LANES, stride=halves * 2 * ROWS)
                w_ref[rows, :] = total[
                    part * LANES : (part + 1) * LANES, half * LANES : (half + 1) * LANES
                ]

    share = w_ref.shape[0] // (columns * sources)
    band_rows = 2 * ROWS
    piece = 2 * band_rows
    for blocks, out_ref in zip(plan, out_refs):
        at = 0
        for across, along, start, stop in blocks:
            owner = lax.rem(chan + across, columns) * sources + lax.rem(tm + along, sources)
            for row in range(start * band_rows, stop * band_rows, piece):
                rows = pl.ds(pl.multiple_of(owner * share + row, piece), piece)
                out_ref[at : at + piece, :] = w_ref[rows, :].astype(jnp.bfloat16)
                at += piece


def channelise(place, chunk, voltages, come, taps_filter, tables, frames, columns, plan):
    sources = 1 + len(come)
    length = taps_filter.shape[1]
    spectra = sources * frames
    twiddle, matrix = tables
    out_rows = length // AVG * 2 * ROWS
    whole = pl.BlockSpec(memory_space=pltpu.VMEM)
    counts = [sum(stop - start for _, _, start, stop in blocks) for blocks in plan]
    flat = pl.pallas_call(
        lambda *refs: channelise_kernel(frames, chunk, columns, plan, *refs),
        out_shape=[
            jax.ShapeDtypeStruct((count * 2 * ROWS, LANES), jnp.bfloat16) for count in counts
        ],
        in_specs=[pl.BlockSpec(memory_space=pltpu.SMEM)]
        + [pl.BlockSpec(memory_space=pl.ANY)] * sources
        + [whole] * 3,
        out_specs=[whole] * len(plan),
        scratch_shapes=[
            pltpu.VMEM((sources, 2, ROWS, frames * length), jnp.bfloat16),
            pltpu.VMEM((RADIX, spectra, 2, ROWS, LANES), jnp.float32),
            pltpu.VMEM((ROWS * RADIX * spectra, LANES), jnp.float32),
            pltpu.VMEM((ROWS * RADIX * spectra, LANES), jnp.float32),
            pltpu.VMEM((out_rows, LANES), jnp.float32),
            pltpu.SemaphoreType.DMA((sources,)),
        ],
        compiler_params=pltpu.CompilerParams(vmem_limit_bytes=40 * 2**20),
        cost_estimate=pl.CostEstimate(
            flops=9 * 10**9, bytes_accessed=4 * 2**20, transcendentals=0
        ),
        name="channelise",
    )(place, voltages, *come, taps_filter, jnp.asarray(twiddle), jnp.asarray(matrix))
    return [piece.reshape(count, 2, ROWS, LANES) for piece, count in zip(flat, counts)]


def correlate_kernel(starts, width, place_ref, left_sel_ref, right_sel_ref, weight_ref, *refs):
    x_refs, (out_ref, x_all, *rows_refs, sems) = refs[: 2 * len(starts)], refs[-7:]
    tiles = out_ref.shape[0]
    step = pl.program_id(0)
    bands = x_all.shape[2]
    spans = [(0, 2), (2, bands)]

    def copies(span):
        first, last = spans[span]
        block = 0
        for index, start in enumerate(starts):
            blocks = x_refs[2 * index].shape[0]
            for side in range(2):
                yield pltpu.make_async_copy(
                    x_refs[2 * index + side].at[:, pl.ds(start + first, last - first)],
                    x_all.at[
                        lax.rem(place_ref[2] + side, 2),
                        pl.ds(block, blocks),
                        pl.ds(first, last - first),
                    ],
                    sems.at[span, 2 * index + side],
                )
            block += blocks

    lower = lax.broadcasted_iota(jnp.int32, (1, 2 * width), 1) < width

    def gather(band, left_ref, right_ref):
        right = []
        for pol in range(2):
            lanes = slice(pol * 2 * LANES, (pol + 1) * 2 * LANES)
            value = jnp.concatenate(
                [
                    jnp.concatenate([x_all[pol, block, band, part] for part in range(2)], axis=1)
                    for block in range(x_all.shape[1])
                ]
            )
            left = jnp.dot(left_sel_ref[...], value, preferred_element_type=jnp.float32)
            for tile in range(tiles):
                rows = slice(tile * width, (tile + 1) * width)
                scaled = left[rows] * weight_ref[pl.ds(tile, 1), :]
                left_ref[rows, lanes] = scaled.astype(jnp.bfloat16)
            right.append(
                lax.dot_general(
                    value,
                    right_sel_ref[pol],
                    (((0,), (0,)), ((), ())),
                    preferred_element_type=jnp.float32,
                )
            )
        for pair in range(tiles // 2):
            first, second = (v[:, pair * 2 * width : (pair + 1) * 2 * width] for v in right)
            even = jnp.where(lower, first, second)
            odd = pltpu.roll(jnp.where(lower, second, first), width, 1)
            right_ref[2 * pair] = even.astype(jnp.bfloat16)
            right_ref[2 * pair + 1] = odd.astype(jnp.bfloat16)

    def multiply(number, left_ref, right_ref):
        for tile in range(tiles):
            rows = slice(tile * width, (tile + 1) * width)
            left = jnp.concatenate(
                [left_ref[rows, lanes : lanes + 2 * LANES] for lanes in (0, 2 * LANES)]
            )
            right = right_ref[tile]
            turned = jnp.concatenate([-right[LANES:], right[:LANES]])
            both = jnp.concatenate([right, turned], axis=1)
            result = jnp.dot(left, both, preferred_element_type=jnp.float32)
            for part in range(2):
                out_ref[tile, number, part] = result[
                    :, part * 2 * width : (part + 1) * 2 * width
                ].reshape(2, width, 2 * width)

    even, odd = rows_refs[:2], rows_refs[2:]

    @pl.when(step == 0)
    def _():
        for span in range(2):
            for copy in copies(span):
                copy.start()
        for copy in copies(0):
            copy.wait()
        gather(0, *even)
        for copy in copies(1):
            copy.wait()

    gather(2 * step + 1, *odd)
    multiply(0, *even)
    gather(jnp.minimum(2 * step + 2, bands - 1), *even)
    multiply(1, *odd)


def correlate_tiles(place, tables, pieces, starts, width, first, count, bands, earlier):
    left_select, _, weight = tables
    tiles = weight.shape[0]
    whole = pl.BlockSpec(memory_space=pltpu.VMEM)
    more = [] if earlier is None else [earlier]
    rows = [
        pltpu.VMEM((tiles * width, 4 * LANES), jnp.bfloat16),
        pltpu.VMEM((tiles, 2 * LANES, 2 * width), jnp.bfloat16),
    ]
    return pl.pallas_call(
        lambda *refs: correlate_kernel(starts, width, *refs),
        grid=(count // 2,),
        out_shape=jax.ShapeDtypeStruct((tiles, bands, 2, 2, width, 2 * width), jnp.float32),
        in_specs=[pl.BlockSpec(memory_space=pltpu.SMEM)]
        + [whole] * len(tables)
        + [pl.BlockSpec(memory_space=pl.ANY)] * (len(pieces) + len(more)),
        out_specs=pl.BlockSpec(
            (tiles, 2, 2, 2, width, 2 * width), lambda g: (0, g + first // 2, 0, 0, 0, 0)
        ),
        scratch_shapes=[
            pltpu.VMEM((2, left_select.shape[1] // ROWS, count, 2, ROWS, LANES), jnp.bfloat16),
            *rows,
            *rows,
            pltpu.SemaphoreType.DMA((2, len(pieces))),
        ],
        input_output_aliases={1 + len(tables) + len(pieces): 0} if more else {},
        compiler_params=pltpu.CompilerParams(vmem_limit_bytes=32 * 2**20),
        cost_estimate=pl.CostEstimate(
            flops=13 * 10**9 * count // bands,
            bytes_accessed=42 * 2**20 * count // bands,
            transcendentals=0,
        ),
        name="correlate",
    )(place, *tables, *pieces, *more)


def tile_tables(tile_a, tile_b, tile_owner, tile_flags, row_of):
    tiles = tile_owner.shape[0]
    held = tile_owner == lax.axis_index("pol")
    order = jnp.arange(tiles, dtype=jnp.int32)
    rank = jnp.sum((held[None, :] & (order[None, :] < order[:, None])).astype(jnp.int32), axis=1)
    slots = jnp.arange(CAP, dtype=jnp.int32)
    pick = (held[None, :] & (rank[None, :] == slots[:, None])).astype(jnp.int32)
    sides = jnp.stack([row_of(tile_a), row_of(tile_b)], axis=1) + 1
    rows = jnp.sum(pick[:, :, None, None] * sides[None], axis=1) - 1
    flags = jnp.sum(pick[:, :, None] * tile_flags[None], axis=1).astype(jnp.float32)
    return rows, flags


def on_device_chunks(voltages, taps_filter, tile_a, tile_b, tile_owner, tile_flags):
    length = taps_filter.shape[1]
    stations = voltages.shape[2]
    frames = voltages.shape[3] // length
    chan_count, time_count = lax.axis_size("chan"), lax.axis_size("tm")
    owners = chan_count * time_count
    chunk_count = stations // (time_count * ROWS)
    width = tile_a.shape[1]
    bands = length // AVG // owners
    tables = fourier_tables(length)

    chan, tm = lax.axis_index("chan"), lax.axis_index("tm")
    place = jnp.stack([chan, tm, lax.axis_index("pol")]).astype(jnp.int32)

    def row_of(station):
        column, rest = station // stations, station % stations
        block, inside = rest // (chunk_count * ROWS), rest % (chunk_count * ROWS)
        across = (chan - column) % chan_count
        behind = (tm - block) % time_count
        piece = behind * chan_count + across
        return ((inside // ROWS) * owners + piece) * ROWS + inside % ROWS

    rows, flags = tile_tables(tile_a, tile_b, tile_owner, tile_flags, row_of)
    total_rows = chunk_count * owners * ROWS
    station_rows = jnp.arange(total_rows, dtype=jnp.int32)
    left_rows = rows[:, 0].reshape(-1)
    left_select = (left_rows[:, None] == station_rows).astype(jnp.bfloat16)
    right_rows = rows[:, 1].reshape(CAP // 2, 2, width)
    right_rows = jnp.stack([right_rows, right_rows[:, ::-1]]).reshape(2, 1, -1)
    right_select = (right_rows == station_rows[:, None]).astype(jnp.bfloat16)
    depth = AVG * time_count * frames
    weight = jnp.tile(flags * (1.0 / depth), (1, 2 * AVG))
    tables_of_tiles = [left_select, right_select, weight]

    samples = voltages.reshape(2, stations, frames * length)

    def travel(value, axes, distances):
        sizes = [lax.axis_size(axis) for axis in axes]
        pairs = []
        for index in np.ndindex(*sizes):
            target = [(i + d) % n for i, d, n in zip(index, distances, sizes)]
            pairs.append(tuple(int(np.ravel_multi_index(x, sizes)) for x in (index, target)))
        return lax.ppermute(value, axes, pairs)

    def after(values, earlier):
        return lax.optimization_barrier((list(values), list(earlier)))

    def block_for(values, chunk, distance):
        first = ((tm + distance) % time_count * chunk_count + chunk) * ROWS
        return lax.dynamic_slice(values, (0, first, 0), (2, ROWS, frames * length))

    def filtered(chunk, arrived, plan):
        return channelise(
            place, chunk, samples, arrived, taps_filter, tables, frames, chan_count, plan
        )

    def over(value, across, along):
        return travel(value, ("chan", "tm"), (across, along))

    def columns(near, far):
        return jnp.stack([near, far])

    cut = bands * 5 // 8
    rest = bands - cut
    pairs = [(x, z) for z in range(time_count) for x in range(chan_count)]
    early_pairs = [(x, z) for z in (1, 3) for x in range(2)]
    late_pairs = [(0, 2), (1, 2), (1, 0)]

    (one,), (values,) = after([block_for(samples, 0, 1)], [samples])
    two, three = (block_for(values, 0, distance) for distance in (2, 3))
    one, two = over(one, 0, 1), over(two, 0, 2)
    (three,), (one,) = after([three], [one])
    three = over(three, 0, 3)
    blocks = [block_for(values, 1, distance) for distance in (1, 2, 3)]
    blocks[:1], (two,) = after(blocks[:1], [two])
    blocks[2:], (three,) = after(blocks[2:], [three])
    first = [one, two, three]
    one, three = over(blocks[0], 0, 1), over(blocks[2], 0, 3)
    (two,), (one,) = after(blocks[1:2], [one])
    second = [one, over(two, 0, 2), three]

    plan = [[(x, z, 0, bands)] for x, z in pairs]
    early = dict(zip(pairs, filtered(0, first, plan)))
    blocks, held = after([early[p] for p in early_pairs], [second[1], *tables_of_tiles])
    second[1], tables_of_tiles = held[0], held[1:]
    early.update((p, over(block, *p)) for p, block in zip(early_pairs, blocks))
    spans = [(0, cut), (cut, bands)]
    hops = [1, 2, 3]
    plan = [[(0, z, *span) for span in spans for z in range(time_count)]]
    plan += [[(1, z, *span) for span in spans for z in hops], [(1, 0, *span) for span in spans]]
    near, far, home = filtered(1, second, plan)
    blocks, (near,) = after([early[p] for p in late_pairs], [near])
    early.update((p, over(block, *p)) for p, block in zip(late_pairs, blocks))
    (far,), held = after([far], [early[p] for p in early_pairs[:4]])
    early.update(zip(early_pairs[:4], held))
    far = over(far, 1, 0)
    def mix(start, index, other_start, other, count):
        first, second = start + index * count, other_start + index * count
        return columns(near[first : first + count], other[second : second + count])

    blocks = {z: mix(0, z, -cut, far, cut) for z in hops}
    order = [2, 1, 3]
    sent = []
    for z in order:
        (value,), (early[0, 2],) = after([blocks[z]], [early[0, 2]])
        sent.append(over(value, 0, z))
    two, one, three = sent
    (home,), (one,) = after([home], [one])
    home = over(home, 1, 0)
    low = [mix(0, 0, 0, home, cut), one, two, three]
    high = [mix(time_count * cut, 0, cut, home, rest)]
    high += [mix(time_count * cut, z, 3 * cut - rest, far, rest) for z in hops]

    def with_other(values):
        return [side for v in values for side in (v, travel(v, ("pol",), (1,)))]

    early = with_other([jnp.stack([early[p] for p in pairs])])
    blocks, held = after(high[1:], [low[2], low[1], early[1]])
    low[2], low[1], early[1] = held
    moved = {z: over(blocks[z - 1], 0, z) for z in (2, 1, 3)}
    high = [high[0]] + [moved[z] for z in (1, 2, 3)]
    low = jnp.stack(low).reshape(2 * time_count, cut, 2, ROWS, LANES)
    visibility = correlate_tiles(
        place, tables_of_tiles, early + with_other([low]),
        [0, 0], width, 0, cut, bands, None,
    )
    high, (visibility,) = after(high, [visibility])
    high = jnp.stack(high).reshape(2 * time_count, rest, 2, ROWS, LANES)
    return correlate_tiles(
        place, tables_of_tiles, early + with_other([high]),
        [cut, 0], width, cut, rest, bands, visibility,
    )


def on_device(voltages, taps_filter, tile_a, tile_b, tile_owner, tile_flags):
    taps, length = taps_filter.shape
    frames = voltages.shape[3] // length
    time_count = lax.axis_size("tm")
    fits = (
        length == RADIX * LANES
        and AVG * time_count * frames == LANES
        and 2 * tile_a.shape[1] == LANES
        and voltages.shape[2] == 2 * time_count * ROWS
        and (lax.axis_size("chan"), time_count) == (2, 4)
    )
    form = on_device_chunks if fits else on_device_any
    return form(voltages, taps_filter, tile_a, tile_b, tile_owner, tile_flags)


def solution(mesh):
    return jax.shard_map(
        on_device,
        mesh=mesh,
        in_specs=(P("grp", "pol", "chan", "tm"), P(), P(), P(), P(), P()),
        out_specs=P("pol", ("chan", "tm"), "grp", None, None, None),
        check_vma=False,
    )
```

```python
import math

import jax
import jax.numpy as jnp
import numpy as np
from jax import lax
from jax.experimental import pallas as pl
from jax.experimental.pallas import tpu as pltpu
from jax.sharding import PartitionSpec as P

AVG = 8
CAP = 8
RADIX = 16
LANES = 128
ROWS = 16


radix_first = 32


def from_behind(value, axis, steps):
    count = lax.axis_size(axis)
    first, last = (max(0, -steps), min(count, count - steps))
    return lax.ppermute(value, axis, [(source, source + steps) for source in range(first, last)])


def fourier(filtered):
    length = filtered.shape[-1]
    second = length // radix_first
    exact_mode = lax.Precision.HIGHEST
    grid = filtered.reshape(filtered.shape[:-1] + (radix_first, second))
    outer = jnp.arange(radix_first, dtype=jnp.int32)
    inner = jnp.arange(second, dtype=jnp.int32)
    phase_one = (
        2.0
        * math.pi
        / radix_first
        * (outer[:, None] * outer[None, :] % radix_first).astype(jnp.float32)
    )
    phase_twist = 2.0 * math.pi / length * (outer[:, None] * inner[None, :]).astype(jnp.float32)
    phase_two = (
        2.0 * math.pi / second * (inner[:, None] * inner[None, :] % second).astype(jnp.float32)
    )
    cos_one, sin_one = (jnp.cos(phase_one), jnp.sin(phase_one))
    cos_twist, sin_twist = (jnp.cos(phase_twist), jnp.sin(phase_twist))
    cos_two, sin_two = (jnp.cos(phase_two), jnp.sin(phase_two))
    first_form = "fk,stkj->stfj"
    section_re = jnp.einsum(first_form, cos_one, grid[0], precision=exact_mode) + jnp.einsum(
        first_form, sin_one, grid[1], precision=exact_mode
    )
    section_im = jnp.einsum(first_form, cos_one, grid[1], precision=exact_mode) - jnp.einsum(
        first_form, sin_one, grid[0], precision=exact_mode
    )
    turned_re = section_re * cos_twist + section_im * sin_twist
    turned_im = section_im * cos_twist - section_re * sin_twist
    second_form = "gj,stfj->stgf"
    final_re = jnp.einsum(second_form, cos_two, turned_re, precision=exact_mode) + jnp.einsum(
        second_form, sin_two, turned_im, precision=exact_mode
    )
    final_im = jnp.einsum(second_form, cos_two, turned_im, precision=exact_mode) - jnp.einsum(
        second_form, sin_two, turned_re, precision=exact_mode
    )
    joined = jnp.stack([final_re, final_im]).reshape(filtered.shape)
    return joined * (1.0 / math.sqrt(length))


def correlate(full, rows_a, rows_b, flags, group_count):
    depth = full.shape[4]
    weight = jnp.tile(flags.astype(jnp.bfloat16), depth // flags.shape[0])
    left_rows = jnp.take(full, rows_a, axis=2) * weight
    right_rows = jnp.take(full, rows_b, axis=2)
    stacked_left = jnp.stack(
        [
            jnp.concatenate([left_rows[0], left_rows[1]], axis=-1),
            jnp.concatenate([left_rows[1], -left_rows[0]], axis=-1),
        ]
    )
    joined_right = jnp.concatenate([right_rows[0], right_rows[1]], axis=-1)
    result = jnp.einsum(
        "rpank,qbnk->nrpaqb", stacked_left, joined_right, preferred_element_type=jnp.float32
    )
    width = rows_a.shape[0]
    return result.reshape(group_count, 2, 2, width, 2 * width) * (1.0 / depth)


def on_device_any(voltages, taps_filter, tile_a, tile_b, tile_owner, tile_flags):
    history = taps_filter.shape[0] - 1
    length = taps_filter.shape[1]
    stations = voltages.shape[2]
    frames = voltages.shape[3] // length
    local_blocks = voltages.reshape(2, stations, frames, length)
    hop_count = -(-history // frames)
    sending = local_blocks
    extended = local_blocks
    for hop_index in range(hop_count):
        sending = from_behind(sending, "tm", 1)
        extended = jnp.concatenate([sending, extended], axis=2)
    extended = extended[:, :, extended.shape[2] - history - frames :]
    filtered = jnp.zeros((2, stations, frames, length), jnp.float32)
    for tap_index in range(history + 1):
        start = history - tap_index
        filtered = filtered + taps_filter[tap_index] * extended[
            :, :, start : start + frames
        ].astype(jnp.float32)
    spectra = fourier(filtered).astype(jnp.bfloat16)
    chan_count = lax.axis_size("chan")
    time_count = lax.axis_size("tm")
    narrow = length // (chan_count * time_count)
    outgoing = spectra.reshape(2, stations, frames, chan_count, time_count, narrow)
    outgoing = outgoing.transpose(0, 3, 4, 5, 1, 2)
    flat = outgoing.reshape(2, chan_count * time_count, narrow, stations * frames)
    moved = lax.all_to_all(flat, ("chan", "tm"), split_axis=1, concat_axis=1, tiled=True)
    moved = moved.reshape(2, chan_count, time_count, narrow, stations, frames)
    bands = narrow // AVG
    every_station = chan_count * stations
    spectra_count = time_count * frames
    arranged = moved.transpose(0, 1, 4, 3, 2, 5).reshape(
        2, 1, every_station, bands, AVG * spectra_count
    )
    full = lax.all_gather(arranged, "pol", axis=1, tiled=True)
    position = lax.axis_index("pol")
    width = tile_a.shape[1]
    capacity = CAP
    held = tile_owner == position
    listed = jnp.nonzero(held, size=capacity, fill_value=0)[0].astype(jnp.int32)
    tally = jnp.sum(held.astype(jnp.int32))
    initial = jnp.zeros((capacity, bands, 2, 2, width, 2 * width), jnp.float32)

    def fill_slot(slot, results):
        chosen_tile = listed[slot]
        return results.at[slot].set(
            correlate(
                full, tile_a[chosen_tile], tile_b[chosen_tile], tile_flags[chosen_tile], bands
            )
        )

    visibility = lax.fori_loop(0, tally, fill_slot, initial)
    return visibility


def fourier_tables(length):
    low = np.arange(RADIX)
    lane = np.arange(LANES)
    turn = 2.0 * np.pi / length * np.outer(low, lane)
    twiddle = np.stack([np.cos(turn), np.sin(turn)]).astype(np.float32)
    angle = 2.0 * np.pi / LANES * (np.outer(lane, lane) % LANES)
    cos, sin = np.cos(angle) / math.sqrt(length), np.sin(angle) / math.sqrt(length)
    matrix = np.block([[cos, sin], [-sin, cos]]).astype(np.float32)
    high = matrix.astype(jnp.bfloat16)
    rest = (matrix - high.astype(np.float32)).astype(jnp.bfloat16)
    return twiddle, np.stack([high, rest])


def butterflies(values):
    count = len(values)
    if count == 1:
        return values
    even, odd = butterflies(values[0::2]), butterflies(values[1::2])
    first, second = [], []
    for index in range(count // 2):
        (a, b), (c, d) = even[index], odd[index]
        if index == 0:
            e, f = c, d
        elif 4 * index == count:
            e, f = d, -c
        elif 8 * index == count:
            root = math.sqrt(0.5)
            e, f = (c + d) * root, (d - c) * root
        elif 8 * index == 3 * count:
            root = math.sqrt(0.5)
            e, f = (d - c) * root, -(c + d) * root
        else:
            turn = 2.0 * math.pi * index / count
            cos, sin = math.cos(turn), math.sin(turn)
            e, f = c * cos + d * sin, d * cos - c * sin
        first.append((a + e, b + f))
        second.append((a - e, b - f))
    return first + second


def channelise_kernel(frames, chunk, columns, plan, place_ref, own_ref, *refs):
    sources = refs[-6].shape[0]
    come_refs = refs[: sources - 1]
    taps_ref, twiddle_ref, matrix_ref = refs[sources - 1 : sources + 2]
    out_refs = refs[sources + 2 : -6]
    x_ref, fil_ref, zr_ref, zi_ref, w_ref, sems = refs[-6:]
    chan, tm = place_ref[0], place_ref[1]
    own_rows = pl.multiple_of((tm * (own_ref.shape[1] // (sources * ROWS)) + chunk) * ROWS, ROWS)
    copies = []
    for behind in range(sources):
        block = come_refs[behind - 1] if behind else own_ref.at[:, pl.ds(own_rows, ROWS), :]
        slot = lax.rem(tm - behind + sources, sources)
        copies.append(pltpu.make_async_copy(block, x_ref.at[slot], sems.at[behind]))
    for copy in copies:
        copy.start()
    for copy in copies:
        copy.wait()
    spectra = sources * frames
    length = taps_ref.shape[1]
    taps = taps_ref.shape[0]
    depth = RADIX * spectra
    z_refs = (zr_ref, zi_ref)

    @pl.loop(0, RADIX)
    def _(section):
        at = pl.multiple_of(section * LANES, LANES)
        weights = [taps_ref[pl.ds(m, 1), pl.ds(at, LANES)] for m in range(taps)]
        for part in range(2):
            blocks = []
            for t in range(spectra):
                lane = pl.multiple_of((t % frames) * length + section * LANES, LANES)
                blocks.append(x_ref[t // frames, part, :, pl.ds(lane, LANES)].astype(jnp.float32))
            for t in range(spectra):
                total = weights[0] * blocks[t]
                for m in range(1, min(t + 1, taps)):
                    total = total + weights[m] * blocks[t - m]
                fil_ref[section, t, part] = total

    @pl.loop(0, spectra)
    def _(t):
        for half in range(ROWS // 8):
            values = [
                tuple(fil_ref[section, t, part, pl.ds(half * 8, 8), :] for part in range(2))
                for section in range(RADIX)
            ]
            for low, (re, im) in enumerate(butterflies(values)):
                if low:
                    cos = twiddle_ref[0, pl.ds(low, 1), :]
                    sin = twiddle_ref[1, pl.ds(low, 1), :]
                    re, im = re * cos + im * sin, im * cos - re * sin
                rows = pl.ds(half * 8 * depth + low * spectra + t, 8, stride=depth)
                zr_ref[rows, :] = re
                zi_ref[rows, :] = im

    form = (((1,), (1,)), ((), ()))
    high_matrix, low_matrix = matrix_ref[0], matrix_ref[1]
    halves = depth // LANES

    @pl.loop(0, ROWS)
    def _(station):
        rows = pl.ds(pl.multiple_of(station * depth, depth), depth)
        value = jnp.concatenate([ref[rows, :] for ref in z_refs], axis=1)
        high = value.astype(jnp.bfloat16)
        rest = (value - high.astype(jnp.float32)).astype(jnp.bfloat16)
        total = lax.dot_general(high_matrix, high, form, preferred_element_type=jnp.float32)
        total += lax.dot_general(high_matrix, rest, form, preferred_element_type=jnp.float32)
        total += lax.dot_general(low_matrix, high, form, preferred_element_type=jnp.float32)
        for half in range(halves):
            for part in range(2):
                rows = pl.ds((half * 2 + part) * ROWS + station, LANES, stride=halves * 2 * ROWS)
                w_ref[rows, :] = total[
                    part * LANES : (part + 1) * LANES, half * LANES : (half + 1) * LANES
                ]

    share = length // AVG * 2 * ROWS // (columns * sources)
    band_rows = 2 * ROWS
    piece = 2 * band_rows
    for blocks, out_ref in zip(plan, out_refs):
        at = 0
        for across, along, start, stop in blocks:
            owner = lax.rem(chan + across, columns) * sources + lax.rem(tm + along, sources)
            for row in range(start * band_rows, stop * band_rows, piece):
                rows = pl.ds(pl.multiple_of(owner * share + row, piece), piece)
                out_ref[at : at + piece, :] = w_ref[rows, :].astype(jnp.bfloat16)
                at += piece


def channelise(place, chunk, voltages, come, taps_filter, tables, frames, columns, plan):
    sources = 1 + len(come)
    length = taps_filter.shape[1]
    spectra = sources * frames
    twiddle, matrix = tables
    out_rows = length // AVG * 2 * ROWS
    whole = pl.BlockSpec(memory_space=pltpu.VMEM)
    counts = [sum(stop - start for _, _, start, stop in blocks) for blocks in plan]
    flat = pl.pallas_call(
        lambda *refs: channelise_kernel(frames, chunk, columns, plan, *refs),
        out_shape=[
            jax.ShapeDtypeStruct((count * 2 * ROWS, LANES), jnp.bfloat16) for count in counts
        ],
        in_specs=[pl.BlockSpec(memory_space=pltpu.SMEM)]
        + [pl.BlockSpec(memory_space=pl.ANY)] * sources
        + [whole] * 3,
        out_specs=[whole] * len(plan),
        scratch_shapes=[
            pltpu.VMEM((sources, 2, ROWS, frames * length), jnp.bfloat16),
            pltpu.VMEM((RADIX, spectra, 2, ROWS, LANES), jnp.float32),
            pltpu.VMEM(((ROWS + 1) * RADIX * spectra, LANES), jnp.float32),
            pltpu.VMEM(((ROWS + 1) * RADIX * spectra, LANES), jnp.float32),
            pltpu.VMEM((out_rows + out_rows // LANES, LANES), jnp.float32),
            pltpu.SemaphoreType.DMA((sources,)),
        ],
        compiler_params=pltpu.CompilerParams(vmem_limit_bytes=40 * 2**20),
        cost_estimate=pl.CostEstimate(
            flops=9 * 10**9, bytes_accessed=4 * 2**20, transcendentals=0
        ),
        name="channelise",
    )(place, voltages, *come, taps_filter, jnp.asarray(twiddle), jnp.asarray(matrix))
    return [piece.reshape(count, 2, ROWS, LANES) for piece, count in zip(flat, counts)]


def correlate_kernel(starts, width, place_ref, left_sel_ref, right_sel_ref, weight_ref, *refs):
    x_refs, (out_ref, x_all, *rows_refs, sems) = refs[: 2 * len(starts)], refs[-7:]
    tiles = out_ref.shape[0]
    step = pl.program_id(0)
    bands = x_all.shape[2]
    spans = [(0, 2), (2, bands)]

    def copies(span):
        first, last = spans[span]
        block = 0
        for index, start in enumerate(starts):
            blocks = x_refs[2 * index].shape[0]
            for side in range(2):
                yield pltpu.make_async_copy(
                    x_refs[2 * index + side].at[:, pl.ds(start + first, last - first)],
                    x_all.at[
                        lax.rem(place_ref[2] + side, 2),
                        pl.ds(block, blocks),
                        pl.ds(first, last - first),
                    ],
                    sems.at[span, 2 * index + side],
                )
            block += blocks

    lower = lax.broadcasted_iota(jnp.int32, (1, 2 * width), 1) < width

    def gather(band, left_ref, right_ref):
        right = []
        for pol in range(2):
            lanes = slice(pol * 2 * LANES, (pol + 1) * 2 * LANES)
            value = jnp.concatenate(
                [
                    jnp.concatenate([x_all[pol, block, band, part] for part in range(2)], axis=1)
                    for block in range(x_all.shape[1])
                ]
            )
            left = jnp.dot(left_sel_ref[...], value, preferred_element_type=jnp.float32)
            for tile in range(tiles):
                rows = slice(tile * width, (tile + 1) * width)
                scaled = left[rows] * weight_ref[pl.ds(tile, 1), :]
                left_ref[rows, lanes] = scaled.astype(jnp.bfloat16)
            right.append(
                lax.dot_general(
                    value,
                    right_sel_ref[pol],
                    (((0,), (0,)), ((), ())),
                    preferred_element_type=jnp.float32,
                )
            )
        for pair in range(tiles // 2):
            first, second = (v[:, pair * 2 * width : (pair + 1) * 2 * width] for v in right)
            even = jnp.where(lower, first, second)
            odd = pltpu.roll(jnp.where(lower, second, first), width, 1)
            right_ref[2 * pair] = even.astype(jnp.bfloat16)
            right_ref[2 * pair + 1] = odd.astype(jnp.bfloat16)

    def multiply(number, left_ref, right_ref):
        for tile in range(tiles):
            rows = slice(tile * width, (tile + 1) * width)
            left = jnp.concatenate(
                [left_ref[rows, lanes : lanes + 2 * LANES] for lanes in (0, 2 * LANES)]
            )
            right = right_ref[tile]
            turned = jnp.concatenate([-right[LANES:], right[:LANES]])
            both = jnp.concatenate([right, turned], axis=1)
            result = jnp.dot(left, both, preferred_element_type=jnp.float32)
            for part in range(2):
                out_ref[tile, number, part] = result[
                    :, part * 2 * width : (part + 1) * 2 * width
                ].reshape(2, width, 2 * width)

    even, odd = rows_refs[:2], rows_refs[2:]

    @pl.when(step == 0)
    def _():
        for span in range(2):
            for copy in copies(span):
                copy.start()
        for copy in copies(0):
            copy.wait()
        gather(0, *even)
        for copy in copies(1):
            copy.wait()

    gather(2 * step + 1, *odd)
    multiply(0, *even)
    gather(jnp.minimum(2 * step + 2, bands - 1), *even)
    multiply(1, *odd)


def correlate_tiles(place, tables, pieces, starts, width, first, count, bands, earlier):
    left_select, _, weight = tables
    tiles = weight.shape[0]
    whole = pl.BlockSpec(memory_space=pltpu.VMEM)
    more = [] if earlier is None else [earlier]
    rows = [
        pltpu.VMEM((tiles * width, 4 * LANES), jnp.bfloat16),
        pltpu.VMEM((tiles, 2 * LANES, 2 * width), jnp.bfloat16),
    ]
    return pl.pallas_call(
        lambda *refs: correlate_kernel(starts, width, *refs),
        grid=(count // 2,),
        out_shape=jax.ShapeDtypeStruct((tiles, bands, 2, 2, width, 2 * width), jnp.float32),
        in_specs=[pl.BlockSpec(memory_space=pltpu.SMEM)]
        + [whole] * len(tables)
        + [pl.BlockSpec(memory_space=pl.ANY)] * (len(pieces) + len(more)),
        out_specs=pl.BlockSpec(
            (tiles, 2, 2, 2, width, 2 * width), lambda g: (0, g + first // 2, 0, 0, 0, 0)
        ),
        scratch_shapes=[
            pltpu.VMEM((2, left_select.shape[1] // ROWS, count, 2, ROWS, LANES), jnp.bfloat16),
            *rows,
            *rows,
            pltpu.SemaphoreType.DMA((2, len(pieces))),
        ],
        input_output_aliases={1 + len(tables) + len(pieces): 0} if more else {},
        compiler_params=pltpu.CompilerParams(vmem_limit_bytes=32 * 2**20),
        cost_estimate=pl.CostEstimate(
            flops=13 * 10**9 * count // bands,
            bytes_accessed=42 * 2**20 * count // bands,
            transcendentals=0,
        ),
        name="correlate",
    )(place, *tables, *pieces, *more)


def tile_tables(tile_a, tile_b, tile_owner, tile_flags, row_of):
    tiles = tile_owner.shape[0]
    held = tile_owner == lax.axis_index("pol")
    order = jnp.arange(tiles, dtype=jnp.int32)
    rank = jnp.sum((held[None, :] & (order[None, :] < order[:, None])).astype(jnp.int32), axis=1)
    slots = jnp.arange(CAP, dtype=jnp.int32)
    pick = (held[None, :] & (rank[None, :] == slots[:, None])).astype(jnp.int32)
    sides = jnp.stack([row_of(tile_a), row_of(tile_b)], axis=1) + 1
    rows = jnp.sum(pick[:, :, None, None] * sides[None], axis=1) - 1
    flags = jnp.sum(pick[:, :, None] * tile_flags[None], axis=1).astype(jnp.float32)
    return rows, flags


def on_device_chunks(voltages, taps_filter, tile_a, tile_b, tile_owner, tile_flags):
    length = taps_filter.shape[1]
    stations = voltages.shape[2]
    frames = voltages.shape[3] // length
    chan_count, time_count = lax.axis_size("chan"), lax.axis_size("tm")
    owners = chan_count * time_count
    chunk_count = stations // (time_count * ROWS)
    width = tile_a.shape[1]
    bands = length // AVG // owners
    tables = fourier_tables(length)

    chan, tm = lax.axis_index("chan"), lax.axis_index("tm")
    place = jnp.stack([chan, tm, lax.axis_index("pol")]).astype(jnp.int32)

    def row_of(station):
        column, rest = station // stations, station % stations
        block, inside = rest // (chunk_count * ROWS), rest % (chunk_count * ROWS)
        across = (chan - column) % chan_count
        behind = (tm - block) % time_count
        piece = behind * chan_count + across
        return ((inside // ROWS) * owners + piece) * ROWS + inside % ROWS

    rows, flags = tile_tables(tile_a, tile_b, tile_owner, tile_flags, row_of)
    total_rows = chunk_count * owners * ROWS
    station_rows = jnp.arange(total_rows, dtype=jnp.int32)
    left_rows = rows[:, 0].reshape(-1)
    left_select = (left_rows[:, None] == station_rows).astype(jnp.bfloat16)
    right_rows = rows[:, 1].reshape(CAP // 2, 2, width)
    right_rows = jnp.stack([right_rows, right_rows[:, ::-1]]).reshape(2, 1, -1)
    right_select = (right_rows == station_rows[:, None]).astype(jnp.bfloat16)
    depth = AVG * time_count * frames
    weight = jnp.tile(flags * (1.0 / depth), (1, 2 * AVG))
    tables_of_tiles = [left_select, right_select, weight]

    samples = voltages.reshape(2, stations, frames * length)

    def travel(value, axes, distances):
        sizes = [lax.axis_size(axis) for axis in axes]
        pairs = []
        for index in np.ndindex(*sizes):
            target = [(i + d) % n for i, d, n in zip(index, distances, sizes)]
            pairs.append(tuple(int(np.ravel_multi_index(x, sizes)) for x in (index, target)))
        return lax.ppermute(value, axes, pairs)

    def after(values, earlier):
        return lax.optimization_barrier((list(values), list(earlier)))

    def block_for(values, chunk, distance):
        first = ((tm + distance) % time_count * chunk_count + chunk) * ROWS
        return lax.dynamic_slice(values, (0, first, 0), (2, ROWS, frames * length))

    def filtered(chunk, arrived, plan):
        return channelise(
            place, chunk, samples, arrived, taps_filter, tables, frames, chan_count, plan
        )

    def over(value, across, along):
        return travel(value, ("chan", "tm"), (across, along))

    def columns(near, far):
        return jnp.stack([near, far])

    cut = bands * 5 // 8
    rest = bands - cut
    pairs = [(x, z) for z in range(time_count) for x in range(chan_count)]
    early_pairs = [(x, z) for z in (1, 3) for x in range(2)]
    late_pairs = [(0, 2), (1, 2), (1, 0)]

    (one,), (values,) = after([block_for(samples, 0, 1)], [samples])
    two, three = (block_for(values, 0, distance) for distance in (2, 3))
    one, two = over(one, 0, 1), over(two, 0, 2)
    (three,), (one,) = after([three], [one])
    three = over(three, 0, 3)
    blocks = [block_for(values, 1, distance) for distance in (1, 2, 3)]
    blocks[:1], (two,) = after(blocks[:1], [two])
    blocks[2:], (three,) = after(blocks[2:], [three])
    first = [one, two, three]
    one, three = over(blocks[0], 0, 1), over(blocks[2], 0, 3)
    (two,), (one,) = after(blocks[1:2], [one])
    second = [one, over(two, 0, 2), three]

    plan = [[(x, z, 0, bands)] for x, z in pairs]
    early = dict(zip(pairs, filtered(0, first, plan)))
    blocks, held = after([early[p] for p in early_pairs], [second[1], *tables_of_tiles])
    second[1], tables_of_tiles = held[0], held[1:]
    early.update((p, over(block, *p)) for p, block in zip(early_pairs, blocks))
    spans = [(0, cut), (cut, bands)]
    hops = [1, 2, 3]
    plan = [[(0, z, *span) for span in spans for z in range(time_count)]]
    plan += [[(1, z, *span) for span in spans for z in hops], [(1, 0, *span) for span in spans]]
    near, far, home = filtered(1, second, plan)
    blocks, (near,) = after([early[p] for p in late_pairs], [near])
    early.update((p, over(block, *p)) for p, block in zip(late_pairs, blocks))
    (far,), held = after([far], [early[p] for p in early_pairs[:4]])
    early.update(zip(early_pairs[:4], held))
    far = over(far, 1, 0)
    def mix(start, index, other_start, other, count):
        first, second = start + index * count, other_start + index * count
        return columns(near[first : first + count], other[second : second + count])

    blocks = {z: mix(0, z, -cut, far, cut) for z in hops}
    order = [2, 1, 3]
    values, held = after([blocks[z] for z in order], [early[p] for p in late_pairs[:1]])
    early.update(zip(late_pairs[:1], held))
    two, one, three = (over(value, 0, z) for value, z in zip(values, order))
    (home,), (one,) = after([home], [one])
    home = over(home, 1, 0)
    low = [mix(0, 0, 0, home, cut), one, two, three]
    high = [mix(time_count * cut, 0, cut, home, rest)]
    high += [mix(time_count * cut, z, 3 * cut - rest, far, rest) for z in hops]

    def with_other(values):
        return [side for v in values for side in (v, travel(v, ("pol",), (1,)))]

    early = with_other([jnp.stack([early[p] for p in pairs])])
    blocks, held = after(high[1:], [low[2], low[1], early[1]])
    low[2], low[1], early[1] = held
    moved = {z: over(blocks[z - 1], 0, z) for z in (2, 1, 3)}
    high = [high[0]] + [moved[z] for z in (1, 2, 3)]
    low = jnp.stack(low).reshape(2 * time_count, cut, 2, ROWS, LANES)
    visibility = correlate_tiles(
        place, tables_of_tiles, early + with_other([low]),
        [0, 0], width, 0, cut, bands, None,
    )
    high, (visibility,) = after(high, [visibility])
    high = jnp.stack(high).reshape(2 * time_count, rest, 2, ROWS, LANES)
    return correlate_tiles(
        place, tables_of_tiles, early + with_other([high]),
        [cut, 0], width, cut, rest, bands, visibility,
    )


def on_device(voltages, taps_filter, tile_a, tile_b, tile_owner, tile_flags):
    taps, length = taps_filter.shape
    frames = voltages.shape[3] // length
    time_count = lax.axis_size("tm")
    fits = (
        length == RADIX * LANES
        and AVG * time_count * frames == LANES
        and 2 * tile_a.shape[1] == LANES
        and voltages.shape[2] == 2 * time_count * ROWS
        and (lax.axis_size("chan"), time_count) == (2, 4)
    )
    form = on_device_chunks if fits else on_device_any
    return form(voltages, taps_filter, tile_a, tile_b, tile_owner, tile_flags)


def solution(mesh):
    return jax.shard_map(
        on_device,
        mesh=mesh,
        in_specs=(P("grp", "pol", "chan", "tm"), P(), P(), P(), P(), P()),
        out_specs=P("pol", ("chan", "tm"), "grp", None, None, None),
        check_vma=False,
    )
```
